32 devices in a mesh: sec: 2 (over core), blk: 16 (over z, y, x).
Axes of the slice: x: 2, y: 2, z: 4, core: 2. Of those that a mesh axis runs over, the one named last changes fastest.
Arguments:
- atm_state: float32 [4, 72, 131072], P(None, None, ('sec', 'blk')), may hold values from -6 to 6
- atm_surface: float32 [4, 131072], P(None, ('sec', 'blk')), may hold values from -6 to 6
- bulk_coef: float32 [4, 131072], P(None, ('sec', 'blk')), may hold values from 0.05 to 0.5
- atm_nbr: int32 [6, 131072], P(None, ('sec', 'blk')), may hold values from 0 to 4607, as said below
- atm_nbr_coef: float32 [6, 131072], P(None, ('sec', 'blk')), may hold values from 0.02 to 0.15
- atm_mix: float32 [72, 72], replicated, may hold values from -0.375 to 0.375
- ocean_state: float32 [4, 80, 131072], P(None, None, ('sec', 'blk')), may hold values from -6 to 6
- ocean_nbr: int32 [6, 131072], P(None, ('sec', 'blk')), may hold values from 0 to 4863, as said below
- ocean_nbr_coef: float32 [6, 131072], P(None, ('sec', 'blk')), may hold values from 0.02 to 0.15
- ocean_mix: float32 [80, 80], replicated, may hold values from -0.3125 to 0.3125
- send_cols: int32 [32, 32, 512], P(('sec', 'blk')), may hold values from 0 to 4095
- remap_slot: int32 [4, 131072], P(None, ('sec', 'blk')), may hold values from 0 to 16383, as said below
- remap_weight: float32 [4, 131072], P(None, ('sec', 'blk')), may hold values from 0.05 to 0.5
Outputs:
- atm_final: float32 [4, 72, 131072], P(None, None, ('sec', 'blk'))
- ocean_final: float32 [4, 80, 131072], P(None, None, ('sec', 'blk'))
- surface_temp: float32 [131072], P(('sec', 'blk'))
The draws below stay inside these ranges and needn't reach their ends.
Inputs may be any that keep to these rules, and one draw needn't show every extreme that they name: `atm_nbr`: entry [k, i] is the position of column i's k-th neighbour among the device's columns extended by 256 columns on each side from the neighbouring devices along the block order, wrapping around; it lies within 256 positions of the column and is never the column itself. `ocean_nbr`: entry [k, j] is the position of cell j's k-th neighbour among the device's cells extended by 384 cells on each side from the neighbouring devices along the block order, wrapping around; it lies within 384 positions of the cell and is never the cell itself. `remap_slot`: entry p * 512 + c names slot c of the list that atmosphere block p sends to the block of the ocean cell; each ocean block reads some slot from every atmosphere block.
All inputs are finite; a program needn't handle non-finite values.
Results may differ from the reference program's by a relative error of at most 0.0001.
Values sent between devices are 32-bit elements; how exact they have to be, the bound alone decides.
No kernel may reach another device: no remote copies, remote signals or barrier semaphores. Data moves between devices by JAX's collectives and lax.ppermute only.
A program may use at most 256 MiB of HBM per device.

```python
import math
import jax
import jax.numpy as jnp
from jax import lax

FIELDS = 4
LA = 72
LO = 80
NBRS = 6
SRCS = 4
ASTEPS = 4
HA = 256
HO = 384
A_DEV = 4096
O_DEV = 4096
TA = 131072
TO = 131072
CAP = 512
DEVICES = 32


def neighbor_lists(key, cols_dev, width, total):
    key_size, key_sign = jax.random.split(key)
    position = jnp.arange(total, dtype=jnp.int32) % cols_dev
    magnitude = jax.random.randint(key_size, (NBRS, total), 1, width + 1)
    sign_pick = jax.random.randint(key_sign, (NBRS, total), 0, 2) * 2 - 1
    offset = magnitude * sign_pick
    first_row = (jnp.arange(NBRS, dtype=jnp.int32) == 0)[:, None]
    offset = jnp.where(first_row & (position == 0)[None, :], -width, offset)
    offset = jnp.where(first_row & (position == cols_dev - 1)[None, :], width, offset)
    return (width + position[None, :] + offset).astype(jnp.int32)


def draw_atm_nbr(key, part):
    key = jax.random.fold_in(key, 3)
    return neighbor_lists(key, A_DEV, HA, TA)


def draw_ocean_nbr(key, part):
    key = jax.random.fold_in(key, 7)
    return neighbor_lists(key, O_DEV, HO, TO)


def draw_remap_slot(key, part):
    key = jax.random.fold_in(key, 11)
    key_count, key_peer, key_slot = jax.random.split(key, 3)
    cells = jnp.arange(TO, dtype=jnp.int32)
    owner = cells // O_DEV
    link = (cells % O_DEV)[None, :] * SRCS + jnp.arange(SRCS, dtype=jnp.int32)[:, None]
    devices_row = jnp.arange(DEVICES, dtype=jnp.int32)
    counts = jax.random.randint(key_count, (DEVICES, DEVICES), 1, CAP + 1)
    partner = (devices_row + DEVICES // 2) % DEVICES
    counts = jnp.where(devices_row[None, :] == partner[:, None], CAP, counts)
    random_peer = jax.random.randint(key_peer, (SRCS, TO), 0, DEVICES)
    peer = jnp.where(link < DEVICES, link, random_peer)
    live = counts[jnp.broadcast_to(owner[None, :], (SRCS, TO)), peer]
    raw = jax.random.randint(key_slot, (SRCS, TO), 0, 1 << 20)
    slot = jnp.where(link < DEVICES, live - 1, raw % live)
    return (peer * CAP + slot).astype(jnp.int32)


def set_ends(values, key, smallest, high):
    longest = values.shape.index(max(values.shape))
    spots = []
    for shift in (0, 1):
        where = [jax.random.randint(jax.random.fold_in(key, axis), (), 0, length) for axis, length in enumerate(values.shape)]
        where[longest] = (where[longest] + shift) % values.shape[longest]
        spots.append(tuple(where))
    return values.at[spots[0]].set(smallest).at[spots[1]].set(high)


def level_of(rng, extent, shards, smallest, high):
    factor_of, own = 1.0, jax.random.fold_in(rng, 6)
    for dim, blocks in shards:
        draws = jnp.exp(jax.random.uniform(jax.random.fold_in(own, dim), (blocks,), jnp.float32, smallest / len(shards), high / len(shards)))
        factor_of = factor_of * jnp.repeat(draws, extent[dim] // blocks).reshape([-1 if axis == dim else 1 for axis in range(len(extent))])
    return factor_of


def noise(key, dims, scale, limit, pieces=(), held_as=jnp.bfloat16):
    entries = jax.random.normal(key, dims, jnp.float32) * scale
    if len(pieces) > 0:
        entries = level_of(key, dims, pieces, -0.22, 0.18) * entries
    return jnp.clip(entries, min=-limit, max=limit).astype(held_as)


def setup_inputs(seed: int = 0) -> dict:
    key_of = jax.random.split(jax.random.key(seed), 14)
    return {
        "atm_state": noise(key_of[0], (FIELDS, LA, TA), 1.0, 6.0, ((2, 32),), jnp.float32),
        "atm_surface": noise(key_of[1], (FIELDS, TA), 1.0, 6.0, ((1, 32),), jnp.float32),
        "bulk_coef": jnp.clip(jnp.exp(math.log(0.5) - 2.3025851 * jax.random.uniform(key_of[2], (FIELDS, TA), jnp.float32) ** level_of(key_of[2], (FIELDS, TA), ((1, 32),), -0.2, 0.2)), 0.05, 0.5),
        "atm_nbr": draw_atm_nbr(jax.random.fold_in(key_of[13], 71), 0),
        "atm_nbr_coef": jnp.clip(jnp.exp(math.log(0.15) - 2.014903 * jax.random.uniform(key_of[4], (NBRS, TA), jnp.float32) ** level_of(key_of[4], (NBRS, TA), ((1, 32),), -0.2, 0.2)), 0.02, 0.15),
        "atm_mix": noise(key_of[5], (LA, LA), (4 * LA) ** -0.5, 0.375, (), jnp.float32),
        "ocean_state": noise(key_of[6], (FIELDS, LO, TO), 1.0, 6.0, ((2, 32),), jnp.float32),
        "ocean_nbr": draw_ocean_nbr(jax.random.fold_in(key_of[13], 71), 0),
        "ocean_nbr_coef": jnp.clip(jnp.exp(math.log(0.15) - 2.014903 * jax.random.uniform(key_of[8], (NBRS, TO), jnp.float32) ** level_of(key_of[8], (NBRS, TO), ((1, 32),), -0.2, 0.2)), 0.02, 0.15),
        "ocean_mix": noise(key_of[9], (LO, LO), (4 * LO) ** -0.5, 0.3125, (), jnp.float32),
        "send_cols": set_ends(jax.random.randint(key_of[10], (DEVICES, DEVICES, CAP), 0, A_DEV), jax.random.fold_in(key_of[10], 1), 0, A_DEV - 1).astype(jnp.int32),
        "remap_slot": draw_remap_slot(jax.random.fold_in(key_of[13], 71), 0),
        "remap_weight": jnp.clip(0.05 + 0.45 * jax.random.uniform(key_of[12], (SRCS, TO), jnp.float32) ** level_of(key_of[12], (SRCS, TO), ((1, 32),), -0.2, 0.2), 0.05, 0.5),
    }


def column_mix(mixing, fields_now):
    return fields_now + jnp.einsum("lm,fmc->flc", mixing, fields_now, precision=lax.Precision.HIGHEST)


def lateral(fields_now, neighbors, weights):
    change = jnp.zeros_like(fields_now)
    for which in range(neighbors.shape[0]):
        change = change + weights[which] * (jnp.take(fields_now, neighbors[which], axis=2) - fields_now)
    return fields_now + change


def reference(atm_state, atm_surface, bulk_coef, atm_nbr, atm_nbr_coef, atm_mix, ocean_state, ocean_nbr, ocean_nbr_coef, ocean_mix, send_cols, remap_slot, remap_weight):
    atm_cols = jnp.arange(TA, dtype=jnp.int32)
    atm_global = ((atm_cols // A_DEV) * A_DEV)[None, :] + atm_nbr - HA
    atm_global = (atm_global % TA).astype(jnp.int32)
    ocean_cols = jnp.arange(TO, dtype=jnp.int32)
    ocean_global = ((ocean_cols // O_DEV) * O_DEV)[None, :] + ocean_nbr - HO
    ocean_global = (ocean_global % TO).astype(jnp.int32)
    fields_now = atm_state
    fluxes = jnp.zeros((FIELDS, TA), jnp.float32)
    for repeat in range(ASTEPS):
        mixed = lateral(fields_now, atm_global, atm_nbr_coef)
        fluxes = bulk_coef * (atm_surface - mixed[:, -1, :])
        mixed = mixed.at[:, -1, :].add(fluxes)
        fields_now = column_mix(atm_mix, mixed)
    source = (jnp.arange(DEVICES, dtype=jnp.int32) * A_DEV)[:, None, None] + send_cols
    source = source.reshape(-1).astype(jnp.int32)
    values = jnp.take(fluxes, source, axis=1).reshape(FIELDS, DEVICES, DEVICES, CAP)
    values = jnp.transpose(values, (0, 2, 1, 3)).reshape(FIELDS, DEVICES * DEVICES * CAP)
    owner = ocean_cols // O_DEV
    slot_global = (owner * (DEVICES * CAP))[None, :] + remap_slot
    slot_global = slot_global.astype(jnp.int32)
    ocean_flux = jnp.zeros((FIELDS, TO), jnp.float32)
    for which in range(SRCS):
        ocean_flux = ocean_flux + remap_weight[which] * jnp.take(values, slot_global[which], axis=1)
    mixed = lateral(ocean_state, ocean_global, ocean_nbr_coef)
    mixed = mixed.at[:, 0, :].add(ocean_flux)
    ocean_final = column_mix(ocean_mix, mixed)
    sea_surface = ocean_final[0, 0, :]
    slot_ids = slot_global.reshape(-1)
    total_slots = DEVICES * DEVICES * CAP
    back_value = jax.ops.segment_sum((remap_weight * sea_surface[None, :]).reshape(-1), slot_ids, total_slots)
    back_weight = jax.ops.segment_sum(remap_weight.reshape(-1), slot_ids, total_slots)
    back_value = jnp.transpose(back_value.reshape(DEVICES, DEVICES, CAP), (1, 0, 2)).reshape(-1)
    back_weight = jnp.transpose(back_weight.reshape(DEVICES, DEVICES, CAP), (1, 0, 2)).reshape(-1)
    gathered_temp = jax.ops.segment_sum(back_value, source, TA)
    gathered_weight = jax.ops.segment_sum(back_weight, source, TA)
    surface_temp = (atm_surface[0] + gathered_temp) / (1.0 + gathered_weight)
    return fields_now, ocean_final, surface_temp
```

```python
import numpy as np

import jax
import jax.numpy as jnp
from jax import lax
from jax.experimental import pallas as pl
from jax.experimental.pallas import tpu as pltpu
from jax.sharding import PartitionSpec as P

ASTEPS = 4
HA = 256
HO = 384
BLK = 256
WIDE = ASTEPS * HA
BF = jnp.bfloat16
F32 = jnp.float32
VMEM_BYTES = 56 * 1024 * 1024
AXES = ("sec", "blk")


def call(body, outs, *, in_specs=None, out_specs=None, scratch=(), flops=0, moved=0, aliases=None):
    vmem = pl.BlockSpec(memory_space=pltpu.VMEM)
    return pl.pallas_call(
        body,
        out_shape=outs,
        in_specs=in_specs,
        out_specs=jax.tree.map(lambda _: vmem, outs) if out_specs is None else out_specs,
        scratch_shapes=list(scratch),
        input_output_aliases=aliases or {},
        compiler_params=pltpu.CompilerParams(vmem_limit_bytes=VMEM_BYTES),
        cost_estimate=pl.CostEstimate(flops=flops, bytes_accessed=moved, transcendentals=0),
    )


def shape(dims, dtype=F32):
    return jax.ShapeDtypeStruct(dims, dtype)


def halves(x):
    high = x.astype(BF)
    return high, (x - high.astype(F32)).astype(BF)


def stacked(x):
    return jnp.concatenate(halves(x), axis=0)


def mm(a, b):
    return jnp.dot(a, b, preferred_element_type=F32)


def mm_t(a, b):
    return lax.dot_general(a, b, (((1,), (1,)), ((), ())), preferred_element_type=F32)


def product(x2, w2):
    rows = x2.shape[0] // 2
    wide = mm(x2, w2[0])
    return wide[:rows] + wide[rows:] + mm(x2[:rows], w2[1])


def iota(dims, axis):
    return lax.broadcasted_iota(jnp.int32, dims, axis)


def build_band(store, nbr, coef, halo):
    rows = BLK + 2 * halo
    count = nbr.shape[0]
    ids = [nbr[k : k + 1] for k in range(count)]
    cs = [coef[k : k + 1] for k in range(count)]
    rest = 1.0 - sum(cs[1:], cs[0])
    for k in range(count - 1, 0, -1):
        alive = jnp.ones_like(ids[k]) > 0
        for j in range(k):
            same = jnp.logical_and(ids[k] == ids[j], alive)
            cs[j] = cs[j] + jnp.where(same, cs[k], 0.0)
            alive = jnp.logical_and(alive, jnp.logical_not(same))
        ids[k] = jnp.where(alive, ids[k], -1)
    lanes = 128
    step = 16
    for half in range(BLK // lanes):
        at = slice(half * lanes, (half + 1) * lanes)
        wide_ids = [jnp.broadcast_to(i[:, at], (step, lanes)) for i in ids]
        wide_cs = [jnp.broadcast_to(c[:, at], (step, lanes)) for c in cs]
        own = iota((step, lanes), 1) + (half * lanes + halo)
        wide_rest = jnp.broadcast_to(rest[:, at], (step, lanes))
        base = iota((step, lanes), 0)
        for first in range(0, rows, step):
            if first + step <= half * lanes or first >= half * lanes + lanes + 2 * halo:
                zero = jnp.zeros((step, lanes), BF)
                store(first, step, at, zero, zero)
                continue
            here = base + first
            value = jnp.where(here == own, wide_rest, 0.0)
            for i, c in zip(wide_ids, wide_cs):
                value = jnp.where(here == i, c, value)
            store(first, step, at, *halves(value))


def one_hot(ids, rows):
    return jnp.where(iota((rows, ids.shape[1]), 0) == ids, 1.0, 0.0).astype(BF)


def fold_rows(x, height):
    total = x[:height]
    for first in range(height, x.shape[0], height):
        total = total + x[first : first + height]
    return total


def prepare_kernel(fields):
    def body(mix, omix, atm, sea, nbr, coef, bulk, surf, spread, code, y, yo, first, last, gains, vertical):
        la = mix.shape[0]
        columns = atm.shape[1]
        eye = iota((la, la), 0) == iota((la, la), 1)
        step = mix[...] + jnp.where(eye, 1.0, 0.0)

        def dot(a, b):
            return jnp.dot(a, b, precision=lax.Precision.HIGHEST, preferred_element_type=F32)

        def col(r, same):
            return jnp.sum(jnp.where(same, r, 0.0), axis=1, keepdims=True)

        def row(c, same):
            return jnp.sum(jnp.where(same, c, 0.0), axis=0, keepdims=True)

        twice = dot(step, step)
        fourth = dot(twice, twice)
        rows_up = [step[la - 1 : la, :]]
        cols_up = [step[:, la - 1 : la]]
        for _ in range(ASTEPS - 2):
            rows_up.append(jnp.sum(step * col(rows_up[-1], eye), axis=0, keepdims=True))
        for _ in range(ASTEPS - 1):
            cols_up.append(jnp.sum(step * row(cols_up[-1], eye), axis=1, keepdims=True))
        slot = iota((fields * ASTEPS, 128), 0) // fields
        lane = iota((fields * ASTEPS, 128), 1)
        value = jnp.zeros((fields * ASTEPS, 128), F32)
        for s in range(1, ASTEPS + 1):
            column = jnp.where(slot == s - 1, 1.0, 0.0)
            for j in range(1, ASTEPS):
                column = jnp.where(slot == s - 1 + j, rows_up[j - 1][:, la - 1 : la], column)
            value = jnp.where(lane == s - 1, column, value)
        gains[...] = value

        tall = jnp.concatenate([fourth] * fields, axis=0)
        spreaded = dot(tall, spread[...])
        filled = jnp.where(code[...] == 1, spreaded, 0.0)
        for m in range(ASTEPS):
            tall = jnp.concatenate([cols_up[ASTEPS - 1 - m]] * fields, axis=0)
            filled = jnp.where(code[...] == 2 + m, tall, filled)
        vertical[...] = stacked(filled)

        weights = [jnp.broadcast_to(col(r, eye), (la, 128)) for r in rows_up]
        lo = omix.shape[0]
        sea_eye = iota((lo, lo), 0) == iota((lo, lo), 1)
        sea_row = omix[0:1, :] + jnp.where(iota((1, lo), 1) == 0, 1.0, 0.0)
        sea_weight = jnp.broadcast_to(col(sea_row, sea_eye), (lo, 128))
        for start in range(0, columns, 128):
            at = slice(start, start + 128)
            for f in range(fields):
                x = atm[f * la : (f + 1) * la, at]
                y[f : f + 1, at] = x[la - 1 : la]
                for k in range(1, ASTEPS):
                    y[k * fields + f : k * fields + f + 1, at] = jnp.sum(
                        x * weights[k - 1], axis=0, keepdims=True
                    )
            yo[:, at] = jnp.sum(sea[:, at] * sea_weight, axis=0, keepdims=True)
        for target, at in ((first, slice(0, WIDE)), (last, slice(columns - WIDE, columns))):
            target[0:16, :] = y[:, at]
            target[16:22, :] = nbr[:, at].astype(F32)
            target[22:28, :] = coef[:, at]
            target[28:32, :] = bulk[:, at]
            target[32:36, :] = surf[:, at]
            target[36:37, :] = yo[:, at]
            target[37:40, :] = jnp.zeros((3, WIDE), F32)

    return body


def interior_kernel(atm, nbr, coef, band, kept, mid, w, sa, sb, sems):
    blocks = atm.shape[1] // BLK

    def out_copy(b):
        return pltpu.make_async_copy(w.at[b], band.at[b + ASTEPS - 1], sems.at[b])

    def build(b, _):
        at = pl.ds(pl.multiple_of(b * BLK, BLK), BLK)

        def store(first, step, lanes, high, low):
            w[b, 0, first : first + step, lanes] = high
            w[b, 1, first : first + step, lanes] = low

        build_band(store, nbr[:, at] - b * BLK, coef[:, at], HA)
        sa[b] = stacked(atm[:, at])
        out_copy(b).start()
        return 0

    lax.fori_loop(0, blocks, build, 0)

    def advance(source, target, shift):
        def one(b, _):
            x2 = jnp.concatenate([source[b - 1], source[b], source[b + 1]], axis=1)
            target[b - shift] = stacked(product(x2, (w[b, 0], w[b, 1])))
            return 0

        return one

    buffers = (sa, sb)
    for s in range(1, ASTEPS + 1):
        source = buffers[(s - 1) % 2]
        if s == ASTEPS:
            lax.fori_loop(s, blocks - s, advance(source, mid, s), 0)
        else:
            target = buffers[s % 2]
            lax.fori_loop(s, blocks - s, advance(source, target, 0), 0)
            for i, b in enumerate((s, s + 1, blocks - 2 - s, blocks - 1 - s)):
                kept[(s - 1) * 4 + i] = target[b]

    def finish(b, _):
        out_copy(b).wait()
        return 0

    lax.fori_loop(0, blocks, finish, 0)


def surface_kernel(y, before, after, bulk, surf, gains, band_in, band, q, w, sa, sb, bulks, surfs, tmp, sems):
    blocks = y.shape[1] // BLK
    columns = y.shape[1]
    fields = bulk.shape[0]
    total = blocks + 2 * ASTEPS

    def in_copy(b):
        return pltpu.make_async_copy(band_in.at[b], w.at[b], sems.at[b])

    def start(b, _):
        in_copy(b).start()
        return 0

    lax.fori_loop(ASTEPS - 1, ASTEPS - 1 + blocks, start, 0)

    halo_blocks = list(range(ASTEPS)) + list(range(ASTEPS + blocks, total))
    outs = []
    for e in halo_blocks:
        pack = before if e < ASTEPS else after
        local = e if e < ASTEPS else e - ASTEPS - blocks
        at = slice(local * BLK, (local + 1) * BLK)
        sa[e] = stacked(pack[0:16, at])
        bulks[e] = jnp.concatenate([pack[28:32, at]] * ASTEPS, axis=0)
        surfs[e] = jnp.concatenate([pack[32:36, at]] * ASTEPS, axis=0)
        if e in (0, total - 1):
            continue
        origin = local * BLK + (columns - WIDE if e < ASTEPS else 0)

        def store(first, step, lanes, high, low, e=e):
            tmp[0, first : first + step, lanes] = high
            tmp[1, first : first + step, lanes] = low

        build_band(store, pack[16:22, at].astype(jnp.int32) - origin, pack[22:28, at], HA)
        w[e - 1] = tmp[...]
        copy = pltpu.make_async_copy(w.at[e - 1], band.at[e - 1], sems.at[e - 1])
        copy.start()
        outs.append(copy)
    for e in range(ASTEPS, ASTEPS + blocks):
        at = slice((e - ASTEPS) * BLK, (e - ASTEPS + 1) * BLK)
        sa[e] = stacked(y[:, at])
        bulks[e] = jnp.concatenate([bulk[:, at]] * ASTEPS, axis=0)
        surfs[e] = jnp.concatenate([surf[:, at]] * ASTEPS, axis=0)

    slot = iota((fields * ASTEPS, BLK), 0) // fields
    buffers = (sa, sb)
    for s in range(1, ASTEPS + 1):
        source, target = buffers[(s - 1) % 2], buffers[s % 2]
        gain = gains[:, s - 1 : s]
        kept = jnp.where(slot == s - 1, 0.0, 1.0)

        def one(e, s=s, source=source, target=target, gain=gain, kept=kept):
            x2 = jnp.concatenate([source[e - 1], source[e], source[e + 1]], axis=1)
            moved = product(x2, (w[e - 1, 0], w[e - 1, 1]))
            lowest = jnp.concatenate([moved[(s - 1) * fields : s * fields]] * ASTEPS, axis=0)
            flux = bulks[e] * (surfs[e] - lowest)
            value = moved * kept + gain * flux
            if s == ASTEPS:
                q[e - ASTEPS] = value
            else:
                target[e] = stacked(value)

        def own(e, _, s=s, one=one):
            if s == 1:
                in_copy(e - 1).wait()
            one(e)
            return 0

        for e in list(range(s, ASTEPS)) + list(range(ASTEPS + blocks, total - s)):
            one(e)
        lax.fori_loop(ASTEPS, ASTEPS + blocks, own, 0, unroll=2)
    for copy in outs:
        copy.wait()


def send_kernel(q, cols, out, table):
    fields = q.shape[1] // ASTEPS
    peers, slots = cols.shape
    blocks = q.shape[0]
    lanes = out.shape[2]
    parts = slots // lanes
    for b in range(blocks):
        table[b * fields : (b + 1) * fields, :] = q[b, (ASTEPS - 1) * fields :, :]
    rows = stacked(table[...])
    half = blocks * fields
    block_of_row = iota((half, slots), 0) // fields

    def one(p, _):
        ids = cols[pl.ds(p, 1), :]
        got = mm(rows, one_hot(ids & (BLK - 1), BLK))
        got = jnp.where(block_of_row == ids // BLK, got[:half] + got[half:], 0.0)
        got = fold_rows(got, 2 * fields)
        got = got[:fields] + got[fields:]
        out[p] = jnp.concatenate([got[:, i * lanes : (i + 1) * lanes] for i in range(parts)], axis=0)
        return 0

    lax.fori_loop(0, peers, one, 0, unroll=4)


def exchange_kernel(recv, slot, weight, yo, before, after, nbr, coef, omix, flux_out, back, rows, tiles, acc):
    peers, per_peer, lanes = recv.shape
    links, columns = slot.shape
    fields = flux_out.shape[0]
    parts = per_peer // fields
    highs = peers * parts
    table = highs * fields
    rows[...] = stacked(recv[...].reshape(table, lanes))
    acc[...] = jnp.zeros_like(acc)
    side = HO // 128
    own_tiles = columns // 128
    for t in range(own_tiles + 2 * side):
        if t < side:
            line = before[36:37, WIDE - HO + t * 128 : WIDE - HO + (t + 1) * 128]
        elif t < side + own_tiles:
            line = yo[:, (t - side) * 128 : (t - side + 1) * 128]
        else:
            line = after[36:37, (t - side - own_tiles) * 128 : (t - side - own_tiles + 1) * 128]
        tiles[t] = jnp.broadcast_to(line, (8, 128))
    corner = omix[0:1, 0:1] + 1.0
    high_of_row = iota((table, BLK), 0) // fields
    back_rows = iota((2 * highs, BLK), 0)
    inner = back_rows % (2 * parts)
    back_high = (back_rows // (2 * parts)) * parts + inner % parts
    pattern = iota((8, BLK), 0) % (2 * parts) // parts
    window = 1 + 2 * side
    neighbors = nbr.shape[0]

    def surface(j, half):
        t0 = j * (BLK // 128) + half
        at = pl.ds(pl.multiple_of(t0 * 128, 128), 128)
        pad = jnp.zeros((8 - neighbors, 128), jnp.int32)
        ids = jnp.concatenate([nbr[:, at] - t0 * 128, pad], axis=0)
        cs = jnp.concatenate([coef[:, at], pad.astype(F32)], axis=0)
        middle = tiles[t0 + side]
        got = jnp.zeros((8, 128), F32)
        for t in range(window):
            pick = jnp.take_along_axis(tiles[t0 + t], ids & 127, axis=1, mode="promise_in_bounds")
            got = jnp.where(ids // 128 == t, pick, got)
        return middle[0:1] + jnp.sum(cs * (got - middle), axis=0, keepdims=True)

    def one(j, _):
        at = pl.ds(pl.multiple_of(j * BLK, BLK), BLK)
        sea = jnp.concatenate([surface(j, h) for h in range(BLK // 128)], axis=1)
        ids = [slot[r : r + 1, at] for r in range(links)]
        ws = [weight[r : r + 1, at] for r in range(links)]
        hots = [one_hot(i & (lanes - 1), lanes) for i in ids]
        flux = jnp.zeros((2 * fields, BLK), F32)
        for r in range(links):
            got = mm(rows[...], hots[r])
            got = jnp.where(high_of_row == ids[r] // lanes, got[:table] + got[table:], 0.0)
            flux = flux + ws[r] * fold_rows(got, 2 * fields)
        flux = flux[:fields] + flux[fields:]
        flux_out[:, at] = flux
        sea = sea + corner * flux[0:1]
        left = []
        for r in range(links):
            both = jnp.where(pattern == 1, ws[r], ws[r] * sea)
            both = jnp.concatenate([both] * (2 * highs // 8), axis=0)
            left.append(stacked(jnp.where(back_high == ids[r] // lanes, both, 0.0)))
        sums = mm_t(jnp.concatenate(left, axis=1), jnp.concatenate(hots, axis=1))
        acc[...] += sums[: 2 * highs] + sums[2 * highs :]
        return 0

    lax.fori_loop(0, columns // BLK, one, 0)
    back[...] = acc[...].reshape(back.shape)


def settle_kernel(back, cols, surf, out, acc):
    peers, per_peer, lanes = back.shape
    parts = per_peer // 2
    blocks = surf.shape[0]
    acc[...] = jnp.zeros_like(acc)
    block_of_row = iota((blocks, lanes), 0)

    def one(d, _):
        left, hots = [], []
        for h in range(parts):
            ids = cols[pl.ds(d, 1), h * lanes : (h + 1) * lanes]
            mask = block_of_row == ids // BLK
            value = jnp.where(mask, back[d, h : h + 1, :], 0.0)
            scale = jnp.where(mask, back[d, parts + h : parts + h + 1, :], 0.0)
            left.append(stacked(jnp.concatenate([value, scale], axis=0)))
            hots.append(one_hot(ids & (BLK - 1), BLK))
        acc[...] += mm_t(jnp.concatenate(left, axis=1), jnp.concatenate(hots, axis=1))
        return 0

    lax.fori_loop(0, peers, one, 0, unroll=4)
    sums = acc[: 2 * blocks] + acc[2 * blocks :]
    out[...] = (surf[...] + sums[:blocks]) / (1.0 + sums[blocks:])


def edge_kernel(before, after, atm, kept, mid, q, vertical, band, out, w, sides, sa, sb, sems):
    blocks = q.shape[0]
    count = 2 * ASTEPS - 1
    total = blocks + 2 * ASTEPS
    copies = []
    for side in range(2):
        at = slice(0, 2 * BLK) if side == 0 else slice((blocks - 2) * BLK, blocks * BLK)
        copy = pltpu.make_async_copy(atm.at[:, at], sides.at[side], sems.at[2 * count + side])
        copy.start()
        copies.append(copy)
    for side in range(2):
        base = 0 if side == 0 else total - 2 - count
        for i in range(count):
            copy = pltpu.make_async_copy(band.at[base + i], w.at[side * count + i], sems.at[side * count + i])
            copy.start()
            copies.append(copy)
    for i in range(ASTEPS):
        at = slice(i * BLK, (i + 1) * BLK)
        sa[i] = stacked(before[:, at])
        sa[6 + 2 + i] = stacked(after[:, at])
    for copy in copies:
        copy.wait()
    for i in range(2):
        at = slice(i * BLK, (i + 1) * BLK)
        sa[ASTEPS + i] = stacked(sides[0, :, at])
        sa[6 + i] = stacked(sides[1, :, at])
    buffers = (sa, sb)
    for s in range(1, ASTEPS + 1):
        source, target = buffers[(s - 1) % 2], buffers[s % 2]
        last = s == ASTEPS

        def one(i, _, s=s, source=source, target=target, last=last):
            for side in range(2):
                base = 6 * side
                k = s - 1 + i if side == 0 else count + ASTEPS - s + i
                x2 = jnp.concatenate([source[base + i + d] for d in range(3)], axis=1)
                value = stacked(product(x2, (w[k, 0], w[k, 1])))
                target[base + i + (2 * side if not last else 0)] = value
            return 0

        lax.fori_loop(0, ASTEPS, one, 0)
        if not last:
            for i in range(2):
                target[ASTEPS + i] = kept[(s - 1) * 4 + i]
                target[6 + i] = kept[(s - 1) * 4 + 2 + i]
    rows = out.shape[0]
    final = buffers[ASTEPS % 2]

    def mixed(source, shift):
        def one(b, _):
            at = pl.ds(pl.multiple_of(b * BLK, BLK), BLK)
            qh, ql = halves(q[b])
            x2 = source[b - shift]
            high = jnp.concatenate([x2[:rows], qh], axis=0)
            low = jnp.concatenate([x2[rows:], ql], axis=0)
            wide = mm(vertical[...], high)
            out[:, at] = wide[:rows] + wide[rows:] + mm(vertical[:rows], low)
            return 0

        return one

    lax.fori_loop(0, ASTEPS, mixed(final, 0), 0)
    lax.fori_loop(ASTEPS, blocks - ASTEPS, mixed(mid, ASTEPS), 0)
    lax.fori_loop(blocks - ASTEPS, blocks, mixed(final, blocks - ASTEPS - 6), 0)


def ocean_kernel(ocean, before, after, nbr, coef, omix, flux, out, x2, w):
    levels = omix.shape[0]
    fields = flux.shape[0]
    columns = ocean.shape[1]
    blocks = columns // BLK
    eye = iota((levels, levels), 0) == iota((levels, levels), 1)
    step = omix[...] + jnp.where(eye, 1.0, 0.0)
    top = jnp.broadcast_to(step[:, 0:1], (levels, BLK))
    mix2 = stacked(step)

    def part(first, width):
        pieces = []
        for ref, begin, size in ((before, -HO, HO), (ocean, 0, columns), (after, columns, HO)):
            lo, hi = max(first, begin), min(first + width, begin + size)
            if lo < hi:
                pieces.append(ref[:, lo - begin : hi - begin])
        return pieces[0] if len(pieces) == 1 else jnp.concatenate(pieces, axis=1)

    for e in range((columns + 2 * HO) // BLK):
        x2[e] = stacked(part(e * BLK - HO, BLK))

    def one(b, _):
        at = pl.ds(pl.multiple_of(b * BLK, BLK), BLK)

        def store(first, size, lanes, high, low):
            w[0, first : first + size, lanes] = high
            w[1, first : first + size, lanes] = low

        build_band(store, nbr[:, at] - b * BLK, coef[:, at], HO)
        source = jnp.concatenate([x2[b + d] for d in range(1 + 2 * HO // BLK)], axis=1)
        moved = product(source, (w[0], w[1]))
        for f in range(fields):
            rows = slice(f * levels, (f + 1) * levels)
            high, low = halves(moved[rows])
            wide = mm(mix2, high)
            out[rows, at] = (
                wide[:levels] + wide[levels:] + mm(mix2[:levels], low) + top * flux[f : f + 1, at]
            )
        return 0

    lax.fori_loop(0, blocks, one, 0)


def after_all(value, *others):
    return lax.optimization_barrier((value, *others))[0]


def per_device(
    atm_state,
    atm_surface,
    bulk_coef,
    atm_nbr,
    atm_nbr_coef,
    atm_mix,
    ocean_state,
    ocean_nbr,
    ocean_nbr_coef,
    ocean_mix,
    send_cols,
    remap_slot,
    remap_weight,
):
    fields, la, columns = atm_state.shape
    lo, cells = ocean_state.shape[1:]
    blocks = columns // BLK
    rows = fields * la
    states = fields * ASTEPS
    picked = send_cols[0]
    peers, slots = picked.shape
    lanes = min(BLK, slots)
    parts = slots // lanes
    atm = atm_state.reshape(rows, columns)
    ocean = ocean_state.reshape(fields * lo, cells)
    depth = lax.axis_size(AXES)
    up = [(i, (i + 1) % depth) for i in range(depth)]
    down = [(j, i) for i, j in up]
    window = BLK + 2 * HA
    vmem = pl.BlockSpec(memory_space=pltpu.VMEM)
    anywhere = pl.BlockSpec(memory_space=pl.ANY)

    depth_k = rows + states
    r_of, c_of = np.arange(rows)[:, None], np.arange(depth_k)[None, :]
    code = np.where(
        c_of < rows,
        (c_of // la == r_of // la) * 1,
        ((c_of - rows) % fields == r_of // la) * (2 + (c_of - rows) // fields),
    ).astype(np.int32)
    spread = ((c_of % la == np.arange(la)[:, None]) & (c_of < rows)).astype(np.float32)

    y, yo, first, last, gains, vertical = call(
        prepare_kernel(fields),
        (
            shape((states, columns)),
            shape((1, columns)),
            shape((40, WIDE)),
            shape((40, WIDE)),
            shape((states, 128)),
            shape((2 * rows, depth_k), BF),
        ),
        in_specs=[vmem] * 10,
        flops=10**8,
        moved=8 * 10**6,
    )(
        atm_mix,
        ocean_mix,
        atm,
        ocean[:lo],
        atm_nbr,
        atm_nbr_coef,
        bulk_coef,
        atm_surface,
        jnp.asarray(spread),
        jnp.asarray(code),
    )
    pack_before = lax.ppermute(last, AXES, up)
    pack_after = lax.ppermute(first, AXES, down)

    later, later_sea = lax.optimization_barrier((atm, ocean, first, last))[:2]
    atm_before = lax.ppermute(later[:, columns - WIDE :], AXES, up)
    atm_after = lax.ppermute(later[:, :WIDE], AXES, down)
    sea_before = lax.ppermute(later_sea[:, cells - HO :], AXES, up)
    sea_after = lax.ppermute(later_sea[:, :HO], AXES, down)

    band, kept, mid = call(
        interior_kernel,
        (
            shape((blocks + 2 * ASTEPS - 2, 2, window, BLK), BF),
            shape((4 * (ASTEPS - 1), 2 * rows, BLK), BF),
            shape((blocks - 2 * ASTEPS, 2 * rows, BLK), BF),
        ),
        in_specs=[vmem] * 3,
        out_specs=(anywhere, vmem, vmem),
        scratch=[
            pltpu.VMEM((blocks, 2, window, BLK), BF),
            pltpu.VMEM((blocks, 2 * rows, BLK), BF),
            pltpu.VMEM((blocks, 2 * rows, BLK), BF),
            pltpu.SemaphoreType.DMA((blocks,)),
        ],
        flops=15 * 10**9,
        moved=25 * 10**6,
    )(atm, atm_nbr, atm_nbr_coef)

    total = blocks + 2 * ASTEPS
    band, q = call(
        surface_kernel,
        (shape(band.shape, BF), shape((blocks, states, BLK))),
        in_specs=[vmem] * 6 + [anywhere],
        out_specs=(anywhere, vmem),
        scratch=[
            pltpu.VMEM((total - 2, 2, window, BLK), BF),
            pltpu.VMEM((total, 2 * states, BLK), BF),
            pltpu.VMEM((total, 2 * states, BLK), BF),
            pltpu.VMEM((total, states, BLK), F32),
            pltpu.VMEM((total, states, BLK), F32),
            pltpu.VMEM((2, window, BLK), BF),
            pltpu.SemaphoreType.DMA((total - 2,)),
        ],
        aliases={6: 0},
        flops=10 * 10**9,
        moved=15 * 10**6,
    )(y, pack_before, pack_after, bulk_coef, atm_surface, gains, band)

    outgoing = call(
        send_kernel,
        shape((peers, parts * fields, lanes)),
        in_specs=[vmem] * 2,
        scratch=[pltpu.VMEM((blocks * fields, BLK), F32)],
        flops=5 * 10**9,
        moved=10**6,
    )(q, picked)
    received = lax.all_to_all(outgoing, AXES, split_axis=0, concat_axis=0, tiled=True)

    atm_final = call(
        edge_kernel,
        shape((rows, columns)),
        in_specs=[
            vmem,
            vmem,
            anywhere,
            vmem,
            vmem,
            vmem,
            vmem,
            anywhere,
        ],
        scratch=[
            pltpu.VMEM((2 * (2 * ASTEPS - 1), 2, window, BLK), BF),
            pltpu.VMEM((2, rows, 2 * BLK), F32),
            pltpu.VMEM((12, 2 * rows, BLK), BF),
            pltpu.VMEM((12, 2 * rows, BLK), BF),
            pltpu.SemaphoreType.DMA((4 * ASTEPS,)),
        ],
        flops=12 * 10**9,
        moved=25 * 10**6,
    )(atm_before, atm_after, atm, kept, mid, q, vertical, band)

    flux, back = call(
        exchange_kernel,
        (shape((fields, cells)), shape((peers, 2 * parts, lanes))),
        in_specs=[vmem] * 9,
        scratch=[
            pltpu.VMEM((2 * peers * parts * fields, lanes), BF),
            pltpu.VMEM((cells // 128 + 2 * HO // 128, 8, 128), F32),
            pltpu.VMEM((2 * peers * parts, lanes), F32),
        ],
        flops=8 * 10**9,
        moved=10**6,
    )(received, remap_slot, remap_weight, yo, pack_before, pack_after, ocean_nbr, ocean_nbr_coef, ocean_mix)
    returned = lax.all_to_all(back, AXES, split_axis=0, concat_axis=0, tiled=True)

    ocean_final = call(
        ocean_kernel,
        shape((fields * lo, cells)),
        in_specs=[vmem] * 7,
        scratch=[
            pltpu.VMEM(((cells + 2 * HO) // BLK, 2 * fields * lo, BLK), BF),
            pltpu.VMEM((2, BLK + 2 * HO, BLK), BF),
        ],
        flops=12 * 10**9,
        moved=12 * 10**6,
    )(ocean, sea_before, sea_after, ocean_nbr, ocean_nbr_coef, ocean_mix, flux)

    surface_temp = call(
        settle_kernel,
        shape((blocks, BLK)),
        in_specs=[vmem] * 3,
        scratch=[pltpu.VMEM((4 * blocks, BLK), F32)],
        flops=2 * 10**9,
        moved=10**6,
    )(returned, picked, atm_surface[0].reshape(blocks, BLK))

    return (
        atm_final.reshape(fields, la, columns),
        ocean_final.reshape(fields, lo, cells),
        surface_temp.reshape(columns),
    )


def solution(mesh):
    placed = (
        P(None, None, AXES),
        P(None, AXES),
        P(None, AXES),
        P(None, AXES),
        P(None, AXES),
        P(),
        P(None, None, AXES),
        P(None, AXES),
        P(None, AXES),
        P(),
        P(AXES, None, None),
        P(None, AXES),
        P(None, AXES),
    )
    return jax.shard_map(
        per_device,
        mesh=mesh,
        in_specs=placed,
        out_specs=(P(None, None, AXES), P(None, None, AXES), P(AXES)),
        check_vma=False,
    )
```

```python
import numpy as np

import jax
import jax.numpy as jnp
from jax import lax
from jax.experimental import pallas as pl
from jax.experimental.pallas import tpu as pltpu
from jax.sharding import PartitionSpec as P

ASTEPS = 4
HA = 256
HO = 384
BLK = 256
WIDE = ASTEPS * HA
BF = jnp.bfloat16
F32 = jnp.float32
VMEM_BYTES = 56 * 1024 * 1024
AXES = ("sec", "blk")


def call(body, outs, *, in_specs=None, out_specs=None, scratch=(), flops=10**6, moved=10**4, aliases=None):
    vmem = pl.BlockSpec(memory_space=pltpu.VMEM)
    return pl.pallas_call(
        body,
        out_shape=outs,
        in_specs=in_specs,
        out_specs=jax.tree.map(lambda _: vmem, outs) if out_specs is None else out_specs,
        scratch_shapes=list(scratch),
        input_output_aliases=aliases or {},
        compiler_params=pltpu.CompilerParams(vmem_limit_bytes=VMEM_BYTES),
        cost_estimate=pl.CostEstimate(flops=flops, bytes_accessed=moved, transcendentals=0),
    )


def shape(dims, dtype=F32):
    return jax.ShapeDtypeStruct(dims, dtype)


def halves(x):
    high = x.astype(BF)
    return high, (x - high.astype(F32)).astype(BF)


def stacked(x):
    return jnp.concatenate(halves(x), axis=0)


def mm(a, b):
    return jnp.dot(a, b, preferred_element_type=F32)


def mm_t(a, b):
    return lax.dot_general(a, b, (((1,), (1,)), ((), ())), preferred_element_type=F32)


def product(x2, w2):
    rows = x2.shape[0] // 2
    wide = mm(x2, w2[0])
    return wide[:rows] + wide[rows:] + mm(x2[:rows], w2[1])


def iota(dims, axis):
    return lax.broadcasted_iota(jnp.int32, dims, axis)


def build_band(store, nbr, coef, halo):
    rows = BLK + 2 * halo
    count = nbr.shape[0]
    ids = [nbr[k : k + 1] for k in range(count)]
    cs = [coef[k : k + 1] for k in range(count)]
    rest = 1.0 - sum(cs[1:], cs[0])
    for k in range(count - 1, 0, -1):
        alive = jnp.ones_like(ids[k]) > 0
        for j in range(k):
            same = jnp.logical_and(ids[k] == ids[j], alive)
            cs[j] = cs[j] + jnp.where(same, cs[k], 0.0)
            alive = jnp.logical_and(alive, jnp.logical_not(same))
        ids[k] = jnp.where(alive, ids[k], -1)
    lanes = 128
    step = 16
    for half in range(BLK // lanes):
        at = slice(half * lanes, (half + 1) * lanes)
        wide_ids = [jnp.broadcast_to(i[:, at], (step, lanes)) for i in ids]
        wide_cs = [jnp.broadcast_to(c[:, at], (step, lanes)) for c in cs]
        own = iota((step, lanes), 1) + (half * lanes + halo)
        wide_rest = jnp.broadcast_to(rest[:, at], (step, lanes))
        base = iota((step, lanes), 0)
        for first in range(0, rows, step):
            if first + step <= half * lanes or first >= half * lanes + lanes + 2 * halo:
                zero = jnp.zeros((step, lanes), BF)
                store(first, step, at, zero, zero)
                continue
            here = base + first
            value = jnp.where(here == own, wide_rest, 0.0)
            for i, c in zip(wide_ids, wide_cs):
                value = jnp.where(here == i, c, value)
            store(first, step, at, *halves(value))


def one_hot(ids, rows):
    return jnp.where(iota((rows, ids.shape[1]), 0) == ids, 1.0, 0.0).astype(BF)


def fold_rows(x, height):
    total = x[:height]
    for first in range(height, x.shape[0], height):
        total = total + x[first : first + height]
    return total


def prepare_kernel(fields):
    def body(mix, omix, atm, sea, nbr, coef, bulk, surf, spread, code, y, yo, first, last, gains, vertical):
        la = mix.shape[0]
        columns = atm.shape[1]
        eye = iota((la, la), 0) == iota((la, la), 1)
        step = mix[...] + jnp.where(eye, 1.0, 0.0)

        def dot(a, b):
            return jnp.dot(a, b, precision=lax.Precision.HIGHEST, preferred_element_type=F32)

        def col(r, same):
            return jnp.sum(jnp.where(same, r, 0.0), axis=1, keepdims=True)

        def row(c, same):
            return jnp.sum(jnp.where(same, c, 0.0), axis=0, keepdims=True)

        twice = dot(step, step)
        fourth = dot(twice, twice)
        rows_up = [step[la - 1 : la, :]]
        cols_up = [step[:, la - 1 : la]]
        for _ in range(ASTEPS - 2):
            rows_up.append(jnp.sum(step * col(rows_up[-1], eye), axis=0, keepdims=True))
        for _ in range(ASTEPS - 1):
            cols_up.append(jnp.sum(step * row(cols_up[-1], eye), axis=1, keepdims=True))
        slot = iota((fields * ASTEPS, 128), 0) // fields
        lane = iota((fields * ASTEPS, 128), 1)
        value = jnp.zeros((fields * ASTEPS, 128), F32)
        for s in range(1, ASTEPS + 1):
            column = jnp.where(slot == s - 1, 1.0, 0.0)
            for j in range(1, ASTEPS):
                column = jnp.where(slot == s - 1 + j, rows_up[j - 1][:, la - 1 : la], column)
            value = jnp.where(lane == s - 1, column, value)
        gains[...] = value

        tall = jnp.concatenate([fourth] * fields, axis=0)
        spreaded = dot(tall, spread[...])
        filled = jnp.where(code[...] == 1, spreaded, 0.0)
        for m in range(ASTEPS):
            tall = jnp.concatenate([cols_up[ASTEPS - 1 - m]] * fields, axis=0)
            filled = jnp.where(code[...] == 2 + m, tall, filled)
        vertical[...] = stacked(filled)

        weights = [jnp.broadcast_to(col(r, eye), (la, 128)) for r in rows_up]
        lo = omix.shape[0]
        sea_eye = iota((lo, lo), 0) == iota((lo, lo), 1)
        sea_row = omix[0:1, :] + jnp.where(iota((1, lo), 1) == 0, 1.0, 0.0)
        sea_weight = jnp.broadcast_to(col(sea_row, sea_eye), (lo, 128))
        for start in range(0, columns, 128):
            at = slice(start, start + 128)
            for f in range(fields):
                x = atm[f * la : (f + 1) * la, at]
                y[f : f + 1, at] = x[la - 1 : la]
                for k in range(1, ASTEPS):
                    y[k * fields + f : k * fields + f + 1, at] = jnp.sum(
                        x * weights[k - 1], axis=0, keepdims=True
                    )
            yo[:, at] = jnp.sum(sea[:, at] * sea_weight, axis=0, keepdims=True)
        for target, at in ((first, slice(0, WIDE)), (last, slice(columns - WIDE, columns))):
            target[0:16, :] = y[:, at]
            target[16:22, :] = nbr[:, at].astype(F32)
            target[22:28, :] = coef[:, at]
            target[28:32, :] = bulk[:, at]
            target[32:36, :] = surf[:, at]
            target[36:37, :] = yo[:, at]
            target[37:40, :] = jnp.zeros((3, WIDE), F32)

    return body


def interior_kernel(atm, nbr, coef, band, kept, mid, w, wa, wb, sa, sb, sems):
    blocks = atm.shape[1] // BLK
    sent = list(range(ASTEPS)) + list(range(blocks - ASTEPS, blocks))

    def split(b, _):
        at = pl.ds(pl.multiple_of(b * BLK, BLK), BLK)
        sa[b] = stacked(atm[:, at])
        return 0

    lax.fori_loop(0, blocks, split, 0, unroll=4)

    def build(b, near):
        at = pl.ds(pl.multiple_of(b * BLK, BLK), BLK)

        def store(first, step, lanes, high, low):
            near[0, first : first + step, lanes] = high
            near[1, first : first + step, lanes] = low
            w[b, 0, first : first + step, lanes] = high
            w[b, 1, first : first + step, lanes] = low

        build_band(store, nbr[:, at] - b * BLK, coef[:, at], HA)

    def window(source, b):
        return jnp.concatenate([source[b - 1], source[b], source[b + 1]], axis=1)

    build(0, wb)
    build(1, wa)

    def first(i, _):
        b = 2 * i + 1
        build(b + 1, wb)
        sb[b] = stacked(product(window(sa, b), (wa[0], wa[1])))
        build(b + 2, wa)
        sb[b + 1] = stacked(product(window(sa, b + 1), (wb[0], wb[1])))
        return 0

    lax.fori_loop(0, (blocks - 2) // 2, first, 0)
    copies = [pltpu.make_async_copy(w.at[b], band.at[i], sems.at[i]) for i, b in enumerate(sent)]
    for copy in copies:
        copy.start()

    def advance(source, target, shift):
        def one(b, _):
            target[b - shift] = stacked(product(window(source, b), (w[b, 0], w[b, 1])))
            return 0

        return one

    buffers = (sa, sb)
    for s in range(1, ASTEPS + 1):
        source = buffers[(s - 1) % 2]
        if s == ASTEPS:
            lax.fori_loop(s, blocks - s, advance(source, mid, s), 0, unroll=2)
        else:
            target = buffers[s % 2]
            if s > 1:
                lax.fori_loop(s, blocks - s, advance(source, target, 0), 0, unroll=2)
            for i, b in enumerate((s, s + 1, blocks - 2 - s, blocks - 1 - s)):
                kept[(s - 1) * 4 + i] = target[b]
    for copy in copies:
        copy.wait()


def surface_kernel(y, before, after, nbr, coef, bulk, surf, gains, q, xa, xb, ids, cs, bulks, surfs):
    columns = y.shape[1]
    fields = bulk.shape[0]
    count = nbr.shape[0]
    side = WIDE // 128
    own = columns // 128
    total = own + 2 * side
    reach = HA // 128
    for t in range(total):
        if t < side or t >= side + own:
            pack = before if t < side else after
            local = t if t < side else t - side - own
            at = slice(local * 128, (local + 1) * 128)
            origin = local * 128 + (columns - WIDE if t < side else 0)
            xa[t] = pack[0:16, at]
            ids[t] = pack[16:22, at].astype(jnp.int32) - origin
            cs[t] = pack[22:28, at]
            bulks[t] = pack[28:32, at]
            surfs[t] = pack[32:36, at]
        else:
            at = slice((t - side) * 128, (t - side + 1) * 128)
            xa[t] = y[:, at]
            ids[t] = nbr[:, at] - (t - side) * 128
            cs[t] = coef[:, at]
            bulks[t] = bulk[:, at]
            surfs[t] = surf[:, at]

    rows = fields * ASTEPS
    slot = iota((rows, 128), 0) // fields
    buffers = (xa, xb)
    for s in range(1, ASTEPS + 1):
        source, target = buffers[(s - 1) % 2], buffers[s % 2]
        gain = jnp.broadcast_to(gains[:, s - 1 : s], (rows, 128))
        kept = jnp.where(slot == s - 1, 0.0, 1.0)

        def tile(t, s=s, source=source, gain=gain, kept=kept):
            middle = source[t]
            around = [source[t - reach + i] for i in range(2 * reach + 1)]
            here, weights = ids[t], cs[t]
            changes = []
            for first in range(0, rows, 8):
                change = jnp.zeros((8, 128), F32)
                for k in range(count):
                    at = jnp.broadcast_to(here[k : k + 1], (8, 128))
                    got = jnp.zeros((8, 128), F32)
                    for i, x in enumerate(around):
                        pick = jnp.take_along_axis(
                            x[first : first + 8], at & 127, axis=1, mode="promise_in_bounds"
                        )
                        got = jnp.where(at // 128 == i, pick, got)
                    change = change + weights[k : k + 1] * (got - middle[first : first + 8])
                changes.append(change)
            moved = middle + jnp.concatenate(changes, axis=0)
            flux = bulks[t] * (surfs[t] - moved[(s - 1) * fields : s * fields])
            return moved * kept + gain * jnp.concatenate([flux] * ASTEPS, axis=0)

        def pair(e, _, s=s, target=target, tile=tile):
            left, right = tile(2 * e), tile(2 * e + 1)
            if s == ASTEPS:
                q[e - ASTEPS] = jnp.concatenate([left, right], axis=1)
            else:
                target[2 * e] = left
                target[2 * e + 1] = right
            return 0

        lax.fori_loop(s, total // 2 - s, pair, 0)


def send_kernel(q, cols, out, table):
    fields = q.shape[1] // ASTEPS
    peers, slots = cols.shape
    blocks = q.shape[0]
    lanes = out.shape[2]
    parts = slots // lanes
    for b in range(blocks):
        table[b * fields : (b + 1) * fields, :] = q[b, (ASTEPS - 1) * fields :, :]
    rows = stacked(table[...])
    half = blocks * fields
    block_of_row = iota((half, slots), 0) // fields

    def one(p, _):
        ids = cols[pl.ds(p, 1), :]
        got = mm(rows, one_hot(ids & (BLK - 1), BLK))
        got = jnp.where(block_of_row == ids // BLK, got[:half] + got[half:], 0.0)
        got = fold_rows(got, 2 * fields)
        got = got[:fields] + got[fields:]
        out[p] = jnp.concatenate([got[:, i * lanes : (i + 1) * lanes] for i in range(parts)], axis=0)
        return 0

    lax.fori_loop(0, peers, one, 0, unroll=4)


def exchange_kernel(recv, slot, weight, yo, before, after, nbr, coef, omix, flux_out, back, rows, tiles, hots, seas, acc):
    peers, per_peer, lanes = recv.shape
    links, columns = slot.shape
    fields = flux_out.shape[0]
    parts = per_peer // fields
    highs = peers * parts
    table = highs * fields
    rows[...] = stacked(recv[...].reshape(table, lanes))
    acc[...] = jnp.zeros_like(acc)
    side = HO // 128
    own_tiles = columns // 128
    for t in range(own_tiles + 2 * side):
        if t < side:
            line = before[36:37, WIDE - HO + t * 128 : WIDE - HO + (t + 1) * 128]
        elif t < side + own_tiles:
            line = yo[:, (t - side) * 128 : (t - side + 1) * 128]
        else:
            line = after[36:37, (t - side - own_tiles) * 128 : (t - side - own_tiles + 1) * 128]
        tiles[t] = jnp.broadcast_to(line, (8, 128))
    corner = omix[0:1, 0:1] + 1.0
    high_of_row = iota((table, BLK), 0) // fields
    back_rows = iota((2 * highs, BLK), 0)
    inner = back_rows % (2 * parts)
    back_high = (back_rows // (2 * parts)) * parts + inner % parts
    pattern = iota((8, BLK), 0) % (2 * parts) // parts
    window = 1 + 2 * side
    neighbors = nbr.shape[0]

    def surface(j, half):
        t0 = j * (BLK // 128) + half
        at = pl.ds(pl.multiple_of(t0 * 128, 128), 128)
        pad = jnp.zeros((8 - neighbors, 128), jnp.int32)
        ids = jnp.concatenate([nbr[:, at] - t0 * 128, pad], axis=0)
        cs = jnp.concatenate([coef[:, at], pad.astype(F32)], axis=0)
        middle = tiles[t0 + side]
        got = jnp.zeros((8, 128), F32)
        for t in range(window):
            pick = jnp.take_along_axis(tiles[t0 + t], ids & 127, axis=1, mode="promise_in_bounds")
            got = jnp.where(ids // 128 == t, pick, got)
        return middle[0:1] + jnp.sum(cs * (got - middle), axis=0, keepdims=True)

    def base(j, _):
        at = pl.ds(pl.multiple_of(j * BLK, BLK), BLK)
        seas[:, at] = jnp.concatenate([surface(j, h) for h in range(BLK // 128)], axis=1)
        return 0

    lax.fori_loop(0, columns // BLK, base, 0, unroll=2)

    def arrive(j, _):
        at = pl.ds(pl.multiple_of(j * BLK, BLK), BLK)
        flux = jnp.zeros((2 * fields, BLK), F32)
        for r in range(links):
            ids = slot[r : r + 1, at]
            hot = one_hot(ids & (lanes - 1), lanes)
            hots[j, :, r * BLK : (r + 1) * BLK] = hot
            got = mm(rows[...], hot)
            got = jnp.where(high_of_row == ids // lanes, got[:table] + got[table:], 0.0)
            flux = flux + weight[r : r + 1, at] * fold_rows(got, 2 * fields)
        flux = flux[:fields] + flux[fields:]
        flux_out[:, at] = flux
        seas[:, at] += corner * flux[0:1]
        return 0

    lax.fori_loop(0, columns // BLK, arrive, 0, unroll=2)

    def leave(j, _):
        at = pl.ds(pl.multiple_of(j * BLK, BLK), BLK)
        sea = seas[:, at]
        left = []
        for r in range(links):
            ids, scale = slot[r : r + 1, at], weight[r : r + 1, at]
            high, low = halves(jnp.where(pattern == 1, scale, scale * sea))
            mask = back_high == ids // lanes
            both = [
                jnp.where(mask, jnp.concatenate([x.astype(F32)] * (2 * highs // 8), axis=0), 0.0).astype(BF)
                for x in (high, low)
            ]
            left.append(jnp.concatenate(both, axis=0))
        acc[...] += mm_t(jnp.concatenate(left, axis=1), hots[j])
        return 0

    lax.fori_loop(0, columns // BLK, leave, 0, unroll=2)
    back[...] = (acc[: 2 * highs] + acc[2 * highs :]).reshape(back.shape)


def settle_kernel(back, cols, surf, out, acc):
    peers, per_peer, lanes = back.shape
    parts = per_peer // 2
    blocks = surf.shape[1] // BLK
    acc[...] = jnp.zeros_like(acc)
    block_of_row = iota((blocks, lanes), 0)

    def one(d, _):
        left, hots = [], []
        for h in range(parts):
            ids = cols[pl.ds(d, 1), h * lanes : (h + 1) * lanes]
            mask = block_of_row == ids // BLK
            value = jnp.where(mask, back[d, h : h + 1, :], 0.0)
            scale = jnp.where(mask, back[d, parts + h : parts + h + 1, :], 0.0)
            left.append(stacked(jnp.concatenate([value, scale], axis=0)))
            hots.append(one_hot(ids & (BLK - 1), BLK))
        acc[...] += mm_t(jnp.concatenate(left, axis=1), jnp.concatenate(hots, axis=1))
        return 0

    lax.fori_loop(0, peers, one, 0, unroll=4)
    sums = acc[: 2 * blocks] + acc[2 * blocks :]
    base = jnp.concatenate([surf[0:1, b * BLK : (b + 1) * BLK] for b in range(blocks)], axis=0)
    value = (base + sums[:blocks]) / (1.0 + sums[blocks:])
    for b in range(blocks):
        for i in range(BLK // 128):
            row = b * (BLK // 128) + i
            out[row : row + 1, :] = value[b : b + 1, i * 128 : (i + 1) * 128]


def edge_kernel(before, after, lists_before, lists_after, atm, kept, mid, q, vertical, band, out, w, sides, sa, sb, sems):
    blocks = q.shape[0]
    count = 2 * ASTEPS - 1
    halo = ASTEPS - 1
    columns = blocks * BLK
    copies = []
    for side in range(2):
        at = slice(0, 2 * BLK) if side == 0 else slice((blocks - 2) * BLK, blocks * BLK)
        copy = pltpu.make_async_copy(atm.at[:, at], sides.at[side], sems.at[2 * count + side])
        copy.start()
        copies.append(copy)
    for i in range(2 * ASTEPS):
        copy = pltpu.make_async_copy(band.at[i], w.at[halo + i], sems.at[i])
        copy.start()
        copies.append(copy)
    for i in range(halo):
        for lists, local, origin, k in (
            (lists_before, i + 1, columns - WIDE, i),
            (lists_after, i, 0, halo + 2 * ASTEPS + i),
        ):
            at = slice(local * BLK, (local + 1) * BLK)

            def store(first, step, lanes, high, low, k=k):
                w[k, 0, first : first + step, lanes] = high
                w[k, 1, first : first + step, lanes] = low

            ids = lists[16:22, at].astype(jnp.int32) - (origin + local * BLK)
            build_band(store, ids, lists[22:28, at], HA)
    for i in range(ASTEPS):
        at = slice(i * BLK, (i + 1) * BLK)
        sa[i] = stacked(before[:, at])
        sa[6 + 2 + i] = stacked(after[:, at])
    for copy in copies:
        copy.wait()
    for i in range(2):
        at = slice(i * BLK, (i + 1) * BLK)
        sa[ASTEPS + i] = stacked(sides[0, :, at])
        sa[6 + i] = stacked(sides[1, :, at])
    buffers = (sa, sb)
    for s in range(1, ASTEPS + 1):
        source, target = buffers[(s - 1) % 2], buffers[s % 2]
        last = s == ASTEPS

        def one(i, _, s=s, source=source, target=target, last=last):
            for side in range(2):
                base = 6 * side
                k = s - 1 + i if side == 0 else count + ASTEPS - s + i
                x2 = jnp.concatenate([source[base + i + d] for d in range(3)], axis=1)
                value = stacked(product(x2, (w[k, 0], w[k, 1])))
                target[base + i + (2 * side if not last else 0)] = value
            return 0

        lax.fori_loop(0, ASTEPS, one, 0, unroll=2)
        if not last:
            for i in range(2):
                target[ASTEPS + i] = kept[(s - 1) * 4 + i]
                target[6 + i] = kept[(s - 1) * 4 + 2 + i]
    rows = out.shape[0]
    final = buffers[ASTEPS % 2]

    def mixed(source, shift):
        def one(b, _):
            at = pl.ds(pl.multiple_of(b * BLK, BLK), BLK)
            qh, ql = halves(q[b])
            x2 = source[b - shift]
            high = jnp.concatenate([x2[:rows], qh], axis=0)
            low = jnp.concatenate([x2[rows:], ql], axis=0)
            wide = mm(vertical[...], high)
            out[:, at] = wide[:rows] + wide[rows:] + mm(vertical[:rows], low)
            return 0

        return one

    lax.fori_loop(0, ASTEPS, mixed(final, 0), 0, unroll=2)
    lax.fori_loop(ASTEPS, blocks - ASTEPS, mixed(mid, ASTEPS), 0, unroll=2)
    lax.fori_loop(blocks - ASTEPS, blocks, mixed(final, blocks - ASTEPS - 6), 0, unroll=2)


def ocean_kernel(ocean, before, after, nbr, coef, omix, flux, out, x2, wa, wb):
    levels = omix.shape[0]
    fields = flux.shape[0]
    columns = ocean.shape[1]
    blocks = columns // BLK
    eye = iota((levels, levels), 0) == iota((levels, levels), 1)
    step = omix[...] + jnp.where(eye, 1.0, 0.0)
    top = jnp.broadcast_to(step[:, 0:1], (levels, BLK))
    mix2 = stacked(step)

    def part(first, width):
        pieces = []
        for ref, begin, size in ((before, -HO, HO), (ocean, 0, columns), (after, columns, HO)):
            lo, hi = max(first, begin), min(first + width, begin + size)
            if lo < hi:
                pieces.append(ref[:, lo - begin : hi - begin])
        return pieces[0] if len(pieces) == 1 else jnp.concatenate(pieces, axis=1)

    for e in range((columns + 2 * HO) // BLK):
        x2[e] = stacked(part(e * BLK - HO, BLK))

    def build(b, w):
        at = pl.ds(pl.multiple_of(b * BLK, BLK), BLK)

        def store(first, size, lanes, high, low):
            w[0, first : first + size, lanes] = high
            w[1, first : first + size, lanes] = low

        build_band(store, nbr[:, at] - b * BLK, coef[:, at], HO)

    def finish(b, w):
        at = pl.ds(pl.multiple_of(b * BLK, BLK), BLK)
        source = jnp.concatenate([x2[b + d] for d in range(1 + 2 * HO // BLK)], axis=1)
        moved = product(source, (w[0], w[1]))
        for f in range(fields):
            rows = slice(f * levels, (f + 1) * levels)
            high, low = halves(moved[rows])
            wide = mm(mix2, high)
            out[rows, at] = (
                wide[:levels] + wide[levels:] + mm(mix2[:levels], low) + top * flux[f : f + 1, at]
            )

    build(0, wa)

    def one(i, _):
        b = 2 * i
        build(b + 1, wb)
        finish(b, wa)
        build(jnp.minimum(b + 2, blocks - 1), wa)
        finish(b + 1, wb)
        return 0

    lax.fori_loop(0, blocks // 2, one, 0)


def per_device(
    atm_state,
    atm_surface,
    bulk_coef,
    atm_nbr,
    atm_nbr_coef,
    atm_mix,
    ocean_state,
    ocean_nbr,
    ocean_nbr_coef,
    ocean_mix,
    send_cols,
    remap_slot,
    remap_weight,
):
    fields, la, columns = atm_state.shape
    lo, cells = ocean_state.shape[1:]
    blocks = columns // BLK
    rows = fields * la
    states = fields * ASTEPS
    picked = send_cols[0]
    peers, slots = picked.shape
    lanes = min(BLK, slots)
    parts = slots // lanes
    atm = atm_state.reshape(rows, columns)
    ocean = ocean_state.reshape(fields * lo, cells)
    depth = lax.axis_size(AXES)
    up = [(i, (i + 1) % depth) for i in range(depth)]
    down = [(j, i) for i, j in up]
    window = BLK + 2 * HA
    vmem = pl.BlockSpec(memory_space=pltpu.VMEM)
    anywhere = pl.BlockSpec(memory_space=pl.ANY)

    depth_k = rows + states
    r_of, c_of = np.arange(rows)[:, None], np.arange(depth_k)[None, :]
    code = np.where(
        c_of < rows,
        (c_of // la == r_of // la) * 1,
        ((c_of - rows) % fields == r_of // la) * (2 + (c_of - rows) // fields),
    ).astype(np.int32)
    spread = ((c_of % la == np.arange(la)[:, None]) & (c_of < rows)).astype(np.float32)

    y, yo, first, last, gains, vertical = call(
        prepare_kernel(fields),
        (
            shape((states, columns)),
            shape((1, columns)),
            shape((40, WIDE)),
            shape((40, WIDE)),
            shape((states, 128)),
            shape((2 * rows, depth_k), BF),
        ),
        in_specs=[vmem] * 10,
    )(
        atm_mix,
        ocean_mix,
        atm,
        ocean[:lo],
        atm_nbr,
        atm_nbr_coef,
        bulk_coef,
        atm_surface,
        jnp.asarray(spread),
        jnp.asarray(code),
    )
    pack_before = lax.ppermute(last, AXES, up)
    pack_after = lax.ppermute(first, AXES, down)

    later, later_sea = lax.optimization_barrier((atm, ocean, first, last))[:2]
    atm_before = lax.ppermute(later[:, columns - WIDE :], AXES, up)
    atm_after = lax.ppermute(later[:, :WIDE], AXES, down)
    sea_before = lax.ppermute(later_sea[:, cells - HO :], AXES, up)
    sea_after = lax.ppermute(later_sea[:, :HO], AXES, down)

    band, kept, mid = call(
        interior_kernel,
        (
            shape((2 * ASTEPS, 2, window, BLK), BF),
            shape((4 * (ASTEPS - 1), 2 * rows, BLK), BF),
            shape((blocks - 2 * ASTEPS, 2 * rows, BLK), BF),
        ),
        in_specs=[vmem] * 3,
        out_specs=(anywhere, vmem, vmem),
        scratch=[
            pltpu.VMEM((blocks, 2, window, BLK), BF),
            pltpu.VMEM((2, window, BLK), BF),
            pltpu.VMEM((2, window, BLK), BF),
            pltpu.VMEM((blocks, 2 * rows, BLK), BF),
            pltpu.VMEM((blocks, 2 * rows, BLK), BF),
            pltpu.SemaphoreType.DMA((2 * ASTEPS,)),
        ],
    )(atm, atm_nbr, atm_nbr_coef)

    tiles = (columns + 2 * WIDE) // 128
    count = atm_nbr.shape[0]
    q = call(
        surface_kernel,
        shape((blocks, states, BLK)),
        in_specs=[vmem] * 8,
        scratch=[
            pltpu.VMEM((tiles, states, 128), F32),
            pltpu.VMEM((tiles, states, 128), F32),
            pltpu.VMEM((tiles, count, 128), jnp.int32),
            pltpu.VMEM((tiles, count, 128), F32),
            pltpu.VMEM((tiles, fields, 128), F32),
            pltpu.VMEM((tiles, fields, 128), F32),
        ],
    )(y, pack_before, pack_after, atm_nbr, atm_nbr_coef, bulk_coef, atm_surface, gains)
    q, atm_before, atm_after = lax.optimization_barrier((q, atm_before, atm_after))

    outgoing = call(
        send_kernel,
        shape((peers, parts * fields, lanes)),
        in_specs=[vmem] * 2,
        scratch=[pltpu.VMEM((blocks * fields, BLK), F32)],
    )(q, picked)
    received = lax.all_to_all(outgoing, AXES, split_axis=0, concat_axis=0, tiled=True)

    atm_final = call(
        edge_kernel,
        shape((rows, columns)),
        in_specs=[
            vmem,
            vmem,
            vmem,
            vmem,
            anywhere,
            vmem,
            vmem,
            vmem,
            vmem,
            anywhere,
        ],
        scratch=[
            pltpu.VMEM((2 * (2 * ASTEPS - 1), 2, window, BLK), BF),
            pltpu.VMEM((2, rows, 2 * BLK), F32),
            pltpu.VMEM((12, 2 * rows, BLK), BF),
            pltpu.VMEM((12, 2 * rows, BLK), BF),
            pltpu.SemaphoreType.DMA((4 * ASTEPS,)),
        ],
    )(atm_before, atm_after, pack_before, pack_after, atm, kept, mid, q, vertical, band)

    received, sea_before, sea_after = lax.optimization_barrier((received, sea_before, sea_after))
    flux, back = call(
        exchange_kernel,
        (shape((fields, cells)), shape((peers, 2 * parts, lanes))),
        in_specs=[vmem] * 9,
        scratch=[
            pltpu.VMEM((2 * peers * parts * fields, lanes), BF),
            pltpu.VMEM((cells // 128 + 2 * HO // 128, 8, 128), F32),
            pltpu.VMEM((cells // BLK, lanes, remap_slot.shape[0] * BLK), BF),
            pltpu.VMEM((1, cells), F32),
            pltpu.VMEM((4 * peers * parts, lanes), F32),
        ],
    )(received, remap_slot, remap_weight, yo, pack_before, pack_after, ocean_nbr, ocean_nbr_coef, ocean_mix)
    returned = lax.all_to_all(back, AXES, split_axis=0, concat_axis=0, tiled=True)

    ocean_final = call(
        ocean_kernel,
        shape((fields * lo, cells)),
        in_specs=[vmem] * 7,
        scratch=[
            pltpu.VMEM(((cells + 2 * HO) // BLK, 2 * fields * lo, BLK), BF),
            pltpu.VMEM((2, BLK + 2 * HO, BLK), BF),
            pltpu.VMEM((2, BLK + 2 * HO, BLK), BF),
        ],
    )(ocean, sea_before, sea_after, ocean_nbr, ocean_nbr_coef, ocean_mix, flux)

    surface_temp = call(
        settle_kernel,
        shape((columns // 128, 128)),
        in_specs=[vmem] * 3,
        scratch=[pltpu.VMEM((4 * blocks, BLK), F32)],
    )(returned, picked, atm_surface)

    return (
        atm_final.reshape(fields, la, columns),
        ocean_final.reshape(fields, lo, cells),
        surface_temp.reshape(columns),
    )


def solution(mesh):
    placed = (
        P(None, None, AXES),
        P(None, AXES),
        P(None, AXES),
        P(None, AXES),
        P(None, AXES),
        P(),
        P(None, None, AXES),
        P(None, AXES),
        P(None, AXES),
        P(),
        P(AXES, None, None),
        P(None, AXES),
        P(None, AXES),
    )
    return jax.shard_map(
        per_device,
        mesh=mesh,
        in_specs=placed,
        out_specs=(P(None, None, AXES), P(None, None, AXES), P(AXES)),
        check_vma=False,
    )
```

```python
import numpy as np

import jax
import jax.numpy as jnp
from jax import lax
from jax.experimental import pallas as pl
from jax.experimental.pallas import tpu as pltpu
from jax.sharding import PartitionSpec as P

ASTEPS = 4
HA = 256
HO = 384
BLK = 256
WIDE = ASTEPS * HA
BF = jnp.bfloat16
F32 = jnp.float32
VMEM_BYTES = 56 * 1024 * 1024
AXES = ("sec", "blk")


def call(body, outs, *, in_specs=None, out_specs=None, scratch=(), flops=10**6, moved=10**4, aliases=None):
    vmem = pl.BlockSpec(memory_space=pltpu.VMEM)
    return pl.pallas_call(
        body,
        out_shape=outs,
        in_specs=in_specs,
        out_specs=jax.tree.map(lambda _: vmem, outs) if out_specs is None else out_specs,
        scratch_shapes=list(scratch),
        input_output_aliases=aliases or {},
        compiler_params=pltpu.CompilerParams(vmem_limit_bytes=VMEM_BYTES),
        cost_estimate=pl.CostEstimate(flops=flops, bytes_accessed=moved, transcendentals=0),
    )


def shape(dims, dtype=F32):
    return jax.ShapeDtypeStruct(dims, dtype)


def halves(x):
    high = x.astype(BF)
    return high, (x - high.astype(F32)).astype(BF)


def stacked(x):
    return jnp.concatenate(halves(x), axis=0)


def mm(a, b):
    return jnp.dot(a, b, preferred_element_type=F32)


def mm_t(a, b):
    return lax.dot_general(a, b, (((1,), (1,)), ((), ())), preferred_element_type=F32)


def product(x2, w2):
    rows = x2.shape[0] // 2
    wide = mm(x2, w2[0])
    return wide[:rows] + wide[rows:] + mm(x2[:rows], w2[1])


def product_long(x2s, w2):
    rows = x2s[0].shape[0] // 2
    highs = [x[:rows] for x in x2s]
    lows = [x[rows:] for x in x2s]
    return mm(
        jnp.concatenate(highs + lows + highs, axis=1),
        jnp.concatenate([w2[0], w2[0], w2[1]], axis=0),
    )


def iota(dims, axis):
    return lax.broadcasted_iota(jnp.int32, dims, axis)


def build_band(store, nbr, coef, halo):
    rows = BLK + 2 * halo
    count = nbr.shape[0]
    ids = [nbr[k : k + 1] for k in range(count)]
    cs = [coef[k : k + 1] for k in range(count)]
    rest = 1.0 - sum(cs[1:], cs[0])
    for k in range(count - 1, 0, -1):
        alive = jnp.ones_like(ids[k]) > 0
        for j in range(k):
            same = jnp.logical_and(ids[k] == ids[j], alive)
            cs[j] = cs[j] + jnp.where(same, cs[k], 0.0)
            alive = jnp.logical_and(alive, jnp.logical_not(same))
        ids[k] = jnp.where(alive, ids[k], -1)
    lanes = 128
    step = 16
    base = iota((step, lanes), 0).astype(F32)
    parts = [halves(c) for c in cs + [rest]]

    def wide(x, at):
        return jnp.broadcast_to(x[:, at].astype(F32), (step, lanes)).astype(BF)

    for half in range(BLK // lanes):
        at = slice(half * lanes, (half + 1) * lanes)
        highs = [wide(p[0], at) for p in parts]
        lows = [wide(p[1], at) for p in parts]
        own = (iota((step, lanes), 1) - iota((step, lanes), 0)).astype(F32).astype(BF)
        zero = jnp.zeros((step, lanes), BF)
        for tile in range(0, rows, BLK):
            near = [wide((i - tile).astype(F32), at) for i in ids]
            for first in range(tile, tile + BLK, step):
                high, low = zero, zero
                if half * lanes - step < first < half * lanes + lanes + 2 * halo:
                    offset = first - halo - half * lanes
                    if 0 <= offset < lanes:
                        same = own == jnp.full((step, lanes), offset, BF)
                        high = jnp.where(same, highs[-1], zero)
                        low = jnp.where(same, lows[-1], zero)
                    here = (base + float(first - tile)).astype(BF)
                    for k in range(count):
                        same = here == near[k]
                        high = jnp.where(same, highs[k], high)
                        low = jnp.where(same, lows[k], low)
                store(first, step, at, high, low)


def one_hot(ids, rows):
    return jnp.where(iota((rows, ids.shape[1]), 0) == ids, 1.0, 0.0).astype(BF)


def fold_rows(x, height):
    total = x[:height]
    for first in range(height, x.shape[0], height):
        total = total + x[first : first + height]
    return total


def prepare_kernel(fields):
    def body(mix, omix, atm, sea, nbr, coef, bulk, surf, spread, code, y, yo, first, last, gains, vertical, top, sem):
        la = mix.shape[0]
        columns = atm.shape[1]
        copy = pltpu.make_async_copy(sea.at[: omix.shape[0], :], top, sem)
        copy.start()
        eye = iota((la, la), 0) == iota((la, la), 1)
        step = mix[...] + jnp.where(eye, 1.0, 0.0)

        def dot(a, b):
            return jnp.dot(a, b, precision=lax.Precision.HIGHEST, preferred_element_type=F32)

        def col(r, same):
            return jnp.sum(jnp.where(same, r, 0.0), axis=1, keepdims=True)

        def row(c, same):
            return jnp.sum(jnp.where(same, c, 0.0), axis=0, keepdims=True)

        twice = dot(step, step)
        fourth = dot(twice, twice)
        rows_up = [step[la - 1 : la, :]]
        cols_up = [step[:, la - 1 : la]]
        for _ in range(ASTEPS - 2):
            rows_up.append(jnp.sum(step * col(rows_up[-1], eye), axis=0, keepdims=True))
        for _ in range(ASTEPS - 1):
            cols_up.append(jnp.sum(step * row(cols_up[-1], eye), axis=1, keepdims=True))
        slot = iota((fields * ASTEPS, 128), 0) // fields
        lane = iota((fields * ASTEPS, 128), 1)
        value = jnp.zeros((fields * ASTEPS, 128), F32)
        for s in range(1, ASTEPS + 1):
            column = jnp.where(slot == s - 1, 1.0, 0.0)
            for j in range(1, ASTEPS):
                column = jnp.where(slot == s - 1 + j, rows_up[j - 1][:, la - 1 : la], column)
            value = jnp.where(lane == s - 1, column, value)
        gains[...] = value

        tall = jnp.concatenate([fourth] * fields, axis=0)
        spreaded = dot(tall, spread[...])
        filled = jnp.where(code[...] == 1, spreaded, 0.0)
        for m in range(ASTEPS):
            tall = jnp.concatenate([cols_up[ASTEPS - 1 - m]] * fields, axis=0)
            filled = jnp.where(code[...] == 2 + m, tall, filled)
        vertical[...] = stacked(filled)

        weights = [jnp.broadcast_to(col(r, eye), (la, 128)) for r in rows_up]
        lo = omix.shape[0]
        sea_eye = iota((lo, lo), 0) == iota((lo, lo), 1)
        sea_row = omix[0:1, :] + jnp.where(iota((1, lo), 1) == 0, 1.0, 0.0)
        sea_weight = jnp.broadcast_to(col(sea_row, sea_eye), (lo, 128))
        copy.wait()
        for start in range(0, columns, 128):
            at = slice(start, start + 128)
            for f in range(fields):
                x = atm[f * la : (f + 1) * la, at]
                y[f : f + 1, at] = x[la - 1 : la]
                for k in range(1, ASTEPS):
                    y[k * fields + f : k * fields + f + 1, at] = jnp.sum(
                        x * weights[k - 1], axis=0, keepdims=True
                    )
            yo[:, at] = jnp.sum(top[:, at] * sea_weight, axis=0, keepdims=True)
        for target, at in ((first, slice(0, WIDE)), (last, slice(columns - WIDE, columns))):
            target[0:16, :] = y[:, at]
            target[16:22, :] = nbr[:, at].astype(F32)
            target[22:28, :] = coef[:, at]
            target[28:32, :] = bulk[:, at]
            target[32:36, :] = surf[:, at]
            target[36:37, :] = yo[:, at]
            target[37:40, :] = jnp.zeros((3, WIDE), F32)

    return body


def band_kernel(nbr, coef, band, w, sems):
    blocks = nbr.shape[1] // BLK

    def copy(b):
        return pltpu.make_async_copy(w.at[b], band.at[b], sems.at[b])

    def build(b, _):
        at = pl.ds(pl.multiple_of(b * BLK, BLK), BLK)

        def store(first, step, lanes, high, low):
            w[b, 0, first : first + step, lanes] = high
            w[b, 1, first : first + step, lanes] = low

        build_band(store, nbr[:, at] - b * BLK, coef[:, at], HA)
        copy(b).start()
        return 0

    lax.fori_loop(0, blocks, build, 0)

    def finish(b, _):
        copy(b).wait()
        return 0

    lax.fori_loop(0, blocks, finish, 0)


def interior_kernel(
    atm, y, before, after, bulk, surf, gains, band, q, kept, mid, far, w, sa, sb, za, zb, bulks, surfs, sems
):
    rows, columns = atm.shape
    blocks = columns // BLK
    fields = bulk.shape[0]
    states = fields * ASTEPS
    total = blocks + 2 * ASTEPS
    halo = ASTEPS - 1

    def arriving(b):
        return pltpu.make_async_copy(band.at[b], w.at[halo + b], sems.at[b])

    def begin(b, _):
        arriving(b).start()
        return 0

    lax.fori_loop(0, blocks, begin, 0)

    leaving = []
    for e in list(range(ASTEPS)) + list(range(ASTEPS + blocks, total)):
        pack = before if e < ASTEPS else after
        local = e if e < ASTEPS else e - ASTEPS - blocks
        at = slice(local * BLK, (local + 1) * BLK)
        za[e] = stacked(pack[0:states, at])
        bulks[e] = pack[28:32, at]
        surfs[e] = pack[32:36, at]
        if e in (0, total - 1):
            continue
        origin = local * BLK + (columns - WIDE if e < ASTEPS else 0)

        def store(first, step, lanes, high, low, e=e):
            w[e - 1, 0, first : first + step, lanes] = high
            w[e - 1, 1, first : first + step, lanes] = low

        build_band(store, pack[16:22, at].astype(jnp.int32) - origin, pack[22:28, at], HA)
        i = e - 1 if e < ASTEPS else e - 1 - blocks
        copy = pltpu.make_async_copy(w.at[e - 1], far.at[i], sems.at[blocks + i])
        copy.start()
        leaving.append(copy)
    for b in range(blocks):
        at = slice(b * BLK, (b + 1) * BLK)
        both = stacked(jnp.concatenate([atm[:, at], y[:, at]], axis=0))
        sa[b] = both
        height = rows + states
        za[b + ASTEPS] = jnp.concatenate([both[rows:height], both[height + rows :]], axis=0)
        bulks[b + ASTEPS] = bulk[:, at]
        surfs[b + ASTEPS] = surf[:, at]

    def arrived(b, _):
        arriving(b).wait()
        return 0

    lax.fori_loop(0, blocks, arrived, 0)

    slot = iota((states, BLK), 0) // fields
    for s in range(1, ASTEPS + 1):
        xs, xt = (sa, sb) if s % 2 else (sb, sa)
        zs, zt = (za, zb) if s % 2 else (zb, za)
        gain = jnp.broadcast_to(gains[:, s - 1 : s], (states, BLK))
        keep = jnp.where(slot == s - 1, 0.0, 1.0)

        def advance(moved, e, s=s, gain=gain, keep=keep):
            flux = bulks[e] * (surfs[e] - moved[(s - 1) * fields : s * fields])
            return moved * keep + gain * jnp.concatenate([flux] * ASTEPS, axis=0)

        def edge(e, s=s, zs=zs, zt=zt, advance=advance):
            x2 = jnp.concatenate([zs[e - 1], zs[e], zs[e + 1]], axis=1)
            value = advance(product(x2, (w[e - 1, 0], w[e - 1, 1])), e)
            if s == ASTEPS:
                q[e - ASTEPS] = value
            else:
                zt[e] = stacked(value)

        def inner(b, s=s, xs=xs, xt=xt, zt=zt, advance=advance):
            x2 = jnp.concatenate([xs[b - 1], xs[b], xs[b + 1]], axis=1)
            moved = product(x2, (w[b + halo, 0], w[b + halo, 1]))
            value = advance(moved[rows:], b + ASTEPS)
            if s == ASTEPS:
                q[b] = value
                mid[b - ASTEPS] = stacked(moved[:rows])
            else:
                high, low = halves(moved[:rows])
                zh, zl = halves(value)
                xt[b] = jnp.concatenate([high, zh, low, zl], axis=0)
                zt[b + ASTEPS] = jnp.concatenate([zh, zl], axis=0)

        def together(i, _, s=s, edge=edge, inner=inner):
            inner(s + 2 * i)
            inner(s + 2 * i + 1)
            edge(s + i)
            edge(blocks + ASTEPS - s + i)
            return 0

        def alone(i, _, s=s, inner=inner):
            inner(s + 2 * i)
            inner(s + 2 * i + 1)
            return 0

        lax.fori_loop(0, ASTEPS, together, 0)
        if blocks // 2 - s > ASTEPS:
            lax.fori_loop(ASTEPS, blocks // 2 - s, alone, 0)
        if s < ASTEPS:
            height = rows + states
            for i, b in enumerate((s, s + 1, blocks - 2 - s, blocks - 1 - s)):
                kept[(s - 1) * 4 + i, :rows] = xt[b, :rows]
                kept[(s - 1) * 4 + i, rows:] = xt[b, height : height + rows]
    for copy in leaving:
        copy.wait()


def send_kernel(q, cols, out, table):
    fields = q.shape[1] // ASTEPS
    peers, slots = cols.shape
    blocks = q.shape[0]
    lanes = out.shape[2]
    parts = slots // lanes
    for b in range(blocks):
        table[b * fields : (b + 1) * fields, :] = q[b, (ASTEPS - 1) * fields :, :]
    rows = stacked(table[...])
    half = blocks * fields
    block_of_row = iota((half, slots), 0) // fields

    def one(p, _):
        ids = cols[pl.ds(p, 1), :]
        got = mm(rows, one_hot(ids & (BLK - 1), BLK))
        got = jnp.where(block_of_row == ids // BLK, got[:half] + got[half:], 0.0)
        got = fold_rows(got, 2 * fields)
        got = got[:fields] + got[fields:]
        out[p] = jnp.concatenate([got[:, i * lanes : (i + 1) * lanes] for i in range(parts)], axis=0)
        return 0

    lax.fori_loop(0, peers, one, 0, unroll=4)


def exchange_kernel(recv, slot, weight, yo, before, after, nbr, coef, omix, flux_out, back, rows, tiles, hots, seas, acc):
    peers, per_peer, lanes = recv.shape
    links, columns = slot.shape
    fields = flux_out.shape[0]
    parts = per_peer // fields
    highs = peers * parts
    table = highs * fields
    rows[...] = stacked(recv[...].reshape(table, lanes))
    acc[...] = jnp.zeros_like(acc)
    side = HO // 128
    own_tiles = columns // 128
    for t in range(own_tiles + 2 * side):
        if t < side:
            line = before[36:37, WIDE - HO + t * 128 : WIDE - HO + (t + 1) * 128]
        elif t < side + own_tiles:
            line = yo[:, (t - side) * 128 : (t - side + 1) * 128]
        else:
            line = after[36:37, (t - side - own_tiles) * 128 : (t - side - own_tiles + 1) * 128]
        tiles[t] = jnp.broadcast_to(line, (8, 128))
    corner = omix[0:1, 0:1] + 1.0
    high_of_row = iota((table, BLK), 0) // fields
    back_rows = iota((2 * highs, BLK), 0)
    inner = back_rows % (2 * parts)
    back_high = (back_rows // (2 * parts)) * parts + inner % parts
    pattern = iota((8, BLK), 0) % (2 * parts) // parts
    window = 1 + 2 * side
    neighbors = nbr.shape[0]

    def surface(j, half):
        t0 = j * (BLK // 128) + half
        at = pl.ds(pl.multiple_of(t0 * 128, 128), 128)
        pad = jnp.zeros((8 - neighbors, 128), jnp.int32)
        ids = jnp.concatenate([nbr[:, at] - t0 * 128, pad], axis=0)
        cs = jnp.concatenate([coef[:, at], pad.astype(F32)], axis=0)
        middle = tiles[t0 + side]
        got = jnp.zeros((8, 128), F32)
        for t in range(window):
            pick = jnp.take_along_axis(tiles[t0 + t], ids & 127, axis=1, mode="promise_in_bounds")
            got = jnp.where(ids // 128 == t, pick, got)
        return middle[0:1] + jnp.sum(cs * (got - middle), axis=0, keepdims=True)

    def base(j, _):
        at = pl.ds(pl.multiple_of(j * BLK, BLK), BLK)
        seas[:, at] = jnp.concatenate([surface(j, h) for h in range(BLK // 128)], axis=1)
        return 0

    lax.fori_loop(0, columns // BLK, base, 0, unroll=2)

    def arrive(j, _):
        at = pl.ds(pl.multiple_of(j * BLK, BLK), BLK)
        flux = jnp.zeros((2 * fields, BLK), F32)
        for r in range(links):
            ids = slot[r : r + 1, at]
            hot = one_hot(ids & (lanes - 1), lanes)
            hots[j, :, r * BLK : (r + 1) * BLK] = hot
            got = mm(rows[...], hot)
            got = jnp.where(high_of_row == ids // lanes, got[:table] + got[table:], 0.0)
            flux = flux + weight[r : r + 1, at] * fold_rows(got, 2 * fields)
        flux = flux[:fields] + flux[fields:]
        flux_out[:, at] = flux
        seas[:, at] += corner * flux[0:1]
        return 0

    lax.fori_loop(0, columns // BLK, arrive, 0, unroll=2)

    def leave(j, _):
        at = pl.ds(pl.multiple_of(j * BLK, BLK), BLK)
        sea = seas[:, at]
        left = []
        for r in range(links):
            ids, scale = slot[r : r + 1, at], weight[r : r + 1, at]
            high, low = halves(jnp.where(pattern == 1, scale, scale * sea))
            mask = back_high == ids // lanes
            both = [
                jnp.where(mask, jnp.concatenate([x.astype(F32)] * (2 * highs // 8), axis=0), 0.0).astype(BF)
                for x in (high, low)
            ]
            left.append(jnp.concatenate(both, axis=0))
        acc[...] += mm_t(jnp.concatenate(left, axis=1), hots[j])
        return 0

    lax.fori_loop(0, columns // BLK, leave, 0, unroll=2)
    back[...] = (acc[: 2 * highs] + acc[2 * highs :]).reshape(back.shape)


def settle_kernel(back, cols, surf, out, acc):
    peers, per_peer, lanes = back.shape
    parts = per_peer // 2
    blocks = surf.shape[1] // BLK
    acc[...] = jnp.zeros_like(acc)
    block_of_row = iota((blocks, lanes), 0)

    def one(d, _):
        left, hots = [], []
        for h in range(parts):
            ids = cols[pl.ds(d, 1), h * lanes : (h + 1) * lanes]
            mask = block_of_row == ids // BLK
            value = jnp.where(mask, back[d, h : h + 1, :], 0.0)
            scale = jnp.where(mask, back[d, parts + h : parts + h + 1, :], 0.0)
            left.append(stacked(jnp.concatenate([value, scale], axis=0)))
            hots.append(one_hot(ids & (BLK - 1), BLK))
        acc[...] += mm_t(jnp.concatenate(left, axis=1), jnp.concatenate(hots, axis=1))
        return 0

    lax.fori_loop(0, peers, one, 0, unroll=4)
    sums = acc[: 2 * blocks] + acc[2 * blocks :]
    base = jnp.concatenate([surf[0:1, b * BLK : (b + 1) * BLK] for b in range(blocks)], axis=0)
    value = (base + sums[:blocks]) / (1.0 + sums[blocks:])
    for b in range(blocks):
        for i in range(BLK // 128):
            row = b * (BLK // 128) + i
            out[row : row + 1, :] = value[b : b + 1, i * 128 : (i + 1) * 128]


def edge_kernel(before, after, atm, kept, mid, q, vertical, band, far, out, w, sides, sa, sb, sems):
    blocks = q.shape[0]
    count = 2 * ASTEPS - 1
    halo = ASTEPS - 1
    copies = []
    for side in range(2):
        at = slice(0, 2 * BLK) if side == 0 else slice((blocks - 2) * BLK, blocks * BLK)
        copy = pltpu.make_async_copy(atm.at[:, at], sides.at[side], sems.at[2 * count + side])
        copy.start()
        copies.append(copy)
    sources = [far.at[i] for i in range(halo)] + [band.at[i] for i in range(ASTEPS)]
    sources += [band.at[blocks - ASTEPS + i] for i in range(ASTEPS)] + [far.at[halo + i] for i in range(halo)]
    for i, source in enumerate(sources):
        copy = pltpu.make_async_copy(source, w.at[i], sems.at[i])
        copy.start()
        copies.append(copy)
    for i in range(ASTEPS):
        at = slice(i * BLK, (i + 1) * BLK)
        sa[i] = stacked(before[:, at])
        sa[6 + 2 + i] = stacked(after[:, at])
    for copy in copies:
        copy.wait()
    for i in range(2):
        at = slice(i * BLK, (i + 1) * BLK)
        sa[ASTEPS + i] = stacked(sides[0, :, at])
        sa[6 + i] = stacked(sides[1, :, at])
    buffers = (sa, sb)
    for s in range(1, ASTEPS + 1):
        source, target = buffers[(s - 1) % 2], buffers[s % 2]
        last = s == ASTEPS

        def one(i, _, s=s, source=source, target=target, last=last):
            for side in range(2):
                base = 6 * side
                k = s - 1 + i if side == 0 else count + ASTEPS - s + i
                value = stacked(product_long([source[base + i + d] for d in range(3)], (w[k, 0], w[k, 1])))
                target[base + i + (2 * side if not last else 0)] = value
            return 0

        lax.fori_loop(0, ASTEPS, one, 0, unroll=2)
        if not last:
            for i in range(2):
                target[ASTEPS + i] = kept[(s - 1) * 4 + i]
                target[6 + i] = kept[(s - 1) * 4 + 2 + i]
    rows = out.shape[0]
    final = buffers[ASTEPS % 2]

    def mixed(source, shift):
        def one(b, _):
            at = pl.ds(pl.multiple_of(b * BLK, BLK), BLK)
            qh, ql = halves(q[b])
            x2 = source[b - shift]
            high = jnp.concatenate([x2[:rows], qh], axis=0)
            low = jnp.concatenate([x2[rows:], ql], axis=0)
            wide = mm(vertical[...], high)
            out[:, at] = wide[:rows] + wide[rows:] + mm(vertical[:rows], low)
            return 0

        return one

    lax.fori_loop(0, ASTEPS, mixed(final, 0), 0, unroll=2)
    lax.fori_loop(ASTEPS, blocks - ASTEPS, mixed(mid, ASTEPS), 0, unroll=2)
    lax.fori_loop(blocks - ASTEPS, blocks, mixed(final, blocks - ASTEPS - 6), 0, unroll=2)


def ocean_kernel(ocean, before, after, nbr, coef, omix, flux, out, x2, wa, wb):
    levels = omix.shape[0]
    fields = flux.shape[0]
    columns = ocean.shape[1]
    blocks = columns // BLK
    eye = iota((levels, levels), 0) == iota((levels, levels), 1)
    step = omix[...] + jnp.where(eye, 1.0, 0.0)
    top = jnp.broadcast_to(step[:, 0:1], (levels, BLK))
    mix2 = stacked(step)

    def part(first, width):
        pieces = []
        for ref, begin, size in ((before, -HO, HO), (ocean, 0, columns), (after, columns, HO)):
            lo, hi = max(first, begin), min(first + width, begin + size)
            if lo < hi:
                pieces.append(ref[:, lo - begin : hi - begin])
        return pieces[0] if len(pieces) == 1 else jnp.concatenate(pieces, axis=1)

    for e in range((columns + 2 * HO) // BLK):
        x2[e] = stacked(part(e * BLK - HO, BLK))

    def build(b, w):
        at = pl.ds(pl.multiple_of(b * BLK, BLK), BLK)

        def store(first, size, lanes, high, low):
            w[0, first : first + size, lanes] = high
            w[1, first : first + size, lanes] = low

        build_band(store, nbr[:, at] - b * BLK, coef[:, at], HO)

    def finish(b, w):
        at = pl.ds(pl.multiple_of(b * BLK, BLK), BLK)
        source = jnp.concatenate([x2[b + d] for d in range(1 + 2 * HO // BLK)], axis=1)
        moved = product(source, (w[0], w[1]))
        for f in range(fields):
            rows = slice(f * levels, (f + 1) * levels)
            high, low = halves(moved[rows])
            wide = mm(mix2, high)
            out[rows, at] = (
                wide[:levels] + wide[levels:] + mm(mix2[:levels], low) + top * flux[f : f + 1, at]
            )

    build(0, wa)

    def one(i, _):
        b = 2 * i
        build(b + 1, wb)
        finish(b, wa)
        build(jnp.minimum(b + 2, blocks - 1), wa)
        finish(b + 1, wb)
        return 0

    lax.fori_loop(0, blocks // 2, one, 0)


def after_all(value, *others):
    return lax.optimization_barrier((value, *others))[0]


def per_device(
    atm_state,
    atm_surface,
    bulk_coef,
    atm_nbr,
    atm_nbr_coef,
    atm_mix,
    ocean_state,
    ocean_nbr,
    ocean_nbr_coef,
    ocean_mix,
    send_cols,
    remap_slot,
    remap_weight,
):
    fields, la, columns = atm_state.shape
    lo, cells = ocean_state.shape[1:]
    blocks = columns // BLK
    rows = fields * la
    states = fields * ASTEPS
    picked = send_cols[0]
    peers, slots = picked.shape
    lanes = min(BLK, slots)
    parts = slots // lanes
    atm = atm_state.reshape(rows, columns)
    ocean = ocean_state.reshape(fields * lo, cells)
    depth = lax.axis_size(AXES)
    up = [(i, (i + 1) % depth) for i in range(depth)]
    down = [(j, i) for i, j in up]
    window = BLK + 2 * HA
    vmem = pl.BlockSpec(memory_space=pltpu.VMEM)
    anywhere = pl.BlockSpec(memory_space=pl.ANY)

    depth_k = rows + states
    r_of, c_of = np.arange(rows)[:, None], np.arange(depth_k)[None, :]
    code = np.where(
        c_of < rows,
        (c_of // la == r_of // la) * 1,
        ((c_of - rows) % fields == r_of // la) * (2 + (c_of - rows) // fields),
    ).astype(np.int32)
    spread = ((c_of % la == np.arange(la)[:, None]) & (c_of < rows)).astype(np.float32)

    y, yo, first, last, gains, vertical = call(
        prepare_kernel(fields),
        (
            shape((states, columns)),
            shape((1, columns)),
            shape((40, WIDE)),
            shape((40, WIDE)),
            shape((states, 128)),
            shape((2 * rows, depth_k), BF),
        ),
        in_specs=[vmem] * 3 + [anywhere] + [vmem] * 6,
        scratch=[pltpu.VMEM((lo, cells), F32), pltpu.SemaphoreType.DMA(())],
    )(
        atm_mix,
        ocean_mix,
        atm,
        ocean,
        atm_nbr,
        atm_nbr_coef,
        bulk_coef,
        atm_surface,
        jnp.asarray(spread),
        jnp.asarray(code),
    )
    pack_before = lax.ppermute(last, AXES, up)
    pack_after = lax.ppermute(first, AXES, down)

    later, later_sea = lax.optimization_barrier((atm, ocean, first, last))[:2]
    atm_before = lax.ppermute(later[:, columns - WIDE :], AXES, up)
    atm_after = lax.ppermute(later[:, :WIDE], AXES, down)
    sea_before = lax.ppermute(later_sea[:, cells - HO :], AXES, up)
    sea_after = lax.ppermute(later_sea[:, :HO], AXES, down)

    band = call(
        band_kernel,
        shape((blocks, 2, window, BLK), BF),
        in_specs=[vmem] * 2,
        out_specs=anywhere,
        scratch=[pltpu.VMEM((blocks, 2, window, BLK), BF), pltpu.SemaphoreType.DMA((blocks,))],
    )(after_all(atm_nbr, y), atm_nbr_coef)

    total = blocks + 2 * ASTEPS
    halo = ASTEPS - 1
    q, kept, mid, far = call(
        interior_kernel,
        (
            shape((blocks, states, BLK)),
            shape((4 * halo, 2 * rows, BLK), BF),
            shape((blocks - 2 * ASTEPS, 2 * rows, BLK), BF),
            shape((2 * halo, 2, window, BLK), BF),
        ),
        in_specs=[vmem] * 7 + [anywhere],
        out_specs=(vmem, vmem, vmem, anywhere),
        scratch=[
            pltpu.VMEM((total - 2, 2, window, BLK), BF),
            pltpu.VMEM((blocks, 2 * depth_k, BLK), BF),
            pltpu.VMEM((blocks, 2 * depth_k, BLK), BF),
            pltpu.VMEM((total, 2 * states, BLK), BF),
            pltpu.VMEM((total, 2 * states, BLK), BF),
            pltpu.VMEM((total, fields, BLK), F32),
            pltpu.VMEM((total, fields, BLK), F32),
            pltpu.SemaphoreType.DMA((blocks + 2 * halo,)),
        ],
    )(atm, y, after_all(pack_before, band), pack_after, bulk_coef, atm_surface, gains, band)

    outgoing = call(
        send_kernel,
        shape((peers, parts * fields, lanes)),
        in_specs=[vmem] * 2,
        scratch=[pltpu.VMEM((blocks * fields, BLK), F32)],
    )(q, picked)
    received = lax.all_to_all(outgoing, AXES, split_axis=0, concat_axis=0, tiled=True)

    atm_final = call(
        edge_kernel,
        shape((rows, columns)),
        in_specs=[vmem] * 2 + [anywhere] + [vmem] * 4 + [anywhere] * 2,
        scratch=[
            pltpu.VMEM((2 * (2 * ASTEPS - 1), 2, window, BLK), BF),
            pltpu.VMEM((2, rows, 2 * BLK), F32),
            pltpu.VMEM((12, 2 * rows, BLK), BF),
            pltpu.VMEM((12, 2 * rows, BLK), BF),
            pltpu.SemaphoreType.DMA((4 * ASTEPS,)),
        ],
    )(after_all(atm_before, outgoing), atm_after, atm, kept, mid, q, vertical, band, far)

    received = after_all(received, atm_final)
    flux, back = call(
        exchange_kernel,
        (shape((fields, cells)), shape((peers, 2 * parts, lanes))),
        in_specs=[vmem] * 9,
        scratch=[
            pltpu.VMEM((2 * peers * parts * fields, lanes), BF),
            pltpu.VMEM((cells // 128 + 2 * HO // 128, 8, 128), F32),
            pltpu.VMEM((cells // BLK, lanes, remap_slot.shape[0] * BLK), BF),
            pltpu.VMEM((1, cells), F32),
            pltpu.VMEM((4 * peers * parts, lanes), F32),
        ],
    )(received, remap_slot, remap_weight, yo, pack_before, pack_after, ocean_nbr, ocean_nbr_coef, ocean_mix)
    returned = lax.all_to_all(back, AXES, split_axis=0, concat_axis=0, tiled=True)

    ocean_final = call(
        ocean_kernel,
        shape((fields * lo, cells)),
        in_specs=[vmem] * 7,
        scratch=[
            pltpu.VMEM(((cells + 2 * HO) // BLK, 2 * fields * lo, BLK), BF),
            pltpu.VMEM((2, BLK + 2 * HO, BLK), BF),
            pltpu.VMEM((2, BLK + 2 * HO, BLK), BF),
        ],
    )(ocean, after_all(sea_before, back), sea_after, ocean_nbr, ocean_nbr_coef, ocean_mix, flux)

    surface_temp = call(
        settle_kernel,
        shape((columns // 128, 128)),
        in_specs=[vmem] * 3,
        scratch=[pltpu.VMEM((4 * blocks, BLK), F32)],
    )(after_all(returned, ocean_final), picked, atm_surface)

    return (
        atm_final.reshape(fields, la, columns),
        ocean_final.reshape(fields, lo, cells),
        surface_temp.reshape(columns),
    )


def solution(mesh):
    placed = (
        P(None, None, AXES),
        P(None, AXES),
        P(None, AXES),
        P(None, AXES),
        P(None, AXES),
        P(),
        P(None, None, AXES),
        P(None, AXES),
        P(None, AXES),
        P(),
        P(AXES, None, None),
        P(None, AXES),
        P(None, AXES),
    )
    return jax.shard_map(
        per_device,
        mesh=mesh,
        in_specs=placed,
        out_specs=(P(None, None, AXES), P(None, None, AXES), P(AXES)),
        check_vma=False,
    )
```

```python
import numpy as np

import jax
import jax.numpy as jnp
from jax import lax
from jax.experimental import pallas as pl
from jax.experimental.pallas import tpu as pltpu
from jax.sharding import PartitionSpec as P

ASTEPS = 4
HA = 256
HO = 384
BLK = 256
WIDE = ASTEPS * HA
BF = jnp.bfloat16
F32 = jnp.float32
VMEM_BYTES = 56 * 1024 * 1024
AXES = ("sec", "blk")


def call(body, outs, *, in_specs=None, out_specs=None, scratch=(), flops=10**6, moved=10**4, aliases=None):
    vmem = pl.BlockSpec(memory_space=pltpu.VMEM)
    return pl.pallas_call(
        body,
        out_shape=outs,
        in_specs=in_specs,
        out_specs=jax.tree.map(lambda _: vmem, outs) if out_specs is None else out_specs,
        scratch_shapes=list(scratch),
        input_output_aliases=aliases or {},
        compiler_params=pltpu.CompilerParams(vmem_limit_bytes=VMEM_BYTES),
        cost_estimate=pl.CostEstimate(flops=flops, bytes_accessed=moved, transcendentals=0),
    )


def shape(dims, dtype=F32):
    return jax.ShapeDtypeStruct(dims, dtype)


def halves(x):
    high = x.astype(BF)
    return high, (x - high.astype(F32)).astype(BF)


def stacked(x):
    return jnp.concatenate(halves(x), axis=0)


def mm(a, b):
    return jnp.dot(a, b, preferred_element_type=F32)


def mm_t(a, b):
    return lax.dot_general(a, b, (((1,), (1,)), ((), ())), preferred_element_type=F32)


def product(x2, w2):
    rows = x2.shape[0] // 2
    wide = mm(x2, w2[0])
    return wide[:rows] + wide[rows:] + mm(x2[:rows], w2[1])


def product_pieces(x2s, w2, result):
    rows = x2s[0].shape[0] // 2
    for t, x2 in enumerate(x2s):
        at = slice(t * BLK, (t + 1) * BLK)
        wide = mm(x2, w2.at[0][at])
        part = wide[:rows] + wide[rows:]
        result[...] = part if t == 0 else result[...] + part
        yield
        result[...] += mm(x2[:rows], w2.at[1][at])
        yield


def interleave(*works):
    works = list(works)
    while works:
        works = [w for w in works if next(w, w) is not w]


def iota(dims, axis):
    return lax.broadcasted_iota(jnp.int32, dims, axis)


def build_band(*args):
    for _ in band_pieces(*args):
        pass


def band_pieces(store, nbr, coef, halo):
    rows = BLK + 2 * halo
    count = nbr.shape[0]
    ids = [nbr[k : k + 1] for k in range(count)]
    cs = [coef[k : k + 1] for k in range(count)]
    rest = 1.0 - sum(cs[1:], cs[0])
    for k in range(count - 1, 0, -1):
        alive = jnp.ones_like(ids[k]) > 0
        for j in range(k):
            same = jnp.logical_and(ids[k] == ids[j], alive)
            cs[j] = cs[j] + jnp.where(same, cs[k], 0.0)
            alive = jnp.logical_and(alive, jnp.logical_not(same))
        ids[k] = jnp.where(alive, ids[k], -1)
    lanes = 128
    step = 16
    base = iota((step, lanes), 0).astype(F32)
    parts = [halves(c) for c in cs + [rest]]

    def wide(x, at):
        return jnp.broadcast_to(x[:, at].astype(F32), (step, lanes)).astype(BF)

    for half in range(BLK // lanes):
        at = slice(half * lanes, (half + 1) * lanes)
        highs = [wide(p[0], at) for p in parts]
        lows = [wide(p[1], at) for p in parts]
        own = (iota((step, lanes), 1) - iota((step, lanes), 0)).astype(F32).astype(BF)
        zero = jnp.zeros((step, lanes), BF)
        for tile in range(0, rows, BLK):
            near = [wide((i - tile).astype(F32), at) for i in ids]
            for first in range(tile, tile + BLK, step):
                high, low = zero, zero
                if half * lanes - step < first < half * lanes + lanes + 2 * halo:
                    offset = first - halo - half * lanes
                    if 0 <= offset < lanes:
                        same = own == jnp.full((step, lanes), offset, BF)
                        high = jnp.where(same, highs[-1], zero)
                        low = jnp.where(same, lows[-1], zero)
                    here = (base + float(first - tile)).astype(BF)
                    for k in range(count):
                        same = here == near[k]
                        high = jnp.where(same, highs[k], high)
                        low = jnp.where(same, lows[k], low)
                store(first, step, at, high, low)
            yield


def one_hot(ids, rows):
    return jnp.where(iota((rows, ids.shape[1]), 0) == ids, 1.0, 0.0).astype(BF)


def fold_rows(x, height):
    total = x[:height]
    for first in range(height, x.shape[0], height):
        total = total + x[first : first + height]
    return total


def prepare_kernel(fields):
    def body(mix, omix, atm, sea, nbr, coef, bulk, surf, spread, code, y, yo, first, last, gains, vertical, top, sem):
        la = mix.shape[0]
        columns = atm.shape[1]
        copy = pltpu.make_async_copy(sea.at[: omix.shape[0], :], top, sem)
        copy.start()
        eye = iota((la, la), 0) == iota((la, la), 1)
        step = mix[...] + jnp.where(eye, 1.0, 0.0)

        def dot(a, b):
            return jnp.dot(a, b, precision=lax.Precision.HIGHEST, preferred_element_type=F32)

        def col(r, same):
            return jnp.sum(jnp.where(same, r, 0.0), axis=1, keepdims=True)

        def row(c, same):
            return jnp.sum(jnp.where(same, c, 0.0), axis=0, keepdims=True)

        twice = dot(step, step)
        fourth = dot(twice, twice)
        rows_up = [step[la - 1 : la, :]]
        cols_up = [step[:, la - 1 : la]]
        for _ in range(ASTEPS - 2):
            rows_up.append(jnp.sum(step * col(rows_up[-1], eye), axis=0, keepdims=True))
        for _ in range(ASTEPS - 1):
            cols_up.append(jnp.sum(step * row(cols_up[-1], eye), axis=1, keepdims=True))
        slot = iota((fields * ASTEPS, 128), 0) // fields
        lane = iota((fields * ASTEPS, 128), 1)
        value = jnp.zeros((fields * ASTEPS, 128), F32)
        for s in range(1, ASTEPS + 1):
            column = jnp.where(slot == s - 1, 1.0, 0.0)
            for j in range(1, ASTEPS):
                column = jnp.where(slot == s - 1 + j, rows_up[j - 1][:, la - 1 : la], column)
            value = jnp.where(lane == s - 1, column, value)
        gains[...] = value

        tall = jnp.concatenate([fourth] * fields, axis=0)
        spreaded = dot(tall, spread[...])
        filled = jnp.where(code[...] == 1, spreaded, 0.0)
        for m in range(ASTEPS):
            tall = jnp.concatenate([cols_up[ASTEPS - 1 - m]] * fields, axis=0)
            filled = jnp.where(code[...] == 2 + m, tall, filled)
        vertical[...] = stacked(filled)

        weights = [jnp.broadcast_to(col(r, eye), (la, 128)) for r in rows_up]
        lo = omix.shape[0]
        sea_eye = iota((lo, lo), 0) == iota((lo, lo), 1)
        sea_row = omix[0:1, :] + jnp.where(iota((1, lo), 1) == 0, 1.0, 0.0)
        sea_weight = jnp.broadcast_to(col(sea_row, sea_eye), (lo, 128))
        copy.wait()
        for start in range(0, columns, 128):
            at = slice(start, start + 128)
            for f in range(fields):
                x = atm[f * la : (f + 1) * la, at]
                y[f : f + 1, at] = x[la - 1 : la]
                for k in range(1, ASTEPS):
                    y[k * fields + f : k * fields + f + 1, at] = jnp.sum(
                        x * weights[k - 1], axis=0, keepdims=True
                    )
            yo[:, at] = jnp.sum(top[:, at] * sea_weight, axis=0, keepdims=True)
        for target, at in ((first, slice(0, WIDE)), (last, slice(columns - WIDE, columns))):
            target[0:16, :] = y[:, at]
            target[16:22, :] = nbr[:, at].astype(F32)
            target[22:28, :] = coef[:, at]
            target[28:32, :] = bulk[:, at]
            target[32:36, :] = surf[:, at]
            target[36:37, :] = yo[:, at]
            target[37:40, :] = jnp.zeros((3, WIDE), F32)

    return body


def band_kernel(nbr, coef, band, w, sems):
    blocks = nbr.shape[1] // BLK

    def copy(b):
        return pltpu.make_async_copy(w.at[b], band.at[b], sems.at[b])

    def build(b, _):
        at = pl.ds(pl.multiple_of(b * BLK, BLK), BLK)

        def store(first, step, lanes, high, low):
            w[b, 0, first : first + step, lanes] = high
            w[b, 1, first : first + step, lanes] = low

        build_band(store, nbr[:, at] - b * BLK, coef[:, at], HA)
        copy(b).start()
        return 0

    lax.fori_loop(0, blocks, build, 0)

    def finish(b, _):
        copy(b).wait()
        return 0

    lax.fori_loop(0, blocks, finish, 0)


def interior_kernel(
    atm, y, before, after, bulk, surf, gains, band, q, kept, mid, far, w, sa, sb, za, zb, bulks, surfs, sems
):
    rows, columns = atm.shape
    blocks = columns // BLK
    fields = bulk.shape[0]
    states = fields * ASTEPS
    total = blocks + 2 * ASTEPS
    halo = ASTEPS - 1

    def arriving(b):
        return pltpu.make_async_copy(band.at[b], w.at[halo + b], sems.at[b])

    for b in [0, blocks - 1] + list(range(1, blocks - 1)):
        arriving(b).start()

    leaving = []
    for e in list(range(ASTEPS)) + list(range(ASTEPS + blocks, total)):
        pack = before if e < ASTEPS else after
        local = e if e < ASTEPS else e - ASTEPS - blocks
        at = slice(local * BLK, (local + 1) * BLK)
        za[e] = stacked(pack[0:states, at])
        bulks[e] = pack[28:32, at]
        surfs[e] = pack[32:36, at]
        if e in (0, total - 1):
            continue
        origin = local * BLK + (columns - WIDE if e < ASTEPS else 0)

        def store(first, step, lanes, high, low, e=e):
            w[e - 1, 0, first : first + step, lanes] = high
            w[e - 1, 1, first : first + step, lanes] = low

        build_band(store, pack[16:22, at].astype(jnp.int32) - origin, pack[22:28, at], HA)
        i = e - 1 if e < ASTEPS else e - 1 - blocks
        copy = pltpu.make_async_copy(w.at[e - 1], far.at[i], sems.at[blocks + i])
        copy.start()
        leaving.append(copy)
    for b in range(blocks):
        at = slice(b * BLK, (b + 1) * BLK)
        both = stacked(jnp.concatenate([atm[:, at], y[:, at]], axis=0))
        sa[b] = both
        height = rows + states
        za[b + ASTEPS] = jnp.concatenate([both[rows:height], both[height + rows :]], axis=0)
        bulks[b + ASTEPS] = bulk[:, at]
        surfs[b + ASTEPS] = surf[:, at]

    arriving(0).wait()
    arriving(blocks - 1).wait()

    slot = iota((states, BLK), 0) // fields
    for s in range(1, ASTEPS + 1):
        xs, xt = (sa, sb) if s % 2 else (sb, sa)
        zs, zt = (za, zb) if s % 2 else (zb, za)
        gain = jnp.broadcast_to(gains[:, s - 1 : s], (states, BLK))
        keep = jnp.where(slot == s - 1, 0.0, 1.0)

        def advance(moved, e, s=s, gain=gain, keep=keep):
            flux = bulks[e] * (surfs[e] - moved[(s - 1) * fields : s * fields])
            return moved * keep + gain * jnp.concatenate([flux] * ASTEPS, axis=0)

        def edge(e, s=s, zs=zs, zt=zt, advance=advance):
            x2 = jnp.concatenate([zs[e - 1], zs[e], zs[e + 1]], axis=1)
            value = advance(product(x2, (w[e - 1, 0], w[e - 1, 1])), e)
            if s == ASTEPS:
                q[e - ASTEPS] = value
            else:
                zt[e] = stacked(value)

        def inner(b, s=s, xs=xs, xt=xt, zt=zt, advance=advance):
            x2 = jnp.concatenate([xs[b - 1], xs[b], xs[b + 1]], axis=1)
            moved = product(x2, (w[b + halo, 0], w[b + halo, 1]))
            value = advance(moved[rows:], b + ASTEPS)
            if s == ASTEPS:
                q[b] = value
                mid[b - ASTEPS] = stacked(moved[:rows])
            else:
                high, low = halves(moved[:rows])
                zh, zl = halves(value)
                xt[b] = jnp.concatenate([high, zh, low, zl], axis=0)
                zt[b + ASTEPS] = jnp.concatenate([zh, zl], axis=0)

        def together(i, _, s=s, edge=edge, inner=inner):
            if s == 1:
                arriving(1 + 2 * i).wait()
                arriving(2 + 2 * i).wait()
            inner(s + 2 * i)
            inner(s + 2 * i + 1)
            edge(s + i)
            edge(blocks + ASTEPS - s + i)
            return 0

        def alone(i, _, s=s, inner=inner):
            if s == 1:
                arriving(1 + 2 * i).wait()
                arriving(2 + 2 * i).wait()
            inner(s + 2 * i)
            inner(s + 2 * i + 1)
            return 0

        lax.fori_loop(0, ASTEPS, together, 0)
        if blocks // 2 - s > ASTEPS:
            lax.fori_loop(ASTEPS, blocks // 2 - s, alone, 0)
        if s < ASTEPS:
            height = rows + states
            for i, b in enumerate((s, s + 1, blocks - 2 - s, blocks - 1 - s)):
                kept[(s - 1) * 4 + i, :rows] = xt[b, :rows]
                kept[(s - 1) * 4 + i, rows:] = xt[b, height : height + rows]
    for copy in leaving:
        copy.wait()


def send_kernel(q, cols, out, table):
    fields = q.shape[1] // ASTEPS
    peers, slots = cols.shape
    blocks = q.shape[0]
    lanes = out.shape[2]
    parts = slots // lanes
    for b in range(blocks):
        table[b * fields : (b + 1) * fields, :] = q[b, (ASTEPS - 1) * fields :, :]
    rows = stacked(table[...])
    half = blocks * fields
    block_of_row = iota((half, slots), 0) // fields

    def one(p, _):
        ids = cols[pl.ds(p, 1), :]
        got = mm(rows, one_hot(ids & (BLK - 1), BLK))
        got = jnp.where(block_of_row == ids // BLK, got[:half] + got[half:], 0.0)
        got = fold_rows(got, 2 * fields)
        got = got[:fields] + got[fields:]
        out[p] = jnp.concatenate([got[:, i * lanes : (i + 1) * lanes] for i in range(parts)], axis=0)
        return 0

    lax.fori_loop(0, peers, one, 0, unroll=4)


def exchange_kernel(recv, slot, weight, yo, before, after, nbr, coef, omix, flux_out, back, rows, tiles, hots, seas, acc):
    peers, per_peer, lanes = recv.shape
    links, columns = slot.shape
    fields = flux_out.shape[0]
    parts = per_peer // fields
    highs = peers * parts
    table = highs * fields
    rows[...] = stacked(recv[...].reshape(table, lanes))
    acc[...] = jnp.zeros_like(acc)
    side = HO // 128
    own_tiles = columns // 128
    for t in range(own_tiles + 2 * side):
        if t < side:
            line = before[36:37, WIDE - HO + t * 128 : WIDE - HO + (t + 1) * 128]
        elif t < side + own_tiles:
            line = yo[:, (t - side) * 128 : (t - side + 1) * 128]
        else:
            line = after[36:37, (t - side - own_tiles) * 128 : (t - side - own_tiles + 1) * 128]
        tiles[t] = jnp.broadcast_to(line, (8, 128))
    corner = omix[0:1, 0:1] + 1.0
    high_of_row = iota((table, BLK), 0) // fields
    back_rows = iota((2 * highs, BLK), 0)
    inner = back_rows % (2 * parts)
    back_high = (back_rows // (2 * parts)) * parts + inner % parts
    pattern = iota((8, BLK), 0) % (2 * parts) // parts
    window = 1 + 2 * side
    neighbors = nbr.shape[0]

    def surface(j, half):
        t0 = j * (BLK // 128) + half
        at = pl.ds(pl.multiple_of(t0 * 128, 128), 128)
        pad = jnp.zeros((8 - neighbors, 128), jnp.int32)
        ids = jnp.concatenate([nbr[:, at] - t0 * 128, pad], axis=0)
        cs = jnp.concatenate([coef[:, at], pad.astype(F32)], axis=0)
        middle = tiles[t0 + side]
        got = jnp.zeros((8, 128), F32)
        for t in range(window):
            pick = jnp.take_along_axis(tiles[t0 + t], ids & 127, axis=1, mode="promise_in_bounds")
            got = jnp.where(ids // 128 == t, pick, got)
        return middle[0:1] + jnp.sum(cs * (got - middle), axis=0, keepdims=True)

    def base(j, _):
        at = pl.ds(pl.multiple_of(j * BLK, BLK), BLK)
        seas[:, at] = jnp.concatenate([surface(j, h) for h in range(BLK // 128)], axis=1)
        return 0

    lax.fori_loop(0, columns // BLK, base, 0, unroll=2)

    def arrive(j, _):
        at = pl.ds(pl.multiple_of(j * BLK, BLK), BLK)
        flux = jnp.zeros((2 * fields, BLK), F32)
        for r in range(links):
            ids = slot[r : r + 1, at]
            hot = one_hot(ids & (lanes - 1), lanes)
            hots[j, :, r * BLK : (r + 1) * BLK] = hot
            got = mm(rows[...], hot)
            got = jnp.where(high_of_row == ids // lanes, got[:table] + got[table:], 0.0)
            flux = flux + weight[r : r + 1, at] * fold_rows(got, 2 * fields)
        flux = flux[:fields] + flux[fields:]
        flux_out[:, at] = flux
        seas[:, at] += corner * flux[0:1]
        return 0

    lax.fori_loop(0, columns // BLK, arrive, 0, unroll=2)

    def leave(j, _):
        at = pl.ds(pl.multiple_of(j * BLK, BLK), BLK)
        sea = seas[:, at]
        left = []
        for r in range(links):
            ids, scale = slot[r : r + 1, at], weight[r : r + 1, at]
            high, low = halves(jnp.where(pattern == 1, scale, scale * sea))
            mask = back_high == ids // lanes
            both = [
                jnp.where(mask, jnp.concatenate([x.astype(F32)] * (2 * highs // 8), axis=0), 0.0).astype(BF)
                for x in (high, low)
            ]
            left.append(jnp.concatenate(both, axis=0))
        acc[...] += mm_t(jnp.concatenate(left, axis=1), hots[j])
        return 0

    lax.fori_loop(0, columns // BLK, leave, 0, unroll=2)
    back[...] = (acc[: 2 * highs] + acc[2 * highs :]).reshape(back.shape)


def settle_kernel(back, cols, surf, out, acc):
    peers, per_peer, lanes = back.shape
    parts = per_peer // 2
    blocks = surf.shape[1] // BLK
    acc[...] = jnp.zeros_like(acc)
    block_of_row = iota((blocks, lanes), 0)

    def one(d, _):
        left, hots = [], []
        for h in range(parts):
            ids = cols[pl.ds(d, 1), h * lanes : (h + 1) * lanes]
            mask = block_of_row == ids // BLK
            value = jnp.where(mask, back[d, h : h + 1, :], 0.0)
            scale = jnp.where(mask, back[d, parts + h : parts + h + 1, :], 0.0)
            left.append(stacked(jnp.concatenate([value, scale], axis=0)))
            hots.append(one_hot(ids & (BLK - 1), BLK))
        acc[...] += mm_t(jnp.concatenate(left, axis=1), jnp.concatenate(hots, axis=1))
        return 0

    lax.fori_loop(0, peers, one, 0, unroll=4)
    sums = acc[: 2 * blocks] + acc[2 * blocks :]
    base = jnp.concatenate([surf[0:1, b * BLK : (b + 1) * BLK] for b in range(blocks)], axis=0)
    value = (base + sums[:blocks]) / (1.0 + sums[blocks:])
    for b in range(blocks):
        for i in range(BLK // 128):
            row = b * (BLK // 128) + i
            out[row : row + 1, :] = value[b : b + 1, i * 128 : (i + 1) * 128]


def edge_kernel(
    before, after, atm, kept, mid, q, vertical, band, far, out, w, halos, sides, sa, sb, staged, wsems, sems, osems
):
    rows = atm.shape[0]
    blocks = q.shape[0]
    halo = ASTEPS - 1
    count = halo + ASTEPS
    arrivals = [
        pltpu.make_async_copy(before, halos.at[0], sems.at[0]),
        pltpu.make_async_copy(after, halos.at[1], sems.at[1]),
        pltpu.make_async_copy(atm.at[:, : 2 * BLK], sides.at[0], sems.at[2]),
        pltpu.make_async_copy(atm.at[:, (blocks - 2) * BLK :], sides.at[1], sems.at[3]),
    ]
    sources = [far.at[i] for i in range(halo)] + [band.at[i] for i in range(ASTEPS)]
    sources += [band.at[blocks - ASTEPS + i] for i in range(ASTEPS)] + [far.at[halo + i] for i in range(halo)]
    bands = [pltpu.make_async_copy(source, w.at[i], wsems.at[i]) for i, source in enumerate(sources)]
    needed = [list(range(ASTEPS)) + list(range(count + halo, 2 * count))]
    needed += [[ASTEPS - 1 + i, count + halo - i] for i in range(1, ASTEPS)]
    for copy in arrivals:
        copy.start()
    for group in needed:
        for i in group:
            bands[i].start()

    def leaving(b):
        at = pl.ds(pl.multiple_of(b * BLK, BLK), BLK)
        return pltpu.make_async_copy(staged.at[b], out.at[:, at], osems.at[b])

    def mixed(source, shift):
        def one(b):
            qh, ql = halves(q[b])
            x2 = source[b - shift]
            high = jnp.concatenate([x2[:rows], qh], axis=0)
            low = jnp.concatenate([x2[rows:], ql], axis=0)
            wide = mm(vertical[...], high)
            staged[b] = wide[:rows] + wide[rows:] + mm(vertical[:rows], low)

        def pair(i, _):
            one(2 * i)
            one(2 * i + 1)
            leaving(2 * i).start()
            leaving(2 * i + 1).start()
            return 0

        return pair

    lax.fori_loop(ASTEPS // 2, (blocks - ASTEPS) // 2, mixed(mid, ASTEPS), 0)
    for copy in arrivals:
        copy.wait()
    for i in range(ASTEPS):
        at = slice(i * BLK, (i + 1) * BLK)
        sa[i] = stacked(halos[0, :, at])
        sa[6 + 2 + i] = stacked(halos[1, :, at])
    for i in range(2):
        at = slice(i * BLK, (i + 1) * BLK)
        sa[ASTEPS + i] = stacked(sides[0, :, at])
        sa[6 + i] = stacked(sides[1, :, at])
    buffers = (sa, sb)
    for s in range(1, ASTEPS + 1):
        source, target = buffers[(s - 1) % 2], buffers[s % 2]
        last = s == ASTEPS
        for i in needed[s - 1]:
            bands[i].wait()

        def one(i, _, s=s, source=source, target=target, last=last):
            for side in range(2):
                base = 6 * side
                k = s - 1 + i if side == 0 else count + ASTEPS - s + i
                x2 = jnp.concatenate([source[base + i + d] for d in range(3)], axis=1)
                value = stacked(product(x2, (w[k, 0], w[k, 1])))
                target[base + i + (2 * side if not last else 0)] = value
            return 0

        lax.fori_loop(0, ASTEPS, one, 0, unroll=2)
        if not last:
            for i in range(2):
                target[ASTEPS + i] = kept[(s - 1) * 4 + i]
                target[6 + i] = kept[(s - 1) * 4 + 2 + i]
    final = buffers[ASTEPS % 2]
    lax.fori_loop(0, ASTEPS // 2, mixed(final, 0), 0)
    lax.fori_loop((blocks - ASTEPS) // 2, blocks // 2, mixed(final, blocks - ASTEPS - 6), 0)

    def done(b, _):
        leaving(b).wait()
        return 0

    lax.fori_loop(0, blocks, done, 0)


def ocean_kernel(ocean, before, after, nbr, coef, omix, flux, out, x2, wa, wb, ma, mb, staged, sems):
    levels = omix.shape[0]
    fields = flux.shape[0]
    columns = ocean.shape[1]
    blocks = columns // BLK
    eye = iota((levels, levels), 0) == iota((levels, levels), 1)
    step = omix[...] + jnp.where(eye, 1.0, 0.0)
    top = jnp.broadcast_to(step[:, 0:1], (levels, BLK))
    mix2 = stacked(step)

    def part(first, width):
        pieces = []
        for ref, begin, size in ((before, -HO, HO), (ocean, 0, columns), (after, columns, HO)):
            lo, hi = max(first, begin), min(first + width, begin + size)
            if lo < hi:
                pieces.append(ref[:, lo - begin : hi - begin])
        return pieces[0] if len(pieces) == 1 else jnp.concatenate(pieces, axis=1)

    for e in range((columns + 2 * HO) // BLK):
        x2[e] = stacked(part(e * BLK - HO, BLK))

    def build(b, w):
        at = pl.ds(pl.multiple_of(b * BLK, BLK), BLK)

        def store(first, size, lanes, high, low):
            w[0, first : first + size, lanes] = high
            w[1, first : first + size, lanes] = low

        return band_pieces(store, nbr[:, at] - b * BLK, coef[:, at], HO)

    def finish(b, w, moved):
        yield from product_pieces([x2[b + d] for d in range(1 + 2 * HO // BLK)], w, moved)
        at = pl.ds(pl.multiple_of(b * BLK, BLK), BLK)
        for f in range(fields):
            rows = slice(f * levels, (f + 1) * levels)
            high, low = halves(moved[rows])
            wide = mm(mix2, high)
            staged[b, rows] = (
                wide[:levels] + wide[levels:] + mm(mix2[:levels], low) + top * flux[f : f + 1, at]
            )
            yield

    def leaving(b):
        at = pl.ds(pl.multiple_of(b * BLK, BLK), BLK)
        return pltpu.make_async_copy(staged.at[b], out.at[:, at], sems.at[b])

    interleave(build(0, wa))

    def one(i, _):
        b = 2 * i
        interleave(build(b + 1, wb), finish(b, wa, ma))
        interleave(build(jnp.minimum(b + 2, blocks - 1), wa), finish(b + 1, wb, mb))
        leaving(b).start()
        leaving(b + 1).start()
        return 0

    lax.fori_loop(0, blocks // 2, one, 0)

    def done(b, _):
        leaving(b).wait()
        return 0

    lax.fori_loop(0, blocks, done, 0)


def after_all(value, *others):
    return lax.optimization_barrier((value, *others))[0]


def per_device(
    atm_state,
    atm_surface,
    bulk_coef,
    atm_nbr,
    atm_nbr_coef,
    atm_mix,
    ocean_state,
    ocean_nbr,
    ocean_nbr_coef,
    ocean_mix,
    send_cols,
    remap_slot,
    remap_weight,
):
    fields, la, columns = atm_state.shape
    lo, cells = ocean_state.shape[1:]
    blocks = columns // BLK
    rows = fields * la
    states = fields * ASTEPS
    picked = send_cols[0]
    peers, slots = picked.shape
    lanes = min(BLK, slots)
    parts = slots // lanes
    atm = atm_state.reshape(rows, columns)
    ocean = ocean_state.reshape(fields * lo, cells)
    depth = lax.axis_size(AXES)
    up = [(i, (i + 1) % depth) for i in range(depth)]
    down = [(j, i) for i, j in up]
    window = BLK + 2 * HA
    vmem = pl.BlockSpec(memory_space=pltpu.VMEM)
    anywhere = pl.BlockSpec(memory_space=pl.ANY)

    depth_k = rows + states
    r_of, c_of = np.arange(rows)[:, None], np.arange(depth_k)[None, :]
    code = np.where(
        c_of < rows,
        (c_of // la == r_of // la) * 1,
        ((c_of - rows) % fields == r_of // la) * (2 + (c_of - rows) // fields),
    ).astype(np.int32)
    spread = ((c_of % la == np.arange(la)[:, None]) & (c_of < rows)).astype(np.float32)

    y, yo, first, last, gains, vertical = call(
        prepare_kernel(fields),
        (
            shape((states, columns)),
            shape((1, columns)),
            shape((40, WIDE)),
            shape((40, WIDE)),
            shape((states, 128)),
            shape((2 * rows, depth_k), BF),
        ),
        in_specs=[vmem] * 3 + [anywhere] + [vmem] * 6,
        scratch=[pltpu.VMEM((lo, cells), F32), pltpu.SemaphoreType.DMA(())],
    )(
        atm_mix,
        ocean_mix,
        atm,
        ocean,
        atm_nbr,
        atm_nbr_coef,
        bulk_coef,
        atm_surface,
        jnp.asarray(spread),
        jnp.asarray(code),
    )
    pack_before = lax.ppermute(last, AXES, up)
    pack_after = lax.ppermute(first, AXES, down)

    band = call(
        band_kernel,
        shape((blocks, 2, window, BLK), BF),
        in_specs=[vmem] * 2,
        out_specs=anywhere,
        scratch=[pltpu.VMEM((blocks, 2, window, BLK), BF), pltpu.SemaphoreType.DMA((blocks,))],
    )(after_all(atm_nbr, y), atm_nbr_coef)

    pack_before, pack_after = lax.optimization_barrier((pack_before, pack_after, band))[:2]
    later, later_sea = lax.optimization_barrier((atm, ocean, pack_before, pack_after))[:2]
    atm_before = lax.ppermute(later[:, columns - WIDE :], AXES, up)
    atm_after = lax.ppermute(later[:, :WIDE], AXES, down)
    sea_before = lax.ppermute(later_sea[:, cells - HO :], AXES, up)
    sea_after = lax.ppermute(later_sea[:, :HO], AXES, down)

    total = blocks + 2 * ASTEPS
    halo = ASTEPS - 1
    q, kept, mid, far = call(
        interior_kernel,
        (
            shape((blocks, states, BLK)),
            shape((4 * halo, 2 * rows, BLK), BF),
            shape((blocks - 2 * ASTEPS, 2 * rows, BLK), BF),
            shape((2 * halo, 2, window, BLK), BF),
        ),
        in_specs=[vmem] * 7 + [anywhere],
        out_specs=(vmem, vmem, vmem, anywhere),
        scratch=[
            pltpu.VMEM((total - 2, 2, window, BLK), BF),
            pltpu.VMEM((blocks, 2 * depth_k, BLK), BF),
            pltpu.VMEM((blocks, 2 * depth_k, BLK), BF),
            pltpu.VMEM((total, 2 * states, BLK), BF),
            pltpu.VMEM((total, 2 * states, BLK), BF),
            pltpu.VMEM((total, fields, BLK), F32),
            pltpu.VMEM((total, fields, BLK), F32),
            pltpu.SemaphoreType.DMA((blocks + 2 * halo,)),
        ],
    )(atm, y, pack_before, pack_after, bulk_coef, atm_surface, gains, band)

    outgoing = call(
        send_kernel,
        shape((peers, parts * fields, lanes)),
        in_specs=[vmem] * 2,
        scratch=[pltpu.VMEM((blocks * fields, BLK), F32)],
    )(q, picked)
    received = lax.all_to_all(outgoing, AXES, split_axis=0, concat_axis=0, tiled=True)

    atm_final = call(
        edge_kernel,
        shape((rows, columns)),
        in_specs=[anywhere] * 3 + [vmem] * 4 + [anywhere] * 2,
        out_specs=anywhere,
        scratch=[
            pltpu.VMEM((2 * (2 * ASTEPS - 1), 2, window, BLK), BF),
            pltpu.VMEM((2, rows, WIDE), F32),
            pltpu.VMEM((2, rows, 2 * BLK), F32),
            pltpu.VMEM((12, 2 * rows, BLK), BF),
            pltpu.VMEM((12, 2 * rows, BLK), BF),
            pltpu.VMEM((blocks, rows, BLK), F32),
            pltpu.SemaphoreType.DMA((2 * (2 * ASTEPS - 1),)),
            pltpu.SemaphoreType.DMA((4,)),
            pltpu.SemaphoreType.DMA((blocks,)),
        ],
    )(after_all(atm_before, outgoing), atm_after, atm, kept, mid, q, vertical, band, far)

    received = after_all(received, atm_final)
    flux, back = call(
        exchange_kernel,
        (shape((fields, cells)), shape((peers, 2 * parts, lanes))),
        in_specs=[vmem] * 9,
        scratch=[
            pltpu.VMEM((2 * peers * parts * fields, lanes), BF),
            pltpu.VMEM((cells // 128 + 2 * HO // 128, 8, 128), F32),
            pltpu.VMEM((cells // BLK, lanes, remap_slot.shape[0] * BLK), BF),
            pltpu.VMEM((1, cells), F32),
            pltpu.VMEM((4 * peers * parts, lanes), F32),
        ],
    )(received, remap_slot, remap_weight, yo, pack_before, pack_after, ocean_nbr, ocean_nbr_coef, ocean_mix)
    returned = lax.all_to_all(back, AXES, split_axis=0, concat_axis=0, tiled=True)

    ocean_final = call(
        ocean_kernel,
        shape((fields * lo, cells)),
        in_specs=[vmem] * 7,
        out_specs=anywhere,
        scratch=[
            pltpu.VMEM(((cells + 2 * HO) // BLK, 2 * fields * lo, BLK), BF),
            pltpu.VMEM((2, BLK + 2 * HO, BLK), BF),
            pltpu.VMEM((2, BLK + 2 * HO, BLK), BF),
            pltpu.VMEM((fields * lo, BLK), F32),
            pltpu.VMEM((fields * lo, BLK), F32),
            pltpu.VMEM((cells // BLK, fields * lo, BLK), F32),
            pltpu.SemaphoreType.DMA((cells // BLK,)),
        ],
    )(ocean, after_all(sea_before, back), sea_after, ocean_nbr, ocean_nbr_coef, ocean_mix, flux)

    surface_temp = call(
        settle_kernel,
        shape((columns // 128, 128)),
        in_specs=[vmem] * 3,
        scratch=[pltpu.VMEM((4 * blocks, BLK), F32)],
    )(after_all(returned, ocean_final), picked, atm_surface)

    return (
        atm_final.reshape(fields, la, columns),
        ocean_final.reshape(fields, lo, cells),
        surface_temp.reshape(columns),
    )


def solution(mesh):
    placed = (
        P(None, None, AXES),
        P(None, AXES),
        P(None, AXES),
        P(None, AXES),
        P(None, AXES),
        P(),
        P(None, None, AXES),
        P(None, AXES),
        P(None, AXES),
        P(),
        P(AXES, None, None),
        P(None, AXES),
        P(None, AXES),
    )
    return jax.shard_map(
        per_device,
        mesh=mesh,
        in_specs=placed,
        out_specs=(P(None, None, AXES), P(None, None, AXES), P(AXES)),
        check_vma=False,
    )
```

```python
import numpy as np

import jax
import jax.numpy as jnp
from jax import lax
from jax.experimental import pallas as pl
from jax.experimental.pallas import tpu as pltpu
from jax.sharding import PartitionSpec as P

ASTEPS = 4
HA = 256
HO = 384
BLK = 256
WIDE = ASTEPS * HA
BF = jnp.bfloat16
F32 = jnp.float32
VMEM_BYTES = 56 * 1024 * 1024
AXES = ("sec", "blk")


def call(body, outs, *, in_specs=None, out_specs=None, scratch=(), flops=10**6, moved=10**4, aliases=None):
    vmem = pl.BlockSpec(memory_space=pltpu.VMEM)
    return pl.pallas_call(
        body,
        out_shape=outs,
        in_specs=in_specs,
        out_specs=jax.tree.map(lambda _: vmem, outs) if out_specs is None else out_specs,
        scratch_shapes=list(scratch),
        input_output_aliases=aliases or {},
        compiler_params=pltpu.CompilerParams(vmem_limit_bytes=VMEM_BYTES),
        cost_estimate=pl.CostEstimate(flops=flops, bytes_accessed=moved, transcendentals=0),
    )


def shape(dims, dtype=F32):
    return jax.ShapeDtypeStruct(dims, dtype)


def halves(x):
    high = x.astype(BF)
    return high, (x - high.astype(F32)).astype(BF)


def stacked(x):
    return jnp.concatenate(halves(x), axis=0)


def mm(a, b):
    return jnp.dot(a, b, preferred_element_type=F32)


def mm_t(a, b):
    return lax.dot_general(a, b, (((1,), (1,)), ((), ())), preferred_element_type=F32)


def product(x2, w2):
    rows = x2.shape[0] // 2
    wide = mm(x2, w2[0])
    return wide[:rows] + wide[rows:] + mm(x2[:rows], w2[1])


def product_chunks(x2s, w2, chunk):
    rows = x2s[0].shape[0] // 2
    parts = []
    for first in range(0, rows, chunk):
        high = jnp.concatenate([x[first : first + chunk] for x in x2s], axis=1)
        low = jnp.concatenate([x[rows + first : rows + first + chunk] for x in x2s], axis=1)
        parts.append(product(jnp.concatenate([high, low], axis=0), w2))
    return jnp.concatenate(parts, axis=0)


def iota(dims, axis):
    return lax.broadcasted_iota(jnp.int32, dims, axis)


def build_band(*args):
    for _ in band_pieces(*args):
        pass


def band_pieces(store, nbr, coef, halo):
    rows = BLK + 2 * halo
    count = nbr.shape[0]
    ids = [nbr[k : k + 1] for k in range(count)]
    cs = [coef[k : k + 1] for k in range(count)]
    rest = 1.0 - sum(cs[1:], cs[0])
    for k in range(count - 1, 0, -1):
        alive = jnp.ones_like(ids[k]) > 0
        for j in range(k):
            same = jnp.logical_and(ids[k] == ids[j], alive)
            cs[j] = cs[j] + jnp.where(same, cs[k], 0.0)
            alive = jnp.logical_and(alive, jnp.logical_not(same))
        ids[k] = jnp.where(alive, ids[k], -1)
    lanes = 128
    step = 16
    base = iota((step, lanes), 0).astype(F32)
    parts = [halves(c) for c in cs + [rest]]

    def wide(x, at):
        return jnp.broadcast_to(x[:, at].astype(F32), (step, lanes)).astype(BF)

    for half in range(BLK // lanes):
        at = slice(half * lanes, (half + 1) * lanes)
        highs = [wide(p[0], at) for p in parts]
        lows = [wide(p[1], at) for p in parts]
        own = (iota((step, lanes), 1) - iota((step, lanes), 0)).astype(F32).astype(BF)
        zero = jnp.zeros((step, lanes), BF)
        for tile in range(0, rows, BLK):
            near = [wide((i - tile).astype(F32), at) for i in ids]
            for first in range(tile, tile + BLK, step):
                high, low = zero, zero
                if half * lanes - step < first < half * lanes + lanes + 2 * halo:
                    offset = first - halo - half * lanes
                    if 0 <= offset < lanes:
                        same = own == jnp.full((step, lanes), offset, BF)
                        high = jnp.where(same, highs[-1], zero)
                        low = jnp.where(same, lows[-1], zero)
                    here = (base + float(first - tile)).astype(BF)
                    for k in range(count):
                        same = here == near[k]
                        high = jnp.where(same, highs[k], high)
                        low = jnp.where(same, lows[k], low)
                store(first, step, at, high, low)
            yield


def one_hot(ids, rows):
    lanes = ids.shape[1]
    wide = jnp.broadcast_to(ids.astype(F32), (rows, lanes)).astype(BF)
    here = iota((rows, lanes), 0).astype(F32).astype(BF)
    return jnp.where(here == wide, jnp.ones((rows, lanes), BF), jnp.zeros((rows, lanes), BF))


def fold_rows(x, height):
    total = x[:height]
    for first in range(height, x.shape[0], height):
        total = total + x[first : first + height]
    return total


def prepare_kernel(fields):
    def body(mix, omix, atm, sea, nbr, coef, bulk, surf, spread, code, y, yo, first, last, gains, vertical, top, sem):
        la = mix.shape[0]
        columns = atm.shape[1]
        copy = pltpu.make_async_copy(sea.at[: omix.shape[0], :], top, sem)
        copy.start()
        eye = iota((la, la), 0) == iota((la, la), 1)
        step = mix[...] + jnp.where(eye, 1.0, 0.0)

        def dot(a, b):
            return jnp.dot(a, b, precision=lax.Precision.HIGHEST, preferred_element_type=F32)

        def col(r, same):
            return jnp.sum(jnp.where(same, r, 0.0), axis=1, keepdims=True)

        def row(c, same):
            return jnp.sum(jnp.where(same, c, 0.0), axis=0, keepdims=True)

        twice = dot(step, step)
        fourth = dot(twice, twice)
        rows_up = [step[la - 1 : la, :]]
        cols_up = [step[:, la - 1 : la]]
        for _ in range(ASTEPS - 2):
            rows_up.append(jnp.sum(step * col(rows_up[-1], eye), axis=0, keepdims=True))
        for _ in range(ASTEPS - 1):
            cols_up.append(jnp.sum(step * row(cols_up[-1], eye), axis=1, keepdims=True))
        slot = iota((fields * ASTEPS, 128), 0) // fields
        lane = iota((fields * ASTEPS, 128), 1)
        value = jnp.zeros((fields * ASTEPS, 128), F32)
        for s in range(1, ASTEPS + 1):
            column = jnp.where(slot == s - 1, 1.0, 0.0)
            for j in range(1, ASTEPS):
                column = jnp.where(slot == s - 1 + j, rows_up[j - 1][:, la - 1 : la], column)
            value = jnp.where(lane == s - 1, column, value)
        gains[...] = value

        tall = jnp.concatenate([fourth] * fields, axis=0)
        spreaded = dot(tall, spread[...])
        filled = jnp.where(code[...] == 1, spreaded, 0.0)
        for m in range(ASTEPS):
            tall = jnp.concatenate([cols_up[ASTEPS - 1 - m]] * fields, axis=0)
            filled = jnp.where(code[...] == 2 + m, tall, filled)
        vertical[...] = stacked(filled)

        weights = [jnp.broadcast_to(col(r, eye), (la, 128)) for r in rows_up]
        lo = omix.shape[0]
        sea_eye = iota((lo, lo), 0) == iota((lo, lo), 1)
        sea_row = omix[0:1, :] + jnp.where(iota((1, lo), 1) == 0, 1.0, 0.0)
        sea_weight = jnp.broadcast_to(col(sea_row, sea_eye), (lo, 128))
        copy.wait()
        for start in range(0, columns, 128):
            at = slice(start, start + 128)
            for f in range(fields):
                x = atm[f * la : (f + 1) * la, at]
                y[f : f + 1, at] = x[la - 1 : la]
                for k in range(1, ASTEPS):
                    y[k * fields + f : k * fields + f + 1, at] = jnp.sum(
                        x * weights[k - 1], axis=0, keepdims=True
                    )
            yo[:, at] = jnp.sum(top[:, at] * sea_weight, axis=0, keepdims=True)
        for target, at in ((first, slice(0, WIDE)), (last, slice(columns - WIDE, columns))):
            target[0:16, :] = y[:, at]
            target[16:22, :] = nbr[:, at].astype(F32)
            target[22:28, :] = coef[:, at]
            target[28:32, :] = bulk[:, at]
            target[32:36, :] = surf[:, at]
            target[36:37, :] = yo[:, at]
            target[37:40, :] = jnp.zeros((3, WIDE), F32)

    return body


def band_kernel(nbr, coef, *refs):
    w, sems, side_sems = refs[-3:]
    band = refs[0] if len(refs) == 4 else refs[2]
    blocks = nbr.shape[1] // BLK
    halo = (w.shape[2] - BLK) // 2
    sides = []
    if len(refs) > 4:
        for i, target in enumerate(refs[3:5]):
            for k, (source, width) in enumerate(zip(refs[:2], (WIDE, HO))):
                rows, columns = source.shape
                first = 0 if i == 0 else columns - width
                copy = pltpu.make_async_copy(
                    source.at[:, first : first + width],
                    target.at[:rows, k * WIDE : k * WIDE + width],
                    side_sems.at[2 * i + k],
                )
                copy.start()
                sides.append(copy)

    def copy(b):
        return pltpu.make_async_copy(w.at[b], band.at[b], sems.at[b])

    def build(b, _):
        at = pl.ds(pl.multiple_of(b * BLK, BLK), BLK)

        def store(first, step, lanes, high, low):
            w[b, 0, first : first + step, lanes] = high
            w[b, 1, first : first + step, lanes] = low

        build_band(store, nbr[:, at] - b * BLK, coef[:, at], halo)
        copy(b).start()
        return 0

    lax.fori_loop(0, blocks, build, 0)

    def finish(b, _):
        copy(b).wait()
        return 0

    lax.fori_loop(0, blocks, finish, 0)
    for side in sides:
        side.wait()


def interior_kernel(
    y, before, after, bulk, surf, gains, atm_in, band, q, kept_out, mid_out, far, w, sa, sb, za, zb, bulks, surfs, atm, kept, mid, sems, csems
):
    rows, columns = atm.shape
    load = pltpu.make_async_copy(atm_in, atm, csems.at[0])
    load.start()
    blocks = columns // BLK
    fields = bulk.shape[0]
    states = fields * ASTEPS
    total = blocks + 2 * ASTEPS
    halo = ASTEPS - 1

    def arriving(b):
        return pltpu.make_async_copy(band.at[b], w.at[halo + b], sems.at[b])

    for b in [0, blocks - 1] + list(range(1, blocks - 1)):
        arriving(b).start()

    leaving = []
    for e in list(range(ASTEPS)) + list(range(ASTEPS + blocks, total)):
        pack = before if e < ASTEPS else after
        local = e if e < ASTEPS else e - ASTEPS - blocks
        at = slice(local * BLK, (local + 1) * BLK)
        za[e] = stacked(pack[0:states, at])
        bulks[e] = pack[28:32, at]
        surfs[e] = pack[32:36, at]
        if e in (0, total - 1):
            continue
        origin = local * BLK + (columns - WIDE if e < ASTEPS else 0)

        def store(first, step, lanes, high, low, e=e):
            w[e - 1, 0, first : first + step, lanes] = high
            w[e - 1, 1, first : first + step, lanes] = low

        build_band(store, pack[16:22, at].astype(jnp.int32) - origin, pack[22:28, at], HA)
        i = e - 1 if e < ASTEPS else e - 1 - blocks
        copy = pltpu.make_async_copy(w.at[e - 1], far.at[i], sems.at[blocks + i])
        copy.start()
        leaving.append(copy)
    load.wait()
    for b in range(blocks):
        at = slice(b * BLK, (b + 1) * BLK)
        both = stacked(jnp.concatenate([atm[:, at], y[:, at]], axis=0))
        sa[b] = both
        height = rows + states
        za[b + ASTEPS] = jnp.concatenate([both[rows:height], both[height + rows :]], axis=0)
        bulks[b + ASTEPS] = bulk[:, at]
        surfs[b + ASTEPS] = surf[:, at]

    arriving(0).wait()
    arriving(blocks - 1).wait()

    slot = iota((states, BLK), 0) // fields
    for s in range(1, ASTEPS + 1):
        xs, xt = (sa, sb) if s % 2 else (sb, sa)
        zs, zt = (za, zb) if s % 2 else (zb, za)
        gain = jnp.broadcast_to(gains[:, s - 1 : s], (states, BLK))
        keep = jnp.where(slot == s - 1, 0.0, 1.0)

        def advance(moved, e, s=s, gain=gain, keep=keep):
            flux = bulks[e] * (surfs[e] - moved[(s - 1) * fields : s * fields])
            return moved * keep + gain * jnp.concatenate([flux] * ASTEPS, axis=0)

        def edge(e, s=s, zs=zs, zt=zt, advance=advance):
            x2 = jnp.concatenate([zs[e - 1], zs[e], zs[e + 1]], axis=1)
            value = advance(product(x2, (w[e - 1, 0], w[e - 1, 1])), e)
            if s == ASTEPS:
                q[e - ASTEPS] = value
            else:
                zt[e] = stacked(value)

        def inner(b, s=s, xs=xs, xt=xt, zt=zt, advance=advance):
            x2 = jnp.concatenate([xs[b - 1], xs[b], xs[b + 1]], axis=1)
            moved = product(x2, (w[b + halo, 0], w[b + halo, 1]))
            value = advance(moved[rows:], b + ASTEPS)
            if s == ASTEPS:
                q[b] = value
                mid[b - ASTEPS] = stacked(moved[:rows])
            else:
                high, low = halves(moved[:rows])
                zh, zl = halves(value)
                xt[b] = jnp.concatenate([high, zh, low, zl], axis=0)
                zt[b + ASTEPS] = jnp.concatenate([zh, zl], axis=0)

        def together(i, _, s=s, edge=edge, inner=inner):
            if s == 1:
                arriving(1 + 2 * i).wait()
                arriving(2 + 2 * i).wait()
            inner(s + 2 * i)
            inner(s + 2 * i + 1)
            edge(s + i)
            edge(blocks + ASTEPS - s + i)
            return 0

        def alone(i, _, s=s, inner=inner):
            if s == 1:
                arriving(1 + 2 * i).wait()
                arriving(2 + 2 * i).wait()
            inner(s + 2 * i)
            inner(s + 2 * i + 1)
            return 0

        lax.fori_loop(0, ASTEPS, together, 0)
        if blocks // 2 - s > ASTEPS:
            lax.fori_loop(ASTEPS, blocks // 2 - s, alone, 0)
        if s < ASTEPS:
            height = rows + states
            for i, b in enumerate((s, s + 1, blocks - 2 - s, blocks - 1 - s)):
                kept[(s - 1) * 4 + i, :rows] = xt[b, :rows]
                kept[(s - 1) * 4 + i, rows:] = xt[b, height : height + rows]
            at = slice((s - 1) * 4, s * 4)
            copy = pltpu.make_async_copy(kept.at[at], kept_out.at[at], csems.at[s])
        else:
            copy = pltpu.make_async_copy(mid, mid_out, csems.at[s])
        copy.start()
        leaving.append(copy)
    for copy in leaving:
        copy.wait()


def send_kernel(q, cols, out, table):
    fields = q.shape[1] // ASTEPS
    peers, slots = cols.shape
    blocks = q.shape[0]
    lanes = out.shape[2]
    parts = slots // lanes
    for b in range(blocks):
        table[b * fields : (b + 1) * fields, :] = q[b, (ASTEPS - 1) * fields :, :]
    rows = stacked(table[...])
    half = blocks * fields
    block_of_row = iota((half, slots), 0) // fields

    def one(p, _):
        ids = cols[pl.ds(p, 1), :]
        got = mm(rows, one_hot(ids & (BLK - 1), BLK))
        got = jnp.where(block_of_row == ids // BLK, got[:half] + got[half:], 0.0)
        got = fold_rows(got, 2 * fields)
        got = got[:fields] + got[fields:]
        out[p] = jnp.concatenate([got[:, i * lanes : (i + 1) * lanes] for i in range(parts)], axis=0)
        return 0

    lax.fori_loop(0, peers, one, 0, unroll=4)


def exchange_kernel(recv, slot, weight, yo, before, after, nbr, coef, omix, flux_out, back, rows, tiles, hots, seas, acc):
    peers, per_peer, lanes = recv.shape
    links, columns = slot.shape
    fields = flux_out.shape[0]
    parts = per_peer // fields
    highs = peers * parts
    table = highs * fields
    rows[...] = stacked(recv[...].reshape(table, lanes))
    acc[...] = jnp.zeros_like(acc)
    side = HO // 128
    own_tiles = columns // 128
    for t in range(own_tiles + 2 * side):
        if t < side:
            line = before[36:37, WIDE - HO + t * 128 : WIDE - HO + (t + 1) * 128]
        elif t < side + own_tiles:
            line = yo[:, (t - side) * 128 : (t - side + 1) * 128]
        else:
            line = after[36:37, (t - side - own_tiles) * 128 : (t - side - own_tiles + 1) * 128]
        tiles[t] = jnp.broadcast_to(line, (8, 128))
    corner = omix[0:1, 0:1] + 1.0
    high_of_row = iota((table, BLK), 0) // fields
    back_rows = iota((2 * highs, BLK), 0)
    inner = back_rows % (2 * parts)
    back_high = (back_rows // (2 * parts)) * parts + inner % parts
    pattern = iota((8, BLK), 0) % (2 * parts) // parts
    window = 1 + 2 * side
    neighbors = nbr.shape[0]

    def surface(j, half):
        t0 = j * (BLK // 128) + half
        at = pl.ds(pl.multiple_of(t0 * 128, 128), 128)
        pad = jnp.zeros((8 - neighbors, 128), jnp.int32)
        ids = jnp.concatenate([nbr[:, at] - t0 * 128, pad], axis=0)
        cs = jnp.concatenate([coef[:, at], pad.astype(F32)], axis=0)
        middle = tiles[t0 + side]
        got = jnp.zeros((8, 128), F32)
        for t in range(window):
            pick = jnp.take_along_axis(tiles[t0 + t], ids & 127, axis=1, mode="promise_in_bounds")
            got = jnp.where(ids // 128 == t, pick, got)
        return middle[0:1] + jnp.sum(cs * (got - middle), axis=0, keepdims=True)

    def base(j, _):
        at = pl.ds(pl.multiple_of(j * BLK, BLK), BLK)
        seas[:, at] = jnp.concatenate([surface(j, h) for h in range(BLK // 128)], axis=1)
        return 0

    lax.fori_loop(0, columns // BLK, base, 0, unroll=2)

    def arrive(j, _):
        at = pl.ds(pl.multiple_of(j * BLK, BLK), BLK)
        flux = jnp.zeros((2 * fields, BLK), F32)
        for r in range(links):
            ids = slot[r : r + 1, at]
            hot = one_hot(ids & (lanes - 1), lanes)
            hots[j, :, r * BLK : (r + 1) * BLK] = hot
            got = mm(rows[...], hot)
            got = jnp.where(high_of_row == ids // lanes, got[:table] + got[table:], 0.0)
            flux = flux + weight[r : r + 1, at] * fold_rows(got, 2 * fields)
        flux = flux[:fields] + flux[fields:]
        flux_out[:, at] = flux
        seas[:, at] += corner * flux[0:1]
        return 0

    lax.fori_loop(0, columns // BLK, arrive, 0, unroll=2)

    def leave(j, _):
        at = pl.ds(pl.multiple_of(j * BLK, BLK), BLK)
        sea = seas[:, at]
        left = []
        for r in range(links):
            ids, scale = slot[r : r + 1, at], weight[r : r + 1, at]
            high, low = halves(jnp.where(pattern == 1, scale, scale * sea))
            mask = back_high == ids // lanes
            both = [
                jnp.where(mask, jnp.concatenate([x.astype(F32)] * (2 * highs // 8), axis=0), 0.0).astype(BF)
                for x in (high, low)
            ]
            left.append(jnp.concatenate(both, axis=0))
        acc[...] += mm_t(jnp.concatenate(left, axis=1), hots[j])
        return 0

    lax.fori_loop(0, columns // BLK, leave, 0, unroll=2)
    back[...] = (acc[: 2 * highs] + acc[2 * highs :]).reshape(back.shape)


def settle_kernel(back, cols, surf, out, acc):
    peers, per_peer, lanes = back.shape
    parts = per_peer // 2
    blocks = surf.shape[1] // BLK
    acc[...] = jnp.zeros_like(acc)
    block_of_row = iota((blocks, lanes), 0)

    def one(d, _):
        left, hots = [], []
        for h in range(parts):
            ids = cols[pl.ds(d, 1), h * lanes : (h + 1) * lanes]
            mask = block_of_row == ids // BLK
            value = jnp.where(mask, back[d, h : h + 1, :], 0.0)
            scale = jnp.where(mask, back[d, parts + h : parts + h + 1, :], 0.0)
            left.append(stacked(jnp.concatenate([value, scale], axis=0)))
            hots.append(one_hot(ids & (BLK - 1), BLK))
        acc[...] += mm_t(jnp.concatenate(left, axis=1), jnp.concatenate(hots, axis=1))
        return 0

    lax.fori_loop(0, peers, one, 0, unroll=4)
    sums = acc[: 2 * blocks] + acc[2 * blocks :]
    base = jnp.concatenate([surf[0:1, b * BLK : (b + 1) * BLK] for b in range(blocks)], axis=0)
    value = (base + sums[:blocks]) / (1.0 + sums[blocks:])
    for b in range(blocks):
        for i in range(BLK // 128):
            row = b * (BLK // 128) + i
            out[row : row + 1, :] = value[b : b + 1, i * 128 : (i + 1) * 128]


def edge_kernel(
    before, after, atm, kept, mid, q, vertical, band, far, out, w, halos, sides, sa, sb, staged, wsems, sems, osems
):
    rows = atm.shape[0]
    blocks = q.shape[0]
    halo = ASTEPS - 1
    count = halo + ASTEPS
    arrivals = [
        pltpu.make_async_copy(before.at[:rows, :WIDE], halos.at[0], sems.at[0]),
        pltpu.make_async_copy(after.at[:rows, :WIDE], halos.at[1], sems.at[1]),
        pltpu.make_async_copy(atm.at[:, : 2 * BLK], sides.at[0], sems.at[2]),
        pltpu.make_async_copy(atm.at[:, (blocks - 2) * BLK :], sides.at[1], sems.at[3]),
    ]
    sources = [far.at[i] for i in range(halo)] + [band.at[i] for i in range(ASTEPS)]
    sources += [band.at[blocks - ASTEPS + i] for i in range(ASTEPS)] + [far.at[halo + i] for i in range(halo)]
    bands = [pltpu.make_async_copy(source, w.at[i], wsems.at[i]) for i, source in enumerate(sources)]
    needed = [list(range(ASTEPS)) + list(range(count + halo, 2 * count))]
    needed += [[ASTEPS - 1 + i, count + halo - i] for i in range(1, ASTEPS)]
    for copy in arrivals:
        copy.start()
    for group in needed:
        for i in group:
            bands[i].start()

    def leaving(b):
        at = pl.ds(pl.multiple_of(b * BLK, BLK), BLK)
        return pltpu.make_async_copy(staged.at[b], out.at[:, at], osems.at[b])

    def mixed(source, shift):
        def one(b):
            qh, ql = halves(q[b])
            x2 = source[b - shift]
            high = jnp.concatenate([x2[:rows], qh], axis=0)
            low = jnp.concatenate([x2[rows:], ql], axis=0)
            wide = mm(vertical[...], high)
            staged[b] = wide[:rows] + wide[rows:] + mm(vertical[:rows], low)

        def pair(i, _):
            one(2 * i)
            one(2 * i + 1)
            leaving(2 * i).start()
            leaving(2 * i + 1).start()
            return 0

        return pair

    lax.fori_loop(ASTEPS // 2, (blocks - ASTEPS) // 2, mixed(mid, ASTEPS), 0)
    for copy in arrivals:
        copy.wait()
    for i in range(ASTEPS):
        at = slice(i * BLK, (i + 1) * BLK)
        sa[i] = stacked(halos[0, :, at])
        sa[6 + 2 + i] = stacked(halos[1, :, at])
    for i in range(2):
        at = slice(i * BLK, (i + 1) * BLK)
        sa[ASTEPS + i] = stacked(sides[0, :, at])
        sa[6 + i] = stacked(sides[1, :, at])
    buffers = (sa, sb)
    for s in range(1, ASTEPS + 1):
        source, target = buffers[(s - 1) % 2], buffers[s % 2]
        last = s == ASTEPS
        for i in needed[s - 1]:
            bands[i].wait()

        def one(i, _, s=s, source=source, target=target, last=last):
            for side in range(2):
                base = 6 * side
                k = s - 1 + i if side == 0 else count + ASTEPS - s + i
                window = [source.at[base + i + d] for d in range(3)]
                value = stacked(product_chunks(window, (w[k, 0], w[k, 1]), rows // 3))
                target[base + i + (2 * side if not last else 0)] = value
            return 0

        lax.fori_loop(0, ASTEPS, one, 0, unroll=2)
        if not last:
            for i in range(2):
                target[ASTEPS + i] = kept[(s - 1) * 4 + i]
                target[6 + i] = kept[(s - 1) * 4 + 2 + i]
    final = buffers[ASTEPS % 2]
    lax.fori_loop(0, ASTEPS // 2, mixed(final, 0), 0)
    lax.fori_loop((blocks - ASTEPS) // 2, blocks // 2, mixed(final, blocks - ASTEPS - 6), 0)

    def done(b, _):
        leaving(b).wait()
        return 0

    lax.fori_loop(0, blocks, done, 0)


def ocean_kernel(ocean, omix, flux, before, after, band, out, w, x2, sides, staged, wsems, sems, osems):
    levels = omix.shape[0]
    fields = flux.shape[0]
    columns = ocean.shape[1]
    blocks = columns // BLK
    arrivals = [
        pltpu.make_async_copy(ref.at[:, WIDE:], sides.at[i], sems.at[i]) for i, ref in enumerate((before, after))
    ]
    for copy in arrivals:
        copy.start()

    def arriving(b):
        return pltpu.make_async_copy(band.at[b], w.at[b], wsems.at[b])

    for b in range(blocks):
        arriving(b).start()
    eye = iota((levels, levels), 0) == iota((levels, levels), 1)
    step = omix[...] + jnp.where(eye, 1.0, 0.0)
    top = jnp.broadcast_to(step[:, 0:1], (levels, BLK))
    mix2 = stacked(step)
    for copy in arrivals:
        copy.wait()

    def part(first, width):
        pieces = []
        for ref, begin, size in ((sides.at[0], -HO, HO), (ocean, 0, columns), (sides.at[1], columns, HO)):
            lo, hi = max(first, begin), min(first + width, begin + size)
            if lo < hi:
                pieces.append(ref[:, lo - begin : hi - begin])
        return pieces[0] if len(pieces) == 1 else jnp.concatenate(pieces, axis=1)

    for e in range((columns + 2 * HO) // BLK):
        x2[e] = stacked(part(e * BLK - HO, BLK))

    def leaving(b):
        at = pl.ds(pl.multiple_of(b * BLK, BLK), BLK)
        return pltpu.make_async_copy(staged.at[b], out.at[:, at], osems.at[b])

    def one(b):
        at = pl.ds(pl.multiple_of(b * BLK, BLK), BLK)
        source = jnp.concatenate([x2[b + d] for d in range(1 + 2 * HO // BLK)], axis=1)
        moved = product(source, (w[b, 0], w[b, 1]))
        for f in range(fields):
            rows = slice(f * levels, (f + 1) * levels)
            high, low = halves(moved[rows])
            wide = mm(mix2, high)
            staged[b, rows] = (
                wide[:levels] + wide[levels:] + mm(mix2[:levels], low) + top * flux[f : f + 1, at]
            )

    group = 4

    def some(i, _):
        for k in range(group):
            arriving(group * i + k).wait()
        for k in range(group):
            one(group * i + k)
        for k in range(group):
            leaving(group * i + k).start()
        return 0

    lax.fori_loop(0, blocks // group, some, 0)

    def done(b, _):
        leaving(b).wait()
        return 0

    lax.fori_loop(0, blocks, done, 0)


def after_all(value, *others):
    return lax.optimization_barrier((value, *others))[0]


def per_device(
    atm_state,
    atm_surface,
    bulk_coef,
    atm_nbr,
    atm_nbr_coef,
    atm_mix,
    ocean_state,
    ocean_nbr,
    ocean_nbr_coef,
    ocean_mix,
    send_cols,
    remap_slot,
    remap_weight,
):
    fields, la, columns = atm_state.shape
    lo, cells = ocean_state.shape[1:]
    blocks = columns // BLK
    rows = fields * la
    states = fields * ASTEPS
    picked = send_cols[0]
    peers, slots = picked.shape
    lanes = min(BLK, slots)
    parts = slots // lanes
    atm = atm_state.reshape(rows, columns)
    ocean = ocean_state.reshape(fields * lo, cells)
    depth = lax.axis_size(AXES)
    up = [(i, (i + 1) % depth) for i in range(depth)]
    down = [(j, i) for i, j in up]
    window = BLK + 2 * HA
    vmem = pl.BlockSpec(memory_space=pltpu.VMEM)
    anywhere = pl.BlockSpec(memory_space=pl.ANY)

    depth_k = rows + states
    r_of, c_of = np.arange(rows)[:, None], np.arange(depth_k)[None, :]
    code = np.where(
        c_of < rows,
        (c_of // la == r_of // la) * 1,
        ((c_of - rows) % fields == r_of // la) * (2 + (c_of - rows) // fields),
    ).astype(np.int32)
    spread = ((c_of % la == np.arange(la)[:, None]) & (c_of < rows)).astype(np.float32)

    y, yo, first, last, gains, vertical = call(
        prepare_kernel(fields),
        (
            shape((states, columns)),
            shape((1, columns)),
            shape((40, WIDE)),
            shape((40, WIDE)),
            shape((states, 128)),
            shape((2 * rows, depth_k), BF),
        ),
        in_specs=[vmem] * 3 + [anywhere] + [vmem] * 6,
        scratch=[pltpu.VMEM((lo, cells), F32), pltpu.SemaphoreType.DMA(())],
    )(
        atm_mix,
        ocean_mix,
        atm,
        ocean,
        atm_nbr,
        atm_nbr_coef,
        bulk_coef,
        atm_surface,
        jnp.asarray(spread),
        jnp.asarray(code),
    )
    pack_before = lax.ppermute(last, AXES, up)
    pack_after = lax.ppermute(first, AXES, down)

    tall = max(rows, fields * lo)
    band, wide_first, wide_last = call(
        band_kernel,
        (shape((blocks, 2, window, BLK), BF), shape((tall, WIDE + HO)), shape((tall, WIDE + HO))),
        in_specs=[vmem] * 2 + [anywhere] * 2,
        out_specs=(anywhere,) * 3,
        scratch=[
            pltpu.VMEM((blocks, 2, window, BLK), BF),
            pltpu.SemaphoreType.DMA((blocks,)),
            pltpu.SemaphoreType.DMA((4,)),
        ],
    )(after_all(atm_nbr, y), atm_nbr_coef, atm, ocean)

    pack_before, pack_after, wide_first, wide_last = lax.optimization_barrier(
        (pack_before, pack_after, wide_first, wide_last)
    )
    wide_before = lax.ppermute(wide_last, AXES, up)
    wide_after = lax.ppermute(wide_first, AXES, down)

    total = blocks + 2 * ASTEPS
    halo = ASTEPS - 1
    q, kept, mid, far = call(
        interior_kernel,
        (
            shape((blocks, states, BLK)),
            shape((4 * halo, 2 * rows, BLK), BF),
            shape((blocks - 2 * ASTEPS, 2 * rows, BLK), BF),
            shape((2 * halo, 2, window, BLK), BF),
        ),
        in_specs=[vmem] * 6 + [anywhere] * 2,
        out_specs=(vmem, anywhere, anywhere, anywhere),
        scratch=[
            pltpu.VMEM((total - 2, 2, window, BLK), BF),
            pltpu.VMEM((blocks, 2 * depth_k, BLK), BF),
            pltpu.VMEM((blocks, 2 * depth_k, BLK), BF),
            pltpu.VMEM((total, 2 * states, BLK), BF),
            pltpu.VMEM((total, 2 * states, BLK), BF),
            pltpu.VMEM((total, fields, BLK), F32),
            pltpu.VMEM((total, fields, BLK), F32),
            pltpu.VMEM((rows, columns), F32),
            pltpu.VMEM((4 * halo, 2 * rows, BLK), BF),
            pltpu.VMEM((blocks - 2 * ASTEPS, 2 * rows, BLK), BF),
            pltpu.SemaphoreType.DMA((blocks + 2 * halo,)),
            pltpu.SemaphoreType.DMA((ASTEPS + 1,)),
        ],
    )(y, pack_before, pack_after, bulk_coef, atm_surface, gains, atm, band)

    outgoing = call(
        send_kernel,
        shape((peers, parts * fields, lanes)),
        in_specs=[vmem] * 2,
        scratch=[pltpu.VMEM((blocks * fields, BLK), F32)],
    )(q, picked)
    received = lax.all_to_all(outgoing, AXES, split_axis=0, concat_axis=0, tiled=True)

    sea_blocks = cells // BLK
    sea_band = call(
        band_kernel,
        shape((sea_blocks, 2, BLK + 2 * HO, BLK), BF),
        in_specs=[vmem] * 2,
        out_specs=anywhere,
        scratch=[
            pltpu.VMEM((sea_blocks, 2, BLK + 2 * HO, BLK), BF),
            pltpu.SemaphoreType.DMA((sea_blocks,)),
            pltpu.SemaphoreType.DMA((4,)),
        ],
    )(after_all(ocean_nbr, outgoing), ocean_nbr_coef)

    flux, back = call(
        exchange_kernel,
        (shape((fields, cells)), shape((peers, 2 * parts, lanes))),
        in_specs=[vmem] * 9,
        scratch=[
            pltpu.VMEM((2 * peers * parts * fields, lanes), BF),
            pltpu.VMEM((cells // 128 + 2 * HO // 128, 8, 128), F32),
            pltpu.VMEM((cells // BLK, lanes, remap_slot.shape[0] * BLK), BF),
            pltpu.VMEM((1, cells), F32),
            pltpu.VMEM((4 * peers * parts, lanes), F32),
        ],
    )(
        after_all(received, sea_band),
        remap_slot,
        remap_weight,
        yo,
        pack_before,
        pack_after,
        ocean_nbr,
        ocean_nbr_coef,
        ocean_mix,
    )
    returned = lax.all_to_all(back, AXES, split_axis=0, concat_axis=0, tiled=True)

    atm_final = call(
        edge_kernel,
        shape((rows, columns)),
        in_specs=[anywhere] * 3 + [vmem] * 4 + [anywhere] * 2,
        out_specs=anywhere,
        scratch=[
            pltpu.VMEM((2 * (2 * ASTEPS - 1), 2, window, BLK), BF),
            pltpu.VMEM((2, rows, WIDE), F32),
            pltpu.VMEM((2, rows, 2 * BLK), F32),
            pltpu.VMEM((12, 2 * rows, BLK), BF),
            pltpu.VMEM((12, 2 * rows, BLK), BF),
            pltpu.VMEM((blocks, rows, BLK), F32),
            pltpu.SemaphoreType.DMA((2 * (2 * ASTEPS - 1),)),
            pltpu.SemaphoreType.DMA((4,)),
            pltpu.SemaphoreType.DMA((blocks,)),
        ],
    )(wide_before, wide_after, atm, kept, mid, after_all(q, back), vertical, band, far)

    ocean_final = call(
        ocean_kernel,
        shape((fields * lo, cells)),
        in_specs=[vmem] * 3 + [anywhere] * 3,
        out_specs=anywhere,
        scratch=[
            pltpu.VMEM((sea_blocks, 2, BLK + 2 * HO, BLK), BF),
            pltpu.VMEM(((cells + 2 * HO) // BLK, 2 * fields * lo, BLK), BF),
            pltpu.VMEM((2, fields * lo, HO), F32),
            pltpu.VMEM((sea_blocks, fields * lo, BLK), F32),
            pltpu.SemaphoreType.DMA((sea_blocks,)),
            pltpu.SemaphoreType.DMA((2,)),
            pltpu.SemaphoreType.DMA((sea_blocks,)),
        ],
    )(ocean, ocean_mix, after_all(flux, atm_final), wide_before, wide_after, sea_band)

    surface_temp = call(
        settle_kernel,
        shape((columns // 128, 128)),
        in_specs=[vmem] * 3,
        scratch=[pltpu.VMEM((4 * blocks, BLK), F32)],
    )(after_all(returned, ocean_final), picked, atm_surface)

    return (
        atm_final.reshape(fields, la, columns),
        ocean_final.reshape(fields, lo, cells),
        surface_temp.reshape(columns),
    )


def solution(mesh):
    placed = (
        P(None, None, AXES),
        P(None, AXES),
        P(None, AXES),
        P(None, AXES),
        P(None, AXES),
        P(),
        P(None, None, AXES),
        P(None, AXES),
        P(None, AXES),
        P(),
        P(AXES, None, None),
        P(None, AXES),
        P(None, AXES),
    )
    return jax.shard_map(
        per_device,
        mesh=mesh,
        in_specs=placed,
        out_specs=(P(None, None, AXES), P(None, None, AXES), P(AXES)),
        check_vma=False,
    )
```

```python
import numpy as np

import jax
import jax.numpy as jnp
from jax import lax
from jax.experimental import pallas as pl
from jax.experimental.pallas import tpu as pltpu
from jax.sharding import PartitionSpec as P

ASTEPS = 4
HA = 256
HO = 384
BLK = 256
WIDE = ASTEPS * HA
BF = jnp.bfloat16
F32 = jnp.float32
VMEM_BYTES = 56 * 1024 * 1024
AXES = ("sec", "blk")


def call(body, outs, *, in_specs=None, out_specs=None, scratch=(), flops=10**6, moved=10**4, aliases=None):
    vmem = pl.BlockSpec(memory_space=pltpu.VMEM)
    return pl.pallas_call(
        body,
        out_shape=outs,
        in_specs=in_specs,
        out_specs=jax.tree.map(lambda _: vmem, outs) if out_specs is None else out_specs,
        scratch_shapes=list(scratch),
        input_output_aliases=aliases or {},
        compiler_params=pltpu.CompilerParams(vmem_limit_bytes=VMEM_BYTES),
        cost_estimate=pl.CostEstimate(flops=flops, bytes_accessed=moved, transcendentals=0),
    )


def shape(dims, dtype=F32):
    return jax.ShapeDtypeStruct(dims, dtype)


def halves(x):
    high = x.astype(BF)
    return high, (x - high.astype(F32)).astype(BF)


def stacked(x):
    return jnp.concatenate(halves(x), axis=0)


def mm(a, b):
    return jnp.dot(a, b, preferred_element_type=F32)


def mm_t(a, b):
    return lax.dot_general(a, b, (((1,), (1,)), ((), ())), preferred_element_type=F32)


def products(x2, w2):
    return mm(x2, w2[0]), mm(x2[: x2.shape[0] // 2], w2[1])


def summed(parts):
    wide, rest = parts
    rows = rest.shape[0]
    return wide[:rows] + wide[rows:] + rest


def in_turn(works):
    waiting = None
    for begin, finish in works:
        parts = begin()
        if waiting is not None:
            waiting[1](summed(waiting[0]))
        waiting = (parts, finish)
    waiting[1](summed(waiting[0]))


def product_pieces(x2s, w2, result):
    rows = x2s[0].shape[0] // 2
    for t, x2 in enumerate(x2s):
        at = slice(t * BLK, (t + 1) * BLK)
        wide = mm(x2, w2.at[0][at])
        part = wide[:rows] + wide[rows:]
        result[...] = part if t == 0 else result[...] + part
        yield
        result[...] += mm(x2[:rows], w2.at[1][at])
        yield


def interleave(*works):
    works = list(works)
    while works:
        works = [w for w in works if next(w, w) is not w]


def iota(dims, axis):
    return lax.broadcasted_iota(jnp.int32, dims, axis)


def build_band(*args):
    for _ in band_pieces(*args):
        pass


def band_pieces(store, nbr, coef, halo):
    rows = BLK + 2 * halo
    count = nbr.shape[0]
    ids = [nbr[k : k + 1] for k in range(count)]
    cs = [coef[k : k + 1] for k in range(count)]
    rest = 1.0 - sum(cs[1:], cs[0])
    for k in range(count - 1, 0, -1):
        alive = jnp.ones_like(ids[k]) > 0
        for j in range(k):
            same = jnp.logical_and(ids[k] == ids[j], alive)
            cs[j] = cs[j] + jnp.where(same, cs[k], 0.0)
            alive = jnp.logical_and(alive, jnp.logical_not(same))
        ids[k] = jnp.where(alive, ids[k], -1)
    lanes = 128
    step = 16
    base = iota((step, lanes), 0).astype(F32)
    parts = [halves(c) for c in cs + [rest]]

    def wide(x, at):
        return jnp.broadcast_to(x[:, at].astype(F32), (step, lanes)).astype(BF)

    for half in range(BLK // lanes):
        at = slice(half * lanes, (half + 1) * lanes)
        highs = [wide(p[0], at) for p in parts]
        lows = [wide(p[1], at) for p in parts]
        own = (iota((step, lanes), 1) - iota((step, lanes), 0)).astype(F32).astype(BF)
        zero = jnp.zeros((step, lanes), BF)
        for tile in range(0, rows, BLK):
            near = [wide((i - tile).astype(F32), at) for i in ids]
            for first in range(tile, tile + BLK, step):
                high, low = zero, zero
                if half * lanes - step < first < half * lanes + lanes + 2 * halo:
                    offset = first - halo - half * lanes
                    if 0 <= offset < lanes:
                        same = own == jnp.full((step, lanes), offset, BF)
                        high = jnp.where(same, highs[-1], zero)
                        low = jnp.where(same, lows[-1], zero)
                    here = (base + float(first - tile)).astype(BF)
                    for k in range(count):
                        same = here == near[k]
                        high = jnp.where(same, highs[k], high)
                        low = jnp.where(same, lows[k], low)
                store(first, step, at, high, low)
            yield


def one_hot(ids, rows):
    lanes = ids.shape[1]
    wide = jnp.broadcast_to(ids.astype(F32), (rows, lanes)).astype(BF)
    here = iota((rows, lanes), 0).astype(F32).astype(BF)
    return jnp.where(here == wide, jnp.ones((rows, lanes), BF), jnp.zeros((rows, lanes), BF))


def fold_rows(x, height):
    total = x[:height]
    for first in range(height, x.shape[0], height):
        total = total + x[first : first + height]
    return total


def prepare_kernel(fields):
    def body(mix, omix, atm, sea, nbr, coef, bulk, surf, spread, code, sea_spread, y, yo, first, last, gains, vertical, sea_vertical, top, sem):
        la = mix.shape[0]
        columns = atm.shape[1]
        copy = pltpu.make_async_copy(sea.at[: omix.shape[0], :], top, sem)
        copy.start()
        eye = iota((la, la), 0) == iota((la, la), 1)
        step = mix[...] + jnp.where(eye, 1.0, 0.0)

        def dot(a, b):
            return jnp.dot(a, b, precision=lax.Precision.HIGHEST, preferred_element_type=F32)

        def col(r, same):
            return jnp.sum(jnp.where(same, r, 0.0), axis=1, keepdims=True)

        def row(c, same):
            return jnp.sum(jnp.where(same, c, 0.0), axis=0, keepdims=True)

        twice = dot(step, step)
        fourth = dot(twice, twice)
        rows_up = [step[la - 1 : la, :]]
        cols_up = [step[:, la - 1 : la]]
        for _ in range(ASTEPS - 2):
            rows_up.append(jnp.sum(step * col(rows_up[-1], eye), axis=0, keepdims=True))
        for _ in range(ASTEPS - 1):
            cols_up.append(jnp.sum(step * row(cols_up[-1], eye), axis=1, keepdims=True))
        slot = iota((fields * ASTEPS, 128), 0) // fields
        lane = iota((fields * ASTEPS, 128), 1)
        value = jnp.zeros((fields * ASTEPS, 128), F32)
        for s in range(1, ASTEPS + 1):
            column = jnp.where(slot == s - 1, 1.0, 0.0)
            for j in range(1, ASTEPS):
                column = jnp.where(slot == s - 1 + j, rows_up[j - 1][:, la - 1 : la], column)
            value = jnp.where(lane == s - 1, column, value)
        gains[...] = value

        spreaded = dot(jnp.concatenate([fourth] * 2, axis=0), spread[...])
        for p in range(fields // 2):
            filled = jnp.where(code[p] == 1, spreaded, 0.0)
            for m in range(ASTEPS):
                tall = jnp.concatenate([cols_up[ASTEPS - 1 - m]] * 2, axis=0)
                filled = jnp.where(code[p] == 2 + m, tall, filled)
            vertical[p] = stacked(filled)
        lo = omix.shape[0]
        sea_eye = iota((lo, lo), 0) == iota((lo, lo), 1)
        sea_step = omix[...] + jnp.where(sea_eye, 1.0, 0.0)
        spreaded = dot(jnp.concatenate([sea_step] * 2, axis=0), sea_spread[...])
        blocks = (iota((2 * lo, 2 * lo), 0) >= lo) == (iota((2 * lo, 2 * lo), 1) >= lo)
        sea_vertical[...] = stacked(jnp.where(blocks, spreaded, 0.0))

        weights = [jnp.broadcast_to(col(r, eye), (la, 128)) for r in rows_up]
        sea_weight = jnp.broadcast_to(col(sea_step[0:1, :], sea_eye), (lo, 128))
        copy.wait()
        for start in range(0, columns, 128):
            at = slice(start, start + 128)
            for f in range(fields):
                x = atm[f * la : (f + 1) * la, at]
                y[f : f + 1, at] = x[la - 1 : la]
                for k in range(1, ASTEPS):
                    y[k * fields + f : k * fields + f + 1, at] = jnp.sum(
                        x * weights[k - 1], axis=0, keepdims=True
                    )
            yo[:, at] = jnp.sum(top[:, at] * sea_weight, axis=0, keepdims=True)
        for target, at in ((first, slice(0, WIDE)), (last, slice(columns - WIDE, columns))):
            target[0:16, :] = y[:, at]
            target[16:22, :] = nbr[:, at].astype(F32)
            target[22:28, :] = coef[:, at]
            target[28:32, :] = bulk[:, at]
            target[32:36, :] = surf[:, at]
            target[36:37, :] = yo[:, at]
            target[37:40, :] = jnp.zeros((3, WIDE), F32)

    return body


def band_kernel(nbr, coef, atm, ocean, band, *refs):
    halos, held, (w, sems, in_sems, out_sems) = refs[:4], refs[4:8], refs[8:]
    blocks = nbr.shape[1] // BLK
    columns = atm.shape[1]
    spans = [(atm, 0, WIDE), (atm, columns - WIDE, WIDE), (ocean, 0, HO), (ocean, ocean.shape[1] - HO, HO)]
    arriving = [
        pltpu.make_async_copy(source.at[:, first : first + width], held[i], in_sems.at[i])
        for i, (source, first, width) in enumerate(spans)
    ]
    leaving = [pltpu.make_async_copy(held[i], halos[i], out_sems.at[i]) for i in range(len(spans))]
    for copy in arriving:
        copy.start()

    def copy(b):
        return pltpu.make_async_copy(w.at[b], band.at[b], sems.at[b])

    def build(b, _):
        at = pl.ds(pl.multiple_of(b * BLK, BLK), BLK)

        def store(first, step, lanes, high, low):
            w[b, 0, first : first + step, lanes] = high
            w[b, 1, first : first + step, lanes] = low

        build_band(store, nbr[:, at] - b * BLK, coef[:, at], HA)
        copy(b).start()
        return 0

    lax.fori_loop(0, blocks // 2, build, 0)
    for here, there in zip(arriving, leaving):
        here.wait()
        there.start()
    lax.fori_loop(blocks // 2, blocks, build, 0)

    def finish(b, _):
        copy(b).wait()
        return 0

    lax.fori_loop(0, blocks, finish, 0)
    for there in leaving:
        there.wait()


def interior_kernel(
    atm, y, before, after, bulk, surf, gains, band, q, kept, mid, far, w, sa, sb, za, zb, bulks, surfs, sems
):
    rows, columns = atm.shape
    blocks = columns // BLK
    fields = bulk.shape[0]
    states = fields * ASTEPS
    total = blocks + 2 * ASTEPS
    halo = ASTEPS - 1

    def arriving(b):
        return pltpu.make_async_copy(band.at[b], w.at[halo + b], sems.at[b])

    for b in [0, blocks - 1] + list(range(1, blocks - 1)):
        arriving(b).start()

    leaving = []
    for e in list(range(ASTEPS)) + list(range(ASTEPS + blocks, total)):
        pack = before if e < ASTEPS else after
        local = e if e < ASTEPS else e - ASTEPS - blocks
        at = slice(local * BLK, (local + 1) * BLK)
        za[e] = stacked(pack[0:states, at])
        bulks[e] = pack[28:32, at]
        surfs[e] = pack[32:36, at]
        if e in (0, total - 1):
            continue
        origin = local * BLK + (columns - WIDE if e < ASTEPS else 0)

        def store(first, step, lanes, high, low, e=e):
            w[e - 1, 0, first : first + step, lanes] = high
            w[e - 1, 1, first : first + step, lanes] = low

        build_band(store, pack[16:22, at].astype(jnp.int32) - origin, pack[22:28, at], HA)
        i = e - 1 if e < ASTEPS else e - 1 - blocks
        copy = pltpu.make_async_copy(w.at[e - 1], far.at[i], sems.at[blocks + i])
        copy.start()
        leaving.append(copy)
    for b in range(blocks):
        at = slice(b * BLK, (b + 1) * BLK)
        both = stacked(jnp.concatenate([atm[:, at], y[:, at]], axis=0))
        sa[b] = both
        height = rows + states
        za[b + ASTEPS] = jnp.concatenate([both[rows:height], both[height + rows :]], axis=0)
        bulks[b + ASTEPS] = bulk[:, at]
        surfs[b + ASTEPS] = surf[:, at]

    arriving(0).wait()
    arriving(blocks - 1).wait()

    slot = iota((states, BLK), 0) // fields
    for s in range(1, ASTEPS + 1):
        xs, xt = (sa, sb) if s % 2 else (sb, sa)
        zs, zt = (za, zb) if s % 2 else (zb, za)
        gain = jnp.broadcast_to(gains[:, s - 1 : s], (states, BLK))
        keep = jnp.where(slot == s - 1, 0.0, 1.0)

        def advance(moved, e, s=s, gain=gain, keep=keep):
            flux = bulks[e] * (surfs[e] - moved[(s - 1) * fields : s * fields])
            return moved * keep + gain * jnp.concatenate([flux] * ASTEPS, axis=0)

        def edge(e, s=s, zs=zs, zt=zt, advance=advance):
            def begin():
                x2 = jnp.concatenate([zs[e - 1], zs[e], zs[e + 1]], axis=1)
                return products(x2, (w[e - 1, 0], w[e - 1, 1]))

            def finish(moved):
                value = advance(moved, e)
                if s == ASTEPS:
                    q[e - ASTEPS] = value
                else:
                    zt[e] = stacked(value)

            return begin, finish

        def inner(b, s=s, xs=xs, xt=xt, zt=zt, advance=advance):
            def begin():
                x2 = jnp.concatenate([xs[b - 1], xs[b], xs[b + 1]], axis=1)
                return products(x2, (w[b + halo, 0], w[b + halo, 1]))

            def finish(moved):
                value = advance(moved[rows:], b + ASTEPS)
                if s == ASTEPS:
                    q[b] = value
                    mid[b - ASTEPS] = stacked(moved[:rows])
                else:
                    high, low = halves(moved[:rows])
                    zh, zl = halves(value)
                    xt[b] = jnp.concatenate([high, zh, low, zl], axis=0)
                    zt[b + ASTEPS] = jnp.concatenate([zh, zl], axis=0)

            return begin, finish

        def together(i, _, s=s, edge=edge, inner=inner):
            if s == 1:
                arriving(1 + 2 * i).wait()
                arriving(2 + 2 * i).wait()
            in_turn(
                [
                    inner(s + 2 * i),
                    edge(s + i),
                    edge(blocks + ASTEPS - s + i),
                    inner(s + 2 * i + 1),
                ]
            )
            return 0

        def alone(i, _, s=s, inner=inner):
            if s == 1:
                arriving(1 + 2 * i).wait()
                arriving(2 + 2 * i).wait()
            in_turn([inner(s + 2 * i), inner(s + 2 * i + 1)])
            return 0

        lax.fori_loop(0, ASTEPS, together, 0)
        if blocks // 2 - s > ASTEPS:
            lax.fori_loop(ASTEPS, blocks // 2 - s, alone, 0)
        if s < ASTEPS:
            height = rows + states
            for i, b in enumerate((s, s + 1, blocks - 2 - s, blocks - 1 - s)):
                kept[(s - 1) * 4 + i, :rows] = xt[b, :rows]
                kept[(s - 1) * 4 + i, rows:] = xt[b, height : height + rows]
    for copy in leaving:
        copy.wait()


def send_kernel(q, cols, out, table):
    fields = q.shape[1] // ASTEPS
    peers, slots = cols.shape
    blocks = q.shape[0]
    lanes = out.shape[2]
    parts = slots // lanes
    for b in range(blocks):
        table[b * fields : (b + 1) * fields, :] = q[b, (ASTEPS - 1) * fields :, :]
    rows = stacked(table[...])
    half = blocks * fields
    block_of_row = iota((half, slots), 0) // fields

    def one(p, _):
        ids = cols[pl.ds(p, 1), :]
        got = mm(rows, one_hot(ids & (BLK - 1), BLK))
        got = jnp.where(block_of_row == ids // BLK, got[:half] + got[half:], 0.0)
        got = fold_rows(got, 2 * fields)
        got = got[:fields] + got[fields:]
        out[p] = jnp.concatenate([got[:, i * lanes : (i + 1) * lanes] for i in range(parts)], axis=0)
        return 0

    lax.fori_loop(0, peers, one, 0, unroll=4)


def exchange_kernel(recv, slot, weight, yo, before, after, nbr, coef, omix, flux_out, back, rows, tiles, hots, seas, acc):
    peers, per_peer, lanes = recv.shape
    links, columns = slot.shape
    fields = flux_out.shape[0]
    parts = per_peer // fields
    highs = peers * parts
    table = highs * fields
    rows[...] = stacked(recv[...].reshape(table, lanes))
    acc[...] = jnp.zeros_like(acc)
    side = HO // 128
    own_tiles = columns // 128
    for t in range(own_tiles + 2 * side):
        if t < side:
            line = before[36:37, WIDE - HO + t * 128 : WIDE - HO + (t + 1) * 128]
        elif t < side + own_tiles:
            line = yo[:, (t - side) * 128 : (t - side + 1) * 128]
        else:
            line = after[36:37, (t - side - own_tiles) * 128 : (t - side - own_tiles + 1) * 128]
        tiles[t] = jnp.broadcast_to(line, (8, 128))
    corner = omix[0:1, 0:1] + 1.0
    high_of_row = iota((table, BLK), 0) // fields
    back_rows = iota((2 * highs, BLK), 0)
    inner = back_rows % (2 * parts)
    back_high = (back_rows // (2 * parts)) * parts + inner % parts
    pattern = iota((8, BLK), 0) % (2 * parts) // parts
    window = 1 + 2 * side
    neighbors = nbr.shape[0]

    def surface(j, half):
        t0 = j * (BLK // 128) + half
        at = pl.ds(pl.multiple_of(t0 * 128, 128), 128)
        pad = jnp.zeros((8 - neighbors, 128), jnp.int32)
        ids = jnp.concatenate([nbr[:, at] - t0 * 128, pad], axis=0)
        cs = jnp.concatenate([coef[:, at], pad.astype(F32)], axis=0)
        middle = tiles[t0 + side]
        got = jnp.zeros((8, 128), F32)
        for t in range(window):
            pick = jnp.take_along_axis(tiles[t0 + t], ids & 127, axis=1, mode="promise_in_bounds")
            got = jnp.where(ids // 128 == t, pick, got)
        return middle[0:1] + jnp.sum(cs * (got - middle), axis=0, keepdims=True)

    def base(j, _):
        at = pl.ds(pl.multiple_of(j * BLK, BLK), BLK)
        seas[:, at] = jnp.concatenate([surface(j, h) for h in range(BLK // 128)], axis=1)
        return 0

    lax.fori_loop(0, columns // BLK, base, 0, unroll=2)

    def arrive(j, _):
        at = pl.ds(pl.multiple_of(j * BLK, BLK), BLK)
        flux = jnp.zeros((2 * fields, BLK), F32)
        for r in range(links):
            ids = slot[r : r + 1, at]
            hot = one_hot(ids & (lanes - 1), lanes)
            hots[j, :, r * BLK : (r + 1) * BLK] = hot
            got = mm(rows[...], hot)
            got = jnp.where(high_of_row == ids // lanes, got[:table] + got[table:], 0.0)
            flux = flux + weight[r : r + 1, at] * fold_rows(got, 2 * fields)
        flux = flux[:fields] + flux[fields:]
        flux_out[:, at] = flux
        seas[:, at] += corner * flux[0:1]
        return 0

    lax.fori_loop(0, columns // BLK, arrive, 0, unroll=2)

    def leave(j, _):
        at = pl.ds(pl.multiple_of(j * BLK, BLK), BLK)
        sea = seas[:, at]
        left = []
        for r in range(links):
            ids, scale = slot[r : r + 1, at], weight[r : r + 1, at]
            high, low = halves(jnp.where(pattern == 1, scale, scale * sea))
            mask = back_high == ids // lanes
            both = [
                jnp.where(mask, jnp.concatenate([x.astype(F32)] * (2 * highs // 8), axis=0), 0.0).astype(BF)
                for x in (high, low)
            ]
            left.append(jnp.concatenate(both, axis=0))
        acc[...] += mm_t(jnp.concatenate(left, axis=1), hots[j])
        return 0

    lax.fori_loop(0, columns // BLK, leave, 0, unroll=2)
    back[...] = (acc[: 2 * highs] + acc[2 * highs :]).reshape(back.shape)


def settle_kernel(back, cols, surf, out, acc):
    peers, per_peer, lanes = back.shape
    parts = per_peer // 2
    blocks = surf.shape[1] // BLK
    acc[...] = jnp.zeros_like(acc)
    block_of_row = iota((blocks, lanes), 0)

    def one(d, _):
        left, hots = [], []
        for h in range(parts):
            ids = cols[pl.ds(d, 1), h * lanes : (h + 1) * lanes]
            mask = block_of_row == ids // BLK
            value = jnp.where(mask, back[d, h : h + 1, :], 0.0)
            scale = jnp.where(mask, back[d, parts + h : parts + h + 1, :], 0.0)
            left.append(stacked(jnp.concatenate([value, scale], axis=0)))
            hots.append(one_hot(ids & (BLK - 1), BLK))
        acc[...] += mm_t(jnp.concatenate(left, axis=1), jnp.concatenate(hots, axis=1))
        return 0

    lax.fori_loop(0, peers, one, 0, unroll=4)
    sums = acc[: 2 * blocks] + acc[2 * blocks :]
    base = jnp.concatenate([surf[0:1, b * BLK : (b + 1) * BLK] for b in range(blocks)], axis=0)
    value = (base + sums[:blocks]) / (1.0 + sums[blocks:])
    for b in range(blocks):
        for i in range(BLK // 128):
            row = b * (BLK // 128) + i
            out[row : row + 1, :] = value[b : b + 1, i * 128 : (i + 1) * 128]


def edge_kernel(
    before, after, atm, kept, mid, q, vertical, band, far, out, w, halos, sides, sa, sb, staged, wsems, sems, osems
):
    rows = atm.shape[0]
    blocks = q.shape[0]
    halo = ASTEPS - 1
    count = halo + ASTEPS
    arrivals = [
        pltpu.make_async_copy(before, halos.at[0], sems.at[0]),
        pltpu.make_async_copy(after, halos.at[1], sems.at[1]),
        pltpu.make_async_copy(atm.at[:, : 2 * BLK], sides.at[0], sems.at[2]),
        pltpu.make_async_copy(atm.at[:, (blocks - 2) * BLK :], sides.at[1], sems.at[3]),
    ]
    sources = [far.at[i] for i in range(halo)] + [band.at[i] for i in range(ASTEPS)]
    sources += [band.at[blocks - ASTEPS + i] for i in range(ASTEPS)] + [far.at[halo + i] for i in range(halo)]
    bands = [pltpu.make_async_copy(source, w.at[i], wsems.at[i]) for i, source in enumerate(sources)]
    needed = [list(range(ASTEPS)) + list(range(count + halo, 2 * count))]
    needed += [[ASTEPS - 1 + i, count + halo - i] for i in range(1, ASTEPS)]
    for copy in arrivals:
        copy.start()
    for group in needed:
        for i in group:
            bands[i].start()

    def leaving(b):
        at = pl.ds(pl.multiple_of(b * BLK, BLK), BLK)
        return pltpu.make_async_copy(staged.at[b], out.at[:, at], osems.at[b])

    levels = rows // 2

    def mixed(source, shift):
        def one(b, p):
            def begin():
                qh, ql = halves(q[b])
                x2 = source[b - shift]
                high = jnp.concatenate([x2[p * levels : (p + 1) * levels], qh], axis=0)
                low = jnp.concatenate([x2[rows + p * levels : rows + (p + 1) * levels], ql], axis=0)
                return mm(vertical[p], high), mm(vertical[p, :levels], low)

            def finish(value):
                staged[b, p * levels : (p + 1) * levels] = value

            return begin, finish

        def four(i, _):
            in_turn([one(4 * i + k, p) for k in range(4) for p in range(2)])
            for k in range(4):
                leaving(4 * i + k).start()
            return 0

        return four

    lax.fori_loop(1, blocks // 4 - 1, mixed(mid, ASTEPS), 0)
    for copy in arrivals:
        copy.wait()
    for i in range(ASTEPS):
        at = slice(i * BLK, (i + 1) * BLK)
        sa[i] = stacked(halos[0, :, at])
        sa[6 + 2 + i] = stacked(halos[1, :, at])
    for i in range(2):
        at = slice(i * BLK, (i + 1) * BLK)
        sa[ASTEPS + i] = stacked(sides[0, :, at])
        sa[6 + i] = stacked(sides[1, :, at])
    buffers = (sa, sb)
    for s in range(1, ASTEPS + 1):
        source, target = buffers[(s - 1) % 2], buffers[s % 2]
        last = s == ASTEPS
        for i in needed[s - 1]:
            bands[i].wait()

        def one(side, i, s=s, source=source, target=target, last=last):
            base = 6 * side
            k = s - 1 + i if side == 0 else count + ASTEPS - s + i

            def begin():
                x2 = jnp.concatenate([source[base + i + d] for d in range(3)], axis=1)
                return products(x2, (w[k, 0], w[k, 1]))

            def finish(moved):
                target[base + i + (2 * side if not last else 0)] = stacked(moved)

            return begin, finish

        in_turn([one(side, i) for i in range(ASTEPS) for side in range(2)])
        if not last:
            for i in range(2):
                target[ASTEPS + i] = kept[(s - 1) * 4 + i]
                target[6 + i] = kept[(s - 1) * 4 + 2 + i]
    final = buffers[ASTEPS % 2]
    lax.fori_loop(0, 1, mixed(final, 0), 0)
    lax.fori_loop(blocks // 4 - 1, blocks // 4, mixed(final, blocks - ASTEPS - 6), 0)

    def done(b, _):
        leaving(b).wait()
        return 0

    lax.fori_loop(0, blocks, done, 0)


def ocean_kernel(ocean, before, after, nbr, coef, vertical, top_of, flux, out, x2, wa, wb, ma, mb, laid, staged, sems):
    fields = flux.shape[0]
    rows, columns = ocean.shape
    levels = rows // fields
    blocks = columns // BLK
    eye = iota((levels, levels), 0) == iota((levels, levels), 1)
    top = jnp.broadcast_to((top_of[...] + jnp.where(eye, 1.0, 0.0))[:, 0:1], (levels, BLK))

    def part(first, width):
        pieces = []
        for ref, begin, size in ((before, -HO, HO), (ocean, 0, columns), (after, columns, HO)):
            lo, hi = max(first, begin), min(first + width, begin + size)
            if lo < hi:
                pieces.append(ref[:, lo - begin : hi - begin])
        return pieces[0] if len(pieces) == 1 else jnp.concatenate(pieces, axis=1)

    for e in range((columns + 2 * HO) // BLK):
        x2[e] = stacked(part(e * BLK - HO, BLK))

    def build(b, w):
        at = pl.ds(pl.multiple_of(b * BLK, BLK), BLK)

        def store(first, size, lanes, high, low):
            w[0, first : first + size, lanes] = high
            w[1, first : first + size, lanes] = low

        return band_pieces(store, nbr[:, at] - b * BLK, coef[:, at], HO)

    def move(b, w, moved):
        yield from product_pieces([x2[b + d] for d in range(1 + 2 * HO // BLK)], w, moved)

    def leaving(b):
        at = pl.ds(pl.multiple_of(b * BLK, BLK), BLK)
        return pltpu.make_async_copy(staged.at[b], out.at[:, at], sems.at[b])

    interleave(build(0, wa))

    def one(i, _):
        b = 2 * i
        interleave(build(b + 1, wb), move(b, wa, ma))
        interleave(build(jnp.minimum(b + 2, blocks - 1), wa), move(b + 1, wb, mb))
        laid[b] = stacked(ma[...])
        laid[b + 1] = stacked(mb[...])
        return 0

    lax.fori_loop(0, blocks // 2, one, 0)
    pair = 2 * levels

    def mixed(b, p):
        at = pl.ds(pl.multiple_of(b * BLK, BLK), BLK)

        def begin():
            high = laid[b, p * pair : (p + 1) * pair]
            low = laid[b, rows + p * pair : rows + (p + 1) * pair]
            return mm(vertical[...], high), mm(vertical[:pair], low)

        def finish(value):
            for k in range(2):
                f = 2 * p + k
                staged[b, f * levels : (f + 1) * levels] = (
                    value[k * levels : (k + 1) * levels] + top * flux[f : f + 1, at]
                )

        return begin, finish

    def four(i, _):
        in_turn([mixed(4 * i + k, p) for k in range(4) for p in range(fields // 2)])
        for k in range(4):
            leaving(4 * i + k).start()
        return 0

    lax.fori_loop(0, blocks // 4, four, 0)

    def done(b, _):
        leaving(b).wait()
        return 0

    lax.fori_loop(0, blocks, done, 0)


def after_all(value, *others):
    return lax.optimization_barrier((value, *others))[0]


def per_device(
    atm_state,
    atm_surface,
    bulk_coef,
    atm_nbr,
    atm_nbr_coef,
    atm_mix,
    ocean_state,
    ocean_nbr,
    ocean_nbr_coef,
    ocean_mix,
    send_cols,
    remap_slot,
    remap_weight,
):
    fields, la, columns = atm_state.shape
    lo, cells = ocean_state.shape[1:]
    blocks = columns // BLK
    rows = fields * la
    states = fields * ASTEPS
    picked = send_cols[0]
    peers, slots = picked.shape
    lanes = min(BLK, slots)
    parts = slots // lanes
    atm = atm_state.reshape(rows, columns)
    ocean = ocean_state.reshape(fields * lo, cells)
    depth = lax.axis_size(AXES)
    up = [(i, (i + 1) % depth) for i in range(depth)]
    down = [(j, i) for i, j in up]
    window = BLK + 2 * HA
    vmem = pl.BlockSpec(memory_space=pltpu.VMEM)
    anywhere = pl.BlockSpec(memory_space=pl.ANY)

    depth_k = rows + states
    half = fields // 2
    p_of = np.arange(half)[:, None, None]
    r_of = np.arange(2 * la)[None, :, None]
    c_of = np.arange(2 * la + states)[None, None, :]
    code = np.where(
        c_of < 2 * la,
        (c_of // la == r_of // la) * 1,
        ((c_of - 2 * la) % fields == 2 * p_of + r_of // la) * (2 + (c_of - 2 * la) // fields),
    )
    code = np.broadcast_to(code, (half, 2 * la, 2 * la + states)).astype(np.int32)
    spread = ((c_of[0] % la == np.arange(la)[:, None]) & (c_of[0] < 2 * la)).astype(np.float32)
    sea_spread = (np.arange(2 * lo)[None, :] % lo == np.arange(lo)[:, None]).astype(np.float32)

    y, yo, first, last, gains, vertical, sea_vertical = call(
        prepare_kernel(fields),
        (
            shape((states, columns)),
            shape((1, columns)),
            shape((40, WIDE)),
            shape((40, WIDE)),
            shape((states, 128)),
            shape((half, 4 * la, 2 * la + states), BF),
            shape((4 * lo, 2 * lo), BF),
        ),
        in_specs=[vmem] * 3 + [anywhere] + [vmem] * 7,
        scratch=[pltpu.VMEM((lo, cells), F32), pltpu.SemaphoreType.DMA(())],
    )(
        atm_mix,
        ocean_mix,
        atm,
        ocean,
        atm_nbr,
        atm_nbr_coef,
        bulk_coef,
        atm_surface,
        jnp.asarray(spread),
        jnp.asarray(code),
        jnp.asarray(sea_spread),
    )
    pack_before = lax.ppermute(last, AXES, up)
    pack_after = lax.ppermute(first, AXES, down)

    halo_shapes = (shape((rows, WIDE)),) * 2 + (shape((fields * lo, HO)),) * 2
    band, atm_first, atm_last, sea_first, sea_last = call(
        band_kernel,
        (shape((blocks, 2, window, BLK), BF),) + halo_shapes,
        in_specs=[vmem] * 2 + [anywhere] * 2,
        out_specs=(anywhere,) * 5,
        scratch=[pltpu.VMEM(h.shape, F32) for h in halo_shapes]
        + [
            pltpu.VMEM((blocks, 2, window, BLK), BF),
            pltpu.SemaphoreType.DMA((blocks,)),
            pltpu.SemaphoreType.DMA((4,)),
            pltpu.SemaphoreType.DMA((4,)),
        ],
    )(after_all(atm_nbr, y), atm_nbr_coef, atm, ocean)

    pack_before, pack_after, atm_first, atm_last = lax.optimization_barrier(
        (pack_before, pack_after, atm_first, atm_last)
    )
    atm_before = lax.ppermute(atm_last, AXES, up)
    atm_after = lax.ppermute(atm_first, AXES, down)

    total = blocks + 2 * ASTEPS
    halo = ASTEPS - 1
    q, kept, mid, far = call(
        interior_kernel,
        (
            shape((blocks, states, BLK)),
            shape((4 * halo, 2 * rows, BLK), BF),
            shape((blocks - 2 * ASTEPS, 2 * rows, BLK), BF),
            shape((2 * halo, 2, window, BLK), BF),
        ),
        in_specs=[vmem] * 7 + [anywhere],
        out_specs=(vmem, vmem, vmem, anywhere),
        scratch=[
            pltpu.VMEM((total - 2, 2, window, BLK), BF),
            pltpu.VMEM((blocks, 2 * depth_k, BLK), BF),
            pltpu.VMEM((blocks, 2 * depth_k, BLK), BF),
            pltpu.VMEM((total, 2 * states, BLK), BF),
            pltpu.VMEM((total, 2 * states, BLK), BF),
            pltpu.VMEM((total, fields, BLK), F32),
            pltpu.VMEM((total, fields, BLK), F32),
            pltpu.SemaphoreType.DMA((blocks + 2 * halo,)),
        ],
    )(atm, y, pack_before, pack_after, bulk_coef, atm_surface, gains, band)

    outgoing = call(
        send_kernel,
        shape((peers, parts * fields, lanes)),
        in_specs=[vmem] * 2,
        scratch=[pltpu.VMEM((blocks * fields, BLK), F32)],
    )(q, picked)
    received = lax.all_to_all(outgoing, AXES, split_axis=0, concat_axis=0, tiled=True)

    sea_first, sea_last, atm_before, atm_after = lax.optimization_barrier(
        (sea_first, sea_last, atm_before, atm_after, outgoing)
    )[:4]
    sea_before = lax.ppermute(sea_last, AXES, up)
    sea_after = lax.ppermute(sea_first, AXES, down)

    atm_final = call(
        edge_kernel,
        shape((rows, columns)),
        in_specs=[anywhere] * 3 + [vmem] * 4 + [anywhere] * 2,
        out_specs=anywhere,
        scratch=[
            pltpu.VMEM((2 * (2 * ASTEPS - 1), 2, window, BLK), BF),
            pltpu.VMEM((2, rows, WIDE), F32),
            pltpu.VMEM((2, rows, 2 * BLK), F32),
            pltpu.VMEM((12, 2 * rows, BLK), BF),
            pltpu.VMEM((12, 2 * rows, BLK), BF),
            pltpu.VMEM((blocks, rows, BLK), F32),
            pltpu.SemaphoreType.DMA((2 * (2 * ASTEPS - 1),)),
            pltpu.SemaphoreType.DMA((4,)),
            pltpu.SemaphoreType.DMA((blocks,)),
        ],
    )(after_all(atm_before, outgoing), atm_after, atm, kept, mid, q, vertical, band, far)

    received = after_all(received, atm_final)
    flux, back = call(
        exchange_kernel,
        (shape((fields, cells)), shape((peers, 2 * parts, lanes))),
        in_specs=[vmem] * 9,
        scratch=[
            pltpu.VMEM((2 * peers * parts * fields, lanes), BF),
            pltpu.VMEM((cells // 128 + 2 * HO // 128, 8, 128), F32),
            pltpu.VMEM((cells // BLK, lanes, remap_slot.shape[0] * BLK), BF),
            pltpu.VMEM((1, cells), F32),
            pltpu.VMEM((4 * peers * parts, lanes), F32),
        ],
    )(received, remap_slot, remap_weight, yo, pack_before, pack_after, ocean_nbr, ocean_nbr_coef, ocean_mix)
    returned = lax.all_to_all(back, AXES, split_axis=0, concat_axis=0, tiled=True)

    ocean_final = call(
        ocean_kernel,
        shape((fields * lo, cells)),
        in_specs=[vmem] * 8,
        out_specs=anywhere,
        scratch=[
            pltpu.VMEM(((cells + 2 * HO) // BLK, 2 * fields * lo, BLK), BF),
            pltpu.VMEM((2, BLK + 2 * HO, BLK), BF),
            pltpu.VMEM((2, BLK + 2 * HO, BLK), BF),
            pltpu.VMEM((fields * lo, BLK), F32),
            pltpu.VMEM((fields * lo, BLK), F32),
            pltpu.VMEM((cells // BLK, 2 * fields * lo, BLK), BF),
            pltpu.VMEM((cells // BLK, fields * lo, BLK), F32),
            pltpu.SemaphoreType.DMA((cells // BLK,)),
        ],
    )(ocean, after_all(sea_before, back), sea_after, ocean_nbr, ocean_nbr_coef, sea_vertical, ocean_mix, flux)

    surface_temp = call(
        settle_kernel,
        shape((columns // 128, 128)),
        in_specs=[vmem] * 3,
        scratch=[pltpu.VMEM((4 * blocks, BLK), F32)],
    )(after_all(returned, ocean_final), picked, atm_surface)

    return (
        atm_final.reshape(fields, la, columns),
        ocean_final.reshape(fields, lo, cells),
        surface_temp.reshape(columns),
    )


def solution(mesh):
    placed = (
        P(None, None, AXES),
        P(None, AXES),
        P(None, AXES),
        P(None, AXES),
        P(None, AXES),
        P(),
        P(None, None, AXES),
        P(None, AXES),
        P(None, AXES),
        P(),
        P(AXES, None, None),
        P(None, AXES),
        P(None, AXES),
    )
    return jax.shard_map(
        per_device,
        mesh=mesh,
        in_specs=placed,
        out_specs=(P(None, None, AXES), P(None, None, AXES), P(AXES)),
        check_vma=False,
    )
```

```python
import itertools

import numpy as np

import jax
import jax.numpy as jnp
from jax import lax
from jax.experimental import pallas as pl
from jax.experimental.pallas import tpu as pltpu
from jax.sharding import PartitionSpec as P

ASTEPS = 4
HA = 256
HO = 384
BLK = 256
WIDE = ASTEPS * HA
BF = jnp.bfloat16
F32 = jnp.float32
VMEM_BYTES = 56 * 1024 * 1024
AXES = ("sec", "blk")


def call(body, outs, *, in_specs=None, out_specs=None, scratch=(), flops=10**6, moved=10**4, aliases=None):
    vmem = pl.BlockSpec(memory_space=pltpu.VMEM)
    return pl.pallas_call(
        body,
        out_shape=outs,
        in_specs=in_specs,
        out_specs=jax.tree.map(lambda _: vmem, outs) if out_specs is None else out_specs,
        scratch_shapes=list(scratch),
        input_output_aliases=aliases or {},
        compiler_params=pltpu.CompilerParams(vmem_limit_bytes=VMEM_BYTES),
        cost_estimate=pl.CostEstimate(flops=flops, bytes_accessed=moved, transcendentals=0),
    )


def shape(dims, dtype=F32):
    return jax.ShapeDtypeStruct(dims, dtype)


def halves(x):
    high = x.astype(BF)
    return high, (x - high.astype(F32)).astype(BF)


def stacked(x):
    return jnp.concatenate(halves(x), axis=0)


def mm(a, b):
    return jnp.dot(a, b, preferred_element_type=F32)


def mm_t(a, b):
    return lax.dot_general(a, b, (((1,), (1,)), ((), ())), preferred_element_type=F32)


def products(x2, w2):
    return mm(x2, w2[0]), mm(x2[: x2.shape[0] // 2], w2[1])


def summed(parts):
    wide, rest = parts
    rows = rest.shape[0]
    return wide[:rows] + wide[rows:] + rest


def in_turn(works):
    waiting = None
    for begin, finish in works:
        parts = begin()
        if waiting is not None:
            waiting[1](summed(waiting[0]))
        waiting = (parts, finish)
    waiting[1](summed(waiting[0]))


def product_pieces(x2s, w2, result):
    rows = x2s[0].shape[0] // 2
    for t, x2 in enumerate(x2s):
        at = slice(t * BLK, (t + 1) * BLK)
        wide = mm(x2, w2.at[0][at])
        part = wide[:rows] + wide[rows:]
        result[...] = part if t == 0 else result[...] + part
        yield
        result[...] += mm(x2[:rows], w2.at[1][at])
        yield


def interleave(*works):
    works = list(works)
    while works:
        works = [w for w in works if next(w, w) is not w]


def iota(dims, axis):
    return lax.broadcasted_iota(jnp.int32, dims, axis)


def build_band(*args):
    for _ in band_pieces(*args):
        pass


def band_pieces(store, nbr, coef, halo):
    rows = BLK + 2 * halo
    count = nbr.shape[0]
    ids = [nbr[k : k + 1] for k in range(count)]
    cs = [coef[k : k + 1] for k in range(count)]
    rest = 1.0 - sum(cs[1:], cs[0])
    for k in range(count - 1, 0, -1):
        alive = jnp.ones_like(ids[k]) > 0
        for j in range(k):
            same = jnp.logical_and(ids[k] == ids[j], alive)
            cs[j] = cs[j] + jnp.where(same, cs[k], 0.0)
            alive = jnp.logical_and(alive, jnp.logical_not(same))
        ids[k] = jnp.where(alive, ids[k], -1)
    lanes = 128
    step = 16
    base = iota((step, lanes), 0).astype(F32)
    parts = [halves(c) for c in cs + [rest]]

    def wide(x, at):
        return jnp.broadcast_to(x[:, at].astype(F32), (step, lanes)).astype(BF)

    for half in range(BLK // lanes):
        at = slice(half * lanes, (half + 1) * lanes)
        highs = [wide(p[0], at) for p in parts]
        lows = [wide(p[1], at) for p in parts]
        own = (iota((step, lanes), 1) - iota((step, lanes), 0)).astype(F32).astype(BF)
        zero = jnp.zeros((step, lanes), BF)
        for tile in range(0, rows, BLK):
            near = [wide((i - tile).astype(F32), at) for i in ids]
            for first in range(tile, tile + BLK, step):
                high, low = zero, zero
                if half * lanes - step < first < half * lanes + lanes + 2 * halo:
                    offset = first - halo - half * lanes
                    if 0 <= offset < lanes:
                        same = own == jnp.full((step, lanes), offset, BF)
                        high = jnp.where(same, highs[-1], zero)
                        low = jnp.where(same, lows[-1], zero)
                    here = (base + float(first - tile)).astype(BF)
                    for k in range(count):
                        same = here == near[k]
                        high = jnp.where(same, highs[k], high)
                        low = jnp.where(same, lows[k], low)
                store(first, step, at, high, low)
            yield


def one_hot(ids, rows):
    lanes = ids.shape[1]
    wide = jnp.broadcast_to(ids.astype(F32), (rows, lanes)).astype(BF)
    here = iota((rows, lanes), 0).astype(F32).astype(BF)
    return jnp.where(here == wide, jnp.ones((rows, lanes), BF), jnp.zeros((rows, lanes), BF))


def fold_rows(x, height):
    total = x[:height]
    for first in range(height, x.shape[0], height):
        total = total + x[first : first + height]
    return total


def prepare_kernel(fields):
    def body(mix, omix, atm, sea, nbr, coef, bulk, surf, spread, code, sea_spread, y, yo, first, last, gains, vertical, sea_vertical, top, sem):
        la = mix.shape[0]
        columns = atm.shape[1]
        copy = pltpu.make_async_copy(sea.at[: omix.shape[0], :], top, sem)
        copy.start()
        eye = iota((la, la), 0) == iota((la, la), 1)
        step = mix[...] + jnp.where(eye, 1.0, 0.0)

        def dot(a, b):
            return jnp.dot(a, b, precision=lax.Precision.HIGHEST, preferred_element_type=F32)

        def col(r, same):
            return jnp.sum(jnp.where(same, r, 0.0), axis=1, keepdims=True)

        def row(c, same):
            return jnp.sum(jnp.where(same, c, 0.0), axis=0, keepdims=True)

        twice = dot(step, step)
        fourth = dot(twice, twice)
        rows_up = [step[la - 1 : la, :]]
        cols_up = [step[:, la - 1 : la]]
        for _ in range(ASTEPS - 2):
            rows_up.append(jnp.sum(step * col(rows_up[-1], eye), axis=0, keepdims=True))
        for _ in range(ASTEPS - 1):
            cols_up.append(jnp.sum(step * row(cols_up[-1], eye), axis=1, keepdims=True))
        slot = iota((fields * ASTEPS, 128), 0) // fields
        lane = iota((fields * ASTEPS, 128), 1)
        value = jnp.zeros((fields * ASTEPS, 128), F32)
        for s in range(1, ASTEPS + 1):
            column = jnp.where(slot == s - 1, 1.0, 0.0)
            for j in range(1, ASTEPS):
                column = jnp.where(slot == s - 1 + j, rows_up[j - 1][:, la - 1 : la], column)
            value = jnp.where(lane == s - 1, column, value)
        gains[...] = value

        spreaded = dot(jnp.concatenate([fourth] * 2, axis=0), spread[...])
        for p in range(fields // 2):
            filled = jnp.where(code[p] == 1, spreaded, 0.0)
            for m in range(ASTEPS):
                tall = jnp.concatenate([cols_up[ASTEPS - 1 - m]] * 2, axis=0)
                filled = jnp.where(code[p] == 2 + m, tall, filled)
            vertical[p] = stacked(filled)
        lo = omix.shape[0]
        sea_eye = iota((lo, lo), 0) == iota((lo, lo), 1)
        sea_step = omix[...] + jnp.where(sea_eye, 1.0, 0.0)
        spreaded = dot(jnp.concatenate([sea_step] * 2, axis=0), sea_spread[...])
        blocks = (iota((2 * lo, 2 * lo), 0) >= lo) == (iota((2 * lo, 2 * lo), 1) >= lo)
        sea_vertical[...] = stacked(jnp.where(blocks, spreaded, 0.0))

        weights = [jnp.broadcast_to(col(r, eye), (la, 128)) for r in rows_up]
        sea_weight = jnp.broadcast_to(col(sea_step[0:1, :], sea_eye), (lo, 128))
        copy.wait()
        for start in range(0, columns, 128):
            at = slice(start, start + 128)
            for f in range(fields):
                x = atm[f * la : (f + 1) * la, at]
                y[f : f + 1, at] = x[la - 1 : la]
                for k in range(1, ASTEPS):
                    y[k * fields + f : k * fields + f + 1, at] = jnp.sum(
                        x * weights[k - 1], axis=0, keepdims=True
                    )
            yo[:, at] = jnp.sum(top[:, at] * sea_weight, axis=0, keepdims=True)
        for target, at in ((first, slice(0, WIDE)), (last, slice(columns - WIDE, columns))):
            target[0:16, :] = y[:, at]
            target[16:22, :] = nbr[:, at].astype(F32)
            target[22:28, :] = coef[:, at]
            target[28:32, :] = bulk[:, at]
            target[32:36, :] = surf[:, at]
            target[36:37, :] = yo[:, at]
            target[37:40, :] = jnp.zeros((3, WIDE), F32)

    return body


def band_kernel(nbr, coef, atm, ocean, band, *refs):
    halos, held, (w, sems, in_sems, out_sems) = refs[:4], refs[4:8], refs[8:]
    blocks = nbr.shape[1] // BLK
    columns = atm.shape[1]
    spans = [(atm, 0, WIDE), (atm, columns - WIDE, WIDE), (ocean, 0, HO), (ocean, ocean.shape[1] - HO, HO)]
    arriving = [
        pltpu.make_async_copy(source.at[:, first : first + width], held[i], in_sems.at[i])
        for i, (source, first, width) in enumerate(spans)
    ]
    leaving = [pltpu.make_async_copy(held[i], halos[i], out_sems.at[i]) for i in range(len(spans))]
    for copy in arriving:
        copy.start()

    def copy(b):
        return pltpu.make_async_copy(w.at[b], band.at[b], sems.at[b])

    def build(b, _):
        at = pl.ds(pl.multiple_of(b * BLK, BLK), BLK)

        def store(first, step, lanes, high, low):
            w[b, 0, first : first + step, lanes] = high
            w[b, 1, first : first + step, lanes] = low

        build_band(store, nbr[:, at] - b * BLK, coef[:, at], HA)
        copy(b).start()
        return 0

    lax.fori_loop(0, blocks // 2, build, 0)
    for here, there in zip(arriving, leaving):
        here.wait()
        there.start()
    lax.fori_loop(blocks // 2, blocks, build, 0)

    def finish(b, _):
        copy(b).wait()
        return 0

    lax.fori_loop(0, blocks, finish, 0)
    for there in leaving:
        there.wait()


def interior_kernel(
    atm, y, before, after, bulk, surf, gains, band, q, kept, mid, far, w, sa, sb, za, zb, bulks, surfs, ma, mb, sems
):
    rows, columns = atm.shape
    blocks = columns // BLK
    fields = bulk.shape[0]
    states = fields * ASTEPS
    total = blocks + 2 * ASTEPS
    halo = ASTEPS - 1

    def arriving(b):
        return pltpu.make_async_copy(band.at[b], w.at[halo + b], sems.at[b])

    for b in list(range(1, blocks - 1)) + [0, blocks - 1]:
        arriving(b).start()

    leaving = []
    for e in list(range(ASTEPS)) + list(range(ASTEPS + blocks, total)):
        pack = before if e < ASTEPS else after
        local = e if e < ASTEPS else e - ASTEPS - blocks
        at = slice(local * BLK, (local + 1) * BLK)
        za[e] = stacked(pack[0:states, at])
        bulks[e] = pack[28:32, at]
        surfs[e] = pack[32:36, at]

    def build_far(e):
        pack = before if e < ASTEPS else after
        local = e if e < ASTEPS else e - ASTEPS - blocks
        at = slice(local * BLK, (local + 1) * BLK)
        origin = local * BLK + (columns - WIDE if e < ASTEPS else 0)

        def store(first, step, lanes, high, low):
            w[e - 1, 0, first : first + step, lanes] = high
            w[e - 1, 1, first : first + step, lanes] = low

        yield from band_pieces(store, pack[16:22, at].astype(jnp.int32) - origin, pack[22:28, at], HA)
        i = e - 1 if e < ASTEPS else e - 1 - blocks
        copy = pltpu.make_async_copy(w.at[e - 1], far.at[i], sems.at[blocks + i])
        copy.start()
        leaving.append(copy)

    for b in range(blocks):
        at = slice(b * BLK, (b + 1) * BLK)
        both = stacked(jnp.concatenate([atm[:, at], y[:, at]], axis=0))
        sa[b] = both
        height = rows + states
        za[b + ASTEPS] = jnp.concatenate([both[rows:height], both[height + rows :]], axis=0)
        bulks[b + ASTEPS] = bulk[:, at]
        surfs[b + ASTEPS] = surf[:, at]

    slot = iota((states, BLK), 0) // fields
    for s in range(1, ASTEPS + 1):
        xs, xt = (sa, sb) if s % 2 else (sb, sa)
        zs, zt = (za, zb) if s % 2 else (zb, za)
        gain = jnp.broadcast_to(gains[:, s - 1 : s], (states, BLK))
        keep = jnp.where(slot == s - 1, 0.0, 1.0)

        def advance(moved, e, s=s, gain=gain, keep=keep):
            flux = bulks[e] * (surfs[e] - moved[(s - 1) * fields : s * fields])
            return moved * keep + gain * jnp.concatenate([flux] * ASTEPS, axis=0)

        def edge(e, s=s, zs=zs, zt=zt, advance=advance):
            def begin():
                x2 = jnp.concatenate([zs[e - 1], zs[e], zs[e + 1]], axis=1)
                return products(x2, (w[e - 1, 0], w[e - 1, 1]))

            def finish(moved):
                value = advance(moved, e)
                if s == ASTEPS:
                    q[e - ASTEPS] = value
                else:
                    zt[e] = stacked(value)

            return begin, finish

        def inner(b, s=s, xs=xs, xt=xt, zt=zt, advance=advance):
            def begin():
                x2 = jnp.concatenate([xs[b - 1], xs[b], xs[b + 1]], axis=1)
                return products(x2, (w[b + halo, 0], w[b + halo, 1]))

            def finish(moved):
                value = advance(moved[rows:], b + ASTEPS)
                if s == ASTEPS:
                    q[b] = value
                    mid[b - ASTEPS] = stacked(moved[:rows])
                else:
                    high, low = halves(moved[:rows])
                    zh, zl = halves(value)
                    xt[b] = jnp.concatenate([high, zh, low, zl], axis=0)
                    zt[b + ASTEPS] = jnp.concatenate([zh, zl], axis=0)

            return begin, finish

        def together(i, _, s=s, edge=edge, inner=inner):
            in_turn(
                [
                    inner(s + 2 * i),
                    edge(s + i),
                    edge(blocks + ASTEPS - s + i),
                    inner(s + 2 * i + 1),
                ]
            )
            return 0

        def alone(i, _, s=s, inner=inner):
            in_turn([inner(s + 2 * i), inner(s + 2 * i + 1)])
            return 0

        if s == 1:
            builds = [build_far(e) for e in list(range(1, ASTEPS)) + list(range(ASTEPS + blocks, total - 1))]

            def pieces(b, moved):
                yield from product_pieces([sa[b + d] for d in (-1, 0, 1)], w.at[b + halo], moved)

            for i in range(blocks // 2 - 1):
                arriving(1 + 2 * i).wait()
                arriving(2 + 2 * i).wait()
                both = itertools.chain(pieces(1 + 2 * i, ma), pieces(2 + 2 * i, mb))
                interleave(both, *builds[i : i + 1])
                inner(1 + 2 * i)[1](ma[...])
                inner(2 + 2 * i)[1](mb[...])
            for rest in builds[blocks // 2 - 1 :]:
                interleave(rest)
            arriving(0).wait()
            arriving(blocks - 1).wait()
            in_turn([edge(e) for i in range(ASTEPS) for e in (1 + i, blocks + ASTEPS - 1 + i)])
        else:
            lax.fori_loop(0, ASTEPS, together, 0)
            if blocks // 2 - s > ASTEPS:
                lax.fori_loop(ASTEPS, blocks // 2 - s, alone, 0)
        if s < ASTEPS:
            height = rows + states
            for i, b in enumerate((s, s + 1, blocks - 2 - s, blocks - 1 - s)):
                kept[(s - 1) * 4 + i, :rows] = xt[b, :rows]
                kept[(s - 1) * 4 + i, rows:] = xt[b, height : height + rows]
    for copy in leaving:
        copy.wait()


def send_kernel(q, cols, out, table):
    fields = q.shape[1] // ASTEPS
    peers, slots = cols.shape
    blocks = q.shape[0]
    lanes = out.shape[2]
    parts = slots // lanes
    for b in range(blocks):
        table[b * fields : (b + 1) * fields, :] = q[b, (ASTEPS - 1) * fields :, :]
    rows = stacked(table[...])
    half = blocks * fields
    block_of_row = iota((half, slots), 0) // fields

    def one(p, _):
        ids = cols[pl.ds(p, 1), :]
        got = mm(rows, one_hot(ids & (BLK - 1), BLK))
        got = jnp.where(block_of_row == ids // BLK, got[:half] + got[half:], 0.0)
        got = fold_rows(got, 2 * fields)
        got = got[:fields] + got[fields:]
        out[p] = jnp.concatenate([got[:, i * lanes : (i + 1) * lanes] for i in range(parts)], axis=0)
        return 0

    lax.fori_loop(0, peers, one, 0, unroll=4)


def exchange_kernel(recv, slot, weight, yo, before, after, nbr, coef, omix, flux_out, back, rows, tiles, hots, seas, acc):
    peers, per_peer, lanes = recv.shape
    links, columns = slot.shape
    fields = flux_out.shape[0]
    parts = per_peer // fields
    highs = peers * parts
    table = highs * fields
    rows[...] = stacked(recv[...].reshape(table, lanes))
    acc[...] = jnp.zeros_like(acc)
    side = HO // 128
    own_tiles = columns // 128
    for t in range(own_tiles + 2 * side):
        if t < side:
            line = before[36:37, WIDE - HO + t * 128 : WIDE - HO + (t + 1) * 128]
        elif t < side + own_tiles:
            line = yo[:, (t - side) * 128 : (t - side + 1) * 128]
        else:
            line = after[36:37, (t - side - own_tiles) * 128 : (t - side - own_tiles + 1) * 128]
        tiles[t] = jnp.broadcast_to(line, (8, 128))
    corner = omix[0:1, 0:1] + 1.0
    high_of_row = iota((table, BLK), 0) // fields
    back_rows = iota((2 * highs, BLK), 0)
    inner = back_rows % (2 * parts)
    back_high = (back_rows // (2 * parts)) * parts + inner % parts
    pattern = iota((8, BLK), 0) % (2 * parts) // parts
    window = 1 + 2 * side
    neighbors = nbr.shape[0]

    def surface(j, half):
        t0 = j * (BLK // 128) + half
        at = pl.ds(pl.multiple_of(t0 * 128, 128), 128)
        pad = jnp.zeros((8 - neighbors, 128), jnp.int32)
        ids = jnp.concatenate([nbr[:, at] - t0 * 128, pad], axis=0)
        cs = jnp.concatenate([coef[:, at], pad.astype(F32)], axis=0)
        middle = tiles[t0 + side]
        got = jnp.zeros((8, 128), F32)
        for t in range(window):
            pick = jnp.take_along_axis(tiles[t0 + t], ids & 127, axis=1, mode="promise_in_bounds")
            got = jnp.where(ids // 128 == t, pick, got)
        return middle[0:1] + jnp.sum(cs * (got - middle), axis=0, keepdims=True)

    def base(j, _):
        at = pl.ds(pl.multiple_of(j * BLK, BLK), BLK)
        seas[:, at] = jnp.concatenate([surface(j, h) for h in range(BLK // 128)], axis=1)
        return 0

    lax.fori_loop(0, columns // BLK, base, 0, unroll=2)

    def arrive(j, _):
        at = pl.ds(pl.multiple_of(j * BLK, BLK), BLK)
        parts = []

        def begin(r):
            ids = slot[r : r + 1, at]
            hot = one_hot(ids & (lanes - 1), lanes)
            hots[j, :, r * BLK : (r + 1) * BLK] = hot
            return mm(rows[...], hot)

        def finish(r, got):
            ids = slot[r : r + 1, at]
            got = jnp.where(high_of_row == ids // lanes, got[:table] + got[table:], 0.0)
            parts.append(weight[r : r + 1, at] * fold_rows(got, 2 * fields))

        last = begin(0)
        for r in range(1, links):
            got = begin(r)
            finish(r - 1, last)
            last = got
        finish(links - 1, last)
        flux = sum(parts[1:], parts[0])
        flux = flux[:fields] + flux[fields:]
        flux_out[:, at] = flux
        seas[:, at] += corner * flux[0:1]
        return 0

    lax.fori_loop(0, columns // BLK, arrive, 0, unroll=2)

    def leave(j, _):
        at = pl.ds(pl.multiple_of(j * BLK, BLK), BLK)
        sea = seas[:, at]
        left = []
        for r in range(links):
            ids, scale = slot[r : r + 1, at], weight[r : r + 1, at]
            high, low = halves(jnp.where(pattern == 1, scale, scale * sea))
            mask = back_high == ids // lanes
            both = [
                jnp.where(mask, jnp.concatenate([x.astype(F32)] * (2 * highs // 8), axis=0), 0.0).astype(BF)
                for x in (high, low)
            ]
            left.append(jnp.concatenate(both, axis=0))
        acc[...] += mm_t(jnp.concatenate(left, axis=1), hots[j])
        return 0

    lax.fori_loop(0, columns // BLK, leave, 0, unroll=2)
    back[...] = (acc[: 2 * highs] + acc[2 * highs :]).reshape(back.shape)


def settle_kernel(back, cols, surf, out, acc):
    peers, per_peer, lanes = back.shape
    parts = per_peer // 2
    blocks = surf.shape[1] // BLK
    acc[...] = jnp.zeros_like(acc)
    block_of_row = iota((blocks, lanes), 0)

    group = 4

    def one(i, _):
        left, hots = [], []
        for k, h in itertools.product(range(group), range(parts)):
            d = group * i + k
            ids = cols[pl.ds(d, 1), h * lanes : (h + 1) * lanes]
            mask = block_of_row == ids // BLK
            value = jnp.where(mask, back[d, h : h + 1, :], 0.0)
            scale = jnp.where(mask, back[d, parts + h : parts + h + 1, :], 0.0)
            left.append(stacked(jnp.concatenate([value, scale], axis=0)))
            hots.append(one_hot(ids & (BLK - 1), BLK))
        acc[...] += mm_t(jnp.concatenate(left, axis=1), jnp.concatenate(hots, axis=1))
        return 0

    lax.fori_loop(0, peers // group, one, 0)
    sums = acc[: 2 * blocks] + acc[2 * blocks :]
    base = jnp.concatenate([surf[0:1, b * BLK : (b + 1) * BLK] for b in range(blocks)], axis=0)
    value = (base + sums[:blocks]) / (1.0 + sums[blocks:])
    for b in range(blocks):
        for i in range(BLK // 128):
            row = b * (BLK // 128) + i
            out[row : row + 1, :] = value[b : b + 1, i * 128 : (i + 1) * 128]


def edge_kernel(
    before, after, atm, kept, mid, q, vertical, band, far, out, w, halos, sides, sa, sb, staged, wsems, sems, osems
):
    rows = atm.shape[0]
    blocks = q.shape[0]
    halo = ASTEPS - 1
    count = halo + ASTEPS
    arrivals = [
        pltpu.make_async_copy(before, halos.at[0], sems.at[0]),
        pltpu.make_async_copy(after, halos.at[1], sems.at[1]),
        pltpu.make_async_copy(atm.at[:, : 2 * BLK], sides.at[0], sems.at[2]),
        pltpu.make_async_copy(atm.at[:, (blocks - 2) * BLK :], sides.at[1], sems.at[3]),
    ]
    sources = [far.at[i] for i in range(halo)] + [band.at[i] for i in range(ASTEPS)]
    sources += [band.at[blocks - ASTEPS + i] for i in range(ASTEPS)] + [far.at[halo + i] for i in range(halo)]
    bands = [pltpu.make_async_copy(source, w.at[i], wsems.at[i]) for i, source in enumerate(sources)]
    needed = [list(range(ASTEPS)) + list(range(count + halo, 2 * count))]
    needed += [[ASTEPS - 1 + i, count + halo - i] for i in range(1, ASTEPS)]
    for copy in arrivals:
        copy.start()
    for group in needed:
        for i in group:
            bands[i].start()

    def leaving(b):
        at = pl.ds(pl.multiple_of(b * BLK, BLK), BLK)
        return pltpu.make_async_copy(staged.at[b], out.at[:, at], osems.at[b])

    levels = rows // 2

    def mixed(source, shift):
        def one(b, p):
            def begin():
                qh, ql = halves(q[b])
                x2 = source[b - shift]
                high = jnp.concatenate([x2[p * levels : (p + 1) * levels], qh], axis=0)
                low = jnp.concatenate([x2[rows + p * levels : rows + (p + 1) * levels], ql], axis=0)
                return mm(vertical[p], high), mm(vertical[p, :levels], low)

            def finish(value):
                staged[b, p * levels : (p + 1) * levels] = value

            return begin, finish

        def four(i, _):
            in_turn([one(4 * i + k, p) for k in range(4) for p in range(2)])
            for k in range(4):
                leaving(4 * i + k).start()
            return 0

        return four

    lax.fori_loop(1, blocks // 4 - 1, mixed(mid, ASTEPS), 0)
    for copy in arrivals:
        copy.wait()
    for i in range(ASTEPS):
        at = slice(i * BLK, (i + 1) * BLK)
        sa[i] = stacked(halos[0, :, at])
        sa[6 + 2 + i] = stacked(halos[1, :, at])
    for i in range(2):
        at = slice(i * BLK, (i + 1) * BLK)
        sa[ASTEPS + i] = stacked(sides[0, :, at])
        sa[6 + i] = stacked(sides[1, :, at])
    buffers = (sa, sb)
    for s in range(1, ASTEPS + 1):
        source, target = buffers[(s - 1) % 2], buffers[s % 2]
        last = s == ASTEPS
        for i in needed[s - 1]:
            bands[i].wait()

        def one(side, i, s=s, source=source, target=target, last=last):
            base = 6 * side
            k = s - 1 + i if side == 0 else count + ASTEPS - s + i

            def begin():
                x2 = jnp.concatenate([source[base + i + d] for d in range(3)], axis=1)
                return products(x2, (w[k, 0], w[k, 1]))

            def finish(moved):
                target[base + i + (2 * side if not last else 0)] = stacked(moved)

            return begin, finish

        in_turn([one(side, i) for i in range(ASTEPS) for side in range(2)])
        if not last:
            for i in range(2):
                target[ASTEPS + i] = kept[(s - 1) * 4 + i]
                target[6 + i] = kept[(s - 1) * 4 + 2 + i]
    final = buffers[ASTEPS % 2]
    lax.fori_loop(0, 1, mixed(final, 0), 0)
    lax.fori_loop(blocks // 4 - 1, blocks // 4, mixed(final, blocks - ASTEPS - 6), 0)

    def done(b, _):
        leaving(b).wait()
        return 0

    lax.fori_loop(0, blocks, done, 0)


def sea_build(nbr, coef, b, w):
    at = pl.ds(pl.multiple_of(b * BLK, BLK), BLK)

    def store(first, size, lanes, high, low):
        w[0, first : first + size, lanes] = high
        w[1, first : first + size, lanes] = low

    return band_pieces(store, nbr[:, at] - b * BLK, coef[:, at], HO)


def sea_inner_kernel(ocean, nbr, coef, laid_out, x2, wa, wb, ma, mb, laid, sems):
    blocks = ocean.shape[1] // BLK
    around = 1 + 2 * HO // BLK
    first = -(-HO // BLK)
    count = blocks - 2 * first
    for i in range(count + around - 1):
        start = (first + i) * BLK - HO
        x2[i] = stacked(ocean[:, start : start + BLK])

    def leaving(i):
        return pltpu.make_async_copy(laid.at[i], laid_out.at[i], sems.at[i])

    def move(i, w, moved):
        yield from product_pieces([x2[i + d] for d in range(around)], w, moved)

    interleave(sea_build(nbr, coef, first, wa))

    def one(k, _):
        i = 2 * k
        interleave(sea_build(nbr, coef, first + i + 1, wb), move(i, wa, ma))
        interleave(sea_build(nbr, coef, jnp.minimum(i + 2, count - 1) + first, wa), move(i + 1, wb, mb))
        laid[i] = stacked(ma[...])
        laid[i + 1] = stacked(mb[...])
        leaving(i).start()
        leaving(i + 1).start()
        return 0

    lax.fori_loop(0, count // 2, one, 0)

    def done(i, _):
        leaving(i).wait()
        return 0

    lax.fori_loop(0, count, done, 0)


def sea_outer_kernel(
    before, after, nbr, coef, vertical, mix, flux, ocean, laid_in, out, ends, x2, wa, wb, ma, mb, laid, staged, sems, osems
):
    fields = flux.shape[0]
    rows, columns = ocean.shape
    levels = rows // fields
    blocks = columns // BLK
    around = 1 + 2 * HO // BLK
    first = -(-HO // BLK)
    count = blocks - 2 * first
    width = ends.shape[2]
    arriving = [
        pltpu.make_async_copy(ocean.at[:, :width], ends.at[0], sems.at[0]),
        pltpu.make_async_copy(ocean.at[:, columns - width :], ends.at[1], sems.at[1]),
        pltpu.make_async_copy(laid_in, laid.at[first : first + count], sems.at[2]),
    ]
    for copy in arriving:
        copy.start()
    eye = iota((levels, levels), 0) == iota((levels, levels), 1)
    top = jnp.broadcast_to((mix[...] + jnp.where(eye, 1.0, 0.0))[:, 0:1], (levels, BLK))
    outer = list(range(first)) + list(range(blocks - first, blocks))
    bands, sums = (wa, wb), (ma, mb)
    interleave(sea_build(nbr, coef, outer[0], wa))
    arriving[0].wait()
    arriving[1].wait()
    spans = ((before, -HO, HO), (ends.at[0], 0, width), (ends.at[1], columns - width, width), (after, columns, HO))
    held = list(range(first + around - 1)) + list(range(blocks - first, blocks + around - 1))
    for i, e in enumerate(held):
        start = e * BLK - HO
        pieces = []
        for ref, begin, size in spans:
            lo, hi = max(start, begin), min(start + BLK, begin + size)
            if lo < hi:
                pieces.append(ref[:, lo - begin : hi - begin])
        x2[i] = stacked(pieces[0] if len(pieces) == 1 else jnp.concatenate(pieces, axis=1))

    def move(b, w, moved):
        yield from product_pieces([x2[held.index(b + d)] for d in range(around)], w, moved)

    for k, b in enumerate(outer):
        works = [move(b, bands[k % 2], sums[k % 2])]
        if k + 1 < len(outer):
            works.insert(0, sea_build(nbr, coef, outer[k + 1], bands[(k + 1) % 2]))
        interleave(*works)
        laid[b] = stacked(sums[k % 2][...])
    arriving[2].wait()
    pair = 2 * levels

    def leaving(b):
        at = pl.ds(pl.multiple_of(b * BLK, BLK), BLK)
        return pltpu.make_async_copy(staged.at[b], out.at[:, at], osems.at[b])

    def mixed(b, p):
        at = pl.ds(pl.multiple_of(b * BLK, BLK), BLK)

        def begin():
            high = laid[b, p * pair : (p + 1) * pair]
            low = laid[b, rows + p * pair : rows + (p + 1) * pair]
            return mm(vertical[...], high), mm(vertical[:pair], low)

        def finish(value):
            for k in range(2):
                f = 2 * p + k
                staged[b, f * levels : (f + 1) * levels] = (
                    value[k * levels : (k + 1) * levels] + top * flux[f : f + 1, at]
                )

        return begin, finish

    def four(i, _):
        in_turn([mixed(4 * i + k, p) for k in range(4) for p in range(fields // 2)])
        for k in range(4):
            leaving(4 * i + k).start()
        return 0

    lax.fori_loop(0, blocks // 4, four, 0)

    def done(b, _):
        leaving(b).wait()
        return 0

    lax.fori_loop(0, blocks, done, 0)


def after_all(value, *others):
    return lax.optimization_barrier((value, *others))[0]


def per_device(
    atm_state,
    atm_surface,
    bulk_coef,
    atm_nbr,
    atm_nbr_coef,
    atm_mix,
    ocean_state,
    ocean_nbr,
    ocean_nbr_coef,
    ocean_mix,
    send_cols,
    remap_slot,
    remap_weight,
):
    fields, la, columns = atm_state.shape
    lo, cells = ocean_state.shape[1:]
    blocks = columns // BLK
    rows = fields * la
    states = fields * ASTEPS
    picked = send_cols[0]
    peers, slots = picked.shape
    lanes = min(BLK, slots)
    parts = slots // lanes
    atm = atm_state.reshape(rows, columns)
    ocean = ocean_state.reshape(fields * lo, cells)
    depth = lax.axis_size(AXES)
    up = [(i, (i + 1) % depth) for i in range(depth)]
    down = [(j, i) for i, j in up]
    window = BLK + 2 * HA
    vmem = pl.BlockSpec(memory_space=pltpu.VMEM)
    anywhere = pl.BlockSpec(memory_space=pl.ANY)

    depth_k = rows + states
    half = fields // 2
    p_of = np.arange(half)[:, None, None]
    r_of = np.arange(2 * la)[None, :, None]
    c_of = np.arange(2 * la + states)[None, None, :]
    code = np.where(
        c_of < 2 * la,
        (c_of // la == r_of // la) * 1,
        ((c_of - 2 * la) % fields == 2 * p_of + r_of // la) * (2 + (c_of - 2 * la) // fields),
    )
    code = np.broadcast_to(code, (half, 2 * la, 2 * la + states)).astype(np.int32)
    spread = ((c_of[0] % la == np.arange(la)[:, None]) & (c_of[0] < 2 * la)).astype(np.float32)
    sea_spread = (np.arange(2 * lo)[None, :] % lo == np.arange(lo)[:, None]).astype(np.float32)

    y, yo, first, last, gains, vertical, sea_vertical = call(
        prepare_kernel(fields),
        (
            shape((states, columns)),
            shape((1, columns)),
            shape((40, WIDE)),
            shape((40, WIDE)),
            shape((states, 128)),
            shape((half, 4 * la, 2 * la + states), BF),
            shape((4 * lo, 2 * lo), BF),
        ),
        in_specs=[vmem] * 3 + [anywhere] + [vmem] * 7,
        scratch=[pltpu.VMEM((lo, cells), F32), pltpu.SemaphoreType.DMA(())],
    )(
        atm_mix,
        ocean_mix,
        atm,
        ocean,
        atm_nbr,
        atm_nbr_coef,
        bulk_coef,
        atm_surface,
        jnp.asarray(spread),
        jnp.asarray(code),
        jnp.asarray(sea_spread),
    )
    pack_before = lax.ppermute(last, AXES, up)
    pack_after = lax.ppermute(first, AXES, down)

    halo_shapes = (shape((rows, WIDE)),) * 2 + (shape((fields * lo, HO)),) * 2
    band, atm_first, atm_last, sea_first, sea_last = call(
        band_kernel,
        (shape((blocks, 2, window, BLK), BF),) + halo_shapes,
        in_specs=[vmem] * 2 + [anywhere] * 2,
        out_specs=(anywhere,) * 5,
        scratch=[pltpu.VMEM(h.shape, F32) for h in halo_shapes]
        + [
            pltpu.VMEM((blocks, 2, window, BLK), BF),
            pltpu.SemaphoreType.DMA((blocks,)),
            pltpu.SemaphoreType.DMA((4,)),
            pltpu.SemaphoreType.DMA((4,)),
        ],
    )(after_all(atm_nbr, y), atm_nbr_coef, atm, ocean)

    pack_before, pack_after, atm_first, atm_last = lax.optimization_barrier(
        (pack_before, pack_after, atm_first, atm_last)
    )
    atm_before = lax.ppermute(atm_last, AXES, up)
    atm_after = lax.ppermute(atm_first, AXES, down)

    total = blocks + 2 * ASTEPS
    halo = ASTEPS - 1
    q, kept, mid, far = call(
        interior_kernel,
        (
            shape((blocks, states, BLK)),
            shape((4 * halo, 2 * rows, BLK), BF),
            shape((blocks - 2 * ASTEPS, 2 * rows, BLK), BF),
            shape((2 * halo, 2, window, BLK), BF),
        ),
        in_specs=[vmem] * 7 + [anywhere],
        out_specs=(vmem, vmem, vmem, anywhere),
        scratch=[
            pltpu.VMEM((total - 2, 2, window, BLK), BF),
            pltpu.VMEM((blocks, 2 * depth_k, BLK), BF),
            pltpu.VMEM((blocks, 2 * depth_k, BLK), BF),
            pltpu.VMEM((total, 2 * states, BLK), BF),
            pltpu.VMEM((total, 2 * states, BLK), BF),
            pltpu.VMEM((total, fields, BLK), F32),
            pltpu.VMEM((total, fields, BLK), F32),
            pltpu.VMEM((depth_k, BLK), F32),
            pltpu.VMEM((depth_k, BLK), F32),
            pltpu.SemaphoreType.DMA((blocks + 2 * halo,)),
        ],
    )(atm, y, pack_before, pack_after, bulk_coef, atm_surface, gains, band)

    outgoing = call(
        send_kernel,
        shape((peers, parts * fields, lanes)),
        in_specs=[vmem] * 2,
        scratch=[pltpu.VMEM((blocks * fields, BLK), F32)],
    )(q, picked)
    received = lax.all_to_all(outgoing, AXES, split_axis=0, concat_axis=0, tiled=True)

    sea_blocks = cells // BLK
    outer = -(-HO // BLK)
    around = 1 + 2 * HO // BLK
    sea_window = BLK + 2 * HO
    sea_rows = fields * lo
    inner = sea_blocks - 2 * outer
    sea_inner = call(
        sea_inner_kernel,
        shape((inner, 2 * sea_rows, BLK), BF),
        in_specs=[vmem] * 3,
        out_specs=anywhere,
        scratch=[
            pltpu.VMEM((inner + around - 1, 2 * sea_rows, BLK), BF),
            pltpu.VMEM((2, sea_window, BLK), BF),
            pltpu.VMEM((2, sea_window, BLK), BF),
            pltpu.VMEM((sea_rows, BLK), F32),
            pltpu.VMEM((sea_rows, BLK), F32),
            pltpu.VMEM((inner, 2 * sea_rows, BLK), BF),
            pltpu.SemaphoreType.DMA((inner,)),
        ],
    )(ocean, after_all(ocean_nbr, outgoing), ocean_nbr_coef)

    sea_first, sea_last, atm_before, atm_after = lax.optimization_barrier(
        (sea_first, sea_last, atm_before, atm_after, sea_inner)
    )[:4]
    sea_before = lax.ppermute(sea_last, AXES, up)
    sea_after = lax.ppermute(sea_first, AXES, down)

    atm_final = call(
        edge_kernel,
        shape((rows, columns)),
        in_specs=[anywhere] * 3 + [vmem] * 4 + [anywhere] * 2,
        out_specs=anywhere,
        scratch=[
            pltpu.VMEM((2 * (2 * ASTEPS - 1), 2, window, BLK), BF),
            pltpu.VMEM((2, rows, WIDE), F32),
            pltpu.VMEM((2, rows, 2 * BLK), F32),
            pltpu.VMEM((12, 2 * rows, BLK), BF),
            pltpu.VMEM((12, 2 * rows, BLK), BF),
            pltpu.VMEM((blocks, rows, BLK), F32),
            pltpu.SemaphoreType.DMA((2 * (2 * ASTEPS - 1),)),
            pltpu.SemaphoreType.DMA((4,)),
            pltpu.SemaphoreType.DMA((blocks,)),
        ],
    )(after_all(atm_before, outgoing), atm_after, atm, kept, mid, q, vertical, band, far)

    received = after_all(received, atm_final)
    flux, back = call(
        exchange_kernel,
        (shape((fields, cells)), shape((peers, 2 * parts, lanes))),
        in_specs=[vmem] * 9,
        scratch=[
            pltpu.VMEM((2 * peers * parts * fields, lanes), BF),
            pltpu.VMEM((cells // 128 + 2 * HO // 128, 8, 128), F32),
            pltpu.VMEM((cells // BLK, lanes, remap_slot.shape[0] * BLK), BF),
            pltpu.VMEM((1, cells), F32),
            pltpu.VMEM((4 * peers * parts, lanes), F32),
        ],
    )(received, remap_slot, remap_weight, yo, pack_before, pack_after, ocean_nbr, ocean_nbr_coef, ocean_mix)
    returned = lax.all_to_all(back, AXES, split_axis=0, concat_axis=0, tiled=True)

    ocean_final = call(
        sea_outer_kernel,
        shape((sea_rows, cells)),
        in_specs=[vmem] * 7 + [anywhere] * 2,
        out_specs=anywhere,
        scratch=[
            pltpu.VMEM((2, sea_rows, (outer + around - 1) * BLK - HO), F32),
            pltpu.VMEM((2 * (outer + around - 1), 2 * sea_rows, BLK), BF),
            pltpu.VMEM((2, sea_window, BLK), BF),
            pltpu.VMEM((2, sea_window, BLK), BF),
            pltpu.VMEM((sea_rows, BLK), F32),
            pltpu.VMEM((sea_rows, BLK), F32),
            pltpu.VMEM((sea_blocks, 2 * sea_rows, BLK), BF),
            pltpu.VMEM((sea_blocks, sea_rows, BLK), F32),
            pltpu.SemaphoreType.DMA((3,)),
            pltpu.SemaphoreType.DMA((sea_blocks,)),
        ],
    )(
        after_all(sea_before, back),
        sea_after,
        ocean_nbr,
        ocean_nbr_coef,
        sea_vertical,
        ocean_mix,
        flux,
        ocean,
        sea_inner,
    )

    surface_temp = call(
        settle_kernel,
        shape((columns // 128, 128)),
        in_specs=[vmem] * 3,
        scratch=[pltpu.VMEM((4 * blocks, BLK), F32)],
    )(after_all(returned, ocean_final), picked, atm_surface)

    return (
        atm_final.reshape(fields, la, columns),
        ocean_final.reshape(fields, lo, cells),
        surface_temp.reshape(columns),
    )


def solution(mesh):
    placed = (
        P(None, None, AXES),
        P(None, AXES),
        P(None, AXES),
        P(None, AXES),
        P(None, AXES),
        P(),
        P(None, None, AXES),
        P(None, AXES),
        P(None, AXES),
        P(),
        P(AXES, None, None),
        P(None, AXES),
        P(None, AXES),
    )
    return jax.shard_map(
        per_device,
        mesh=mesh,
        in_specs=placed,
        out_specs=(P(None, None, AXES), P(None, None, AXES), P(AXES)),
        check_vma=False,
    )
```

```python
import itertools

import numpy as np

import jax
import jax.numpy as jnp
from jax import lax
from jax.experimental import pallas as pl
from jax.experimental.pallas import tpu as pltpu
from jax.sharding import PartitionSpec as P

ASTEPS = 4
HA = 256
HO = 384
BLK = 256
WIDE = ASTEPS * HA
BF = jnp.bfloat16
F32 = jnp.float32
VMEM_BYTES = 56 * 1024 * 1024
AXES = ("sec", "blk")


def call(body, outs, *, in_specs=None, out_specs=None, scratch=(), flops=10**6, moved=10**4, aliases=None):
    vmem = pl.BlockSpec(memory_space=pltpu.VMEM)
    return pl.pallas_call(
        body,
        out_shape=outs,
        in_specs=in_specs,
        out_specs=jax.tree.map(lambda _: vmem, outs) if out_specs is None else out_specs,
        scratch_shapes=list(scratch),
        input_output_aliases=aliases or {},
        compiler_params=pltpu.CompilerParams(vmem_limit_bytes=VMEM_BYTES),
        cost_estimate=pl.CostEstimate(flops=flops, bytes_accessed=moved, transcendentals=0),
    )


def shape(dims, dtype=F32):
    return jax.ShapeDtypeStruct(dims, dtype)


def halves(x):
    high = x.astype(BF)
    return high, (x - high.astype(F32)).astype(BF)


def stacked(x):
    return jnp.concatenate(halves(x), axis=0)


def mm(a, b):
    return jnp.dot(a, b, preferred_element_type=F32)


def mm_t(a, b):
    return lax.dot_general(a, b, (((1,), (1,)), ((), ())), preferred_element_type=F32)


def products(x2, w2):
    return mm(x2, w2[0]), mm(x2[: x2.shape[0] // 2], w2[1])


def summed(parts):
    wide, rest = parts
    rows = rest.shape[0]
    return wide[:rows] + wide[rows:] + rest


def in_turn(works):
    waiting = None
    for begin, finish in works:
        parts = begin()
        if waiting is not None:
            waiting[1](summed(waiting[0]))
        waiting = (parts, finish)
    waiting[1](summed(waiting[0]))


def product_pieces(x2s, w2, result):
    rows = x2s[0].shape[0] // 2
    for t, x2 in enumerate(x2s):
        at = slice(t * BLK, (t + 1) * BLK)
        wide = mm(x2, w2.at[0][at])
        part = wide[:rows] + wide[rows:]
        result[...] = part if t == 0 else result[...] + part
        yield
        result[...] += mm(x2[:rows], w2.at[1][at])
        yield


def interleave(*works):
    works = list(works)
    while works:
        works = [w for w in works if next(w, w) is not w]


def iota(dims, axis):
    return lax.broadcasted_iota(jnp.int32, dims, axis)


def build_band(*args):
    for _ in band_pieces(*args):
        pass


def band_pieces(store, nbr, coef, halo):
    rows = BLK + 2 * halo
    count = nbr.shape[0]
    ids = [nbr[k : k + 1] for k in range(count)]
    cs = [coef[k : k + 1] for k in range(count)]
    rest = 1.0 - sum(cs[1:], cs[0])
    for k in range(count - 1, 0, -1):
        alive = jnp.ones_like(ids[k]) > 0
        for j in range(k):
            same = jnp.logical_and(ids[k] == ids[j], alive)
            cs[j] = cs[j] + jnp.where(same, cs[k], 0.0)
            alive = jnp.logical_and(alive, jnp.logical_not(same))
        ids[k] = jnp.where(alive, ids[k], -1)
    lanes = 128
    step = 16
    base = iota((step, lanes), 0).astype(F32)
    parts = [halves(c) for c in cs + [rest]]

    def wide(x, at):
        return jnp.broadcast_to(x[:, at].astype(F32), (step, lanes)).astype(BF)

    for half in range(BLK // lanes):
        at = slice(half * lanes, (half + 1) * lanes)
        highs = [wide(p[0], at) for p in parts]
        lows = [wide(p[1], at) for p in parts]
        own = (iota((step, lanes), 1) - iota((step, lanes), 0)).astype(F32).astype(BF)
        zero = jnp.zeros((step, lanes), BF)
        for tile in range(0, rows, BLK):
            near = [wide((i - tile).astype(F32), at) for i in ids]
            for first in range(tile, tile + BLK, step):
                high, low = zero, zero
                if half * lanes - step < first < half * lanes + lanes + 2 * halo:
                    offset = first - halo - half * lanes
                    if 0 <= offset < lanes:
                        same = own == jnp.full((step, lanes), offset, BF)
                        high = jnp.where(same, highs[-1], zero)
                        low = jnp.where(same, lows[-1], zero)
                    here = (base + float(first - tile)).astype(BF)
                    for k in range(count):
                        same = here == near[k]
                        high = jnp.where(same, highs[k], high)
                        low = jnp.where(same, lows[k], low)
                store(first, step, at, high, low)
            yield


def one_hot(ids, rows):
    lanes = ids.shape[1]
    wide = jnp.broadcast_to(ids.astype(F32), (rows, lanes)).astype(BF)
    here = iota((rows, lanes), 0).astype(F32).astype(BF)
    return jnp.where(here == wide, jnp.ones((rows, lanes), BF), jnp.zeros((rows, lanes), BF))


def fold_rows(x, height):
    total = x[:height]
    for first in range(height, x.shape[0], height):
        total = total + x[first : first + height]
    return total


def prepare_kernel(fields):
    def body(
        mix, omix, atm, nbr, coef, bulk, surf, spread, code, sea_spread, sea,
        y, yo, gains, lift, vertical, sea_vertical, wide_first, wide_last, sea_first, sea_last,
        top, lists, ends, sems,
    ):
        la = mix.shape[0]
        rows, columns = atm.shape
        cells = sea.shape[1]
        copy = pltpu.make_async_copy(sea.at[: omix.shape[0], :], top, sems.at[0])
        copy.start()
        arriving = [
            pltpu.make_async_copy(sea.at[:, :HO], ends.at[0], sems.at[1]),
            pltpu.make_async_copy(sea.at[:, cells - HO :], ends.at[1], sems.at[2]),
        ]
        leaving = [
            pltpu.make_async_copy(atm.at[:, :WIDE], wide_first.at[:rows], sems.at[3]),
            pltpu.make_async_copy(atm.at[:, columns - WIDE :], wide_last.at[:rows], sems.at[4]),
            pltpu.make_async_copy(lists.at[0], wide_first.at[rows:], sems.at[5]),
            pltpu.make_async_copy(lists.at[1], wide_last.at[rows:], sems.at[6]),
            pltpu.make_async_copy(ends.at[0], sea_first, sems.at[7]),
            pltpu.make_async_copy(ends.at[1], sea_last, sems.at[8]),
        ]
        for i, at in enumerate((slice(0, WIDE), slice(columns - WIDE, columns))):
            lists[i, 0:6] = nbr[:, at].astype(F32)
            lists[i, 6:12] = coef[:, at]
            lists[i, 12:16] = bulk[:, at]
            lists[i, 16:20] = surf[:, at]
            lists[i, 20:24] = jnp.zeros((4, WIDE), F32)
        for here in arriving:
            here.start()
        for out in leaving[:4]:
            out.start()
        eye = iota((la, la), 0) == iota((la, la), 1)
        step = mix[...] + jnp.where(eye, 1.0, 0.0)

        def dot(a, b):
            return jnp.dot(a, b, precision=lax.Precision.HIGHEST, preferred_element_type=F32)

        def col(r, same):
            return jnp.sum(jnp.where(same, r, 0.0), axis=1, keepdims=True)

        def row(c, same):
            return jnp.sum(jnp.where(same, c, 0.0), axis=0, keepdims=True)

        twice = dot(step, step)
        fourth = dot(twice, twice)
        rows_up = [step[la - 1 : la, :]]
        cols_up = [step[:, la - 1 : la]]
        for _ in range(ASTEPS - 2):
            rows_up.append(jnp.sum(step * col(rows_up[-1], eye), axis=0, keepdims=True))
        for _ in range(ASTEPS - 1):
            cols_up.append(jnp.sum(step * row(cols_up[-1], eye), axis=1, keepdims=True))
        slot = iota((fields * ASTEPS, 128), 0) // fields
        lane = iota((fields * ASTEPS, 128), 1)
        value = jnp.zeros((fields * ASTEPS, 128), F32)
        for s in range(1, ASTEPS + 1):
            column = jnp.where(slot == s - 1, 1.0, 0.0)
            for j in range(1, ASTEPS):
                column = jnp.where(slot == s - 1 + j, rows_up[j - 1][:, la - 1 : la], column)
            value = jnp.where(lane == s - 1, column, value)
        gains[...] = value

        spreaded = dot(jnp.concatenate([fourth] * 2, axis=0), spread[...])
        for p in range(fields // 2):
            filled = jnp.where(code[p] == 1, spreaded, 0.0)
            for m in range(ASTEPS):
                tall = jnp.concatenate([cols_up[ASTEPS - 1 - m]] * 2, axis=0)
                filled = jnp.where(code[p] == 2 + m, tall, filled)
            vertical[p] = stacked(filled)
        lo = omix.shape[0]
        sea_eye = iota((lo, lo), 0) == iota((lo, lo), 1)
        sea_step = omix[...] + jnp.where(sea_eye, 1.0, 0.0)
        spreaded = dot(jnp.concatenate([sea_step] * 2, axis=0), sea_spread[...])
        blocks = (iota((2 * lo, 2 * lo), 0) >= lo) == (iota((2 * lo, 2 * lo), 1) >= lo)
        sea_vertical[...] = stacked(jnp.where(blocks, spreaded, 0.0))

        weights = [jnp.broadcast_to(col(r, eye), (la, 128)) for r in rows_up]
        for k, weight in enumerate(weights):
            lift[k] = weight
        sea_weight = jnp.broadcast_to(col(sea_step[0:1, :], sea_eye), (lo, 128))
        copy.wait()
        for start in range(0, columns, 128):
            at = slice(start, start + 128)
            for f in range(fields):
                x = atm[f * la : (f + 1) * la, at]
                y[f : f + 1, at] = x[la - 1 : la]
                for k in range(1, ASTEPS):
                    y[k * fields + f : k * fields + f + 1, at] = jnp.sum(
                        x * weights[k - 1], axis=0, keepdims=True
                    )
            yo[:, at] = jnp.sum(top[:, at] * sea_weight, axis=0, keepdims=True)
        for here, out in zip(arriving, leaving[4:]):
            here.wait()
            out.start()
        for out in leaving:
            out.wait()

    return body


def band_build(ids, coef, w, k):
    def store(first, step, lanes, high, low):
        w[k, 0, first : first + step, lanes] = high
        w[k, 1, first : first + step, lanes] = low

    return band_pieces(store, ids, coef, HA)


def advance(moved, s, gains, bulk, surf):
    fields = bulk.shape[0]
    states = moved.shape[0]
    slot = iota((states, BLK), 0) // fields
    flux = bulk * (surf - moved[(s - 1) * fields : s * fields])
    kept = jnp.where(slot == s - 1, 0.0, moved)
    return kept + gains[:, s - 1 : s] * jnp.concatenate([flux] * ASTEPS, axis=0)


def interior_kernel(
    atm, y, nbr, coef, bulk, surf, gains, q, kept_out, mid_out, band, w, sa, sb, ma, mb, kept, mid, sems
):
    rows, columns = atm.shape
    states = y.shape[0]
    height = rows + states
    blocks = columns // BLK
    sent = list(range(ASTEPS)) + list(range(blocks - ASTEPS, blocks))
    leaving = []

    def depart(copy):
        copy.start()
        leaving.append(copy)

    def build(b):
        at = slice(b * BLK, (b + 1) * BLK)
        yield from band_build(nbr[:, at] - b * BLK, coef[:, at], w, b)

    def split(b):
        at = slice(b * BLK, (b + 1) * BLK)
        sa[b] = stacked(jnp.concatenate([atm[:, at], y[:, at]], axis=0))
        yield

    def pieces(b, moved):
        yield from product_pieces([sa[b + d] for d in (-1, 0, 1)], w.at[b], moved)

    def finish(b, s, moved, target):
        at = pl.ds(pl.multiple_of(b * BLK, BLK), BLK)
        value = advance(moved[rows:], s, gains, bulk[:, at], surf[:, at])
        if s == ASTEPS:
            q[b - ASTEPS] = value
            mid[b - ASTEPS] = stacked(moved[:rows])
        else:
            high, low = halves(moved[:rows])
            zh, zl = halves(value)
            target[b] = jnp.concatenate([high, zh, low, zl], axis=0)

    interleave(itertools.chain(*[split(b) for b in range(4)]))
    interleave(build(1))
    interleave(build(2))
    for i in range(blocks // 2 - 1):
        b = 2 * i + 1
        nexts = [b + 2, b + 3] if b + 3 < blocks - 1 else [0, blocks - 1]
        works = [itertools.chain(pieces(b, ma), pieces(b + 1, mb)), itertools.chain(*[build(k) for k in nexts])]
        if b + 4 < blocks:
            works.append(itertools.chain(split(b + 3), split(b + 4)))
        interleave(*works)
        finish(b, 1, ma[...], sb)
        finish(b + 1, 1, mb[...], sb)
    for i, b in enumerate(sent):
        depart(pltpu.make_async_copy(w.at[b], band.at[i], sems.at[i]))

    for s in range(1, ASTEPS + 1):
        xs, xt = (sa, sb) if s % 2 else (sb, sa)

        def inner(b, s=s, xs=xs, xt=xt):
            def begin():
                x2 = jnp.concatenate([xs[b - 1], xs[b], xs[b + 1]], axis=1)
                return products(x2, (w[b, 0], w[b, 1]))

            return begin, lambda moved: finish(b, s, moved, xt)

        def pair(i, _, s=s, inner=inner):
            in_turn([inner(s + 2 * i), inner(s + 2 * i + 1)])
            return 0

        if s > 1:
            lax.fori_loop(0, blocks // 2 - s, pair, 0)
        if s < ASTEPS:
            at = slice((s - 1) * 4, s * 4)
            for i, b in enumerate((s, s + 1, blocks - 2 - s, blocks - 1 - s)):
                kept[(s - 1) * 4 + i] = xt[b]
            depart(pltpu.make_async_copy(kept.at[at], kept_out.at[at], sems.at[len(sent) + s]))
    depart(pltpu.make_async_copy(mid, mid_out, sems.at[len(sent)]))
    for copy in leaving:
        copy.wait()


def block_place(b, blocks, ends, middle):
    if b < ASTEPS:
        return ends, b
    if b < blocks - ASTEPS:
        return middle, b - ASTEPS
    return ends, b - blocks + 2 * ASTEPS


def send_kernel(q_ends, q_mid, cols, out, table):
    fields = q_mid.shape[1] // ASTEPS
    peers, slots = cols.shape
    blocks = q_ends.shape[0] + q_mid.shape[0]
    lanes = out.shape[2]
    parts = slots // lanes
    for b in range(blocks):
        ref, i = block_place(b, blocks, q_ends, q_mid)
        table[b * fields : (b + 1) * fields, :] = ref[i, (ASTEPS - 1) * fields :, :]
    rows = stacked(table[...])
    half = blocks * fields
    block_of_row = iota((half, slots), 0) // fields

    def one(p, _):
        ids = cols[pl.ds(p, 1), :]
        got = mm(rows, one_hot(ids & (BLK - 1), BLK))
        got = jnp.where(block_of_row == ids // BLK, got[:half] + got[half:], 0.0)
        got = fold_rows(got, 2 * fields)
        got = got[:fields] + got[fields:]
        out[p] = jnp.concatenate([got[:, i * lanes : (i + 1) * lanes] for i in range(parts)], axis=0)
        return 0

    lax.fori_loop(0, peers, one, 0, unroll=4)


def exchange_kernel(
    recv, slot, weight, yo, nbr, coef, omix, before_in, after_in, flux_out, back, rows, tiles, hots, seas, acc, held, sems
):
    peers, per_peer, lanes = recv.shape
    links, columns = slot.shape
    fields = flux_out.shape[0]
    parts = per_peer // fields
    highs = peers * parts
    table = highs * fields
    arriving = [
        pltpu.make_async_copy(ref.at[: held.shape[1]], held.at[i], sems.at[i])
        for i, ref in enumerate((before_in, after_in))
    ]
    for copy in arriving:
        copy.start()
    rows[...] = jnp.concatenate(halves(recv[...].reshape(table, lanes)), axis=1)
    levels = omix.shape[0]
    eye = iota((levels, levels), 0) == iota((levels, levels), 1)
    corner = omix[0:1, 0:1] + 1.0
    top = omix[0:1, :] + jnp.where(iota((1, levels), 1) == 0, 1.0, 0.0)
    top = jnp.sum(jnp.where(eye, top, 0.0), axis=1, keepdims=True)
    for copy in arriving:
        copy.wait()
    before, after = [jnp.sum(held[i] * top, axis=0, keepdims=True) for i in range(2)]
    acc[...] = jnp.zeros_like(acc)
    side = HO // 128
    own_tiles = columns // 128
    for t in range(own_tiles + 2 * side):
        if t < side:
            line = before[:, t * 128 : (t + 1) * 128]
        elif t < side + own_tiles:
            line = yo[:, (t - side) * 128 : (t - side + 1) * 128]
        else:
            line = after[:, (t - side - own_tiles) * 128 : (t - side - own_tiles + 1) * 128]
        tiles[t] = jnp.broadcast_to(line, (8, 128))
    high_of_row = iota((table, BLK), 0) // fields
    back_rows = iota((2 * highs, BLK), 0)
    inner = back_rows % (2 * parts)
    back_high = (back_rows // (2 * parts)) * parts + inner % parts
    pattern = iota((8, BLK), 0) % (2 * parts) // parts
    window = 1 + 2 * side
    neighbors = nbr.shape[0]

    def surface(j, half):
        t0 = j * (BLK // 128) + half
        at = pl.ds(pl.multiple_of(t0 * 128, 128), 128)
        pad = jnp.zeros((8 - neighbors, 128), jnp.int32)
        ids = jnp.concatenate([nbr[:, at] - t0 * 128, pad], axis=0)
        cs = jnp.concatenate([coef[:, at], pad.astype(F32)], axis=0)
        middle = tiles[t0 + side]
        got = jnp.zeros((8, 128), F32)
        for t in range(window):
            pick = jnp.take_along_axis(tiles[t0 + t], ids & 127, axis=1, mode="promise_in_bounds")
            got = jnp.where(ids // 128 == t, pick, got)
        return middle[0:1] + jnp.sum(cs * (got - middle), axis=0, keepdims=True)

    def base(j, _):
        at = pl.ds(pl.multiple_of(j * BLK, BLK), BLK)
        seas[:, at] = jnp.concatenate([surface(j, h) for h in range(BLK // 128)], axis=1)
        return 0

    lax.fori_loop(0, columns // BLK, base, 0, unroll=2)

    def arrive(j, _):
        at = pl.ds(pl.multiple_of(j * BLK, BLK), BLK)
        parts = []

        def begin(r):
            ids = slot[r : r + 1, at]
            hot = one_hot(ids & (lanes - 1), lanes)
            hots[j, :, r * BLK : (r + 1) * BLK] = hot
            return mm(rows[...], jnp.concatenate([hot, hot], axis=0))

        def finish(r, got):
            ids = slot[r : r + 1, at]
            got = jnp.where(high_of_row == ids // lanes, got, 0.0)
            parts.append(weight[r : r + 1, at] * fold_rows(got, 2 * fields))

        last = begin(0)
        for r in range(1, links):
            got = begin(r)
            finish(r - 1, last)
            last = got
        finish(links - 1, last)
        flux = sum(parts[1:], parts[0])
        flux = flux[:fields] + flux[fields:]
        flux_out[:, at] = flux
        seas[:, at] += corner * flux[0:1]
        return 0

    lax.fori_loop(0, columns // BLK, arrive, 0, unroll=2)

    def leave(j, _):
        at = pl.ds(pl.multiple_of(j * BLK, BLK), BLK)
        sea = seas[:, at]
        left = []
        for r in range(links):
            ids, scale = slot[r : r + 1, at], weight[r : r + 1, at]
            high, low = halves(jnp.where(pattern == 1, scale, scale * sea))
            mask = back_high == ids // lanes
            both = [
                jnp.where(mask, jnp.concatenate([x.astype(F32)] * (2 * highs // 8), axis=0), 0.0).astype(BF)
                for x in (high, low)
            ]
            left.append(jnp.concatenate(both, axis=0))
        acc[...] += mm_t(jnp.concatenate(left, axis=1), hots[j])
        return 0

    lax.fori_loop(0, columns // BLK, leave, 0, unroll=2)
    back[...] = (acc[: 2 * highs] + acc[2 * highs :]).reshape(back.shape)


def settle_kernel(back, cols, surf, out, acc):
    peers, per_peer, lanes = back.shape
    parts = per_peer // 2
    blocks = surf.shape[1] // BLK
    acc[...] = jnp.zeros_like(acc)
    block_of_row = iota((blocks, lanes), 0)

    group = 4

    def one(i, _):
        left, hots = [], []
        for k, h in itertools.product(range(group), range(parts)):
            d = group * i + k
            ids = cols[pl.ds(d, 1), h * lanes : (h + 1) * lanes]
            mask = block_of_row == ids // BLK
            value = jnp.where(mask, back[d, h : h + 1, :], 0.0)
            scale = jnp.where(mask, back[d, parts + h : parts + h + 1, :], 0.0)
            left.append(stacked(jnp.concatenate([value, scale], axis=0)))
            hots.append(one_hot(ids & (BLK - 1), BLK))
        acc[...] += mm_t(jnp.concatenate(left, axis=1), jnp.concatenate(hots, axis=1))
        return 0

    lax.fori_loop(0, peers // group, one, 0)
    sums = acc[: 2 * blocks] + acc[2 * blocks :]
    base = jnp.concatenate([surf[0:1, b * BLK : (b + 1) * BLK] for b in range(blocks)], axis=0)
    value = (base + sums[:blocks]) / (1.0 + sums[blocks:])
    for b in range(blocks):
        for i in range(BLK // 128):
            row = b * (BLK // 128) + i
            out[row : row + 1, :] = value[b : b + 1, i * 128 : (i + 1) * 128]


def edge_kernel(
    y, bulk, surf, gains, lift, before, after, atm, kept_in, band, q, ends_out,
    w, wide, sides, kept, sa, sb, ma, mb, ends, sems,
):
    rows = atm.shape[0]
    levels = lift.shape[1]
    fields = bulk.shape[0]
    states = y.shape[0]
    columns = y.shape[1]
    blocks = columns // BLK
    halo = ASTEPS - 1
    count = halo + ASTEPS
    total = blocks + 2 * ASTEPS
    arriving = [
        pltpu.make_async_copy(before, wide.at[0], sems.at[0]),
        pltpu.make_async_copy(after, wide.at[1], sems.at[1]),
        pltpu.make_async_copy(atm.at[:, : 2 * BLK], sides.at[0], sems.at[2]),
        pltpu.make_async_copy(atm.at[:, columns - 2 * BLK :], sides.at[1], sems.at[3]),
    ]
    bands = [pltpu.make_async_copy(band.at[i], w.at[halo + i], sems.at[4 + i]) for i in range(2 * ASTEPS)]
    keeps = pltpu.make_async_copy(kept_in, kept, sems.at[4 + 2 * ASTEPS])
    needed = [[0, 2 * ASTEPS - 1]] + [[i, 2 * ASTEPS - 1 - i] for i in range(1, ASTEPS)]
    for copy in arriving:
        copy.start()
    for group in needed:
        for i in group:
            bands[i].start()
    keeps.start()

    def place(e):
        if e < ASTEPS:
            return wide.at[0], e
        if e >= total - ASTEPS:
            return wide.at[1], e - total + ASTEPS
        return None, e - ASTEPS

    def coefs(e):
        ref, local = place(e)
        at = slice(local * BLK, (local + 1) * BLK)
        if ref is None:
            return bulk[:, at], surf[:, at]
        return ref[rows + 12 : rows + 16, at], ref[rows + 16 : rows + 20, at]

    def build(e):
        ref, local = place(e)
        origin = local * BLK + (columns - WIDE if e < ASTEPS else 0)
        at = slice(local * BLK, (local + 1) * BLK)
        ids = ref[rows : rows + 6, at].astype(jnp.int32) - origin
        k = e - 1 if e < ASTEPS else e - (total - 1) + 2 * count
        yield from band_build(ids, ref[rows + 6 : rows + 12, at], w, k)

    for copy in arriving:
        copy.wait()
    for i in range(ASTEPS):
        at = slice(i * BLK, (i + 1) * BLK)
        for side in range(2):
            x = wide[side, :rows, at]
            lifted = [x[(f + 1) * levels - 1 : (f + 1) * levels] for f in range(fields)]
            for k in range(ASTEPS - 1):
                weight = jnp.concatenate([lift[k]] * (BLK // 128), axis=1)
                for f in range(fields):
                    lifted.append(jnp.sum(x[f * levels : (f + 1) * levels] * weight, axis=0, keepdims=True))
            sa[i if side == 0 else 8 + i] = stacked(jnp.concatenate([x] + lifted, axis=0))
    for i in range(2):
        at = slice(i * BLK, (i + 1) * BLK)
        far = slice(columns - (2 - i) * BLK, columns - (1 - i) * BLK)
        sa[ASTEPS + i] = stacked(jnp.concatenate([sides[0, :, at], y[:, at]], axis=0))
        sa[6 + i] = stacked(jnp.concatenate([sides[1, :, at], y[:, far]], axis=0))

    buffers = (sa, sb)
    builds = [itertools.chain(build(1 + i), build(total - 2 - i)) for i in range(halo)]
    interleave(builds[0])
    for s in range(1, ASTEPS + 1):
        source, target = buffers[(s - 1) % 2], buffers[s % 2]
        last = s == ASTEPS

        def finish(side, i, moved, s=s, target=target, last=last):
            e = s + i if side == 0 else total - 1 - s - halo + i
            value = advance(moved[rows:], s, gains, *coefs(e))
            if last:
                q[4 * side + i] = value
                ends[4 * side + i] = stacked(moved[:rows])
            else:
                target[6 * side + i + 2 * side] = stacked(jnp.concatenate([moved[:rows], value], axis=0))

        def band_of(side, i, s=s):
            return s - 1 + i if side == 0 else count + ASTEPS - s + i

        def one(side, i, source=source, finish=finish, band_of=band_of):
            def begin():
                x2 = jnp.concatenate([source[6 * side + i + d] for d in range(3)], axis=1)
                k = band_of(side, i)
                return products(x2, (w[k, 0], w[k, 1]))

            return begin, lambda moved: finish(side, i, moved)

        if s == 1:
            for i in range(halo):
                pieces = [
                    product_pieces([source[6 * side + j + d] for d in range(3)], w.at[band_of(side, j)], m)
                    for side, j, m in ((0, i, ma), (1, halo - i, mb))
                ]
                interleave(itertools.chain(*pieces), *builds[i + 1 : i + 2])
                finish(0, i, ma[...])
                finish(1, halo - i, mb[...])
            for k in needed[0]:
                bands[k].wait()
            in_turn([one(0, halo), one(1, 0)])
            keeps.wait()
        else:
            for k in needed[s - 1]:
                bands[k].wait()
            in_turn([one(side, i) for i in range(ASTEPS) for side in range(2)])
        if not last:
            for i in range(2):
                target[ASTEPS + i] = kept[(s - 1) * 4 + i]
                target[6 + i] = kept[(s - 1) * 4 + 2 + i]
    out = pltpu.make_async_copy(ends, ends_out, sems.at[5 + 2 * ASTEPS])
    out.start()
    out.wait()


def finish_kernel(q_ends, q_mid, vertical, ends_in, mid_in, out, ends, mid, staged, sems, osems):
    rows = ends.shape[1] // 2
    levels = rows // 2
    blocks = staged.shape[0]
    arriving = [
        pltpu.make_async_copy(mid_in, mid, sems.at[0]),
        pltpu.make_async_copy(ends_in, ends, sems.at[1]),
    ]
    for copy in arriving:
        copy.start()

    def leaving(b):
        at = slice(b * BLK, (b + 1) * BLK)
        return pltpu.make_async_copy(staged.at[b], out.at[:, at], osems.at[b])

    def one(b, p):
        ref, i = block_place(b, blocks, ends, mid)
        share, _ = block_place(b, blocks, q_ends, q_mid)

        def begin():
            qh, ql = halves(share[i])
            high = jnp.concatenate([ref[i, p * levels : (p + 1) * levels], qh], axis=0)
            low = jnp.concatenate([ref[i, rows + p * levels : rows + (p + 1) * levels], ql], axis=0)
            return mm(vertical[p], high), mm(vertical[p, :levels], low)

        def finish(value):
            staged[b, p * levels : (p + 1) * levels] = value

        return begin, finish

    middle = list(range(ASTEPS, blocks - ASTEPS))
    outer = list(range(ASTEPS)) + list(range(blocks - ASTEPS, blocks))
    for copy, group in zip(arriving, (middle, outer)):
        copy.wait()
        for start in range(0, len(group), 4):
            some = group[start : start + 4]
            in_turn([one(b, p) for b in some for p in range(2)])
            for b in some:
                leaving(b).start()
    for b in range(blocks):
        leaving(b).wait()


def sea_build(nbr, coef, b, w):
    at = pl.ds(pl.multiple_of(b * BLK, BLK), BLK)

    def store(first, size, lanes, high, low):
        w[0, first : first + size, lanes] = high
        w[1, first : first + size, lanes] = low

    return band_pieces(store, nbr[:, at] - b * BLK, coef[:, at], HO)


def sea_inner_kernel(ocean, nbr, coef, laid_out, x2, wa, wb, ma, mb, laid, sems):
    blocks = ocean.shape[1] // BLK
    around = 1 + 2 * HO // BLK
    first = -(-HO // BLK)
    count = blocks - 2 * first
    for i in range(count + around - 1):
        start = (first + i) * BLK - HO
        x2[i] = stacked(ocean[:, start : start + BLK])

    def leaving(i):
        return pltpu.make_async_copy(laid.at[i], laid_out.at[i], sems.at[i])

    def move(i, w, moved):
        yield from product_pieces([x2[i + d] for d in range(around)], w, moved)

    interleave(sea_build(nbr, coef, first, wa))

    def one(k, _):
        i = 2 * k
        interleave(sea_build(nbr, coef, first + i + 1, wb), move(i, wa, ma))
        interleave(sea_build(nbr, coef, jnp.minimum(i + 2, count - 1) + first, wa), move(i + 1, wb, mb))
        laid[i] = stacked(ma[...])
        laid[i + 1] = stacked(mb[...])
        leaving(i).start()
        leaving(i + 1).start()
        return 0

    lax.fori_loop(0, count // 2, one, 0)

    def done(i, _):
        leaving(i).wait()
        return 0

    lax.fori_loop(0, count, done, 0)


def sea_outer_kernel(
    before, after, nbr, coef, vertical, mix, flux, ocean, laid_in, out, ends, x2, wa, wb, ma, mb, laid, staged, sems, osems
):
    fields = flux.shape[0]
    rows, columns = ocean.shape
    levels = rows // fields
    blocks = columns // BLK
    around = 1 + 2 * HO // BLK
    first = -(-HO // BLK)
    count = blocks - 2 * first
    width = ends.shape[2]
    arriving = [
        pltpu.make_async_copy(ocean.at[:, :width], ends.at[0], sems.at[0]),
        pltpu.make_async_copy(ocean.at[:, columns - width :], ends.at[1], sems.at[1]),
        pltpu.make_async_copy(laid_in, laid.at[first : first + count], sems.at[2]),
    ]
    for copy in arriving:
        copy.start()
    eye = iota((levels, levels), 0) == iota((levels, levels), 1)
    top = jnp.broadcast_to((mix[...] + jnp.where(eye, 1.0, 0.0))[:, 0:1], (levels, BLK))
    outer = list(range(first)) + list(range(blocks - first, blocks))
    bands, sums = (wa, wb), (ma, mb)
    interleave(sea_build(nbr, coef, outer[0], wa))
    arriving[0].wait()
    arriving[1].wait()
    spans = ((before, -HO, HO), (ends.at[0], 0, width), (ends.at[1], columns - width, width), (after, columns, HO))
    held = list(range(first + around - 1)) + list(range(blocks - first, blocks + around - 1))
    for i, e in enumerate(held):
        start = e * BLK - HO
        pieces = []
        for ref, begin, size in spans:
            lo, hi = max(start, begin), min(start + BLK, begin + size)
            if lo < hi:
                pieces.append(ref[:, lo - begin : hi - begin])
        x2[i] = stacked(pieces[0] if len(pieces) == 1 else jnp.concatenate(pieces, axis=1))

    def move(b, w, moved):
        yield from product_pieces([x2[held.index(b + d)] for d in range(around)], w, moved)

    for k, b in enumerate(outer):
        works = [move(b, bands[k % 2], sums[k % 2])]
        if k + 1 < len(outer):
            works.insert(0, sea_build(nbr, coef, outer[k + 1], bands[(k + 1) % 2]))
        interleave(*works)
        laid[b] = stacked(sums[k % 2][...])
    arriving[2].wait()
    pair = 2 * levels

    def leaving(b):
        at = pl.ds(pl.multiple_of(b * BLK, BLK), BLK)
        return pltpu.make_async_copy(staged.at[b], out.at[:, at], osems.at[b])

    def mixed(b, p):
        at = pl.ds(pl.multiple_of(b * BLK, BLK), BLK)

        def begin():
            high = laid[b, p * pair : (p + 1) * pair]
            low = laid[b, rows + p * pair : rows + (p + 1) * pair]
            return mm(vertical[...], high), mm(vertical[:pair], low)

        def finish(value):
            for k in range(2):
                f = 2 * p + k
                staged[b, f * levels : (f + 1) * levels] = (
                    value[k * levels : (k + 1) * levels] + top * flux[f : f + 1, at]
                )

        return begin, finish

    def four(i, _):
        in_turn([mixed(4 * i + k, p) for k in range(4) for p in range(fields // 2)])
        for k in range(4):
            leaving(4 * i + k).start()
        return 0

    lax.fori_loop(0, blocks // 4, four, 0)

    def done(b, _):
        leaving(b).wait()
        return 0

    lax.fori_loop(0, blocks, done, 0)


def after_all(value, *others):
    return lax.optimization_barrier((value, *others))[0]


def per_device(
    atm_state,
    atm_surface,
    bulk_coef,
    atm_nbr,
    atm_nbr_coef,
    atm_mix,
    ocean_state,
    ocean_nbr,
    ocean_nbr_coef,
    ocean_mix,
    send_cols,
    remap_slot,
    remap_weight,
):
    fields, la, columns = atm_state.shape
    lo, cells = ocean_state.shape[1:]
    blocks = columns // BLK
    rows = fields * la
    states = fields * ASTEPS
    picked = send_cols[0]
    peers, slots = picked.shape
    lanes = min(BLK, slots)
    parts = slots // lanes
    atm = atm_state.reshape(rows, columns)
    ocean = ocean_state.reshape(fields * lo, cells)
    depth = lax.axis_size(AXES)
    up = [(i, (i + 1) % depth) for i in range(depth)]
    down = [(j, i) for i, j in up]
    window = BLK + 2 * HA
    vmem = pl.BlockSpec(memory_space=pltpu.VMEM)
    anywhere = pl.BlockSpec(memory_space=pl.ANY)

    depth_k = rows + states
    half = fields // 2
    p_of = np.arange(half)[:, None, None]
    r_of = np.arange(2 * la)[None, :, None]
    c_of = np.arange(2 * la + states)[None, None, :]
    code = np.where(
        c_of < 2 * la,
        (c_of // la == r_of // la) * 1,
        ((c_of - 2 * la) % fields == 2 * p_of + r_of // la) * (2 + (c_of - 2 * la) // fields),
    )
    code = np.broadcast_to(code, (half, 2 * la, 2 * la + states)).astype(np.int32)
    spread = ((c_of[0] % la == np.arange(la)[:, None]) & (c_of[0] < 2 * la)).astype(np.float32)
    sea_spread = (np.arange(2 * lo)[None, :] % lo == np.arange(lo)[:, None]).astype(np.float32)

    wide_rows = rows + 24
    y, yo, gains, lift, vertical, sea_vertical, wide_first, wide_last, sea_first, sea_last = call(
        prepare_kernel(fields),
        (
            shape((states, columns)),
            shape((1, columns)),
            shape((states, 128)),
            shape((ASTEPS - 1, la, 128)),
            shape((half, 4 * la, 2 * la + states), BF),
            shape((4 * lo, 2 * lo), BF),
            shape((wide_rows, WIDE)),
            shape((wide_rows, WIDE)),
            shape((fields * lo, HO)),
            shape((fields * lo, HO)),
        ),
        in_specs=[vmem] * 10 + [anywhere],
        out_specs=(vmem,) * 6 + (anywhere,) * 4,
        scratch=[
            pltpu.VMEM((lo, cells), F32),
            pltpu.VMEM((2, 24, WIDE), F32),
            pltpu.VMEM((2, fields * lo, HO), F32),
            pltpu.SemaphoreType.DMA((9,)),
        ],
    )(
        atm_mix,
        ocean_mix,
        atm,
        atm_nbr,
        atm_nbr_coef,
        bulk_coef,
        atm_surface,
        jnp.asarray(spread),
        jnp.asarray(code),
        jnp.asarray(sea_spread),
        ocean,
    )
    wide_before = lax.ppermute(wide_last, AXES, up)
    wide_after = lax.ppermute(wide_first, AXES, down)

    ends = 2 * ASTEPS
    q_mid, kept, mid, band = call(
        interior_kernel,
        (
            shape((blocks - ends, states, BLK)),
            shape((4 * (ASTEPS - 1), 2 * depth_k, BLK), BF),
            shape((blocks - ends, 2 * rows, BLK), BF),
            shape((ends, 2, window, BLK), BF),
        ),
        in_specs=[vmem] * 7,
        out_specs=(vmem, anywhere, anywhere, anywhere),
        scratch=[
            pltpu.VMEM((blocks, 2, window, BLK), BF),
            pltpu.VMEM((blocks, 2 * depth_k, BLK), BF),
            pltpu.VMEM((blocks, 2 * depth_k, BLK), BF),
            pltpu.VMEM((depth_k, BLK), F32),
            pltpu.VMEM((depth_k, BLK), F32),
            pltpu.VMEM((4 * (ASTEPS - 1), 2 * depth_k, BLK), BF),
            pltpu.VMEM((blocks - ends, 2 * rows, BLK), BF),
            pltpu.SemaphoreType.DMA((ends + ASTEPS,)),
        ],
    )(atm, y, atm_nbr, atm_nbr_coef, bulk_coef, atm_surface, gains)

    sea_blocks = cells // BLK
    outer = -(-HO // BLK)
    around = 1 + 2 * HO // BLK
    sea_window = BLK + 2 * HO
    sea_rows = fields * lo
    inner = sea_blocks - 2 * outer
    sea_inner = call(
        sea_inner_kernel,
        shape((inner, 2 * sea_rows, BLK), BF),
        in_specs=[vmem] * 3,
        out_specs=anywhere,
        scratch=[
            pltpu.VMEM((inner + around - 1, 2 * sea_rows, BLK), BF),
            pltpu.VMEM((2, sea_window, BLK), BF),
            pltpu.VMEM((2, sea_window, BLK), BF),
            pltpu.VMEM((sea_rows, BLK), F32),
            pltpu.VMEM((sea_rows, BLK), F32),
            pltpu.VMEM((inner, 2 * sea_rows, BLK), BF),
            pltpu.SemaphoreType.DMA((inner,)),
        ],
    )(ocean, after_all(ocean_nbr, q_mid), ocean_nbr_coef)

    sea_first, sea_last, wide_before, wide_after = lax.optimization_barrier(
        (sea_first, sea_last, wide_before, wide_after, sea_inner)
    )[:4]
    sea_before = lax.ppermute(sea_last, AXES, up)
    sea_after = lax.ppermute(sea_first, AXES, down)

    q_ends, tips = call(
        edge_kernel,
        (shape((ends, states, BLK)), shape((ends, 2 * rows, BLK), BF)),
        in_specs=[vmem] * 5 + [anywhere] * 5,
        out_specs=(vmem, anywhere),
        scratch=[
            pltpu.VMEM((2 * (2 * ASTEPS - 1), 2, window, BLK), BF),
            pltpu.VMEM((2, wide_rows, WIDE), F32),
            pltpu.VMEM((2, rows, 2 * BLK), F32),
            pltpu.VMEM((4 * (ASTEPS - 1), 2 * depth_k, BLK), BF),
            pltpu.VMEM((12, 2 * depth_k, BLK), BF),
            pltpu.VMEM((12, 2 * depth_k, BLK), BF),
            pltpu.VMEM((depth_k, BLK), F32),
            pltpu.VMEM((depth_k, BLK), F32),
            pltpu.VMEM((ends, 2 * rows, BLK), BF),
            pltpu.SemaphoreType.DMA((6 + 2 * ASTEPS,)),
        ],
    )(y, bulk_coef, atm_surface, gains, lift, wide_before, wide_after, atm, kept, band)

    outgoing = call(
        send_kernel,
        shape((peers, parts * fields, lanes)),
        in_specs=[vmem] * 3,
        scratch=[pltpu.VMEM((blocks * fields, BLK), F32)],
    )(q_ends, q_mid, picked)
    received = lax.all_to_all(outgoing, AXES, split_axis=0, concat_axis=0, tiled=True)

    atm_final = call(
        finish_kernel,
        shape((rows, columns)),
        in_specs=[vmem] * 3 + [anywhere] * 2,
        out_specs=anywhere,
        scratch=[
            pltpu.VMEM((ends, 2 * rows, BLK), BF),
            pltpu.VMEM((blocks - ends, 2 * rows, BLK), BF),
            pltpu.VMEM((blocks, rows, BLK), F32),
            pltpu.SemaphoreType.DMA((2,)),
            pltpu.SemaphoreType.DMA((blocks,)),
        ],
    )(after_all(q_ends, outgoing), q_mid, vertical, tips, mid)

    flux, back = call(
        exchange_kernel,
        (shape((fields, cells)), shape((peers, 2 * parts, lanes))),
        in_specs=[vmem] * 7 + [anywhere] * 2,
        scratch=[
            pltpu.VMEM((peers * parts * fields, 2 * lanes), BF),
            pltpu.VMEM((cells // 128 + 2 * HO // 128, 8, 128), F32),
            pltpu.VMEM((cells // BLK, lanes, remap_slot.shape[0] * BLK), BF),
            pltpu.VMEM((1, cells), F32),
            pltpu.VMEM((4 * peers * parts, lanes), F32),
            pltpu.VMEM((2, lo, HO), F32),
            pltpu.SemaphoreType.DMA((2,)),
        ],
    )(
        after_all(received, atm_final),
        remap_slot,
        remap_weight,
        yo,
        ocean_nbr,
        ocean_nbr_coef,
        ocean_mix,
        sea_before,
        sea_after,
    )
    returned = lax.all_to_all(back, AXES, split_axis=0, concat_axis=0, tiled=True)

    ocean_final = call(
        sea_outer_kernel,
        shape((sea_rows, cells)),
        in_specs=[vmem] * 7 + [anywhere] * 2,
        out_specs=anywhere,
        scratch=[
            pltpu.VMEM((2, sea_rows, (outer + around - 1) * BLK - HO), F32),
            pltpu.VMEM((2 * (outer + around - 1), 2 * sea_rows, BLK), BF),
            pltpu.VMEM((2, sea_window, BLK), BF),
            pltpu.VMEM((2, sea_window, BLK), BF),
            pltpu.VMEM((sea_rows, BLK), F32),
            pltpu.VMEM((sea_rows, BLK), F32),
            pltpu.VMEM((sea_blocks, 2 * sea_rows, BLK), BF),
            pltpu.VMEM((sea_blocks, sea_rows, BLK), F32),
            pltpu.SemaphoreType.DMA((3,)),
            pltpu.SemaphoreType.DMA((sea_blocks,)),
        ],
    )(
        after_all(sea_before, back),
        sea_after,
        ocean_nbr,
        ocean_nbr_coef,
        sea_vertical,
        ocean_mix,
        flux,
        ocean,
        sea_inner,
    )

    surface_temp = call(
        settle_kernel,
        shape((columns // 128, 128)),
        in_specs=[vmem] * 3,
        scratch=[pltpu.VMEM((4 * blocks, BLK), F32)],
    )(after_all(returned, ocean_final), picked, atm_surface)

    return (
        atm_final.reshape(fields, la, columns),
        ocean_final.reshape(fields, lo, cells),
        surface_temp.reshape(columns),
    )


def solution(mesh):
    placed = (
        P(None, None, AXES),
        P(None, AXES),
        P(None, AXES),
        P(None, AXES),
        P(None, AXES),
        P(),
        P(None, None, AXES),
        P(None, AXES),
        P(None, AXES),
        P(),
        P(AXES, None, None),
        P(None, AXES),
        P(None, AXES),
    )
    return jax.shard_map(
        per_device,
        mesh=mesh,
        in_specs=placed,
        out_specs=(P(None, None, AXES), P(None, None, AXES), P(AXES)),
        check_vma=False,
    )
```

```python
import itertools

import numpy as np

import jax
import jax.numpy as jnp
from jax import lax
from jax.experimental import pallas as pl
from jax.experimental.pallas import tpu as pltpu
from jax.sharding import PartitionSpec as P

ASTEPS = 4
HA = 256
HO = 384
BLK = 256
WIDE = ASTEPS * HA
BF = jnp.bfloat16
F32 = jnp.float32
VMEM_BYTES = 56 * 1024 * 1024
AXES = ("sec", "blk")


def call(body, outs, *, in_specs=None, out_specs=None, scratch=(), flops=10**6, moved=10**4, aliases=None):
    vmem = pl.BlockSpec(memory_space=pltpu.VMEM)
    return pl.pallas_call(
        body,
        out_shape=outs,
        in_specs=in_specs,
        out_specs=jax.tree.map(lambda _: vmem, outs) if out_specs is None else out_specs,
        scratch_shapes=list(scratch),
        input_output_aliases=aliases or {},
        compiler_params=pltpu.CompilerParams(vmem_limit_bytes=VMEM_BYTES),
        cost_estimate=pl.CostEstimate(flops=flops, bytes_accessed=moved, transcendentals=0),
    )


def shape(dims, dtype=F32):
    return jax.ShapeDtypeStruct(dims, dtype)


def halves(x):
    high = x.astype(BF)
    return high, (x - high.astype(F32)).astype(BF)


def stacked(x):
    return jnp.concatenate(halves(x), axis=0)


def mm(a, b):
    return jnp.dot(a, b, preferred_element_type=F32)


def mm_t(a, b):
    return lax.dot_general(a, b, (((1,), (1,)), ((), ())), preferred_element_type=F32)


def products(x2, w2):
    return mm(x2, w2[0]), mm(x2[: x2.shape[0] // 2], w2[1])


def summed(parts):
    wide, rest = parts
    rows = rest.shape[0]
    return wide[:rows] + wide[rows:] + rest


def in_turn(works):
    waiting = None
    for begin, finish in works:
        parts = begin()
        if waiting is not None:
            waiting[1](summed(waiting[0]))
        waiting = (parts, finish)
    waiting[1](summed(waiting[0]))


def product_pieces(x2s, w2, result):
    rows = x2s[0].shape[0] // 2
    for t, x2 in enumerate(x2s):
        at = slice(t * BLK, (t + 1) * BLK)
        wide = mm(x2, w2.at[0][at])
        part = wide[:rows] + wide[rows:]
        result[...] = part if t == 0 else result[...] + part
        yield
        result[...] += mm(x2[:rows], w2.at[1][at])
        yield


def interleave(*works):
    works = list(works)
    while works:
        works = [w for w in works if next(w, w) is not w]


def iota(dims, axis):
    return lax.broadcasted_iota(jnp.int32, dims, axis)


def build_band(*args):
    for _ in band_pieces(*args):
        pass


def band_pieces(store, nbr, coef, halo):
    rows = BLK + 2 * halo
    count = nbr.shape[0]
    ids = [nbr[k : k + 1] for k in range(count)]
    cs = [coef[k : k + 1] for k in range(count)]
    rest = 1.0 - sum(cs[1:], cs[0])
    for k in range(count - 1, 0, -1):
        alive = jnp.ones_like(ids[k]) > 0
        for j in range(k):
            same = jnp.logical_and(ids[k] == ids[j], alive)
            cs[j] = cs[j] + jnp.where(same, cs[k], 0.0)
            alive = jnp.logical_and(alive, jnp.logical_not(same))
        ids[k] = jnp.where(alive, ids[k], -1)
    lanes = 128
    step = 16
    base = iota((step, lanes), 0).astype(F32)
    parts = [halves(c) for c in cs + [rest]]

    def wide(x, at):
        return jnp.broadcast_to(x[:, at].astype(F32), (step, lanes)).astype(BF)

    for half in range(BLK // lanes):
        at = slice(half * lanes, (half + 1) * lanes)
        highs = [wide(p[0], at) for p in parts]
        lows = [wide(p[1], at) for p in parts]
        own = (iota((step, lanes), 1) - iota((step, lanes), 0)).astype(F32).astype(BF)
        zero = jnp.zeros((step, lanes), BF)
        for tile in range(0, rows, BLK):
            near = [wide((i - tile).astype(F32), at) for i in ids]
            for first in range(tile, tile + BLK, step):
                high, low = zero, zero
                if half * lanes - step < first < half * lanes + lanes + 2 * halo:
                    offset = first - halo - half * lanes
                    if 0 <= offset < lanes:
                        same = own == jnp.full((step, lanes), offset, BF)
                        high = jnp.where(same, highs[-1], zero)
                        low = jnp.where(same, lows[-1], zero)
                    here = (base + float(first - tile)).astype(BF)
                    for k in range(count):
                        same = here == near[k]
                        high = jnp.where(same, highs[k], high)
                        low = jnp.where(same, lows[k], low)
                store(first, step, at, high, low)
            yield


def one_hot(ids, rows):
    lanes = ids.shape[1]
    wide = jnp.broadcast_to(ids.astype(F32), (rows, lanes)).astype(BF)
    here = iota((rows, lanes), 0).astype(F32).astype(BF)
    return jnp.where(here == wide, jnp.ones((rows, lanes), BF), jnp.zeros((rows, lanes), BF))


def fold_rows(x, height):
    total = x[:height]
    for first in range(height, x.shape[0], height):
        total = total + x[first : first + height]
    return total


def pack_kernel(nbr, coef, bulk, surf, atm, sea, wide_first, wide_last, sea_first, sea_last, *refs):
    held, lists, sems = refs[:4], refs[4], refs[5]
    rows, columns = atm.shape
    cells = sea.shape[1]
    sources = (
        atm.at[:, :WIDE],
        atm.at[:, columns - WIDE :],
        sea.at[:, :HO],
        sea.at[:, cells - HO :],
    )
    targets = (wide_first.at[:rows], wide_last.at[:rows], sea_first, sea_last)
    arriving = [pltpu.make_async_copy(x, held[i], sems.at[i]) for i, x in enumerate(sources)]
    leaving = [pltpu.make_async_copy(held[i], x, sems.at[4 + i]) for i, x in enumerate(targets)]
    for copy in arriving:
        copy.start()
    need = WIDE - BLK
    for i, first in enumerate((0, columns - need)):
        at = slice(first, first + need)
        lists[i, 0:6, :need] = nbr[:, at].astype(F32)
        lists[i, 6:12, :need] = coef[:, at]
        lists[i, 12:16, :need] = bulk[:, at]
        lists[i, 12:16, need:] = jnp.zeros((4, BLK), F32)
        for j in range(ASTEPS - 1):
            lists[i, 4 * j : 4 * j + 4, need:] = surf[:, first + j * BLK : first + (j + 1) * BLK]
    for i, target in enumerate((wide_first, wide_last)):
        copy = pltpu.make_async_copy(lists.at[i], target.at[rows:], sems.at[8 + i])
        copy.start()
        leaving.append(copy)
    for here, there in zip(arriving, leaving[:4]):
        here.wait()
        there.start()
    for copy in leaving:
        copy.wait()


def prepare_kernel(fields):
    def body(
        mix, omix, atm, spread, code, sea_spread, sea, y, yo, gains, lift, vertical, sea_vertical, top, sem
    ):
        la = mix.shape[0]
        columns = atm.shape[1]
        copy = pltpu.make_async_copy(sea.at[: omix.shape[0], :], top, sem)
        copy.start()
        eye = iota((la, la), 0) == iota((la, la), 1)
        step = mix[...] + jnp.where(eye, 1.0, 0.0)

        def dot(a, b):
            return jnp.dot(a, b, precision=lax.Precision.HIGHEST, preferred_element_type=F32)

        def col(r, same):
            return jnp.sum(jnp.where(same, r, 0.0), axis=1, keepdims=True)

        def row(c, same):
            return jnp.sum(jnp.where(same, c, 0.0), axis=0, keepdims=True)

        twice = dot(step, step)
        fourth = dot(twice, twice)
        rows_up = [step[la - 1 : la, :]]
        cols_up = [step[:, la - 1 : la]]
        for _ in range(ASTEPS - 2):
            rows_up.append(jnp.sum(step * col(rows_up[-1], eye), axis=0, keepdims=True))
        for _ in range(ASTEPS - 1):
            cols_up.append(jnp.sum(step * row(cols_up[-1], eye), axis=1, keepdims=True))
        slot = iota((fields * ASTEPS, 128), 0) // fields
        lane = iota((fields * ASTEPS, 128), 1)
        value = jnp.zeros((fields * ASTEPS, 128), F32)
        for s in range(1, ASTEPS + 1):
            column = jnp.where(slot == s - 1, 1.0, 0.0)
            for j in range(1, ASTEPS):
                column = jnp.where(slot == s - 1 + j, rows_up[j - 1][:, la - 1 : la], column)
            value = jnp.where(lane == s - 1, column, value)
        gains[...] = value

        spreaded = dot(jnp.concatenate([fourth] * 2, axis=0), spread[...])
        for p in range(fields // 2):
            filled = jnp.where(code[p] == 1, spreaded, 0.0)
            for m in range(ASTEPS):
                tall = jnp.concatenate([cols_up[ASTEPS - 1 - m]] * 2, axis=0)
                filled = jnp.where(code[p] == 2 + m, tall, filled)
            vertical[p] = stacked(filled)
        lo = omix.shape[0]
        sea_eye = iota((lo, lo), 0) == iota((lo, lo), 1)
        sea_step = omix[...] + jnp.where(sea_eye, 1.0, 0.0)
        spreaded = dot(jnp.concatenate([sea_step] * 2, axis=0), sea_spread[...])
        blocks = (iota((2 * lo, 2 * lo), 0) >= lo) == (iota((2 * lo, 2 * lo), 1) >= lo)
        sea_vertical[...] = stacked(jnp.where(blocks, spreaded, 0.0))

        weights = [jnp.broadcast_to(col(r, eye), (la, 128)) for r in rows_up]
        for k, weight in enumerate(weights):
            lift[k] = weight
        sea_weight = jnp.broadcast_to(col(sea_step[0:1, :], sea_eye), (lo, 128))
        copy.wait()
        for start in range(0, columns, 128):
            at = slice(start, start + 128)
            for f in range(fields):
                x = atm[f * la : (f + 1) * la, at]
                y[f : f + 1, at] = x[la - 1 : la]
                for k in range(1, ASTEPS):
                    y[k * fields + f : k * fields + f + 1, at] = jnp.sum(
                        x * weights[k - 1], axis=0, keepdims=True
                    )
            yo[:, at] = jnp.sum(top[:, at] * sea_weight, axis=0, keepdims=True)

    return body


def band_build(ids, coef, w, k):
    def store(first, step, lanes, high, low):
        w[k, 0, first : first + step, lanes] = high
        w[k, 1, first : first + step, lanes] = low

    return band_pieces(store, ids, coef, HA)


def advance(moved, s, gains, bulk, surf):
    fields = bulk.shape[0]
    states = moved.shape[0]
    slot = iota((states, BLK), 0) // fields
    flux = bulk * (surf - moved[(s - 1) * fields : s * fields])
    kept = jnp.where(slot == s - 1, 0.0, moved)
    return kept + gains[:, s - 1 : s] * jnp.concatenate([flux] * ASTEPS, axis=0)


def interior_kernel(
    atm, y, nbr, coef, bulk, surf, gains, q, kept_out, mid_out, band, w, sa, sb, ma, mb, kept, mid, sems
):
    rows, columns = atm.shape
    states = y.shape[0]
    height = rows + states
    blocks = columns // BLK
    sent = list(range(ASTEPS)) + list(range(blocks - ASTEPS, blocks))
    leaving = []

    def depart(copy):
        copy.start()
        leaving.append(copy)

    def build(b):
        at = slice(b * BLK, (b + 1) * BLK)
        yield from band_build(nbr[:, at] - b * BLK, coef[:, at], w, b)

    def split(b):
        at = slice(b * BLK, (b + 1) * BLK)
        sa[b] = stacked(jnp.concatenate([atm[:, at], y[:, at]], axis=0))
        yield

    def pieces(b, moved):
        yield from product_pieces([sa[b + d] for d in (-1, 0, 1)], w.at[b], moved)

    def finish(b, s, moved, target):
        at = pl.ds(pl.multiple_of(b * BLK, BLK), BLK)
        value = advance(moved[rows:], s, gains, bulk[:, at], surf[:, at])
        if s == ASTEPS:
            q[b - ASTEPS] = value
            mid[b - ASTEPS] = stacked(moved[:rows])
        else:
            high, low = halves(moved[:rows])
            zh, zl = halves(value)
            target[b] = jnp.concatenate([high, zh, low, zl], axis=0)

    interleave(itertools.chain(*[split(b) for b in range(4)]))
    interleave(build(1))
    interleave(build(2))
    for i in range(blocks // 2 - 1):
        b = 2 * i + 1
        nexts = [b + 2, b + 3] if b + 3 < blocks - 1 else [0, blocks - 1]
        works = [itertools.chain(pieces(b, ma), pieces(b + 1, mb)), itertools.chain(*[build(k) for k in nexts])]
        if b + 4 < blocks:
            works.append(itertools.chain(split(b + 3), split(b + 4)))
        interleave(*works)
        finish(b, 1, ma[...], sb)
        finish(b + 1, 1, mb[...], sb)
    for i, b in enumerate(sent):
        depart(pltpu.make_async_copy(w.at[b], band.at[i], sems.at[i]))

    for s in range(1, ASTEPS + 1):
        xs, xt = (sa, sb) if s % 2 else (sb, sa)

        def inner(b, s=s, xs=xs, xt=xt):
            def begin():
                x2 = jnp.concatenate([xs[b - 1], xs[b], xs[b + 1]], axis=1)
                return products(x2, (w[b, 0], w[b, 1]))

            return begin, lambda moved: finish(b, s, moved, xt)

        def pair(i, _, s=s, inner=inner):
            in_turn([inner(s + 2 * i), inner(s + 2 * i + 1)])
            return 0

        if s > 1:
            lax.fori_loop(0, blocks // 2 - s, pair, 0)
        if s < ASTEPS:
            at = slice((s - 1) * 4, s * 4)
            for i, b in enumerate((s, s + 1, blocks - 2 - s, blocks - 1 - s)):
                kept[(s - 1) * 4 + i] = xt[b]
            depart(pltpu.make_async_copy(kept.at[at], kept_out.at[at], sems.at[len(sent) + s]))
    depart(pltpu.make_async_copy(mid, mid_out, sems.at[len(sent)]))
    for copy in leaving:
        copy.wait()


def block_place(b, blocks, ends, middle):
    if b < ASTEPS:
        return ends, b
    if b < blocks - ASTEPS:
        return middle, b - ASTEPS
    return ends, b - blocks + 2 * ASTEPS


def send_kernel(q_ends, q_mid, cols, out, table):
    fields = q_mid.shape[1] // ASTEPS
    peers, slots = cols.shape
    blocks = q_ends.shape[0] + q_mid.shape[0]
    lanes = out.shape[2]
    parts = slots // lanes
    for b in range(blocks):
        ref, i = block_place(b, blocks, q_ends, q_mid)
        table[b * fields : (b + 1) * fields, :] = ref[i, (ASTEPS - 1) * fields :, :]
    rows = stacked(table[...])
    half = blocks * fields
    block_of_row = iota((half, slots), 0) // fields

    def one(p, _):
        ids = cols[pl.ds(p, 1), :]
        got = mm(rows, one_hot(ids & (BLK - 1), BLK))
        got = jnp.where(block_of_row == ids // BLK, got[:half] + got[half:], 0.0)
        got = fold_rows(got, 2 * fields)
        got = got[:fields] + got[fields:]
        out[p] = jnp.concatenate([got[:, i * lanes : (i + 1) * lanes] for i in range(parts)], axis=0)
        return 0

    lax.fori_loop(0, peers, one, 0, unroll=4)


def exchange_kernel(
    recv, slot, weight, yo, nbr, coef, omix, before_in, after_in, flux_out, back, rows, tiles, hots, seas, acc, held, sems
):
    peers, per_peer, lanes = recv.shape
    links, columns = slot.shape
    fields = flux_out.shape[0]
    parts = per_peer // fields
    highs = peers * parts
    table = highs * fields
    arriving = [
        pltpu.make_async_copy(ref.at[: held.shape[1]], held.at[i], sems.at[i])
        for i, ref in enumerate((before_in, after_in))
    ]
    for copy in arriving:
        copy.start()
    rows[...] = stacked(recv[...].reshape(table, lanes))
    levels = omix.shape[0]
    eye = iota((levels, levels), 0) == iota((levels, levels), 1)
    corner = omix[0:1, 0:1] + 1.0
    top = omix[0:1, :] + jnp.where(iota((1, levels), 1) == 0, 1.0, 0.0)
    top = jnp.sum(jnp.where(eye, top, 0.0), axis=1, keepdims=True)
    for copy in arriving:
        copy.wait()
    before, after = [jnp.sum(held[i] * top, axis=0, keepdims=True) for i in range(2)]
    acc[...] = jnp.zeros_like(acc)
    side = HO // 128
    own_tiles = columns // 128
    for t in range(own_tiles + 2 * side):
        if t < side:
            line = before[:, t * 128 : (t + 1) * 128]
        elif t < side + own_tiles:
            line = yo[:, (t - side) * 128 : (t - side + 1) * 128]
        else:
            line = after[:, (t - side - own_tiles) * 128 : (t - side - own_tiles + 1) * 128]
        tiles[t] = jnp.broadcast_to(line, (8, 128))
    high_of_row = iota((table, BLK), 0) // fields
    back_rows = iota((2 * highs, BLK), 0)
    inner = back_rows % (2 * parts)
    back_high = (back_rows // (2 * parts)) * parts + inner % parts
    pattern = iota((8, BLK), 0) % (2 * parts) // parts
    window = 1 + 2 * side
    neighbors = nbr.shape[0]

    def surface(j, half):
        t0 = j * (BLK // 128) + half
        at = pl.ds(pl.multiple_of(t0 * 128, 128), 128)
        pad = jnp.zeros((8 - neighbors, 128), jnp.int32)
        ids = jnp.concatenate([nbr[:, at] - t0 * 128, pad], axis=0)
        cs = jnp.concatenate([coef[:, at], pad.astype(F32)], axis=0)
        middle = tiles[t0 + side]
        got = jnp.zeros((8, 128), F32)
        for t in range(window):
            pick = jnp.take_along_axis(tiles[t0 + t], ids & 127, axis=1, mode="promise_in_bounds")
            got = jnp.where(ids // 128 == t, pick, got)
        return middle[0:1] + jnp.sum(cs * (got - middle), axis=0, keepdims=True)

    def base(j, _):
        at = pl.ds(pl.multiple_of(j * BLK, BLK), BLK)
        seas[:, at] = jnp.concatenate([surface(j, h) for h in range(BLK // 128)], axis=1)
        return 0

    lax.fori_loop(0, columns // BLK, base, 0, unroll=2)

    def arrive(j, _):
        at = pl.ds(pl.multiple_of(j * BLK, BLK), BLK)
        parts = []

        def begin(r):
            ids = slot[r : r + 1, at]
            hot = one_hot(ids & (lanes - 1), lanes)
            hots[j, :, r * BLK : (r + 1) * BLK] = hot
            return mm(rows[...], hot)

        def finish(r, got):
            ids = slot[r : r + 1, at]
            got = jnp.where(high_of_row == ids // lanes, got[:table] + got[table:], 0.0)
            parts.append(weight[r : r + 1, at] * fold_rows(got, 2 * fields))

        last = begin(0)
        for r in range(1, links):
            got = begin(r)
            finish(r - 1, last)
            last = got
        finish(links - 1, last)
        flux = sum(parts[1:], parts[0])
        flux = flux[:fields] + flux[fields:]
        flux_out[:, at] = flux
        seas[:, at] += corner * flux[0:1]
        return 0

    lax.fori_loop(0, columns // BLK, arrive, 0, unroll=2)

    def leave(j, _):
        at = pl.ds(pl.multiple_of(j * BLK, BLK), BLK)
        sea = seas[:, at]
        left = []
        for r in range(links):
            ids, scale = slot[r : r + 1, at], weight[r : r + 1, at]
            high, low = halves(jnp.where(pattern == 1, scale, scale * sea))
            mask = back_high == ids // lanes
            both = [
                jnp.where(mask, jnp.concatenate([x.astype(F32)] * (2 * highs // 8), axis=0), 0.0).astype(BF)
                for x in (high, low)
            ]
            left.append(jnp.concatenate(both, axis=0))
        acc[...] += mm_t(jnp.concatenate(left, axis=1), hots[j])
        return 0

    lax.fori_loop(0, columns // BLK, leave, 0, unroll=2)
    back[...] = (acc[: 2 * highs] + acc[2 * highs :]).reshape(back.shape)


def settle_kernel(back, cols, surf, out, acc):
    peers, per_peer, lanes = back.shape
    parts = per_peer // 2
    blocks = surf.shape[1] // BLK
    acc[...] = jnp.zeros_like(acc)
    block_of_row = iota((blocks, lanes), 0)

    group = 4

    def one(i, _):
        left, hots = [], []
        for k, h in itertools.product(range(group), range(parts)):
            d = group * i + k
            ids = cols[pl.ds(d, 1), h * lanes : (h + 1) * lanes]
            mask = block_of_row == ids // BLK
            value = jnp.where(mask, back[d, h : h + 1, :], 0.0)
            scale = jnp.where(mask, back[d, parts + h : parts + h + 1, :], 0.0)
            left.append(stacked(jnp.concatenate([value, scale], axis=0)))
            hots.append(one_hot(ids & (BLK - 1), BLK))
        acc[...] += mm_t(jnp.concatenate(left, axis=1), jnp.concatenate(hots, axis=1))
        return 0

    lax.fori_loop(0, peers // group, one, 0)
    sums = acc[: 2 * blocks] + acc[2 * blocks :]
    base = jnp.concatenate([surf[0:1, b * BLK : (b + 1) * BLK] for b in range(blocks)], axis=0)
    value = (base + sums[:blocks]) / (1.0 + sums[blocks:])
    for b in range(blocks):
        for i in range(BLK // 128):
            row = b * (BLK // 128) + i
            out[row : row + 1, :] = value[b : b + 1, i * 128 : (i + 1) * 128]


def edge_kernel(
    y, bulk, surf, gains, lift, before, after, atm, kept_in, band, q, ends_out,
    w, wide, sides, kept, sa, sb, ma, mb, ends, sems,
):
    rows = atm.shape[0]
    levels = lift.shape[1]
    fields = bulk.shape[0]
    states = y.shape[0]
    columns = y.shape[1]
    blocks = columns // BLK
    halo = ASTEPS - 1
    count = halo + ASTEPS
    total = blocks + 2 * ASTEPS
    arriving = [
        pltpu.make_async_copy(before, wide.at[0], sems.at[0]),
        pltpu.make_async_copy(after, wide.at[1], sems.at[1]),
        pltpu.make_async_copy(atm.at[:, : 2 * BLK], sides.at[0], sems.at[2]),
        pltpu.make_async_copy(atm.at[:, columns - 2 * BLK :], sides.at[1], sems.at[3]),
    ]
    bands = [pltpu.make_async_copy(band.at[i], w.at[halo + i], sems.at[4 + i]) for i in range(2 * ASTEPS)]
    keeps = pltpu.make_async_copy(kept_in, kept, sems.at[4 + 2 * ASTEPS])
    needed = [[0, 2 * ASTEPS - 1]] + [[i, 2 * ASTEPS - 1 - i] for i in range(1, ASTEPS)]
    for copy in arriving:
        copy.start()
    for group in needed:
        for i in group:
            bands[i].start()
    keeps.start()

    def place(e):
        if e < ASTEPS:
            return wide.at[0], e
        if e >= total - ASTEPS:
            return wide.at[1], e - total + ASTEPS
        return None, e - ASTEPS

    def coefs(e):
        ref, local = place(e)
        at = slice(local * BLK, (local + 1) * BLK)
        if ref is None:
            return bulk[:, at], surf[:, at]
        j = local - 1 if e < ASTEPS else local
        at = slice(j * BLK, (j + 1) * BLK)
        return ref[rows + 12 : rows + 16, at], ref[rows + 4 * j : rows + 4 * j + 4, WIDE - BLK :]

    def build(e):
        ref, local = place(e)
        origin = local * BLK + (columns - WIDE if e < ASTEPS else 0)
        j = local - 1 if e < ASTEPS else local
        at = slice(j * BLK, (j + 1) * BLK)
        ids = ref[rows : rows + 6, at].astype(jnp.int32) - origin
        k = e - 1 if e < ASTEPS else e - (total - 1) + 2 * count
        yield from band_build(ids, ref[rows + 6 : rows + 12, at], w, k)

    for copy in arriving:
        copy.wait()
    for i in range(ASTEPS):
        at = slice(i * BLK, (i + 1) * BLK)
        for side in range(2):
            x = wide[side, :rows, at]
            lifted = [x[(f + 1) * levels - 1 : (f + 1) * levels] for f in range(fields)]
            for k in range(ASTEPS - 1):
                weight = jnp.concatenate([lift[k]] * (BLK // 128), axis=1)
                for f in range(fields):
                    lifted.append(jnp.sum(x[f * levels : (f + 1) * levels] * weight, axis=0, keepdims=True))
            sa[i if side == 0 else 8 + i] = stacked(jnp.concatenate([x] + lifted, axis=0))
    for i in range(2):
        at = slice(i * BLK, (i + 1) * BLK)
        far = slice(columns - (2 - i) * BLK, columns - (1 - i) * BLK)
        sa[ASTEPS + i] = stacked(jnp.concatenate([sides[0, :, at], y[:, at]], axis=0))
        sa[6 + i] = stacked(jnp.concatenate([sides[1, :, at], y[:, far]], axis=0))

    buffers = (sa, sb)
    builds = [itertools.chain(build(1 + i), build(total - 2 - i)) for i in range(halo)]
    interleave(builds[0])
    for s in range(1, ASTEPS + 1):
        source, target = buffers[(s - 1) % 2], buffers[s % 2]
        last = s == ASTEPS

        def finish(side, i, moved, s=s, target=target, last=last):
            e = s + i if side == 0 else total - 1 - s - halo + i
            value = advance(moved[rows:], s, gains, *coefs(e))
            if last:
                q[4 * side + i] = value
                ends[4 * side + i] = stacked(moved[:rows])
            else:
                target[6 * side + i + 2 * side] = stacked(jnp.concatenate([moved[:rows], value], axis=0))

        def band_of(side, i, s=s):
            return s - 1 + i if side == 0 else count + ASTEPS - s + i

        def one(side, i, source=source, finish=finish, band_of=band_of):
            def begin():
                x2 = jnp.concatenate([source[6 * side + i + d] for d in range(3)], axis=1)
                k = band_of(side, i)
                return products(x2, (w[k, 0], w[k, 1]))

            return begin, lambda moved: finish(side, i, moved)

        if s == 1:
            for i in range(halo):
                pieces = [
                    product_pieces([source[6 * side + j + d] for d in range(3)], w.at[band_of(side, j)], m)
                    for side, j, m in ((0, i, ma), (1, halo - i, mb))
                ]
                interleave(itertools.chain(*pieces), *builds[i + 1 : i + 2])
                finish(0, i, ma[...])
                finish(1, halo - i, mb[...])
            for k in needed[0]:
                bands[k].wait()
            in_turn([one(0, halo), one(1, 0)])
            keeps.wait()
        else:
            for k in needed[s - 1]:
                bands[k].wait()
            in_turn([one(side, i) for i in range(ASTEPS) for side in range(2)])
        if not last:
            for i in range(2):
                target[ASTEPS + i] = kept[(s - 1) * 4 + i]
                target[6 + i] = kept[(s - 1) * 4 + 2 + i]
    out = pltpu.make_async_copy(ends, ends_out, sems.at[5 + 2 * ASTEPS])
    out.start()
    out.wait()


def mix_kernel(blocks):
    def body(q, vertical, x_in, *refs):
        out, x, staged, sem, osems = refs[-5:]
        rows = x.shape[1] // 2
        levels = rows // 2
        arriving = pltpu.make_async_copy(x_in, x, sem)
        arriving.start()
        arriving.wait()

        def leaving(i):
            at = slice(blocks[i] * BLK, (blocks[i] + 1) * BLK)
            return pltpu.make_async_copy(staged.at[i], out.at[:, at], osems.at[i])

        def one(i, p):
            def begin():
                qh, ql = halves(q[i])
                high = jnp.concatenate([x[i, p * levels : (p + 1) * levels], qh], axis=0)
                low = jnp.concatenate([x[i, rows + p * levels : rows + (p + 1) * levels], ql], axis=0)
                return mm(vertical[p], high), mm(vertical[p, :levels], low)

            def finish(value):
                staged[i, p * levels : (p + 1) * levels] = value

            return begin, finish

        for start in range(0, len(blocks), 4):
            in_turn([one(i, p) for i in range(start, start + 4) for p in range(2)])
            for i in range(start, start + 4):
                leaving(i).start()
        for i in range(len(blocks)):
            leaving(i).wait()

    return body


def sea_build(nbr, coef, b, w):
    at = pl.ds(pl.multiple_of(b * BLK, BLK), BLK)

    def store(first, size, lanes, high, low):
        w[0, first : first + size, lanes] = high
        w[1, first : first + size, lanes] = low

    return band_pieces(store, nbr[:, at] - b * BLK, coef[:, at], HO)


def sea_inner_kernel(ocean, nbr, coef, laid_out, x2, wa, wb, ma, mb, laid, sems):
    blocks = ocean.shape[1] // BLK
    around = 1 + 2 * HO // BLK
    first = -(-HO // BLK)
    count = blocks - 2 * first
    for i in range(count + around - 1):
        start = (first + i) * BLK - HO
        x2[i] = stacked(ocean[:, start : start + BLK])

    def leaving(i):
        return pltpu.make_async_copy(laid.at[i], laid_out.at[i], sems.at[i])

    def move(i, w, moved):
        yield from product_pieces([x2[i + d] for d in range(around)], w, moved)

    interleave(sea_build(nbr, coef, first, wa))

    def one(k, _):
        i = 2 * k
        interleave(sea_build(nbr, coef, first + i + 1, wb), move(i, wa, ma))
        interleave(sea_build(nbr, coef, jnp.minimum(i + 2, count - 1) + first, wa), move(i + 1, wb, mb))
        laid[i] = stacked(ma[...])
        laid[i + 1] = stacked(mb[...])
        leaving(i).start()
        leaving(i + 1).start()
        return 0

    lax.fori_loop(0, count // 2, one, 0)

    def done(i, _):
        leaving(i).wait()
        return 0

    lax.fori_loop(0, count, done, 0)


def sea_outer_kernel(nbr, coef, ocean, before_in, after_in, laid_out, ends, halos, x2, wa, wb, ma, mb, laid, sems):
    columns = ocean.shape[1]
    blocks = columns // BLK
    around = 1 + 2 * HO // BLK
    first = -(-HO // BLK)
    width = ends.shape[2]
    arriving = [
        pltpu.make_async_copy(ocean.at[:, :width], ends.at[0], sems.at[0]),
        pltpu.make_async_copy(ocean.at[:, columns - width :], ends.at[1], sems.at[1]),
        pltpu.make_async_copy(before_in, halos.at[0], sems.at[2]),
        pltpu.make_async_copy(after_in, halos.at[1], sems.at[3]),
    ]
    for copy in arriving:
        copy.start()
    outer = list(range(first)) + list(range(blocks - first, blocks))
    bands, sums = (wa, wb), (ma, mb)
    interleave(sea_build(nbr, coef, outer[0], wa))
    for copy in arriving:
        copy.wait()
    spans = (
        (halos.at[0], -HO, HO),
        (ends.at[0], 0, width),
        (ends.at[1], columns - width, width),
        (halos.at[1], columns, HO),
    )
    held = list(range(first + around - 1)) + list(range(blocks - first, blocks + around - 1))
    for i, e in enumerate(held):
        start = e * BLK - HO
        pieces = []
        for ref, begin, size in spans:
            lo, hi = max(start, begin), min(start + BLK, begin + size)
            if lo < hi:
                pieces.append(ref[:, lo - begin : hi - begin])
        x2[i] = stacked(pieces[0] if len(pieces) == 1 else jnp.concatenate(pieces, axis=1))

    def move(b, w, moved):
        yield from product_pieces([x2[held.index(b + d)] for d in range(around)], w, moved)

    for k, b in enumerate(outer):
        works = [move(b, bands[k % 2], sums[k % 2])]
        if k + 1 < len(outer):
            works.insert(0, sea_build(nbr, coef, outer[k + 1], bands[(k + 1) % 2]))
        interleave(*works)
        laid[k] = stacked(sums[k % 2][...])
    out = pltpu.make_async_copy(laid, laid_out, sems.at[4])
    out.start()
    out.wait()


def sea_mix_kernel(vertical, mix, flux, inner_in, outer_in, out, laid, staged, sems, osems):
    fields = flux.shape[0]
    rows = out.shape[0]
    levels = rows // fields
    blocks = staged.shape[0]
    side = outer_in.shape[0] // 2
    copies = [
        pltpu.make_async_copy(outer_in.at[:side], laid.at[:side], sems.at[0]),
        pltpu.make_async_copy(inner_in, laid.at[side : blocks - side], sems.at[1]),
        pltpu.make_async_copy(outer_in.at[side:], laid.at[blocks - side :], sems.at[2]),
    ]
    for copy in copies:
        copy.start()
    eye = iota((levels, levels), 0) == iota((levels, levels), 1)
    top = jnp.broadcast_to((mix[...] + jnp.where(eye, 1.0, 0.0))[:, 0:1], (levels, BLK))
    for copy in copies:
        copy.wait()
    pair = 2 * levels

    def leaving(b):
        at = pl.ds(pl.multiple_of(b * BLK, BLK), BLK)
        return pltpu.make_async_copy(staged.at[b], out.at[:, at], osems.at[b])

    def mixed(b, p):
        at = pl.ds(pl.multiple_of(b * BLK, BLK), BLK)

        def begin():
            high = laid[b, p * pair : (p + 1) * pair]
            low = laid[b, rows + p * pair : rows + (p + 1) * pair]
            return mm(vertical[...], high), mm(vertical[:pair], low)

        def finish(value):
            for k in range(2):
                f = 2 * p + k
                staged[b, f * levels : (f + 1) * levels] = (
                    value[k * levels : (k + 1) * levels] + top * flux[f : f + 1, at]
                )

        return begin, finish

    def four(i, _):
        in_turn([mixed(4 * i + k, p) for k in range(4) for p in range(fields // 2)])
        for k in range(4):
            leaving(4 * i + k).start()
        return 0

    lax.fori_loop(0, blocks // 4, four, 0)

    def done(b, _):
        leaving(b).wait()
        return 0

    lax.fori_loop(0, blocks, done, 0)


def after_all(value, *others):
    return lax.optimization_barrier((value, *others))[0]


def per_device(
    atm_state,
    atm_surface,
    bulk_coef,
    atm_nbr,
    atm_nbr_coef,
    atm_mix,
    ocean_state,
    ocean_nbr,
    ocean_nbr_coef,
    ocean_mix,
    send_cols,
    remap_slot,
    remap_weight,
):
    fields, la, columns = atm_state.shape
    lo, cells = ocean_state.shape[1:]
    blocks = columns // BLK
    rows = fields * la
    states = fields * ASTEPS
    picked = send_cols[0]
    peers, slots = picked.shape
    lanes = min(BLK, slots)
    parts = slots // lanes
    atm = atm_state.reshape(rows, columns)
    ocean = ocean_state.reshape(fields * lo, cells)
    depth = lax.axis_size(AXES)
    up = [(i, (i + 1) % depth) for i in range(depth)]
    down = [(j, i) for i, j in up]
    window = BLK + 2 * HA
    vmem = pl.BlockSpec(memory_space=pltpu.VMEM)
    anywhere = pl.BlockSpec(memory_space=pl.ANY)

    depth_k = rows + states
    half = fields // 2
    p_of = np.arange(half)[:, None, None]
    r_of = np.arange(2 * la)[None, :, None]
    c_of = np.arange(2 * la + states)[None, None, :]
    code = np.where(
        c_of < 2 * la,
        (c_of // la == r_of // la) * 1,
        ((c_of - 2 * la) % fields == 2 * p_of + r_of // la) * (2 + (c_of - 2 * la) // fields),
    )
    code = np.broadcast_to(code, (half, 2 * la, 2 * la + states)).astype(np.int32)
    spread = ((c_of[0] % la == np.arange(la)[:, None]) & (c_of[0] < 2 * la)).astype(np.float32)
    sea_spread = (np.arange(2 * lo)[None, :] % lo == np.arange(lo)[:, None]).astype(np.float32)

    wide_rows = rows + 16
    sea_rows = fields * lo
    halo_shapes = (shape((rows, WIDE)),) * 2 + (shape((sea_rows, HO)),) * 2
    wide_first, wide_last, sea_first, sea_last = call(
        pack_kernel,
        (shape((wide_rows, WIDE)),) * 2 + halo_shapes[2:],
        in_specs=[vmem] * 4 + [anywhere] * 2,
        out_specs=(anywhere,) * 4,
        scratch=[pltpu.VMEM(h.shape, F32) for h in halo_shapes]
        + [pltpu.VMEM((2, 16, WIDE), F32), pltpu.SemaphoreType.DMA((10,))],
    )(atm_nbr, atm_nbr_coef, bulk_coef, atm_surface, atm, ocean)
    wide_before = lax.ppermute(wide_last, AXES, up)
    wide_after = lax.ppermute(wide_first, AXES, down)

    y, yo, gains, lift, vertical, sea_vertical = call(
        prepare_kernel(fields),
        (
            shape((states, columns)),
            shape((1, columns)),
            shape((states, 128)),
            shape((ASTEPS - 1, la, 128)),
            shape((half, 4 * la, 2 * la + states), BF),
            shape((4 * lo, 2 * lo), BF),
        ),
        in_specs=[vmem] * 6 + [anywhere],
        scratch=[pltpu.VMEM((lo, cells), F32), pltpu.SemaphoreType.DMA(())],
    )(
        after_all(atm_mix, wide_first),
        ocean_mix,
        atm,
        jnp.asarray(spread),
        jnp.asarray(code),
        jnp.asarray(sea_spread),
        ocean,
    )

    ends = 2 * ASTEPS
    q_mid, kept, mid, band = call(
        interior_kernel,
        (
            shape((blocks - ends, states, BLK)),
            shape((4 * (ASTEPS - 1), 2 * depth_k, BLK), BF),
            shape((blocks - ends, 2 * rows, BLK), BF),
            shape((ends, 2, window, BLK), BF),
        ),
        in_specs=[vmem] * 7,
        out_specs=(vmem, anywhere, anywhere, anywhere),
        scratch=[
            pltpu.VMEM((blocks, 2, window, BLK), BF),
            pltpu.VMEM((blocks, 2 * depth_k, BLK), BF),
            pltpu.VMEM((blocks, 2 * depth_k, BLK), BF),
            pltpu.VMEM((depth_k, BLK), F32),
            pltpu.VMEM((depth_k, BLK), F32),
            pltpu.VMEM((4 * (ASTEPS - 1), 2 * depth_k, BLK), BF),
            pltpu.VMEM((blocks - ends, 2 * rows, BLK), BF),
            pltpu.SemaphoreType.DMA((ends + ASTEPS,)),
        ],
    )(atm, y, atm_nbr, atm_nbr_coef, bulk_coef, atm_surface, gains)

    sea_blocks = cells // BLK
    outer = -(-HO // BLK)
    around = 1 + 2 * HO // BLK
    sea_window = BLK + 2 * HO
    inner = sea_blocks - 2 * outer
    sea_inner = call(
        sea_inner_kernel,
        shape((inner, 2 * sea_rows, BLK), BF),
        in_specs=[vmem] * 3,
        out_specs=anywhere,
        scratch=[
            pltpu.VMEM((inner + around - 1, 2 * sea_rows, BLK), BF),
            pltpu.VMEM((2, sea_window, BLK), BF),
            pltpu.VMEM((2, sea_window, BLK), BF),
            pltpu.VMEM((sea_rows, BLK), F32),
            pltpu.VMEM((sea_rows, BLK), F32),
            pltpu.VMEM((inner, 2 * sea_rows, BLK), BF),
            pltpu.SemaphoreType.DMA((inner,)),
        ],
    )(ocean, after_all(ocean_nbr, q_mid), ocean_nbr_coef)

    middle = list(range(ASTEPS, blocks - ASTEPS))
    rest = list(range(ASTEPS)) + list(range(blocks - ASTEPS, blocks))

    def mixed(which, *args, aliases=None):
        return call(
            mix_kernel(which),
            shape((rows, columns)),
            in_specs=[vmem] * 2 + [anywhere] * (len(args) - 2),
            out_specs=anywhere,
            scratch=[
                pltpu.VMEM((len(which), 2 * rows, BLK), BF),
                pltpu.VMEM((len(which), rows, BLK), F32),
                pltpu.SemaphoreType.DMA(()),
                pltpu.SemaphoreType.DMA((len(which),)),
            ],
            aliases=aliases,
        )(*args)

    atm_half = mixed(middle, after_all(q_mid, sea_inner), vertical, mid)
    sea_first, sea_last = lax.optimization_barrier((sea_first, sea_last, q_mid))[:2]
    sea_before = lax.ppermute(sea_last, AXES, up)
    sea_after = lax.ppermute(sea_first, AXES, down)

    q_ends, tips = call(
        edge_kernel,
        (shape((ends, states, BLK)), shape((ends, 2 * rows, BLK), BF)),
        in_specs=[vmem] * 5 + [anywhere] * 5,
        out_specs=(vmem, anywhere),
        scratch=[
            pltpu.VMEM((2 * (2 * ASTEPS - 1), 2, window, BLK), BF),
            pltpu.VMEM((2, wide_rows, WIDE), F32),
            pltpu.VMEM((2, rows, 2 * BLK), F32),
            pltpu.VMEM((4 * (ASTEPS - 1), 2 * depth_k, BLK), BF),
            pltpu.VMEM((12, 2 * depth_k, BLK), BF),
            pltpu.VMEM((12, 2 * depth_k, BLK), BF),
            pltpu.VMEM((depth_k, BLK), F32),
            pltpu.VMEM((depth_k, BLK), F32),
            pltpu.VMEM((ends, 2 * rows, BLK), BF),
            pltpu.SemaphoreType.DMA((6 + 2 * ASTEPS,)),
        ],
    )(after_all(y, atm_half), bulk_coef, atm_surface, gains, lift, wide_before, wide_after, atm, kept, band)

    q_ends, sea_before, sea_after = lax.optimization_barrier((q_ends, sea_before, sea_after))
    outgoing = call(
        send_kernel,
        shape((peers, parts * fields, lanes)),
        in_specs=[vmem] * 3,
        scratch=[pltpu.VMEM((blocks * fields, BLK), F32)],
    )(q_ends, q_mid, picked)
    received = lax.all_to_all(outgoing, AXES, split_axis=0, concat_axis=0, tiled=True)

    atm_final = mixed(rest, after_all(q_ends, outgoing), vertical, tips, atm_half, aliases={3: 0})

    sea_outer = call(
        sea_outer_kernel,
        shape((2 * outer, 2 * sea_rows, BLK), BF),
        in_specs=[vmem] * 2 + [anywhere] * 3,
        out_specs=anywhere,
        scratch=[
            pltpu.VMEM((2, sea_rows, (outer + around - 1) * BLK - HO), F32),
            pltpu.VMEM((2, sea_rows, HO), F32),
            pltpu.VMEM((2 * (outer + around - 1), 2 * sea_rows, BLK), BF),
            pltpu.VMEM((2, sea_window, BLK), BF),
            pltpu.VMEM((2, sea_window, BLK), BF),
            pltpu.VMEM((sea_rows, BLK), F32),
            pltpu.VMEM((sea_rows, BLK), F32),
            pltpu.VMEM((2 * outer, 2 * sea_rows, BLK), BF),
            pltpu.SemaphoreType.DMA((5,)),
        ],
    )(after_all(ocean_nbr, atm_final), ocean_nbr_coef, ocean, sea_before, sea_after)

    flux, back = call(
        exchange_kernel,
        (shape((fields, cells)), shape((peers, 2 * parts, lanes))),
        in_specs=[vmem] * 7 + [anywhere] * 2,
        scratch=[
            pltpu.VMEM((2 * peers * parts * fields, lanes), BF),
            pltpu.VMEM((cells // 128 + 2 * HO // 128, 8, 128), F32),
            pltpu.VMEM((cells // BLK, lanes, remap_slot.shape[0] * BLK), BF),
            pltpu.VMEM((1, cells), F32),
            pltpu.VMEM((4 * peers * parts, lanes), F32),
            pltpu.VMEM((2, lo, HO), F32),
            pltpu.SemaphoreType.DMA((2,)),
        ],
    )(
        after_all(received, sea_outer),
        remap_slot,
        remap_weight,
        yo,
        ocean_nbr,
        ocean_nbr_coef,
        ocean_mix,
        sea_before,
        sea_after,
    )
    returned = lax.all_to_all(back, AXES, split_axis=0, concat_axis=0, tiled=True)

    ocean_final = call(
        sea_mix_kernel,
        shape((sea_rows, cells)),
        in_specs=[vmem] * 3 + [anywhere] * 2,
        out_specs=anywhere,
        scratch=[
            pltpu.VMEM((sea_blocks, 2 * sea_rows, BLK), BF),
            pltpu.VMEM((sea_blocks, sea_rows, BLK), F32),
            pltpu.SemaphoreType.DMA((3,)),
            pltpu.SemaphoreType.DMA((sea_blocks,)),
        ],
    )(sea_vertical, ocean_mix, after_all(flux, back), sea_inner, sea_outer)

    surface_temp = call(
        settle_kernel,
        shape((columns // 128, 128)),
        in_specs=[vmem] * 3,
        scratch=[pltpu.VMEM((4 * blocks, BLK), F32)],
    )(after_all(returned, ocean_final), picked, atm_surface)

    return (
        atm_final.reshape(fields, la, columns),
        ocean_final.reshape(fields, lo, cells),
        surface_temp.reshape(columns),
    )


def solution(mesh):
    placed = (
        P(None, None, AXES),
        P(None, AXES),
        P(None, AXES),
        P(None, AXES),
        P(None, AXES),
        P(),
        P(None, None, AXES),
        P(None, AXES),
        P(None, AXES),
        P(),
        P(AXES, None, None),
        P(None, AXES),
        P(None, AXES),
    )
    return jax.shard_map(
        per_device,
        mesh=mesh,
        in_specs=placed,
        out_specs=(P(None, None, AXES), P(None, None, AXES), P(AXES)),
        check_vma=False,
    )
```

```python
import itertools

import numpy as np

import jax
import jax.numpy as jnp
from jax import lax
from jax.experimental import pallas as pl
from jax.experimental.pallas import tpu as pltpu
from jax.sharding import PartitionSpec as P

ASTEPS = 4
HA = 256
HO = 384
BLK = 256
WIDE = ASTEPS * HA
BF = jnp.bfloat16
F32 = jnp.float32
VMEM_BYTES = 56 * 1024 * 1024
AXES = ("sec", "blk")


def call(body, outs, *, in_specs=None, out_specs=None, scratch=(), flops=10**6, moved=10**4, aliases=None):
    vmem = pl.BlockSpec(memory_space=pltpu.VMEM)
    return pl.pallas_call(
        body,
        out_shape=outs,
        in_specs=in_specs,
        out_specs=jax.tree.map(lambda _: vmem, outs) if out_specs is None else out_specs,
        scratch_shapes=list(scratch),
        input_output_aliases=aliases or {},
        compiler_params=pltpu.CompilerParams(vmem_limit_bytes=VMEM_BYTES),
        cost_estimate=pl.CostEstimate(flops=flops, bytes_accessed=moved, transcendentals=0),
    )


def shape(dims, dtype=F32):
    return jax.ShapeDtypeStruct(dims, dtype)


def halves(x):
    high = x.astype(BF)
    return high, (x - high.astype(F32)).astype(BF)


def stacked(x):
    return jnp.concatenate(halves(x), axis=0)


def mm(a, b):
    return jnp.dot(a, b, preferred_element_type=F32)


def mm_t(a, b):
    return lax.dot_general(a, b, (((1,), (1,)), ((), ())), preferred_element_type=F32)


def products(x2, w2):
    return mm(x2, w2[0]), mm(x2[: x2.shape[0] // 2], w2[1])


def summed(parts):
    wide, rest = parts
    rows = rest.shape[0]
    return wide[:rows] + wide[rows:] + rest


def in_turn(works):
    waiting = None
    for begin, finish in works:
        parts = begin()
        if waiting is not None:
            waiting[1](summed(waiting[0]))
        waiting = (parts, finish)
    waiting[1](summed(waiting[0]))


def product_pieces(x2s, w2, result):
    rows = x2s[0].shape[0] // 2
    for t, x2 in enumerate(x2s):
        at = slice(t * BLK, (t + 1) * BLK)
        wide = mm(x2, w2.at[0][at])
        part = wide[:rows] + wide[rows:]
        result[...] = part if t == 0 else result[...] + part
        yield
        result[...] += mm(x2[:rows], w2.at[1][at])
        yield


def interleave(*works):
    works = list(works)
    while works:
        works = [w for w in works if next(w, w) is not w]


def iota(dims, axis):
    return lax.broadcasted_iota(jnp.int32, dims, axis)


def build_band(*args):
    for _ in band_pieces(*args):
        pass


def band_pieces(store, nbr, coef, halo):
    rows = BLK + 2 * halo
    count = nbr.shape[0]
    ids = [nbr[k : k + 1] for k in range(count)]
    cs = [coef[k : k + 1] for k in range(count)]
    rest = 1.0 - sum(cs[1:], cs[0])
    for k in range(count - 1, 0, -1):
        alive = jnp.ones_like(ids[k]) > 0
        for j in range(k):
            same = jnp.logical_and(ids[k] == ids[j], alive)
            cs[j] = cs[j] + jnp.where(same, cs[k], 0.0)
            alive = jnp.logical_and(alive, jnp.logical_not(same))
        ids[k] = jnp.where(alive, ids[k], -1)
    lanes = 128
    step = 16
    base = iota((step, lanes), 0).astype(F32)
    parts = [halves(c) for c in cs + [rest]]

    def wide(x, at):
        return jnp.broadcast_to(x[:, at].astype(F32), (step, lanes)).astype(BF)

    for half in range(BLK // lanes):
        at = slice(half * lanes, (half + 1) * lanes)
        highs = [wide(p[0], at) for p in parts]
        lows = [wide(p[1], at) for p in parts]
        own = (iota((step, lanes), 1) - iota((step, lanes), 0)).astype(F32).astype(BF)
        zero = jnp.zeros((step, lanes), BF)
        for tile in range(0, rows, BLK):
            near = [wide((i - tile).astype(F32), at) for i in ids]
            for first in range(tile, tile + BLK, step):
                high, low = zero, zero
                if half * lanes - step < first < half * lanes + lanes + 2 * halo:
                    offset = first - halo - half * lanes
                    if 0 <= offset < lanes:
                        same = own == jnp.full((step, lanes), offset, BF)
                        high = jnp.where(same, highs[-1], zero)
                        low = jnp.where(same, lows[-1], zero)
                    here = (base + float(first - tile)).astype(BF)
                    for k in range(count):
                        same = here == near[k]
                        high = jnp.where(same, highs[k], high)
                        low = jnp.where(same, lows[k], low)
                store(first, step, at, high, low)
            yield


def one_hot(ids, rows):
    lanes = ids.shape[1]
    wide = jnp.broadcast_to(ids.astype(F32), (rows, lanes)).astype(BF)
    here = iota((rows, lanes), 0).astype(F32).astype(BF)
    return jnp.where(here == wide, jnp.ones((rows, lanes), BF), jnp.zeros((rows, lanes), BF))


def fold_rows(x, height):
    total = x[:height]
    for first in range(height, x.shape[0], height):
        total = total + x[first : first + height]
    return total


def pack_kernel(nbr, coef, bulk, surf, atm, sea, wide_first, wide_last, sea_first, sea_last, *refs):
    held, lists, sems = refs[:4], refs[4], refs[5]
    rows, columns = atm.shape
    cells = sea.shape[1]
    sources = (
        atm.at[:, :WIDE],
        atm.at[:, columns - WIDE :],
        sea.at[:, :HO],
        sea.at[:, cells - HO :],
    )
    targets = (wide_first.at[:rows], wide_last.at[:rows], sea_first, sea_last)
    arriving = [pltpu.make_async_copy(x, held[i], sems.at[i]) for i, x in enumerate(sources)]
    leaving = [pltpu.make_async_copy(held[i], x, sems.at[4 + i]) for i, x in enumerate(targets)]
    for copy in arriving:
        copy.start()
    need = WIDE - BLK
    for i, first in enumerate((0, columns - need)):
        at = slice(first, first + need)
        lists[i, 0:6, :need] = nbr[:, at].astype(F32)
        lists[i, 6:12, :need] = coef[:, at]
        lists[i, 12:16, :need] = bulk[:, at]
        lists[i, 12:16, need:] = jnp.zeros((4, BLK), F32)
        for j in range(ASTEPS - 1):
            lists[i, 4 * j : 4 * j + 4, need:] = surf[:, first + j * BLK : first + (j + 1) * BLK]
    for i, target in enumerate((wide_first, wide_last)):
        copy = pltpu.make_async_copy(lists.at[i], target.at[rows:], sems.at[8 + i])
        copy.start()
        leaving.append(copy)
    for here, there in zip(arriving, leaving[:4]):
        here.wait()
        there.start()
    for copy in leaving:
        copy.wait()


def prepare_kernel(fields):
    def body(
        mix, omix, atm, spread, code, sea_spread, sea, y, yo, gains, lift, vertical, sea_vertical, top, sem
    ):
        la = mix.shape[0]
        columns = atm.shape[1]
        copy = pltpu.make_async_copy(sea.at[: omix.shape[0], :], top, sem)
        copy.start()
        eye = iota((la, la), 0) == iota((la, la), 1)
        step = mix[...] + jnp.where(eye, 1.0, 0.0)

        def dot(a, b):
            return jnp.dot(a, b, precision=lax.Precision.HIGHEST, preferred_element_type=F32)

        def col(r, same):
            return jnp.sum(jnp.where(same, r, 0.0), axis=1, keepdims=True)

        def row(c, same):
            return jnp.sum(jnp.where(same, c, 0.0), axis=0, keepdims=True)

        twice = dot(step, step)
        fourth = dot(twice, twice)
        rows_up = [step[la - 1 : la, :]]
        cols_up = [step[:, la - 1 : la]]
        for _ in range(ASTEPS - 2):
            rows_up.append(jnp.sum(step * col(rows_up[-1], eye), axis=0, keepdims=True))
        for _ in range(ASTEPS - 1):
            cols_up.append(jnp.sum(step * row(cols_up[-1], eye), axis=1, keepdims=True))
        slot = iota((fields * ASTEPS, 128), 0) // fields
        lane = iota((fields * ASTEPS, 128), 1)
        value = jnp.zeros((fields * ASTEPS, 128), F32)
        for s in range(1, ASTEPS + 1):
            column = jnp.where(slot == s - 1, 1.0, 0.0)
            for j in range(1, ASTEPS):
                column = jnp.where(slot == s - 1 + j, rows_up[j - 1][:, la - 1 : la], column)
            value = jnp.where(lane == s - 1, column, value)
        gains[...] = value

        spreaded = dot(jnp.concatenate([fourth] * 2, axis=0), spread[...])
        for p in range(fields // 2):
            filled = jnp.where(code[p] == 1, spreaded, 0.0)
            for m in range(ASTEPS):
                tall = jnp.concatenate([cols_up[ASTEPS - 1 - m]] * 2, axis=0)
                filled = jnp.where(code[p] == 2 + m, tall, filled)
            vertical[p] = stacked(filled)
        lo = omix.shape[0]
        sea_eye = iota((lo, lo), 0) == iota((lo, lo), 1)
        sea_step = omix[...] + jnp.where(sea_eye, 1.0, 0.0)
        spreaded = dot(jnp.concatenate([sea_step] * 2, axis=0), sea_spread[...])
        blocks = (iota((2 * lo, 2 * lo), 0) >= lo) == (iota((2 * lo, 2 * lo), 1) >= lo)
        sea_vertical[...] = stacked(jnp.where(blocks, spreaded, 0.0))

        weights = [jnp.broadcast_to(col(r, eye), (la, 128)) for r in rows_up]
        for k, weight in enumerate(weights):
            lift[k] = weight
        sea_weight = jnp.broadcast_to(col(sea_step[0:1, :], sea_eye), (lo, 128))
        copy.wait()
        for start in range(0, columns, 128):
            at = slice(start, start + 128)
            for f in range(fields):
                x = atm[f * la : (f + 1) * la, at]
                y[f : f + 1, at] = x[la - 1 : la]
                for k in range(1, ASTEPS):
                    y[k * fields + f : k * fields + f + 1, at] = jnp.sum(
                        x * weights[k - 1], axis=0, keepdims=True
                    )
            yo[:, at] = jnp.sum(top[:, at] * sea_weight, axis=0, keepdims=True)

    return body


def band_build(ids, coef, w, k):
    def store(first, step, lanes, high, low):
        w[k, 0, first : first + step, lanes] = high
        w[k, 1, first : first + step, lanes] = low

    return band_pieces(store, ids, coef, HA)


def advance(moved, s, gains, bulk, surf):
    fields = bulk.shape[0]
    states = moved.shape[0]
    slot = iota((states, BLK), 0) // fields
    flux = bulk * (surf - moved[(s - 1) * fields : s * fields])
    kept = jnp.where(slot == s - 1, 0.0, moved)
    return kept + gains[:, s - 1 : s] * jnp.concatenate([flux] * ASTEPS, axis=0)


def interior_kernel(
    atm, y, nbr, coef, bulk, surf, gains, q, kept_out, mid_out, band, w, sa, sb, ma, mb, kept, mid, sems
):
    rows, columns = atm.shape
    states = y.shape[0]
    height = rows + states
    blocks = columns // BLK
    sent = list(range(ASTEPS)) + list(range(blocks - ASTEPS, blocks))
    leaving = []

    def depart(copy):
        copy.start()
        leaving.append(copy)

    def build(b):
        at = slice(b * BLK, (b + 1) * BLK)
        yield from band_build(nbr[:, at] - b * BLK, coef[:, at], w, b)

    def split(b):
        at = slice(b * BLK, (b + 1) * BLK)
        sa[b] = stacked(jnp.concatenate([atm[:, at], y[:, at]], axis=0))
        yield

    def pieces(b, moved):
        yield from product_pieces([sa[b + d] for d in (-1, 0, 1)], w.at[b], moved)

    def finish(b, s, moved, target):
        at = pl.ds(pl.multiple_of(b * BLK, BLK), BLK)
        value = advance(moved[rows:], s, gains, bulk[:, at], surf[:, at])
        if s == ASTEPS:
            q[b - ASTEPS] = value
            mid[b - ASTEPS] = stacked(moved[:rows])
        else:
            high, low = halves(moved[:rows])
            zh, zl = halves(value)
            target[b] = jnp.concatenate([high, zh, low, zl], axis=0)

    interleave(itertools.chain(*[split(b) for b in range(4)]))
    interleave(build(1))
    interleave(build(2))
    for i in range(blocks // 2 - 1):
        b = 2 * i + 1
        nexts = [b + 2, b + 3] if b + 3 < blocks - 1 else [0, blocks - 1]
        works = [itertools.chain(pieces(b, ma), pieces(b + 1, mb)), itertools.chain(*[build(k) for k in nexts])]
        if b + 4 < blocks:
            works.append(itertools.chain(split(b + 3), split(b + 4)))
        interleave(*works)
        finish(b, 1, ma[...], sb)
        finish(b + 1, 1, mb[...], sb)
    for i, b in enumerate(sent):
        depart(pltpu.make_async_copy(w.at[b], band.at[i], sems.at[i]))

    for s in range(1, ASTEPS + 1):
        xs, xt = (sa, sb) if s % 2 else (sb, sa)

        def inner(b, s=s, xs=xs, xt=xt):
            def begin():
                x2 = jnp.concatenate([xs[b - 1], xs[b], xs[b + 1]], axis=1)
                return products(x2, (w[b, 0], w[b, 1]))

            return begin, lambda moved: finish(b, s, moved, xt)

        def pair(i, _, s=s, inner=inner):
            in_turn([inner(s + 2 * i), inner(s + 2 * i + 1)])
            return 0

        if s > 1:
            lax.fori_loop(0, blocks // 2 - s, pair, 0)
        if s < ASTEPS:
            at = slice((s - 1) * 4, s * 4)
            for i, b in enumerate((s, s + 1, blocks - 2 - s, blocks - 1 - s)):
                kept[(s - 1) * 4 + i] = xt[b]
            depart(pltpu.make_async_copy(kept.at[at], kept_out.at[at], sems.at[len(sent) + s]))
    depart(pltpu.make_async_copy(mid, mid_out, sems.at[len(sent)]))
    for copy in leaving:
        copy.wait()


def block_place(b, blocks, ends, middle):
    if b < ASTEPS:
        return ends, b
    if b < blocks - ASTEPS:
        return middle, b - ASTEPS
    return ends, b - blocks + 2 * ASTEPS


def send(q_ends, q_mid, cols, out, table):
    fields = q_mid.shape[1] // ASTEPS
    peers, slots = cols.shape
    blocks = q_ends.shape[0] + q_mid.shape[0]
    lanes = out.shape[2]
    parts = slots // lanes
    for b in range(blocks):
        ref, i = block_place(b, blocks, q_ends, q_mid)
        table[b * fields : (b + 1) * fields, :] = ref[i, (ASTEPS - 1) * fields :, :]
    rows = stacked(table[...])
    half = blocks * fields
    block_of_row = iota((half, slots), 0) // fields

    def one(p, _):
        ids = cols[pl.ds(p, 1), :]
        got = mm(rows, one_hot(ids & (BLK - 1), BLK))
        got = jnp.where(block_of_row == ids // BLK, got[:half] + got[half:], 0.0)
        got = fold_rows(got, 2 * fields)
        got = got[:fields] + got[fields:]
        out[p] = jnp.concatenate([got[:, i * lanes : (i + 1) * lanes] for i in range(parts)], axis=0)
        return 0

    lax.fori_loop(0, peers, one, 0, unroll=4)


def exchange_kernel(
    recv, slot, weight, yo, nbr, coef, omix, before_in, after_in, flux_out, back, rows, tiles, hots, seas, acc, held, sems
):
    peers, per_peer, lanes = recv.shape
    links, columns = slot.shape
    fields = flux_out.shape[0]
    parts = per_peer // fields
    highs = peers * parts
    table = highs * fields
    arriving = [
        pltpu.make_async_copy(ref.at[: held.shape[1]], held.at[i], sems.at[i])
        for i, ref in enumerate((before_in, after_in))
    ]
    for copy in arriving:
        copy.start()
    rows[...] = stacked(recv[...].reshape(table, lanes))
    levels = omix.shape[0]
    eye = iota((levels, levels), 0) == iota((levels, levels), 1)
    corner = omix[0:1, 0:1] + 1.0
    top = omix[0:1, :] + jnp.where(iota((1, levels), 1) == 0, 1.0, 0.0)
    top = jnp.sum(jnp.where(eye, top, 0.0), axis=1, keepdims=True)
    high_of_row = iota((table, BLK), 0) // fields
    back_rows = iota((2 * highs, BLK), 0)
    inner = back_rows % (2 * parts)
    back_high = (back_rows // (2 * parts)) * parts + inner % parts
    pattern = iota((8, BLK), 0) % (2 * parts) // parts
    side = HO // 128
    window = 1 + 2 * side
    neighbors = nbr.shape[0]

    def surface(j, half):
        t0 = j * (BLK // 128) + half
        at = pl.ds(pl.multiple_of(t0 * 128, 128), 128)
        pad = jnp.zeros((8 - neighbors, 128), jnp.int32)
        ids = jnp.concatenate([nbr[:, at] - t0 * 128, pad], axis=0)
        cs = jnp.concatenate([coef[:, at], pad.astype(F32)], axis=0)
        middle = tiles[t0 + side]
        got = jnp.zeros((8, 128), F32)
        for t in range(window):
            pick = jnp.take_along_axis(tiles[t0 + t], ids & 127, axis=1, mode="promise_in_bounds")
            got = jnp.where(ids // 128 == t, pick, got)
        return middle[0:1] + jnp.sum(cs * (got - middle), axis=0, keepdims=True)

    def arrive(j, _):
        at = pl.ds(pl.multiple_of(j * BLK, BLK), BLK)
        parts = []

        def begin(r):
            ids = slot[r : r + 1, at]
            hot = one_hot(ids & (lanes - 1), lanes)
            hots[j, :, r * BLK : (r + 1) * BLK] = hot
            return mm(rows[...], hot)

        def finish(r, got):
            ids = slot[r : r + 1, at]
            got = jnp.where(high_of_row == ids // lanes, got[:table] + got[table:], 0.0)
            parts.append(weight[r : r + 1, at] * fold_rows(got, 2 * fields))

        last = begin(0)
        for r in range(1, links):
            got = begin(r)
            finish(r - 1, last)
            last = got
        finish(links - 1, last)
        flux = sum(parts[1:], parts[0])
        flux = flux[:fields] + flux[fields:]
        flux_out[:, at] = flux
        seas[:, at] = corner * flux[0:1]
        return 0

    lax.fori_loop(0, columns // BLK, arrive, 0, unroll=2)
    for copy in arriving:
        copy.wait()
    before, after = [jnp.sum(held[i] * top, axis=0, keepdims=True) for i in range(2)]
    acc[...] = jnp.zeros_like(acc)
    own_tiles = columns // 128
    for t in range(own_tiles + 2 * side):
        if t < side:
            line = before[:, t * 128 : (t + 1) * 128]
        elif t < side + own_tiles:
            line = yo[:, (t - side) * 128 : (t - side + 1) * 128]
        else:
            line = after[:, (t - side - own_tiles) * 128 : (t - side - own_tiles + 1) * 128]
        tiles[t] = jnp.broadcast_to(line, (8, 128))

    def base(j, _):
        at = pl.ds(pl.multiple_of(j * BLK, BLK), BLK)
        seas[:, at] += jnp.concatenate([surface(j, h) for h in range(BLK // 128)], axis=1)
        return 0

    lax.fori_loop(0, columns // BLK, base, 0, unroll=2)

    def leave(j, _):
        at = pl.ds(pl.multiple_of(j * BLK, BLK), BLK)
        sea = seas[:, at]
        left = []
        for r in range(links):
            ids, scale = slot[r : r + 1, at], weight[r : r + 1, at]
            high, low = halves(jnp.where(pattern == 1, scale, scale * sea))
            mask = back_high == ids // lanes
            both = [
                jnp.where(mask, jnp.concatenate([x.astype(F32)] * (2 * highs // 8), axis=0), 0.0).astype(BF)
                for x in (high, low)
            ]
            left.append(jnp.concatenate(both, axis=0))
        acc[...] += mm_t(jnp.concatenate(left, axis=1), hots[j])
        return 0

    lax.fori_loop(0, columns // BLK, leave, 0, unroll=2)
    back[...] = (acc[: 2 * highs] + acc[2 * highs :]).reshape(back.shape)


def settle_kernel(back, cols, surf, out, acc):
    peers, per_peer, lanes = back.shape
    parts = per_peer // 2
    blocks = surf.shape[1] // BLK
    acc[...] = jnp.zeros_like(acc)
    block_of_row = iota((blocks, lanes), 0)

    group = 4

    def one(i, _):
        left, hots = [], []
        for k, h in itertools.product(range(group), range(parts)):
            d = group * i + k
            ids = cols[pl.ds(d, 1), h * lanes : (h + 1) * lanes]
            mask = block_of_row == ids // BLK
            value = jnp.where(mask, back[d, h : h + 1, :], 0.0)
            scale = jnp.where(mask, back[d, parts + h : parts + h + 1, :], 0.0)
            left.append(stacked(jnp.concatenate([value, scale], axis=0)))
            hots.append(one_hot(ids & (BLK - 1), BLK))
        acc[...] += mm_t(jnp.concatenate(left, axis=1), jnp.concatenate(hots, axis=1))
        return 0

    lax.fori_loop(0, peers // group, one, 0)
    sums = acc[: 2 * blocks] + acc[2 * blocks :]
    base = jnp.concatenate([surf[0:1, b * BLK : (b + 1) * BLK] for b in range(blocks)], axis=0)
    value = (base + sums[:blocks]) / (1.0 + sums[blocks:])
    for b in range(blocks):
        for i in range(BLK // 128):
            row = b * (BLK // 128) + i
            out[row : row + 1, :] = value[b : b + 1, i * 128 : (i + 1) * 128]


def edge_kernel(
    y, bulk, surf, gains, lift, q_mid, cols, before, after, atm, kept_in, band, q, ends_out, outgoing,
    w, wide, sides, kept, sa, sb, ma, mb, ends, table, sems,
):
    rows = atm.shape[0]
    levels = lift.shape[1]
    fields = bulk.shape[0]
    states = y.shape[0]
    columns = y.shape[1]
    blocks = columns // BLK
    halo = ASTEPS - 1
    count = halo + ASTEPS
    total = blocks + 2 * ASTEPS
    arriving = [
        pltpu.make_async_copy(before, wide.at[0], sems.at[0]),
        pltpu.make_async_copy(after, wide.at[1], sems.at[1]),
        pltpu.make_async_copy(atm.at[:, : 2 * BLK], sides.at[0], sems.at[2]),
        pltpu.make_async_copy(atm.at[:, columns - 2 * BLK :], sides.at[1], sems.at[3]),
    ]
    bands = [pltpu.make_async_copy(band.at[i], w.at[halo + i], sems.at[4 + i]) for i in range(2 * ASTEPS)]
    keeps = pltpu.make_async_copy(kept_in, kept, sems.at[4 + 2 * ASTEPS])
    needed = [[0, 2 * ASTEPS - 1]] + [[i, 2 * ASTEPS - 1 - i] for i in range(1, ASTEPS)]
    for copy in arriving:
        copy.start()
    for group in needed:
        for i in group:
            bands[i].start()
    keeps.start()

    def place(e):
        if e < ASTEPS:
            return wide.at[0], e
        if e >= total - ASTEPS:
            return wide.at[1], e - total + ASTEPS
        return None, e - ASTEPS

    def coefs(e):
        ref, local = place(e)
        at = slice(local * BLK, (local + 1) * BLK)
        if ref is None:
            return bulk[:, at], surf[:, at]
        j = local - 1 if e < ASTEPS else local
        at = slice(j * BLK, (j + 1) * BLK)
        return ref[rows + 12 : rows + 16, at], ref[rows + 4 * j : rows + 4 * j + 4, WIDE - BLK :]

    def build(e):
        ref, local = place(e)
        origin = local * BLK + (columns - WIDE if e < ASTEPS else 0)
        j = local - 1 if e < ASTEPS else local
        at = slice(j * BLK, (j + 1) * BLK)
        ids = ref[rows : rows + 6, at].astype(jnp.int32) - origin
        k = e - 1 if e < ASTEPS else e - (total - 1) + 2 * count
        yield from band_build(ids, ref[rows + 6 : rows + 12, at], w, k)

    for copy in arriving:
        copy.wait()
    for i in range(ASTEPS):
        at = slice(i * BLK, (i + 1) * BLK)
        for side in range(2):
            x = wide[side, :rows, at]
            lifted = [x[(f + 1) * levels - 1 : (f + 1) * levels] for f in range(fields)]
            for k in range(ASTEPS - 1):
                weight = jnp.concatenate([lift[k]] * (BLK // 128), axis=1)
                for f in range(fields):
                    lifted.append(jnp.sum(x[f * levels : (f + 1) * levels] * weight, axis=0, keepdims=True))
            sa[i if side == 0 else 8 + i] = stacked(jnp.concatenate([x] + lifted, axis=0))
    for i in range(2):
        at = slice(i * BLK, (i + 1) * BLK)
        far = slice(columns - (2 - i) * BLK, columns - (1 - i) * BLK)
        sa[ASTEPS + i] = stacked(jnp.concatenate([sides[0, :, at], y[:, at]], axis=0))
        sa[6 + i] = stacked(jnp.concatenate([sides[1, :, at], y[:, far]], axis=0))

    buffers = (sa, sb)
    builds = [itertools.chain(build(1 + i), build(total - 2 - i)) for i in range(halo)]
    interleave(builds[0])
    for s in range(1, ASTEPS + 1):
        source, target = buffers[(s - 1) % 2], buffers[s % 2]
        last = s == ASTEPS

        def finish(side, i, moved, s=s, target=target, last=last):
            e = s + i if side == 0 else total - 1 - s - halo + i
            value = advance(moved[rows:], s, gains, *coefs(e))
            if last:
                q[4 * side + i] = value
                ends[4 * side + i] = stacked(moved[:rows])
            else:
                target[6 * side + i + 2 * side] = stacked(jnp.concatenate([moved[:rows], value], axis=0))

        def band_of(side, i, s=s):
            return s - 1 + i if side == 0 else count + ASTEPS - s + i

        def one(side, i, source=source, finish=finish, band_of=band_of):
            def begin():
                x2 = jnp.concatenate([source[6 * side + i + d] for d in range(3)], axis=1)
                k = band_of(side, i)
                return products(x2, (w[k, 0], w[k, 1]))

            return begin, lambda moved: finish(side, i, moved)

        if s == 1:
            for i in range(halo):
                pieces = [
                    product_pieces([source[6 * side + j + d] for d in range(3)], w.at[band_of(side, j)], m)
                    for side, j, m in ((0, i, ma), (1, halo - i, mb))
                ]
                interleave(itertools.chain(*pieces), *builds[i + 1 : i + 2])
                finish(0, i, ma[...])
                finish(1, halo - i, mb[...])
            for k in needed[0]:
                bands[k].wait()
            in_turn([one(0, halo), one(1, 0)])
            keeps.wait()
        else:
            for k in needed[s - 1]:
                bands[k].wait()
            in_turn([one(side, i) for i in range(ASTEPS) for side in range(2)])
        if not last:
            for i in range(2):
                target[ASTEPS + i] = kept[(s - 1) * 4 + i]
                target[6 + i] = kept[(s - 1) * 4 + 2 + i]
    out = pltpu.make_async_copy(ends, ends_out, sems.at[5 + 2 * ASTEPS])
    out.start()
    send(q, q_mid, cols, outgoing, table)
    out.wait()


def finish_kernel(q_ends, q_mid, vertical, ends_in, mid_in, out, ends, mid, staged, sems, osems):
    rows = ends.shape[1] // 2
    levels = rows // 2
    blocks = staged.shape[0]
    arriving = [
        pltpu.make_async_copy(mid_in, mid, sems.at[0]),
        pltpu.make_async_copy(ends_in, ends, sems.at[1]),
    ]
    for copy in arriving:
        copy.start()

    def leaving(b):
        at = slice(b * BLK, (b + 1) * BLK)
        return pltpu.make_async_copy(staged.at[b], out.at[:, at], osems.at[b])

    def one(b, p):
        ref, i = block_place(b, blocks, ends, mid)
        share, _ = block_place(b, blocks, q_ends, q_mid)

        def begin():
            qh, ql = halves(share[i])
            high = jnp.concatenate([ref[i, p * levels : (p + 1) * levels], qh], axis=0)
            low = jnp.concatenate([ref[i, rows + p * levels : rows + (p + 1) * levels], ql], axis=0)
            return mm(vertical[p], high), mm(vertical[p, :levels], low)

        def finish(value):
            staged[b, p * levels : (p + 1) * levels] = value

        return begin, finish

    middle = list(range(ASTEPS, blocks - ASTEPS))
    outer = list(range(ASTEPS)) + list(range(blocks - ASTEPS, blocks))
    for copy, group in zip(arriving, (middle, outer)):
        copy.wait()
        for start in range(0, len(group), 4):
            some = group[start : start + 4]
            in_turn([one(b, p) for b in some for p in range(2)])
            for b in some:
                leaving(b).start()
    for b in range(blocks):
        leaving(b).wait()


def sea_build(nbr, coef, b, w):
    at = pl.ds(pl.multiple_of(b * BLK, BLK), BLK)

    def store(first, size, lanes, high, low):
        w[0, first : first + size, lanes] = high
        w[1, first : first + size, lanes] = low

    return band_pieces(store, nbr[:, at] - b * BLK, coef[:, at], HO)


def sea_inner_kernel(ocean, nbr, coef, laid_out, x2, wa, wb, ma, mb, laid, sems):
    blocks = ocean.shape[1] // BLK
    around = 1 + 2 * HO // BLK
    first = -(-HO // BLK)
    count = blocks - 2 * first
    for i in range(count + around - 1):
        start = (first + i) * BLK - HO
        x2[i] = stacked(ocean[:, start : start + BLK])

    def leaving(i):
        return pltpu.make_async_copy(laid.at[i], laid_out.at[i], sems.at[i])

    def move(i, w, moved):
        yield from product_pieces([x2[i + d] for d in range(around)], w, moved)

    interleave(sea_build(nbr, coef, first, wa))

    def one(k, _):
        i = 2 * k
        interleave(sea_build(nbr, coef, first + i + 1, wb), move(i, wa, ma))
        interleave(sea_build(nbr, coef, jnp.minimum(i + 2, count - 1) + first, wa), move(i + 1, wb, mb))
        laid[i] = stacked(ma[...])
        laid[i + 1] = stacked(mb[...])
        leaving(i).start()
        leaving(i + 1).start()
        return 0

    lax.fori_loop(0, count // 2, one, 0)

    def done(i, _):
        leaving(i).wait()
        return 0

    lax.fori_loop(0, count, done, 0)


def sea_outer_kernel(
    before, after, nbr, coef, vertical, mix, flux, ocean, laid_in, out, ends, x2, wa, wb, ma, mb, laid, staged, sems, osems
):
    fields = flux.shape[0]
    rows, columns = ocean.shape
    levels = rows // fields
    blocks = columns // BLK
    around = 1 + 2 * HO // BLK
    first = -(-HO // BLK)
    count = blocks - 2 * first
    width = ends.shape[2]
    arriving = [
        pltpu.make_async_copy(ocean.at[:, :width], ends.at[0], sems.at[0]),
        pltpu.make_async_copy(ocean.at[:, columns - width :], ends.at[1], sems.at[1]),
        pltpu.make_async_copy(laid_in, laid.at[first : first + count], sems.at[2]),
    ]
    for copy in arriving:
        copy.start()
    eye = iota((levels, levels), 0) == iota((levels, levels), 1)
    top = jnp.broadcast_to((mix[...] + jnp.where(eye, 1.0, 0.0))[:, 0:1], (levels, BLK))
    outer = list(range(first)) + list(range(blocks - first, blocks))
    bands, sums = (wa, wb), (ma, mb)
    interleave(sea_build(nbr, coef, outer[0], wa))
    arriving[0].wait()
    arriving[1].wait()
    spans = ((before, -HO, HO), (ends.at[0], 0, width), (ends.at[1], columns - width, width), (after, columns, HO))
    held = list(range(first + around - 1)) + list(range(blocks - first, blocks + around - 1))
    for i, e in enumerate(held):
        start = e * BLK - HO
        pieces = []
        for ref, begin, size in spans:
            lo, hi = max(start, begin), min(start + BLK, begin + size)
            if lo < hi:
                pieces.append(ref[:, lo - begin : hi - begin])
        x2[i] = stacked(pieces[0] if len(pieces) == 1 else jnp.concatenate(pieces, axis=1))

    def move(b, w, moved):
        yield from product_pieces([x2[held.index(b + d)] for d in range(around)], w, moved)

    for k, b in enumerate(outer):
        works = [move(b, bands[k % 2], sums[k % 2])]
        if k + 1 < len(outer):
            works.insert(0, sea_build(nbr, coef, outer[k + 1], bands[(k + 1) % 2]))
        interleave(*works)
        laid[b] = stacked(sums[k % 2][...])
    arriving[2].wait()
    pair = 2 * levels

    def leaving(b):
        at = pl.ds(pl.multiple_of(b * BLK, BLK), BLK)
        return pltpu.make_async_copy(staged.at[b], out.at[:, at], osems.at[b])

    def mixed(b, p):
        at = pl.ds(pl.multiple_of(b * BLK, BLK), BLK)

        def begin():
            high = laid[b, p * pair : (p + 1) * pair]
            low = laid[b, rows + p * pair : rows + (p + 1) * pair]
            return mm(vertical[...], high), mm(vertical[:pair], low)

        def finish(value):
            for k in range(2):
                f = 2 * p + k
                staged[b, f * levels : (f + 1) * levels] = (
                    value[k * levels : (k + 1) * levels] + top * flux[f : f + 1, at]
                )

        return begin, finish

    def four(i, _):
        in_turn([mixed(4 * i + k, p) for k in range(4) for p in range(fields // 2)])
        for k in range(4):
            leaving(4 * i + k).start()
        return 0

    lax.fori_loop(0, blocks // 4, four, 0)

    def done(b, _):
        leaving(b).wait()
        return 0

    lax.fori_loop(0, blocks, done, 0)


def after_all(value, *others):
    return lax.optimization_barrier((value, *others))[0]


def per_device(
    atm_state,
    atm_surface,
    bulk_coef,
    atm_nbr,
    atm_nbr_coef,
    atm_mix,
    ocean_state,
    ocean_nbr,
    ocean_nbr_coef,
    ocean_mix,
    send_cols,
    remap_slot,
    remap_weight,
):
    fields, la, columns = atm_state.shape
    lo, cells = ocean_state.shape[1:]
    blocks = columns // BLK
    rows = fields * la
    states = fields * ASTEPS
    picked = send_cols[0]
    peers, slots = picked.shape
    lanes = min(BLK, slots)
    parts = slots // lanes
    atm = atm_state.reshape(rows, columns)
    ocean = ocean_state.reshape(fields * lo, cells)
    depth = lax.axis_size(AXES)
    up = [(i, (i + 1) % depth) for i in range(depth)]
    down = [(j, i) for i, j in up]
    window = BLK + 2 * HA
    vmem = pl.BlockSpec(memory_space=pltpu.VMEM)
    anywhere = pl.BlockSpec(memory_space=pl.ANY)

    depth_k = rows + states
    half = fields // 2
    p_of = np.arange(half)[:, None, None]
    r_of = np.arange(2 * la)[None, :, None]
    c_of = np.arange(2 * la + states)[None, None, :]
    code = np.where(
        c_of < 2 * la,
        (c_of // la == r_of // la) * 1,
        ((c_of - 2 * la) % fields == 2 * p_of + r_of // la) * (2 + (c_of - 2 * la) // fields),
    )
    code = np.broadcast_to(code, (half, 2 * la, 2 * la + states)).astype(np.int32)
    spread = ((c_of[0] % la == np.arange(la)[:, None]) & (c_of[0] < 2 * la)).astype(np.float32)
    sea_spread = (np.arange(2 * lo)[None, :] % lo == np.arange(lo)[:, None]).astype(np.float32)

    wide_rows = rows + 16
    sea_rows = fields * lo
    halo_shapes = (shape((rows, WIDE)),) * 2 + (shape((sea_rows, HO)),) * 2
    wide_first, wide_last, sea_first, sea_last = call(
        pack_kernel,
        (shape((wide_rows, WIDE)),) * 2 + halo_shapes[2:],
        in_specs=[vmem] * 4 + [anywhere] * 2,
        out_specs=(anywhere,) * 4,
        scratch=[pltpu.VMEM(h.shape, F32) for h in halo_shapes]
        + [pltpu.VMEM((2, 16, WIDE), F32), pltpu.SemaphoreType.DMA((10,))],
    )(atm_nbr, atm_nbr_coef, bulk_coef, atm_surface, atm, ocean)
    wide_before = lax.ppermute(wide_last, AXES, up)
    wide_after = lax.ppermute(wide_first, AXES, down)

    y, yo, gains, lift, vertical, sea_vertical = call(
        prepare_kernel(fields),
        (
            shape((states, columns)),
            shape((1, columns)),
            shape((states, 128)),
            shape((ASTEPS - 1, la, 128)),
            shape((half, 4 * la, 2 * la + states), BF),
            shape((4 * lo, 2 * lo), BF),
        ),
        in_specs=[vmem] * 6 + [anywhere],
        scratch=[pltpu.VMEM((lo, cells), F32), pltpu.SemaphoreType.DMA(())],
    )(
        after_all(atm_mix, wide_first),
        ocean_mix,
        atm,
        jnp.asarray(spread),
        jnp.asarray(code),
        jnp.asarray(sea_spread),
        ocean,
    )

    ends = 2 * ASTEPS
    q_mid, kept, mid, band = call(
        interior_kernel,
        (
            shape((blocks - ends, states, BLK)),
            shape((4 * (ASTEPS - 1), 2 * depth_k, BLK), BF),
            shape((blocks - ends, 2 * rows, BLK), BF),
            shape((ends, 2, window, BLK), BF),
        ),
        in_specs=[vmem] * 7,
        out_specs=(vmem, anywhere, anywhere, anywhere),
        scratch=[
            pltpu.VMEM((blocks, 2, window, BLK), BF),
            pltpu.VMEM((blocks, 2 * depth_k, BLK), BF),
            pltpu.VMEM((blocks, 2 * depth_k, BLK), BF),
            pltpu.VMEM((depth_k, BLK), F32),
            pltpu.VMEM((depth_k, BLK), F32),
            pltpu.VMEM((4 * (ASTEPS - 1), 2 * depth_k, BLK), BF),
            pltpu.VMEM((blocks - ends, 2 * rows, BLK), BF),
            pltpu.SemaphoreType.DMA((ends + ASTEPS,)),
        ],
    )(atm, y, atm_nbr, atm_nbr_coef, bulk_coef, atm_surface, gains)

    sea_blocks = cells // BLK
    outer = -(-HO // BLK)
    around = 1 + 2 * HO // BLK
    sea_window = BLK + 2 * HO
    inner = sea_blocks - 2 * outer
    sea_inner = call(
        sea_inner_kernel,
        shape((inner, 2 * sea_rows, BLK), BF),
        in_specs=[vmem] * 3,
        out_specs=anywhere,
        scratch=[
            pltpu.VMEM((inner + around - 1, 2 * sea_rows, BLK), BF),
            pltpu.VMEM((2, sea_window, BLK), BF),
            pltpu.VMEM((2, sea_window, BLK), BF),
            pltpu.VMEM((sea_rows, BLK), F32),
            pltpu.VMEM((sea_rows, BLK), F32),
            pltpu.VMEM((inner, 2 * sea_rows, BLK), BF),
            pltpu.SemaphoreType.DMA((inner,)),
        ],
    )(ocean, after_all(ocean_nbr, q_mid), ocean_nbr_coef)

    sea_first, sea_last = lax.optimization_barrier((sea_first, sea_last, sea_inner))[:2]
    sea_before = lax.ppermute(sea_last, AXES, up)
    sea_after = lax.ppermute(sea_first, AXES, down)

    q_ends, tips, outgoing = call(
        edge_kernel,
        (
            shape((ends, states, BLK)),
            shape((ends, 2 * rows, BLK), BF),
            shape((peers, parts * fields, lanes)),
        ),
        in_specs=[vmem] * 7 + [anywhere] * 5,
        out_specs=(vmem, anywhere, vmem),
        scratch=[
            pltpu.VMEM((2 * (2 * ASTEPS - 1), 2, window, BLK), BF),
            pltpu.VMEM((2, wide_rows, WIDE), F32),
            pltpu.VMEM((2, rows, 2 * BLK), F32),
            pltpu.VMEM((4 * (ASTEPS - 1), 2 * depth_k, BLK), BF),
            pltpu.VMEM((12, 2 * depth_k, BLK), BF),
            pltpu.VMEM((12, 2 * depth_k, BLK), BF),
            pltpu.VMEM((depth_k, BLK), F32),
            pltpu.VMEM((depth_k, BLK), F32),
            pltpu.VMEM((ends, 2 * rows, BLK), BF),
            pltpu.VMEM((blocks * fields, BLK), F32),
            pltpu.SemaphoreType.DMA((6 + 2 * ASTEPS,)),
        ],
    )(after_all(y, sea_inner), bulk_coef, atm_surface, gains, lift, q_mid, picked, wide_before, wide_after, atm, kept, band)

    sea_before, sea_after, outgoing = lax.optimization_barrier((sea_before, sea_after, outgoing))
    received = lax.all_to_all(outgoing, AXES, split_axis=0, concat_axis=0, tiled=True)

    atm_final = call(
        finish_kernel,
        shape((rows, columns)),
        in_specs=[vmem] * 3 + [anywhere] * 2,
        out_specs=anywhere,
        scratch=[
            pltpu.VMEM((ends, 2 * rows, BLK), BF),
            pltpu.VMEM((blocks - ends, 2 * rows, BLK), BF),
            pltpu.VMEM((blocks, rows, BLK), F32),
            pltpu.SemaphoreType.DMA((2,)),
            pltpu.SemaphoreType.DMA((blocks,)),
        ],
    )(after_all(q_ends, outgoing), q_mid, vertical, tips, mid)

    flux, back = call(
        exchange_kernel,
        (shape((fields, cells)), shape((peers, 2 * parts, lanes))),
        in_specs=[vmem] * 7 + [anywhere] * 2,
        scratch=[
            pltpu.VMEM((2 * peers * parts * fields, lanes), BF),
            pltpu.VMEM((cells // 128 + 2 * HO // 128, 8, 128), F32),
            pltpu.VMEM((cells // BLK, lanes, remap_slot.shape[0] * BLK), BF),
            pltpu.VMEM((1, cells), F32),
            pltpu.VMEM((4 * peers * parts, lanes), F32),
            pltpu.VMEM((2, lo, HO), F32),
            pltpu.SemaphoreType.DMA((2,)),
        ],
    )(
        after_all(received, atm_final),
        remap_slot,
        remap_weight,
        yo,
        ocean_nbr,
        ocean_nbr_coef,
        ocean_mix,
        sea_before,
        sea_after,
    )
    returned = lax.all_to_all(back, AXES, split_axis=0, concat_axis=0, tiled=True)

    ocean_final = call(
        sea_outer_kernel,
        shape((sea_rows, cells)),
        in_specs=[vmem] * 7 + [anywhere] * 2,
        out_specs=anywhere,
        scratch=[
            pltpu.VMEM((2, sea_rows, (outer + around - 1) * BLK - HO), F32),
            pltpu.VMEM((2 * (outer + around - 1), 2 * sea_rows, BLK), BF),
            pltpu.VMEM((2, sea_window, BLK), BF),
            pltpu.VMEM((2, sea_window, BLK), BF),
            pltpu.VMEM((sea_rows, BLK), F32),
            pltpu.VMEM((sea_rows, BLK), F32),
            pltpu.VMEM((sea_blocks, 2 * sea_rows, BLK), BF),
            pltpu.VMEM((sea_blocks, sea_rows, BLK), F32),
            pltpu.SemaphoreType.DMA((3,)),
            pltpu.SemaphoreType.DMA((sea_blocks,)),
        ],
    )(
        after_all(sea_before, back),
        sea_after,
        ocean_nbr,
        ocean_nbr_coef,
        sea_vertical,
        ocean_mix,
        flux,
        ocean,
        sea_inner,
    )

    surface_temp = call(
        settle_kernel,
        shape((columns // 128, 128)),
        in_specs=[vmem] * 3,
        scratch=[pltpu.VMEM((4 * blocks, BLK), F32)],
    )(after_all(returned, ocean_final), picked, atm_surface)

    return (
        atm_final.reshape(fields, la, columns),
        ocean_final.reshape(fields, lo, cells),
        surface_temp.reshape(columns),
    )


def solution(mesh):
    placed = (
        P(None, None, AXES),
        P(None, AXES),
        P(None, AXES),
        P(None, AXES),
        P(None, AXES),
        P(),
        P(None, None, AXES),
        P(None, AXES),
        P(None, AXES),
        P(),
        P(AXES, None, None),
        P(None, AXES),
        P(None, AXES),
    )
    return jax.shard_map(
        per_device,
        mesh=mesh,
        in_specs=placed,
        out_specs=(P(None, None, AXES), P(None, None, AXES), P(AXES)),
        check_vma=False,
    )
```

```python
import itertools

import numpy as np

import jax
import jax.numpy as jnp
from jax import lax
from jax.experimental import pallas as pl
from jax.experimental.pallas import tpu as pltpu
from jax.sharding import PartitionSpec as P

ASTEPS = 4
HA = 256
HO = 384
BLK = 256
WIDE = ASTEPS * HA
BF = jnp.bfloat16
F32 = jnp.float32
VMEM_BYTES = 63 * 1024 * 1024
AXES = ("sec", "blk")


def call(body, outs, *, in_specs=None, out_specs=None, scratch=(), flops=10**6, moved=10**4, aliases=None):
    vmem = pl.BlockSpec(memory_space=pltpu.VMEM)
    return pl.pallas_call(
        body,
        out_shape=outs,
        in_specs=in_specs,
        out_specs=jax.tree.map(lambda _: vmem, outs) if out_specs is None else out_specs,
        scratch_shapes=list(scratch),
        input_output_aliases=aliases or {},
        compiler_params=pltpu.CompilerParams(vmem_limit_bytes=VMEM_BYTES),
        cost_estimate=pl.CostEstimate(flops=flops, bytes_accessed=moved, transcendentals=0),
    )


def shape(dims, dtype=F32):
    return jax.ShapeDtypeStruct(dims, dtype)


def halves(x):
    high = x.astype(BF)
    return high, (x - high.astype(F32)).astype(BF)


def stacked(x):
    return jnp.concatenate(halves(x), axis=0)


def mm(a, b):
    return jnp.dot(a, b, preferred_element_type=F32)


def mm_t(a, b):
    return lax.dot_general(a, b, (((1,), (1,)), ((), ())), preferred_element_type=F32)


def products(x2, w2):
    return mm(x2, w2[0]), mm(x2[: x2.shape[0] // 2], w2[1])


def summed(parts):
    wide, rest = parts
    rows = rest.shape[0]
    return wide[:rows] + wide[rows:] + rest


def in_turn(works):
    waiting = None
    for begin, finish in works:
        parts = begin()
        if waiting is not None:
            waiting[1](summed(waiting[0]))
        waiting = (parts, finish)
    waiting[1](summed(waiting[0]))


def product_pieces(x2s, w2, result):
    rows = x2s[0].shape[0] // 2
    for t, x2 in enumerate(x2s):
        at = slice(t * BLK, (t + 1) * BLK)
        wide = mm(x2, w2.at[0][at])
        part = wide[:rows] + wide[rows:]
        result[...] = part if t == 0 else result[...] + part
        yield
        result[...] += mm(x2[:rows], w2.at[1][at])
        yield


def interleave(*works):
    works = list(works)
    while works:
        works = [w for w in works if next(w, w) is not w]


def iota(dims, axis):
    return lax.broadcasted_iota(jnp.int32, dims, axis)


def build_band(*args):
    for _ in band_pieces(*args):
        pass


def band_pieces(store, nbr, coef, halo):
    rows = BLK + 2 * halo
    count = nbr.shape[0]
    ids = [nbr[k : k + 1] for k in range(count)]
    cs = [coef[k : k + 1] for k in range(count)]
    rest = 1.0 - sum(cs[1:], cs[0])
    for k in range(count - 1, 0, -1):
        alive = jnp.ones_like(ids[k]) > 0
        for j in range(k):
            same = jnp.logical_and(ids[k] == ids[j], alive)
            cs[j] = cs[j] + jnp.where(same, cs[k], 0.0)
            alive = jnp.logical_and(alive, jnp.logical_not(same))
        ids[k] = jnp.where(alive, ids[k], -1)
    lanes = 128
    step = 16
    base = iota((step, lanes), 0).astype(F32)
    parts = [halves(c) for c in cs + [rest]]

    def wide(x, at):
        return jnp.broadcast_to(x[:, at].astype(F32), (step, lanes)).astype(BF)

    for half in range(BLK // lanes):
        at = slice(half * lanes, (half + 1) * lanes)
        highs = [wide(p[0], at) for p in parts]
        lows = [wide(p[1], at) for p in parts]
        own = (iota((step, lanes), 1) - iota((step, lanes), 0)).astype(F32).astype(BF)
        zero = jnp.zeros((step, lanes), BF)
        for tile in range(0, rows, BLK):
            near = [wide((i - tile).astype(F32), at) for i in ids]
            for first in range(tile, tile + BLK, step):
                high, low = zero, zero
                if half * lanes - step < first < half * lanes + lanes + 2 * halo:
                    offset = first - halo - half * lanes
                    if 0 <= offset < lanes:
                        same = own == jnp.full((step, lanes), offset, BF)
                        high = jnp.where(same, highs[-1], zero)
                        low = jnp.where(same, lows[-1], zero)
                    here = (base + float(first - tile)).astype(BF)
                    for k in range(count):
                        same = here == near[k]
                        high = jnp.where(same, highs[k], high)
                        low = jnp.where(same, lows[k], low)
                store(first, step, at, high, low)
            yield


def one_hot(ids, rows):
    lanes = ids.shape[1]
    wide = jnp.broadcast_to(ids.astype(F32), (rows, lanes)).astype(BF)
    here = iota((rows, lanes), 0).astype(F32).astype(BF)
    return jnp.where(here == wide, jnp.ones((rows, lanes), BF), jnp.zeros((rows, lanes), BF))


def fold_rows(x, height):
    total = x[:height]
    for first in range(height, x.shape[0], height):
        total = total + x[first : first + height]
    return total


def pack_kernel(nbr, coef, bulk, surf, atm, sea, wide_first, wide_last, sea_first, sea_last, *refs):
    held, lists, sems = refs[:4], refs[4], refs[5]
    rows, columns = atm.shape
    cells = sea.shape[1]
    sources = (
        atm.at[:, :WIDE],
        atm.at[:, columns - WIDE :],
        sea.at[:, :HO],
        sea.at[:, cells - HO :],
    )
    targets = (wide_first.at[:rows], wide_last.at[:rows], sea_first, sea_last)
    arriving = [pltpu.make_async_copy(x, held[i], sems.at[i]) for i, x in enumerate(sources)]
    leaving = [pltpu.make_async_copy(held[i], x, sems.at[4 + i]) for i, x in enumerate(targets)]
    for copy in arriving:
        copy.start()
    need = WIDE - BLK
    for i, first in enumerate((0, columns - need)):
        at = slice(first, first + need)
        lists[i, 0:6, :need] = nbr[:, at].astype(F32)
        lists[i, 6:12, :need] = coef[:, at]
        lists[i, 12:16, :need] = bulk[:, at]
        lists[i, 12:16, need:] = jnp.zeros((4, BLK), F32)
        for j in range(ASTEPS - 1):
            lists[i, 4 * j : 4 * j + 4, need:] = surf[:, first + j * BLK : first + (j + 1) * BLK]
    for i, target in enumerate((wide_first, wide_last)):
        copy = pltpu.make_async_copy(lists.at[i], target.at[rows:], sems.at[8 + i])
        copy.start()
        leaving.append(copy)
    for here, there in zip(arriving, leaving[:4]):
        here.wait()
        there.start()
    for copy in leaving:
        copy.wait()


def prepare_kernel(fields):
    def body(
        mix, omix, atm, spread, code, sea_spread, sea, y, yo, gains, lift, vertical, sea_vertical, top, sem
    ):
        la = mix.shape[0]
        columns = atm.shape[1]
        copy = pltpu.make_async_copy(sea.at[: omix.shape[0], :], top, sem)
        copy.start()
        eye = iota((la, la), 0) == iota((la, la), 1)
        step = mix[...] + jnp.where(eye, 1.0, 0.0)

        def dot(a, b):
            return jnp.dot(a, b, precision=lax.Precision.HIGHEST, preferred_element_type=F32)

        def col(r, same):
            return jnp.sum(jnp.where(same, r, 0.0), axis=1, keepdims=True)

        def row(c, same):
            return jnp.sum(jnp.where(same, c, 0.0), axis=0, keepdims=True)

        twice = dot(step, step)
        fourth = dot(twice, twice)
        rows_up = [step[la - 1 : la, :]]
        cols_up = [step[:, la - 1 : la]]
        for _ in range(ASTEPS - 2):
            rows_up.append(jnp.sum(step * col(rows_up[-1], eye), axis=0, keepdims=True))
        for _ in range(ASTEPS - 1):
            cols_up.append(jnp.sum(step * row(cols_up[-1], eye), axis=1, keepdims=True))
        slot = iota((fields * ASTEPS, 128), 0) // fields
        lane = iota((fields * ASTEPS, 128), 1)
        value = jnp.zeros((fields * ASTEPS, 128), F32)
        for s in range(1, ASTEPS + 1):
            column = jnp.where(slot == s - 1, 1.0, 0.0)
            for j in range(1, ASTEPS):
                column = jnp.where(slot == s - 1 + j, rows_up[j - 1][:, la - 1 : la], column)
            value = jnp.where(lane == s - 1, column, value)
        gains[...] = value

        spreaded = dot(jnp.concatenate([fourth] * 2, axis=0), spread[...])
        for p in range(fields // 2):
            filled = jnp.where(code[p] == 1, spreaded, 0.0)
            for m in range(ASTEPS):
                tall = jnp.concatenate([cols_up[ASTEPS - 1 - m]] * 2, axis=0)
                filled = jnp.where(code[p] == 2 + m, tall, filled)
            vertical[p] = stacked(filled)
        lo = omix.shape[0]
        sea_eye = iota((lo, lo), 0) == iota((lo, lo), 1)
        sea_step = omix[...] + jnp.where(sea_eye, 1.0, 0.0)
        spreaded = dot(jnp.concatenate([sea_step] * 2, axis=0), sea_spread[...])
        blocks = (iota((2 * lo, 2 * lo), 0) >= lo) == (iota((2 * lo, 2 * lo), 1) >= lo)
        sea_vertical[...] = stacked(jnp.where(blocks, spreaded, 0.0))

        weights = [jnp.broadcast_to(col(r, eye), (la, 128)) for r in rows_up]
        for k, weight in enumerate(weights):
            lift[k] = weight
        sea_weight = jnp.broadcast_to(col(sea_step[0:1, :], sea_eye), (lo, 128))
        copy.wait()
        for start in range(0, columns, 128):
            at = slice(start, start + 128)
            for f in range(fields):
                x = atm[f * la : (f + 1) * la, at]
                y[f : f + 1, at] = x[la - 1 : la]
                for k in range(1, ASTEPS):
                    y[k * fields + f : k * fields + f + 1, at] = jnp.sum(
                        x * weights[k - 1], axis=0, keepdims=True
                    )
            yo[:, at] = jnp.sum(top[:, at] * sea_weight, axis=0, keepdims=True)

    return body


def band_build(ids, coef, w, k):
    def store(first, step, lanes, high, low):
        w[k, 0, first : first + step, lanes] = high
        w[k, 1, first : first + step, lanes] = low

    return band_pieces(store, ids, coef, HA)


def advance(moved, s, gains, bulk, surf):
    fields = bulk.shape[0]
    states = moved.shape[0]
    slot = iota((states, BLK), 0) // fields
    flux = bulk * (surf - moved[(s - 1) * fields : s * fields])
    kept = jnp.where(slot == s - 1, 0.0, moved)
    return kept + gains[:, s - 1 : s] * jnp.concatenate([flux] * ASTEPS, axis=0)


def interior_kernel(
    atm, y, nbr, coef, bulk, surf, gains, q, kept_out, mid_out, band, w, sa, sb, ma, mb, kept, mid, sems
):
    rows, columns = atm.shape
    states = y.shape[0]
    height = rows + states
    blocks = columns // BLK
    sent = list(range(ASTEPS)) + list(range(blocks - ASTEPS, blocks))
    leaving = []

    def depart(copy):
        copy.start()
        leaving.append(copy)

    def build(b):
        at = slice(b * BLK, (b + 1) * BLK)
        yield from band_build(nbr[:, at] - b * BLK, coef[:, at], w, b)

    def split(b):
        at = slice(b * BLK, (b + 1) * BLK)
        sa[b] = stacked(jnp.concatenate([atm[:, at], y[:, at]], axis=0))
        yield

    def pieces(b, moved):
        yield from product_pieces([sa[b + d] for d in (-1, 0, 1)], w.at[b], moved)

    def finish(b, s, moved, target):
        at = pl.ds(pl.multiple_of(b * BLK, BLK), BLK)
        value = advance(moved[rows:], s, gains, bulk[:, at], surf[:, at])
        if s == ASTEPS:
            q[b - ASTEPS] = value
            mid[b - ASTEPS] = stacked(moved[:rows])
        else:
            high, low = halves(moved[:rows])
            zh, zl = halves(value)
            target[b] = jnp.concatenate([high, zh, low, zl], axis=0)

    interleave(itertools.chain(*[split(b) for b in range(4)]))
    interleave(build(1))
    interleave(build(2))
    for i in range(blocks // 2 - 1):
        b = 2 * i + 1
        nexts = [b + 2, b + 3] if b + 3 < blocks - 1 else [0, blocks - 1]
        works = [itertools.chain(pieces(b, ma), pieces(b + 1, mb)), itertools.chain(*[build(k) for k in nexts])]
        if b + 4 < blocks:
            works.append(itertools.chain(split(b + 3), split(b + 4)))
        interleave(*works)
        finish(b, 1, ma[...], sb)
        finish(b + 1, 1, mb[...], sb)
    for i, b in enumerate(sent):
        depart(pltpu.make_async_copy(w.at[b], band.at[i], sems.at[i]))

    for s in range(1, ASTEPS + 1):
        xs, xt = (sa, sb) if s % 2 else (sb, sa)

        def inner(b, s=s, xs=xs, xt=xt):
            def begin():
                x2 = jnp.concatenate([xs[b - 1], xs[b], xs[b + 1]], axis=1)
                return products(x2, (w[b, 0], w[b, 1]))

            return begin, lambda moved: finish(b, s, moved, xt)

        def pair(i, _, s=s, inner=inner):
            in_turn([inner(s + 2 * i), inner(s + 2 * i + 1)])
            return 0

        if s > 1:
            lax.fori_loop(0, blocks // 2 - s, pair, 0)
        if s < ASTEPS:
            at = slice((s - 1) * 4, s * 4)
            for i, b in enumerate((s, s + 1, blocks - 2 - s, blocks - 1 - s)):
                kept[(s - 1) * 4 + i] = xt[b]
            depart(pltpu.make_async_copy(kept.at[at], kept_out.at[at], sems.at[len(sent) + s]))
    depart(pltpu.make_async_copy(mid, mid_out, sems.at[len(sent)]))
    for copy in leaving:
        copy.wait()


def block_place(b, blocks, ends, middle):
    if b < ASTEPS:
        return ends, b
    if b < blocks - ASTEPS:
        return middle, b - ASTEPS
    return ends, b - blocks + 2 * ASTEPS


def send(q_ends, q_mid, cols, out, table):
    fields = q_mid.shape[1] // ASTEPS
    peers, slots = cols.shape
    blocks = q_ends.shape[0] + q_mid.shape[0]
    lanes = out.shape[2]
    parts = slots // lanes
    for b in range(blocks):
        ref, i = block_place(b, blocks, q_ends, q_mid)
        table[b * fields : (b + 1) * fields, :] = ref[i, (ASTEPS - 1) * fields :, :]
    rows = stacked(table[...])
    half = blocks * fields
    block_of_row = iota((half, slots), 0) // fields

    def one(p, _):
        ids = cols[pl.ds(p, 1), :]
        got = mm(rows, one_hot(ids & (BLK - 1), BLK))
        got = jnp.where(block_of_row == ids // BLK, got[:half] + got[half:], 0.0)
        got = fold_rows(got, 2 * fields)
        got = got[:fields] + got[fields:]
        out[p] = jnp.concatenate([got[:, i * lanes : (i + 1) * lanes] for i in range(parts)], axis=0)
        return 0

    lax.fori_loop(0, peers, one, 0, unroll=4)


def exchange_kernel(
    recv, slot, weight, yo, nbr, coef, omix, before_in, after_in, flux_out, back, rows, tiles, hots, seas, acc, held, sems
):
    peers, per_peer, lanes = recv.shape
    links, columns = slot.shape
    fields = flux_out.shape[0]
    parts = per_peer // fields
    highs = peers * parts
    table = highs * fields
    arriving = [
        pltpu.make_async_copy(ref.at[: held.shape[1]], held.at[i], sems.at[i])
        for i, ref in enumerate((before_in, after_in))
    ]
    for copy in arriving:
        copy.start()
    rows[...] = stacked(recv[...].reshape(table, lanes))
    levels = omix.shape[0]
    eye = iota((levels, levels), 0) == iota((levels, levels), 1)
    corner = omix[0:1, 0:1] + 1.0
    top = omix[0:1, :] + jnp.where(iota((1, levels), 1) == 0, 1.0, 0.0)
    top = jnp.sum(jnp.where(eye, top, 0.0), axis=1, keepdims=True)
    high_of_row = iota((table, BLK), 0) // fields
    back_rows = iota((2 * highs, BLK), 0)
    inner = back_rows % (2 * parts)
    back_high = (back_rows // (2 * parts)) * parts + inner % parts
    pattern = iota((8, BLK), 0) % (2 * parts) // parts
    side = HO // 128
    window = 1 + 2 * side
    neighbors = nbr.shape[0]

    def surface(j, half):
        t0 = j * (BLK // 128) + half
        at = pl.ds(pl.multiple_of(t0 * 128, 128), 128)
        pad = jnp.zeros((8 - neighbors, 128), jnp.int32)
        ids = jnp.concatenate([nbr[:, at] - t0 * 128, pad], axis=0)
        cs = jnp.concatenate([coef[:, at], pad.astype(F32)], axis=0)
        middle = tiles[t0 + side]
        got = jnp.zeros((8, 128), F32)
        for t in range(window):
            pick = jnp.take_along_axis(tiles[t0 + t], ids & 127, axis=1, mode="promise_in_bounds")
            got = jnp.where(ids // 128 == t, pick, got)
        return middle[0:1] + jnp.sum(cs * (got - middle), axis=0, keepdims=True)

    def arrive(j, _):
        at = pl.ds(pl.multiple_of(j * BLK, BLK), BLK)
        parts = []

        def begin(r):
            ids = slot[r : r + 1, at]
            hot = one_hot(ids & (lanes - 1), lanes)
            hots[j, :, r * BLK : (r + 1) * BLK] = hot
            return mm(rows[...], hot)

        def finish(r, got):
            ids = slot[r : r + 1, at]
            got = jnp.where(high_of_row == ids // lanes, got[:table] + got[table:], 0.0)
            parts.append(weight[r : r + 1, at] * fold_rows(got, 2 * fields))

        last = begin(0)
        for r in range(1, links):
            got = begin(r)
            finish(r - 1, last)
            last = got
        finish(links - 1, last)
        flux = sum(parts[1:], parts[0])
        flux = flux[:fields] + flux[fields:]
        flux_out[:, at] = flux
        seas[:, at] = corner * flux[0:1]
        return 0

    lax.fori_loop(0, columns // BLK, arrive, 0, unroll=2)
    for copy in arriving:
        copy.wait()
    before, after = [jnp.sum(held[i] * top, axis=0, keepdims=True) for i in range(2)]
    acc[...] = jnp.zeros_like(acc)
    own_tiles = columns // 128
    for t in range(own_tiles + 2 * side):
        if t < side:
            line = before[:, t * 128 : (t + 1) * 128]
        elif t < side + own_tiles:
            line = yo[:, (t - side) * 128 : (t - side + 1) * 128]
        else:
            line = after[:, (t - side - own_tiles) * 128 : (t - side - own_tiles + 1) * 128]
        tiles[t] = jnp.broadcast_to(line, (8, 128))

    def base(j, _):
        at = pl.ds(pl.multiple_of(j * BLK, BLK), BLK)
        seas[:, at] += jnp.concatenate([surface(j, h) for h in range(BLK // 128)], axis=1)
        return 0

    lax.fori_loop(0, columns // BLK, base, 0, unroll=2)

    def leave(j, _):
        at = pl.ds(pl.multiple_of(j * BLK, BLK), BLK)
        sea = seas[:, at]
        left = []
        for r in range(links):
            ids, scale = slot[r : r + 1, at], weight[r : r + 1, at]
            high, low = halves(jnp.where(pattern == 1, scale, scale * sea))
            mask = back_high == ids // lanes
            both = [
                jnp.where(mask, jnp.concatenate([x.astype(F32)] * (2 * highs // 8), axis=0), 0.0).astype(BF)
                for x in (high, low)
            ]
            left.append(jnp.concatenate(both, axis=0))
        acc[...] += mm_t(jnp.concatenate(left, axis=1), hots[j])
        return 0

    lax.fori_loop(0, columns // BLK, leave, 0, unroll=2)
    back[...] = (acc[: 2 * highs] + acc[2 * highs :]).reshape(back.shape)


def settle_kernel(back, cols, surf, out, acc):
    peers, per_peer, lanes = back.shape
    parts = per_peer // 2
    blocks = surf.shape[1] // BLK
    acc[...] = jnp.zeros_like(acc)
    block_of_row = iota((blocks, lanes), 0)

    group = 4

    def one(i, _):
        left, hots = [], []
        for k, h in itertools.product(range(group), range(parts)):
            d = group * i + k
            ids = cols[pl.ds(d, 1), h * lanes : (h + 1) * lanes]
            mask = block_of_row == ids // BLK
            value = jnp.where(mask, back[d, h : h + 1, :], 0.0)
            scale = jnp.where(mask, back[d, parts + h : parts + h + 1, :], 0.0)
            left.append(stacked(jnp.concatenate([value, scale], axis=0)))
            hots.append(one_hot(ids & (BLK - 1), BLK))
        acc[...] += mm_t(jnp.concatenate(left, axis=1), jnp.concatenate(hots, axis=1))
        return 0

    lax.fori_loop(0, peers // group, one, 0)
    sums = acc[: 2 * blocks] + acc[2 * blocks :]
    base = jnp.concatenate([surf[0:1, b * BLK : (b + 1) * BLK] for b in range(blocks)], axis=0)
    value = (base + sums[:blocks]) / (1.0 + sums[blocks:])
    for b in range(blocks):
        for i in range(BLK // 128):
            row = b * (BLK // 128) + i
            out[row : row + 1, :] = value[b : b + 1, i * 128 : (i + 1) * 128]


def edge_kernel(
    y, bulk, surf, gains, lift, q_mid, cols, before, after, atm, kept_in, band, q, ends_out, outgoing,
    w, wide, sides, kept, sa, sb, ma, mb, ends, table, sems,
):
    rows = atm.shape[0]
    levels = lift.shape[1]
    fields = bulk.shape[0]
    states = y.shape[0]
    columns = y.shape[1]
    blocks = columns // BLK
    halo = ASTEPS - 1
    count = halo + ASTEPS
    total = blocks + 2 * ASTEPS
    arriving = [
        pltpu.make_async_copy(before, wide.at[0], sems.at[0]),
        pltpu.make_async_copy(after, wide.at[1], sems.at[1]),
        pltpu.make_async_copy(atm.at[:, : 2 * BLK], sides.at[0], sems.at[2]),
        pltpu.make_async_copy(atm.at[:, columns - 2 * BLK :], sides.at[1], sems.at[3]),
    ]
    bands = [pltpu.make_async_copy(band.at[i], w.at[halo + i], sems.at[4 + i]) for i in range(2 * ASTEPS)]
    keeps = pltpu.make_async_copy(kept_in, kept, sems.at[4 + 2 * ASTEPS])
    needed = [[0, 2 * ASTEPS - 1]] + [[i, 2 * ASTEPS - 1 - i] for i in range(1, ASTEPS)]
    for copy in arriving:
        copy.start()
    for group in needed:
        for i in group:
            bands[i].start()
    keeps.start()

    def place(e):
        if e < ASTEPS:
            return wide.at[0], e
        if e >= total - ASTEPS:
            return wide.at[1], e - total + ASTEPS
        return None, e - ASTEPS

    def coefs(e):
        ref, local = place(e)
        at = slice(local * BLK, (local + 1) * BLK)
        if ref is None:
            return bulk[:, at], surf[:, at]
        j = local - 1 if e < ASTEPS else local
        at = slice(j * BLK, (j + 1) * BLK)
        return ref[rows + 12 : rows + 16, at], ref[rows + 4 * j : rows + 4 * j + 4, WIDE - BLK :]

    def build(e):
        ref, local = place(e)
        origin = local * BLK + (columns - WIDE if e < ASTEPS else 0)
        j = local - 1 if e < ASTEPS else local
        at = slice(j * BLK, (j + 1) * BLK)
        ids = ref[rows : rows + 6, at].astype(jnp.int32) - origin
        k = e - 1 if e < ASTEPS else e - (total - 1) + 2 * count
        yield from band_build(ids, ref[rows + 6 : rows + 12, at], w, k)

    for copy in arriving:
        copy.wait()
    for i in range(ASTEPS):
        at = slice(i * BLK, (i + 1) * BLK)
        for side in range(2):
            x = wide[side, :rows, at]
            lifted = [x[(f + 1) * levels - 1 : (f + 1) * levels] for f in range(fields)]
            for k in range(ASTEPS - 1):
                weight = jnp.concatenate([lift[k]] * (BLK // 128), axis=1)
                for f in range(fields):
                    lifted.append(jnp.sum(x[f * levels : (f + 1) * levels] * weight, axis=0, keepdims=True))
            sa[i if side == 0 else 8 + i] = stacked(jnp.concatenate([x] + lifted, axis=0))
    for i in range(2):
        at = slice(i * BLK, (i + 1) * BLK)
        far = slice(columns - (2 - i) * BLK, columns - (1 - i) * BLK)
        sa[ASTEPS + i] = stacked(jnp.concatenate([sides[0, :, at], y[:, at]], axis=0))
        sa[6 + i] = stacked(jnp.concatenate([sides[1, :, at], y[:, far]], axis=0))

    buffers = (sa, sb)
    builds = [itertools.chain(build(1 + i), build(total - 2 - i)) for i in range(halo)]
    interleave(builds[0])
    for s in range(1, ASTEPS + 1):
        source, target = buffers[(s - 1) % 2], buffers[s % 2]
        last = s == ASTEPS

        def finish(side, i, moved, s=s, target=target, last=last):
            e = s + i if side == 0 else total - 1 - s - halo + i
            value = advance(moved[rows:], s, gains, *coefs(e))
            if last:
                q[4 * side + i] = value
                ends[4 * side + i] = stacked(moved[:rows])
            else:
                target[6 * side + i + 2 * side] = stacked(jnp.concatenate([moved[:rows], value], axis=0))

        def band_of(side, i, s=s):
            return s - 1 + i if side == 0 else count + ASTEPS - s + i

        def one(side, i, source=source, finish=finish, band_of=band_of):
            def begin():
                x2 = jnp.concatenate([source[6 * side + i + d] for d in range(3)], axis=1)
                k = band_of(side, i)
                return products(x2, (w[k, 0], w[k, 1]))

            return begin, lambda moved: finish(side, i, moved)

        if s == 1:
            for i in range(halo):
                pieces = [
                    product_pieces([source[6 * side + j + d] for d in range(3)], w.at[band_of(side, j)], m)
                    for side, j, m in ((0, i, ma), (1, halo - i, mb))
                ]
                interleave(itertools.chain(*pieces), *builds[i + 1 : i + 2])
                finish(0, i, ma[...])
                finish(1, halo - i, mb[...])
            for k in needed[0]:
                bands[k].wait()
            in_turn([one(0, halo), one(1, 0)])
            keeps.wait()
        else:
            for k in needed[s - 1]:
                bands[k].wait()
            in_turn([one(side, i) for i in range(ASTEPS) for side in range(2)])
        if not last:
            for i in range(2):
                target[ASTEPS + i] = kept[(s - 1) * 4 + i]
                target[6 + i] = kept[(s - 1) * 4 + 2 + i]
    out = pltpu.make_async_copy(ends, ends_out, sems.at[5 + 2 * ASTEPS])
    out.start()
    send(q, q_mid, cols, outgoing, table)
    out.wait()


def finish_kernel(q_ends, q_mid, vertical, ends_in, mid_in, out, ends, mid, staged, sems, osems):
    rows = ends.shape[1] // 2
    levels = rows // 2
    blocks = staged.shape[0]
    arriving = [
        pltpu.make_async_copy(mid_in, mid, sems.at[0]),
        pltpu.make_async_copy(ends_in, ends, sems.at[1]),
    ]
    for copy in arriving:
        copy.start()

    def leaving(b):
        at = slice(b * BLK, (b + 1) * BLK)
        return pltpu.make_async_copy(staged.at[b], out.at[:, at], osems.at[b])

    def one(b, p):
        ref, i = block_place(b, blocks, ends, mid)
        share, _ = block_place(b, blocks, q_ends, q_mid)

        def begin():
            qh, ql = halves(share[i])
            high = jnp.concatenate([ref[i, p * levels : (p + 1) * levels], qh], axis=0)
            low = jnp.concatenate([ref[i, rows + p * levels : rows + (p + 1) * levels], ql], axis=0)
            return mm(vertical[p], high), mm(vertical[p, :levels], low)

        def finish(value):
            staged[b, p * levels : (p + 1) * levels] = value

        return begin, finish

    middle = list(range(ASTEPS, blocks - ASTEPS))
    outer = list(range(ASTEPS)) + list(range(blocks - ASTEPS, blocks))
    for copy, group in zip(arriving, (middle, outer)):
        copy.wait()
        for start in range(0, len(group), 4):
            some = group[start : start + 4]
            in_turn([one(b, p) for b in some for p in range(2)])
            for b in some:
                leaving(b).start()
    for b in range(blocks):
        leaving(b).wait()


def sea_build(nbr, coef, b, w):
    at = pl.ds(pl.multiple_of(b * BLK, BLK), BLK)

    def store(first, size, lanes, high, low):
        w[0, first : first + size, lanes] = high
        w[1, first : first + size, lanes] = low

    return band_pieces(store, nbr[:, at] - b * BLK, coef[:, at], HO)


def sea_inner_kernel(ocean, nbr, coef, laid_out, x2, wa, wb, ma, mb, laid, sems):
    blocks = ocean.shape[1] // BLK
    around = 1 + 2 * HO // BLK
    first = -(-HO // BLK)
    count = blocks - 2 * first
    for i in range(count + around - 1):
        start = (first + i) * BLK - HO
        x2[i] = stacked(ocean[:, start : start + BLK])

    def leaving(i):
        return pltpu.make_async_copy(laid.at[i], laid_out.at[i], sems.at[i])

    def move(i, w, moved):
        yield from product_pieces([x2[i + d] for d in range(around)], w, moved)

    interleave(sea_build(nbr, coef, first, wa))

    def one(k, _):
        i = 2 * k
        interleave(sea_build(nbr, coef, first + i + 1, wb), move(i, wa, ma))
        interleave(sea_build(nbr, coef, jnp.minimum(i + 2, count - 1) + first, wa), move(i + 1, wb, mb))
        laid[i] = stacked(ma[...])
        laid[i + 1] = stacked(mb[...])
        leaving(i).start()
        leaving(i + 1).start()
        return 0

    lax.fori_loop(0, count // 2, one, 0)

    def done(i, _):
        leaving(i).wait()
        return 0

    lax.fori_loop(0, count, done, 0)


def sea_outer_kernel(
    before, after, nbr, coef, vertical, mix, flux, ocean, laid_in, out, ends, x2, wa, wb, ma, mb, laid, staged, sems, osems
):
    fields = flux.shape[0]
    rows, columns = ocean.shape
    levels = rows // fields
    blocks = columns // BLK
    around = 1 + 2 * HO // BLK
    first = -(-HO // BLK)
    count = blocks - 2 * first
    width = ends.shape[2]
    arriving = [
        pltpu.make_async_copy(ocean.at[:, :width], ends.at[0], sems.at[0]),
        pltpu.make_async_copy(ocean.at[:, columns - width :], ends.at[1], sems.at[1]),
        pltpu.make_async_copy(laid_in, laid.at[first : first + count], sems.at[2]),
    ]
    for copy in arriving:
        copy.start()
    eye = iota((levels, levels), 0) == iota((levels, levels), 1)
    top = jnp.broadcast_to((mix[...] + jnp.where(eye, 1.0, 0.0))[:, 0:1], (levels, BLK))
    outer = list(range(first)) + list(range(blocks - first, blocks))
    bands, sums = (wa, wb), (ma, mb)
    interleave(sea_build(nbr, coef, outer[0], wa))
    arriving[0].wait()
    arriving[1].wait()
    spans = ((before, -HO, HO), (ends.at[0], 0, width), (ends.at[1], columns - width, width), (after, columns, HO))
    held = list(range(first + around - 1)) + list(range(blocks - first, blocks + around - 1))
    for i, e in enumerate(held):
        start = e * BLK - HO
        pieces = []
        for ref, begin, size in spans:
            lo, hi = max(start, begin), min(start + BLK, begin + size)
            if lo < hi:
                pieces.append(ref[:, lo - begin : hi - begin])
        x2[i] = stacked(pieces[0] if len(pieces) == 1 else jnp.concatenate(pieces, axis=1))

    def move(b, w, moved):
        yield from product_pieces([x2[held.index(b + d)] for d in range(around)], w, moved)

    for k, b in enumerate(outer):
        works = [move(b, bands[k % 2], sums[k % 2])]
        if k + 1 < len(outer):
            works.insert(0, sea_build(nbr, coef, outer[k + 1], bands[(k + 1) % 2]))
        interleave(*works)
        laid[b] = stacked(sums[k % 2][...])
    arriving[2].wait()
    pair = 2 * levels

    def leaving(b):
        at = pl.ds(pl.multiple_of(b * BLK, BLK), BLK)
        return pltpu.make_async_copy(staged.at[b], out.at[:, at], osems.at[b])

    def mixed(b, p):
        at = pl.ds(pl.multiple_of(b * BLK, BLK), BLK)

        def begin():
            high = laid[b, p * pair : (p + 1) * pair]
            low = laid[b, rows + p * pair : rows + (p + 1) * pair]
            return mm(vertical[...], high), mm(vertical[:pair], low)

        def finish(value):
            for k in range(2):
                f = 2 * p + k
                staged[b, f * levels : (f + 1) * levels] = (
                    value[k * levels : (k + 1) * levels] + top * flux[f : f + 1, at]
                )

        return begin, finish

    def four(i, _):
        in_turn([mixed(4 * i + k, p) for k in range(4) for p in range(fields // 2)])
        for k in range(4):
            leaving(4 * i + k).start()
        return 0

    lax.fori_loop(0, blocks // 4, four, 0)

    def done(b, _):
        leaving(b).wait()
        return 0

    lax.fori_loop(0, blocks, done, 0)


def after_all(value, *others):
    return lax.optimization_barrier((value, *others))[0]


def per_device(
    atm_state,
    atm_surface,
    bulk_coef,
    atm_nbr,
    atm_nbr_coef,
    atm_mix,
    ocean_state,
    ocean_nbr,
    ocean_nbr_coef,
    ocean_mix,
    send_cols,
    remap_slot,
    remap_weight,
):
    fields, la, columns = atm_state.shape
    lo, cells = ocean_state.shape[1:]
    blocks = columns // BLK
    rows = fields * la
    states = fields * ASTEPS
    picked = send_cols[0]
    peers, slots = picked.shape
    lanes = min(BLK, slots)
    parts = slots // lanes
    atm = atm_state.reshape(rows, columns)
    ocean = ocean_state.reshape(fields * lo, cells)
    depth = lax.axis_size(AXES)
    up = [(i, (i + 1) % depth) for i in range(depth)]
    down = [(j, i) for i, j in up]
    window = BLK + 2 * HA
    vmem = pl.BlockSpec(memory_space=pltpu.VMEM)
    anywhere = pl.BlockSpec(memory_space=pl.ANY)

    depth_k = rows + states
    half = fields // 2
    p_of = np.arange(half)[:, None, None]
    r_of = np.arange(2 * la)[None, :, None]
    c_of = np.arange(2 * la + states)[None, None, :]
    code = np.where(
        c_of < 2 * la,
        (c_of // la == r_of // la) * 1,
        ((c_of - 2 * la) % fields == 2 * p_of + r_of // la) * (2 + (c_of - 2 * la) // fields),
    )
    code = np.broadcast_to(code, (half, 2 * la, 2 * la + states)).astype(np.int32)
    spread = ((c_of[0] % la == np.arange(la)[:, None]) & (c_of[0] < 2 * la)).astype(np.float32)
    sea_spread = (np.arange(2 * lo)[None, :] % lo == np.arange(lo)[:, None]).astype(np.float32)

    wide_rows = rows + 16
    sea_rows = fields * lo
    halo_shapes = (shape((rows, WIDE)),) * 2 + (shape((sea_rows, HO)),) * 2
    wide_first, wide_last, sea_first, sea_last = call(
        pack_kernel,
        (shape((wide_rows, WIDE)),) * 2 + halo_shapes[2:],
        in_specs=[vmem] * 4 + [anywhere] * 2,
        out_specs=(anywhere,) * 4,
        scratch=[pltpu.VMEM(h.shape, F32) for h in halo_shapes]
        + [pltpu.VMEM((2, 16, WIDE), F32), pltpu.SemaphoreType.DMA((10,))],
    )(atm_nbr, atm_nbr_coef, bulk_coef, atm_surface, atm, ocean)
    wide_before = lax.ppermute(wide_last, AXES, up)
    wide_after = lax.ppermute(wide_first, AXES, down)

    y, yo, gains, lift, vertical, sea_vertical = call(
        prepare_kernel(fields),
        (
            shape((states, columns)),
            shape((1, columns)),
            shape((states, 128)),
            shape((ASTEPS - 1, la, 128)),
            shape((half, 4 * la, 2 * la + states), BF),
            shape((4 * lo, 2 * lo), BF),
        ),
        in_specs=[vmem] * 6 + [anywhere],
        scratch=[pltpu.VMEM((lo, cells), F32), pltpu.SemaphoreType.DMA(())],
    )(
        after_all(atm_mix, wide_first),
        ocean_mix,
        atm,
        jnp.asarray(spread),
        jnp.asarray(code),
        jnp.asarray(sea_spread),
        ocean,
    )

    ends = 2 * ASTEPS
    q_mid, kept, mid, band = call(
        interior_kernel,
        (
            shape((blocks - ends, states, BLK)),
            shape((4 * (ASTEPS - 1), 2 * depth_k, BLK), BF),
            shape((blocks - ends, 2 * rows, BLK), BF),
            shape((ends, 2, window, BLK), BF),
        ),
        in_specs=[vmem] * 7,
        out_specs=(vmem, anywhere, anywhere, anywhere),
        scratch=[
            pltpu.VMEM((blocks, 2, window, BLK), BF),
            pltpu.VMEM((blocks, 2 * depth_k, BLK), BF),
            pltpu.VMEM((blocks, 2 * depth_k, BLK), BF),
            pltpu.VMEM((depth_k, BLK), F32),
            pltpu.VMEM((depth_k, BLK), F32),
            pltpu.VMEM((4 * (ASTEPS - 1), 2 * depth_k, BLK), BF),
            pltpu.VMEM((blocks - ends, 2 * rows, BLK), BF),
            pltpu.SemaphoreType.DMA((ends + ASTEPS,)),
        ],
    )(atm, y, atm_nbr, atm_nbr_coef, bulk_coef, atm_surface, gains)

    sea_blocks = cells // BLK
    outer = -(-HO // BLK)
    around = 1 + 2 * HO // BLK
    sea_window = BLK + 2 * HO
    inner = sea_blocks - 2 * outer
    sea_inner = call(
        sea_inner_kernel,
        shape((inner, 2 * sea_rows, BLK), BF),
        in_specs=[vmem] * 3,
        out_specs=anywhere,
        scratch=[
            pltpu.VMEM((inner + around - 1, 2 * sea_rows, BLK), BF),
            pltpu.VMEM((2, sea_window, BLK), BF),
            pltpu.VMEM((2, sea_window, BLK), BF),
            pltpu.VMEM((sea_rows, BLK), F32),
            pltpu.VMEM((sea_rows, BLK), F32),
            pltpu.VMEM((inner, 2 * sea_rows, BLK), BF),
            pltpu.SemaphoreType.DMA((inner,)),
        ],
    )(ocean, after_all(ocean_nbr, q_mid), ocean_nbr_coef)

    sea_first, sea_last, wide_before, wide_after = lax.optimization_barrier(
        (sea_first, sea_last, wide_before, wide_after, sea_inner)
    )[:4]
    sea_before = lax.ppermute(sea_last, AXES, up)
    sea_after = lax.ppermute(sea_first, AXES, down)

    q_ends, tips, outgoing = call(
        edge_kernel,
        (
            shape((ends, states, BLK)),
            shape((ends, 2 * rows, BLK), BF),
            shape((peers, parts * fields, lanes)),
        ),
        in_specs=[vmem] * 7 + [anywhere] * 5,
        out_specs=(vmem, anywhere, vmem),
        scratch=[
            pltpu.VMEM((2 * (2 * ASTEPS - 1), 2, window, BLK), BF),
            pltpu.VMEM((2, wide_rows, WIDE), F32),
            pltpu.VMEM((2, rows, 2 * BLK), F32),
            pltpu.VMEM((4 * (ASTEPS - 1), 2 * depth_k, BLK), BF),
            pltpu.VMEM((12, 2 * depth_k, BLK), BF),
            pltpu.VMEM((12, 2 * depth_k, BLK), BF),
            pltpu.VMEM((depth_k, BLK), F32),
            pltpu.VMEM((depth_k, BLK), F32),
            pltpu.VMEM((ends, 2 * rows, BLK), BF),
            pltpu.VMEM((blocks * fields, BLK), F32),
            pltpu.SemaphoreType.DMA((6 + 2 * ASTEPS,)),
        ],
    )(after_all(y, sea_inner), bulk_coef, atm_surface, gains, lift, q_mid, picked, wide_before, wide_after, atm, kept, band)

    sea_before, sea_after, outgoing = lax.optimization_barrier((sea_before, sea_after, outgoing))
    received = lax.all_to_all(outgoing, AXES, split_axis=0, concat_axis=0, tiled=True)

    atm_final = call(
        finish_kernel,
        shape((rows, columns)),
        in_specs=[vmem] * 3 + [anywhere] * 2,
        out_specs=anywhere,
        scratch=[
            pltpu.VMEM((ends, 2 * rows, BLK), BF),
            pltpu.VMEM((blocks - ends, 2 * rows, BLK), BF),
            pltpu.VMEM((blocks, rows, BLK), F32),
            pltpu.SemaphoreType.DMA((2,)),
            pltpu.SemaphoreType.DMA((blocks,)),
        ],
    )(after_all(q_ends, outgoing), q_mid, vertical, tips, mid)

    flux, back = call(
        exchange_kernel,
        (shape((fields, cells)), shape((peers, 2 * parts, lanes))),
        in_specs=[vmem] * 7 + [anywhere] * 2,
        scratch=[
            pltpu.VMEM((2 * peers * parts * fields, lanes), BF),
            pltpu.VMEM((cells // 128 + 2 * HO // 128, 8, 128), F32),
            pltpu.VMEM((cells // BLK, lanes, remap_slot.shape[0] * BLK), BF),
            pltpu.VMEM((1, cells), F32),
            pltpu.VMEM((4 * peers * parts, lanes), F32),
            pltpu.VMEM((2, lo, HO), F32),
            pltpu.SemaphoreType.DMA((2,)),
        ],
    )(
        after_all(received, atm_final),
        remap_slot,
        remap_weight,
        yo,
        ocean_nbr,
        ocean_nbr_coef,
        ocean_mix,
        sea_before,
        sea_after,
    )
    returned = lax.all_to_all(back, AXES, split_axis=0, concat_axis=0, tiled=True)

    ocean_final = call(
        sea_outer_kernel,
        shape((sea_rows, cells)),
        in_specs=[vmem] * 7 + [anywhere] * 2,
        out_specs=anywhere,
        scratch=[
            pltpu.VMEM((2, sea_rows, (outer + around - 1) * BLK - HO), F32),
            pltpu.VMEM((2 * (outer + around - 1), 2 * sea_rows, BLK), BF),
            pltpu.VMEM((2, sea_window, BLK), BF),
            pltpu.VMEM((2, sea_window, BLK), BF),
            pltpu.VMEM((sea_rows, BLK), F32),
            pltpu.VMEM((sea_rows, BLK), F32),
            pltpu.VMEM((sea_blocks, 2 * sea_rows, BLK), BF),
            pltpu.VMEM((sea_blocks, sea_rows, BLK), F32),
            pltpu.SemaphoreType.DMA((3,)),
            pltpu.SemaphoreType.DMA((sea_blocks,)),
        ],
    )(
        after_all(sea_before, back),
        sea_after,
        ocean_nbr,
        ocean_nbr_coef,
        sea_vertical,
        ocean_mix,
        flux,
        ocean,
        sea_inner,
    )

    surface_temp = call(
        settle_kernel,
        shape((columns // 128, 128)),
        in_specs=[vmem] * 3,
        scratch=[pltpu.VMEM((4 * blocks, BLK), F32)],
    )(after_all(returned, ocean_final), picked, atm_surface)

    return (
        atm_final.reshape(fields, la, columns),
        ocean_final.reshape(fields, lo, cells),
        surface_temp.reshape(columns),
    )


def solution(mesh):
    placed = (
        P(None, None, AXES),
        P(None, AXES),
        P(None, AXES),
        P(None, AXES),
        P(None, AXES),
        P(),
        P(None, None, AXES),
        P(None, AXES),
        P(None, AXES),
        P(),
        P(AXES, None, None),
        P(None, AXES),
        P(None, AXES),
    )
    return jax.shard_map(
        per_device,
        mesh=mesh,
        in_specs=placed,
        out_specs=(P(None, None, AXES), P(None, None, AXES), P(AXES)),
        check_vma=False,
    )
```

```python
import itertools

import numpy as np

import jax
import jax.numpy as jnp
from jax import lax
from jax.experimental import pallas as pl
from jax.experimental.pallas import tpu as pltpu
from jax.sharding import PartitionSpec as P

ASTEPS = 4
HA = 256
HO = 384
BLK = 256
WIDE = ASTEPS * HA
BF = jnp.bfloat16
F32 = jnp.float32
VMEM_BYTES = 63 * 1024 * 1024
AXES = ("sec", "blk")


def call(body, outs, *, in_specs=None, out_specs=None, scratch=(), flops=10**6, moved=10**4, aliases=None):
    vmem = pl.BlockSpec(memory_space=pltpu.VMEM)
    return pl.pallas_call(
        body,
        out_shape=outs,
        in_specs=in_specs,
        out_specs=jax.tree.map(lambda _: vmem, outs) if out_specs is None else out_specs,
        scratch_shapes=list(scratch),
        input_output_aliases=aliases or {},
        compiler_params=pltpu.CompilerParams(vmem_limit_bytes=VMEM_BYTES),
        cost_estimate=pl.CostEstimate(flops=flops, bytes_accessed=moved, transcendentals=0),
    )


def shape(dims, dtype=F32):
    return jax.ShapeDtypeStruct(dims, dtype)


def halves(x):
    high = x.astype(BF)
    return high, (x - high.astype(F32)).astype(BF)


def stacked(x):
    return jnp.concatenate(halves(x), axis=0)


def mm(a, b):
    return jnp.dot(a, b, preferred_element_type=F32)


def mm_t(a, b):
    return lax.dot_general(a, b, (((1,), (1,)), ((), ())), preferred_element_type=F32)


def products(x2, w2):
    return mm(x2, w2[0]), mm(x2[: x2.shape[0] // 2], w2[1])


def summed(parts):
    wide, rest = parts
    rows = rest.shape[0]
    return wide[:rows] + wide[rows:] + rest


def in_turn(works):
    waiting = None
    for begin, finish in works:
        parts = begin()
        if waiting is not None:
            waiting[1](summed(waiting[0]))
        waiting = (parts, finish)
    waiting[1](summed(waiting[0]))


def product_pieces(x2s, w2, result):
    rows = x2s[0].shape[0] // 2
    for t, x2 in enumerate(x2s):
        at = slice(t * BLK, (t + 1) * BLK)
        wide = mm(x2, w2.at[0][at])
        part = wide[:rows] + wide[rows:]
        result[...] = part if t == 0 else result[...] + part
        yield
        result[...] += mm(x2[:rows], w2.at[1][at])
        yield


def interleave(*works):
    works = list(works)
    while works:
        works = [w for w in works if next(w, w) is not w]


def iota(dims, axis):
    return lax.broadcasted_iota(jnp.int32, dims, axis)


def build_band(*args):
    for _ in band_pieces(*args):
        pass


def band_pieces(store, nbr, coef, halo):
    rows = BLK + 2 * halo
    count = nbr.shape[0]
    ids = [nbr[k : k + 1] for k in range(count)]
    cs = [coef[k : k + 1] for k in range(count)]
    rest = 1.0 - sum(cs[1:], cs[0])
    for k in range(count - 1, 0, -1):
        alive = jnp.ones_like(ids[k]) > 0
        for j in range(k):
            same = jnp.logical_and(ids[k] == ids[j], alive)
            cs[j] = cs[j] + jnp.where(same, cs[k], 0.0)
            alive = jnp.logical_and(alive, jnp.logical_not(same))
        ids[k] = jnp.where(alive, ids[k], -1)
    lanes = 128
    step = 16
    base = iota((step, lanes), 0).astype(F32)
    parts = [halves(c) for c in cs + [rest]]

    def wide(x, at):
        return jnp.broadcast_to(x[:, at].astype(F32), (step, lanes)).astype(BF)

    for half in range(BLK // lanes):
        at = slice(half * lanes, (half + 1) * lanes)
        highs = [wide(p[0], at) for p in parts]
        lows = [wide(p[1], at) for p in parts]
        own = (iota((step, lanes), 1) - iota((step, lanes), 0)).astype(F32).astype(BF)
        zero = jnp.zeros((step, lanes), BF)
        for tile in range(0, rows, BLK):
            near = [wide((i - tile).astype(F32), at) for i in ids]
            for first in range(tile, tile + BLK, step):
                high, low = zero, zero
                if half * lanes - step < first < half * lanes + lanes + 2 * halo:
                    offset = first - halo - half * lanes
                    if 0 <= offset < lanes:
                        same = own == jnp.full((step, lanes), offset, BF)
                        high = jnp.where(same, highs[-1], zero)
                        low = jnp.where(same, lows[-1], zero)
                    here = (base + float(first - tile)).astype(BF)
                    for k in range(count):
                        same = here == near[k]
                        high = jnp.where(same, highs[k], high)
                        low = jnp.where(same, lows[k], low)
                store(first, step, at, high, low)
            yield


def one_hot(ids, rows):
    lanes = ids.shape[1]
    wide = jnp.broadcast_to(ids.astype(F32), (rows, lanes)).astype(BF)
    here = iota((rows, lanes), 0).astype(F32).astype(BF)
    return jnp.where(here == wide, jnp.ones((rows, lanes), BF), jnp.zeros((rows, lanes), BF))


def fold_rows(x, height):
    total = x[:height]
    for first in range(height, x.shape[0], height):
        total = total + x[first : first + height]
    return total


def pack_kernel(nbr, coef, bulk, surf, atm, sea, wide_first, wide_last, sea_first, sea_last, *refs):
    held, lists, sems = refs[:4], refs[4], refs[5]
    rows, columns = atm.shape
    cells = sea.shape[1]
    sources = (
        atm.at[:, :WIDE],
        atm.at[:, columns - WIDE :],
        sea.at[:, :HO],
        sea.at[:, cells - HO :],
    )
    targets = (wide_first.at[:rows], wide_last.at[:rows], sea_first, sea_last)
    arriving = [pltpu.make_async_copy(x, held[i], sems.at[i]) for i, x in enumerate(sources)]
    leaving = [pltpu.make_async_copy(held[i], x, sems.at[4 + i]) for i, x in enumerate(targets)]
    for copy in arriving:
        copy.start()
    need = WIDE - BLK
    for i, first in enumerate((0, columns - need)):
        at = slice(first, first + need)
        lists[i, 0:6, :need] = nbr[:, at].astype(F32)
        lists[i, 6:12, :need] = coef[:, at]
        lists[i, 12:16, :need] = bulk[:, at]
        lists[i, 12:16, need:] = jnp.zeros((4, BLK), F32)
        for j in range(ASTEPS - 1):
            lists[i, 4 * j : 4 * j + 4, need:] = surf[:, first + j * BLK : first + (j + 1) * BLK]
    for i, target in enumerate((wide_first, wide_last)):
        copy = pltpu.make_async_copy(lists.at[i], target.at[rows:], sems.at[8 + i])
        copy.start()
        leaving.append(copy)
    for here, there in zip(arriving, leaving[:4]):
        here.wait()
        there.start()
    for copy in leaving:
        copy.wait()


def prepare_kernel(fields):
    def body(
        mix, omix, atm, spread, code, sea_spread, sea, y, yo, gains, lift, vertical, sea_vertical, top, sem
    ):
        la = mix.shape[0]
        columns = atm.shape[1]
        copy = pltpu.make_async_copy(sea.at[: omix.shape[0], :], top, sem)
        copy.start()
        eye = iota((la, la), 0) == iota((la, la), 1)
        step = mix[...] + jnp.where(eye, 1.0, 0.0)

        def dot(a, b):
            return jnp.dot(a, b, precision=lax.Precision.HIGHEST, preferred_element_type=F32)

        def col(r, same):
            return jnp.sum(jnp.where(same, r, 0.0), axis=1, keepdims=True)

        def row(c, same):
            return jnp.sum(jnp.where(same, c, 0.0), axis=0, keepdims=True)

        twice = dot(step, step)
        fourth = dot(twice, twice)
        rows_up = [step[la - 1 : la, :]]
        cols_up = [step[:, la - 1 : la]]
        for _ in range(ASTEPS - 2):
            rows_up.append(jnp.sum(step * col(rows_up[-1], eye), axis=0, keepdims=True))
        for _ in range(ASTEPS - 1):
            cols_up.append(jnp.sum(step * row(cols_up[-1], eye), axis=1, keepdims=True))
        slot = iota((fields * ASTEPS, 128), 0) // fields
        lane = iota((fields * ASTEPS, 128), 1)
        value = jnp.zeros((fields * ASTEPS, 128), F32)
        for s in range(1, ASTEPS + 1):
            column = jnp.where(slot == s - 1, 1.0, 0.0)
            for j in range(1, ASTEPS):
                column = jnp.where(slot == s - 1 + j, rows_up[j - 1][:, la - 1 : la], column)
            value = jnp.where(lane == s - 1, column, value)
        gains[...] = value

        spreaded = dot(jnp.concatenate([fourth] * 2, axis=0), spread[...])
        for p in range(fields // 2):
            filled = jnp.where(code[p] == 1, spreaded, 0.0)
            for m in range(ASTEPS):
                tall = jnp.concatenate([cols_up[ASTEPS - 1 - m]] * 2, axis=0)
                filled = jnp.where(code[p] == 2 + m, tall, filled)
            vertical[p] = stacked(filled)
        lo = omix.shape[0]
        sea_eye = iota((lo, lo), 0) == iota((lo, lo), 1)
        sea_step = omix[...] + jnp.where(sea_eye, 1.0, 0.0)
        spreaded = dot(jnp.concatenate([sea_step] * 2, axis=0), sea_spread[...])
        blocks = (iota((2 * lo, 2 * lo), 0) >= lo) == (iota((2 * lo, 2 * lo), 1) >= lo)
        sea_vertical[...] = stacked(jnp.where(blocks, spreaded, 0.0))

        weights = [jnp.broadcast_to(col(r, eye), (la, 128)) for r in rows_up]
        for k, weight in enumerate(weights):
            lift[k] = weight
        sea_weight = jnp.broadcast_to(col(sea_step[0:1, :], sea_eye), (lo, 128))
        copy.wait()
        for start in range(0, columns, 128):
            at = slice(start, start + 128)
            for f in range(fields):
                x = atm[f * la : (f + 1) * la, at]
                y[f : f + 1, at] = x[la - 1 : la]
                for k in range(1, ASTEPS):
                    y[k * fields + f : k * fields + f + 1, at] = jnp.sum(
                        x * weights[k - 1], axis=0, keepdims=True
                    )
            yo[:, at] = jnp.sum(top[:, at] * sea_weight, axis=0, keepdims=True)

    return body


def band_build(ids, coef, w, k):
    def store(first, step, lanes, high, low):
        w[k, 0, first : first + step, lanes] = high
        w[k, 1, first : first + step, lanes] = low

    return band_pieces(store, ids, coef, HA)


def advance(moved, s, gains, bulk, surf):
    fields = bulk.shape[0]
    states = moved.shape[0]
    slot = iota((states, BLK), 0) // fields
    flux = bulk * (surf - moved[(s - 1) * fields : s * fields])
    kept = jnp.where(slot == s - 1, 0.0, moved)
    return kept + gains[:, s - 1 : s] * jnp.concatenate([flux] * ASTEPS, axis=0)


def interior_kernel(
    atm, y, nbr, coef, bulk, surf, gains, q, kept_out, mid_out, band, w, sa, sb, ma, mb, kept, mid, sems
):
    rows, columns = atm.shape
    states = y.shape[0]
    height = rows + states
    blocks = columns // BLK
    sent = list(range(ASTEPS)) + list(range(blocks - ASTEPS, blocks))
    leaving = []

    def depart(copy):
        copy.start()
        leaving.append(copy)

    def build(b):
        at = slice(b * BLK, (b + 1) * BLK)
        yield from band_build(nbr[:, at] - b * BLK, coef[:, at], w, b)

    def split(b):
        at = slice(b * BLK, (b + 1) * BLK)
        sa[b] = stacked(jnp.concatenate([atm[:, at], y[:, at]], axis=0))
        yield

    def pieces(b, moved):
        yield from product_pieces([sa[b + d] for d in (-1, 0, 1)], w.at[b], moved)

    def finish(b, s, moved, target):
        at = pl.ds(pl.multiple_of(b * BLK, BLK), BLK)
        value = advance(moved[rows:], s, gains, bulk[:, at], surf[:, at])
        if s == ASTEPS:
            q[b - ASTEPS] = value
            mid[b - ASTEPS] = stacked(moved[:rows])
        else:
            high, low = halves(moved[:rows])
            zh, zl = halves(value)
            target[b] = jnp.concatenate([high, zh, low, zl], axis=0)

    interleave(itertools.chain(*[split(b) for b in range(4)]))
    interleave(build(1))
    interleave(build(2))
    for i in range(blocks // 2 - 1):
        b = 2 * i + 1
        nexts = [b + 2, b + 3] if b + 3 < blocks - 1 else [0, blocks - 1]
        works = [itertools.chain(pieces(b, ma), pieces(b + 1, mb)), itertools.chain(*[build(k) for k in nexts])]
        if b + 4 < blocks:
            works.append(itertools.chain(split(b + 3), split(b + 4)))
        interleave(*works)
        finish(b, 1, ma[...], sb)
        finish(b + 1, 1, mb[...], sb)
    for i, b in enumerate(sent):
        depart(pltpu.make_async_copy(w.at[b], band.at[i], sems.at[i]))

    for s in range(1, ASTEPS + 1):
        xs, xt = (sa, sb) if s % 2 else (sb, sa)

        def inner(b, s=s, xs=xs, xt=xt):
            def begin():
                x2 = jnp.concatenate([xs[b - 1], xs[b], xs[b + 1]], axis=1)
                return products(x2, (w[b, 0], w[b, 1]))

            return begin, lambda moved: finish(b, s, moved, xt)

        def pair(i, _, s=s, inner=inner):
            in_turn([inner(s + 2 * i), inner(s + 2 * i + 1)])
            return 0

        if s > 1:
            lax.fori_loop(0, blocks // 2 - s, pair, 0)
        if s < ASTEPS:
            at = slice((s - 1) * 4, s * 4)
            for i, b in enumerate((s, s + 1, blocks - 2 - s, blocks - 1 - s)):
                kept[(s - 1) * 4 + i] = xt[b]
            depart(pltpu.make_async_copy(kept.at[at], kept_out.at[at], sems.at[len(sent) + s]))
    depart(pltpu.make_async_copy(mid, mid_out, sems.at[len(sent)]))
    for copy in leaving:
        copy.wait()


def block_place(b, blocks, ends, middle):
    if b < ASTEPS:
        return ends, b
    if b < blocks - ASTEPS:
        return middle, b - ASTEPS
    return ends, b - blocks + 2 * ASTEPS


def send(q_ends, q_mid, cols, out, table):
    fields = q_mid.shape[1] // ASTEPS
    peers, slots = cols.shape
    blocks = q_ends.shape[0] + q_mid.shape[0]
    lanes = out.shape[2]
    parts = slots // lanes
    for b in range(blocks):
        ref, i = block_place(b, blocks, q_ends, q_mid)
        table[b * fields : (b + 1) * fields, :] = ref[i, (ASTEPS - 1) * fields :, :]
    rows = stacked(table[...])
    half = blocks * fields
    block_of_row = iota((half, slots), 0) // fields

    def one(p, _):
        ids = cols[pl.ds(p, 1), :]
        got = mm(rows, one_hot(ids & (BLK - 1), BLK))
        got = jnp.where(block_of_row == ids // BLK, got[:half] + got[half:], 0.0)
        got = fold_rows(got, 2 * fields)
        got = got[:fields] + got[fields:]
        out[p] = jnp.concatenate([got[:, i * lanes : (i + 1) * lanes] for i in range(parts)], axis=0)
        return 0

    lax.fori_loop(0, peers, one, 0, unroll=4)


def sea_row_kernel(yo, nbr, coef, omix, before_in, after_in, out, tiles, held, sems):
    columns = yo.shape[1]
    arriving = [
        pltpu.make_async_copy(ref.at[: held.shape[1]], held.at[i], sems.at[i])
        for i, ref in enumerate((before_in, after_in))
    ]
    for copy in arriving:
        copy.start()
    levels = omix.shape[0]
    eye = iota((levels, levels), 0) == iota((levels, levels), 1)
    top = omix[0:1, :] + jnp.where(iota((1, levels), 1) == 0, 1.0, 0.0)
    top = jnp.sum(jnp.where(eye, top, 0.0), axis=1, keepdims=True)
    side = HO // 128
    window = 1 + 2 * side
    neighbors = nbr.shape[0]
    for copy in arriving:
        copy.wait()
    before, after = [jnp.sum(held[i] * top, axis=0, keepdims=True) for i in range(2)]
    own_tiles = columns // 128
    for t in range(own_tiles + 2 * side):
        if t < side:
            line = before[:, t * 128 : (t + 1) * 128]
        elif t < side + own_tiles:
            line = yo[:, (t - side) * 128 : (t - side + 1) * 128]
        else:
            line = after[:, (t - side - own_tiles) * 128 : (t - side - own_tiles + 1) * 128]
        tiles[t] = jnp.broadcast_to(line, (8, 128))

    def surface(j, half):
        t0 = j * (BLK // 128) + half
        at = pl.ds(pl.multiple_of(t0 * 128, 128), 128)
        pad = jnp.zeros((8 - neighbors, 128), jnp.int32)
        ids = jnp.concatenate([nbr[:, at] - t0 * 128, pad], axis=0)
        cs = jnp.concatenate([coef[:, at], pad.astype(F32)], axis=0)
        middle = tiles[t0 + side]
        got = jnp.zeros((8, 128), F32)
        for t in range(window):
            pick = jnp.take_along_axis(tiles[t0 + t], ids & 127, axis=1, mode="promise_in_bounds")
            got = jnp.where(ids // 128 == t, pick, got)
        return middle[0:1] + jnp.sum(cs * (got - middle), axis=0, keepdims=True)

    def base(j, _):
        at = pl.ds(pl.multiple_of(j * BLK, BLK), BLK)
        out[:, at] = jnp.concatenate([surface(j, h) for h in range(BLK // 128)], axis=1)
        return 0

    lax.fori_loop(0, columns // BLK, base, 0, unroll=2)


def exchange_kernel(
    recv, slot, weight, base, omix, flux_out, back, rows, hots, seas, acc
):
    peers, per_peer, lanes = recv.shape
    links, columns = slot.shape
    fields = flux_out.shape[0]
    parts = per_peer // fields
    highs = peers * parts
    table = highs * fields
    rows[...] = stacked(recv[...].reshape(table, lanes))
    corner = omix[0:1, 0:1] + 1.0
    high_of_row = iota((table, BLK), 0) // fields
    back_rows = iota((2 * highs, BLK), 0)
    inner = back_rows % (2 * parts)
    back_high = (back_rows // (2 * parts)) * parts + inner % parts
    pattern = iota((8, BLK), 0) % (2 * parts) // parts

    def arrive(j, _):
        at = pl.ds(pl.multiple_of(j * BLK, BLK), BLK)
        parts = []

        def begin(r):
            ids = slot[r : r + 1, at]
            hot = one_hot(ids & (lanes - 1), lanes)
            hots[j, :, r * BLK : (r + 1) * BLK] = hot
            return mm(rows[...], hot)

        def finish(r, got):
            ids = slot[r : r + 1, at]
            got = jnp.where(high_of_row == ids // lanes, got[:table] + got[table:], 0.0)
            parts.append(weight[r : r + 1, at] * fold_rows(got, 2 * fields))

        last = begin(0)
        for r in range(1, links):
            got = begin(r)
            finish(r - 1, last)
            last = got
        finish(links - 1, last)
        flux = sum(parts[1:], parts[0])
        flux = flux[:fields] + flux[fields:]
        flux_out[:, at] = flux
        seas[:, at] = base[:, at] + corner * flux[0:1]
        return 0

    lax.fori_loop(0, columns // BLK, arrive, 0, unroll=2)
    acc[...] = jnp.zeros_like(acc)
    def leave(j, _):
        at = pl.ds(pl.multiple_of(j * BLK, BLK), BLK)
        sea = seas[:, at]
        left = []
        for r in range(links):
            ids, scale = slot[r : r + 1, at], weight[r : r + 1, at]
            high, low = halves(jnp.where(pattern == 1, scale, scale * sea))
            mask = back_high == ids // lanes
            both = [
                jnp.where(mask, jnp.concatenate([x.astype(F32)] * (2 * highs // 8), axis=0), 0.0).astype(BF)
                for x in (high, low)
            ]
            left.append(jnp.concatenate(both, axis=0))
        acc[...] += mm_t(jnp.concatenate(left, axis=1), hots[j])
        return 0

    lax.fori_loop(0, columns // BLK, leave, 0, unroll=2)
    back[...] = (acc[: 2 * highs] + acc[2 * highs :]).reshape(back.shape)


def settle_kernel(back, cols, surf, out, acc):
    peers, per_peer, lanes = back.shape
    parts = per_peer // 2
    blocks = surf.shape[1] // BLK
    acc[...] = jnp.zeros_like(acc)
    block_of_row = iota((blocks, lanes), 0)

    group = 4

    def one(i, _):
        left, hots = [], []
        for k, h in itertools.product(range(group), range(parts)):
            d = group * i + k
            ids = cols[pl.ds(d, 1), h * lanes : (h + 1) * lanes]
            mask = block_of_row == ids // BLK
            value = jnp.where(mask, back[d, h : h + 1, :], 0.0)
            scale = jnp.where(mask, back[d, parts + h : parts + h + 1, :], 0.0)
            left.append(stacked(jnp.concatenate([value, scale], axis=0)))
            hots.append(one_hot(ids & (BLK - 1), BLK))
        acc[...] += mm_t(jnp.concatenate(left, axis=1), jnp.concatenate(hots, axis=1))
        return 0

    lax.fori_loop(0, peers // group, one, 0)
    sums = acc[: 2 * blocks] + acc[2 * blocks :]
    base = jnp.concatenate([surf[0:1, b * BLK : (b + 1) * BLK] for b in range(blocks)], axis=0)
    value = (base + sums[:blocks]) / (1.0 + sums[blocks:])
    for b in range(blocks):
        for i in range(BLK // 128):
            row = b * (BLK // 128) + i
            out[row : row + 1, :] = value[b : b + 1, i * 128 : (i + 1) * 128]


def edge_kernel(
    y, bulk, surf, gains, lift, q_mid, cols, before, after, atm, kept_in, band, q, ends_out, outgoing,
    w, wide, sides, kept, sa, sb, ma, mb, ends, table, sems,
):
    rows = atm.shape[0]
    levels = lift.shape[1]
    fields = bulk.shape[0]
    states = y.shape[0]
    columns = y.shape[1]
    blocks = columns // BLK
    halo = ASTEPS - 1
    count = halo + ASTEPS
    total = blocks + 2 * ASTEPS
    arriving = [
        pltpu.make_async_copy(before, wide.at[0], sems.at[0]),
        pltpu.make_async_copy(after, wide.at[1], sems.at[1]),
        pltpu.make_async_copy(atm.at[:, : 2 * BLK], sides.at[0], sems.at[2]),
        pltpu.make_async_copy(atm.at[:, columns - 2 * BLK :], sides.at[1], sems.at[3]),
    ]
    bands = [pltpu.make_async_copy(band.at[i], w.at[halo + i], sems.at[4 + i]) for i in range(2 * ASTEPS)]
    keeps = pltpu.make_async_copy(kept_in, kept, sems.at[4 + 2 * ASTEPS])
    needed = [[0, 2 * ASTEPS - 1]] + [[i, 2 * ASTEPS - 1 - i] for i in range(1, ASTEPS)]
    for copy in arriving:
        copy.start()
    for group in needed:
        for i in group:
            bands[i].start()
    keeps.start()

    def place(e):
        if e < ASTEPS:
            return wide.at[0], e
        if e >= total - ASTEPS:
            return wide.at[1], e - total + ASTEPS
        return None, e - ASTEPS

    def coefs(e):
        ref, local = place(e)
        at = slice(local * BLK, (local + 1) * BLK)
        if ref is None:
            return bulk[:, at], surf[:, at]
        j = local - 1 if e < ASTEPS else local
        at = slice(j * BLK, (j + 1) * BLK)
        return ref[rows + 12 : rows + 16, at], ref[rows + 4 * j : rows + 4 * j + 4, WIDE - BLK :]

    def build(e):
        ref, local = place(e)
        origin = local * BLK + (columns - WIDE if e < ASTEPS else 0)
        j = local - 1 if e < ASTEPS else local
        at = slice(j * BLK, (j + 1) * BLK)
        ids = ref[rows : rows + 6, at].astype(jnp.int32) - origin
        k = e - 1 if e < ASTEPS else e - (total - 1) + 2 * count
        yield from band_build(ids, ref[rows + 6 : rows + 12, at], w, k)

    for copy in arriving:
        copy.wait()
    for i in range(ASTEPS):
        at = slice(i * BLK, (i + 1) * BLK)
        for side in range(2):
            x = wide[side, :rows, at]
            lifted = [x[(f + 1) * levels - 1 : (f + 1) * levels] for f in range(fields)]
            for k in range(ASTEPS - 1):
                weight = jnp.concatenate([lift[k]] * (BLK // 128), axis=1)
                for f in range(fields):
                    lifted.append(jnp.sum(x[f * levels : (f + 1) * levels] * weight, axis=0, keepdims=True))
            sa[i if side == 0 else 8 + i] = stacked(jnp.concatenate([x] + lifted, axis=0))
    for i in range(2):
        at = slice(i * BLK, (i + 1) * BLK)
        far = slice(columns - (2 - i) * BLK, columns - (1 - i) * BLK)
        sa[ASTEPS + i] = stacked(jnp.concatenate([sides[0, :, at], y[:, at]], axis=0))
        sa[6 + i] = stacked(jnp.concatenate([sides[1, :, at], y[:, far]], axis=0))

    buffers = (sa, sb)
    builds = [itertools.chain(build(1 + i), build(total - 2 - i)) for i in range(halo)]
    interleave(builds[0])
    for s in range(1, ASTEPS + 1):
        source, target = buffers[(s - 1) % 2], buffers[s % 2]
        last = s == ASTEPS

        def finish(side, i, moved, s=s, target=target, last=last):
            e = s + i if side == 0 else total - 1 - s - halo + i
            value = advance(moved[rows:], s, gains, *coefs(e))
            if last:
                q[4 * side + i] = value
                ends[4 * side + i] = stacked(moved[:rows])
            else:
                target[6 * side + i + 2 * side] = stacked(jnp.concatenate([moved[:rows], value], axis=0))

        def band_of(side, i, s=s):
            return s - 1 + i if side == 0 else count + ASTEPS - s + i

        def one(side, i, source=source, finish=finish, band_of=band_of):
            def begin():
                x2 = jnp.concatenate([source[6 * side + i + d] for d in range(3)], axis=1)
                k = band_of(side, i)
                return products(x2, (w[k, 0], w[k, 1]))

            return begin, lambda moved: finish(side, i, moved)

        if s == 1:
            for i in range(halo):
                pieces = [
                    product_pieces([source[6 * side + j + d] for d in range(3)], w.at[band_of(side, j)], m)
                    for side, j, m in ((0, i, ma), (1, halo - i, mb))
                ]
                interleave(itertools.chain(*pieces), *builds[i + 1 : i + 2])
                finish(0, i, ma[...])
                finish(1, halo - i, mb[...])
            for k in needed[0]:
                bands[k].wait()
            in_turn([one(0, halo), one(1, 0)])
            keeps.wait()
        else:
            for k in needed[s - 1]:
                bands[k].wait()
            in_turn([one(side, i) for i in range(ASTEPS) for side in range(2)])
        if not last:
            for i in range(2):
                target[ASTEPS + i] = kept[(s - 1) * 4 + i]
                target[6 + i] = kept[(s - 1) * 4 + 2 + i]
    out = pltpu.make_async_copy(ends, ends_out, sems.at[5 + 2 * ASTEPS])
    out.start()
    send(q, q_mid, cols, outgoing, table)
    out.wait()


def finish_kernel(q_ends, q_mid, vertical, ends_in, mid_in, out, ends, mid, staged, sems, osems):
    rows = ends.shape[1] // 2
    levels = rows // 2
    blocks = staged.shape[0]
    arriving = [
        pltpu.make_async_copy(mid_in, mid, sems.at[0]),
        pltpu.make_async_copy(ends_in, ends, sems.at[1]),
    ]
    for copy in arriving:
        copy.start()

    def leaving(b):
        at = slice(b * BLK, (b + 1) * BLK)
        return pltpu.make_async_copy(staged.at[b], out.at[:, at], osems.at[b])

    def one(b, p):
        ref, i = block_place(b, blocks, ends, mid)
        share, _ = block_place(b, blocks, q_ends, q_mid)

        def begin():
            qh, ql = halves(share[i])
            high = jnp.concatenate([ref[i, p * levels : (p + 1) * levels], qh], axis=0)
            low = jnp.concatenate([ref[i, rows + p * levels : rows + (p + 1) * levels], ql], axis=0)
            return mm(vertical[p], high), mm(vertical[p, :levels], low)

        def finish(value):
            staged[b, p * levels : (p + 1) * levels] = value

        return begin, finish

    middle = list(range(ASTEPS, blocks - ASTEPS))
    outer = list(range(ASTEPS)) + list(range(blocks - ASTEPS, blocks))
    for copy, group in zip(arriving, (middle, outer)):
        copy.wait()
        for start in range(0, len(group), 4):
            some = group[start : start + 4]
            in_turn([one(b, p) for b in some for p in range(2)])
            for b in some:
                leaving(b).start()
    for b in range(blocks):
        leaving(b).wait()


def sea_build(nbr, coef, b, w):
    at = pl.ds(pl.multiple_of(b * BLK, BLK), BLK)

    def store(first, size, lanes, high, low):
        w[0, first : first + size, lanes] = high
        w[1, first : first + size, lanes] = low

    return band_pieces(store, nbr[:, at] - b * BLK, coef[:, at], HO)


def sea_inner_kernel(ocean, nbr, coef, laid_out, x2, wa, wb, ma, mb, laid, sems):
    blocks = ocean.shape[1] // BLK
    around = 1 + 2 * HO // BLK
    first = -(-HO // BLK)
    count = blocks - 2 * first
    for i in range(count + around - 1):
        start = (first + i) * BLK - HO
        x2[i] = stacked(ocean[:, start : start + BLK])

    def leaving(i):
        return pltpu.make_async_copy(laid.at[i], laid_out.at[i], sems.at[i])

    def move(i, w, moved):
        yield from product_pieces([x2[i + d] for d in range(around)], w, moved)

    interleave(sea_build(nbr, coef, first, wa))

    def one(k, _):
        i = 2 * k
        interleave(sea_build(nbr, coef, first + i + 1, wb), move(i, wa, ma))
        interleave(sea_build(nbr, coef, jnp.minimum(i + 2, count - 1) + first, wa), move(i + 1, wb, mb))
        laid[i] = stacked(ma[...])
        laid[i + 1] = stacked(mb[...])
        leaving(i).start()
        leaving(i + 1).start()
        return 0

    lax.fori_loop(0, count // 2, one, 0)

    def done(i, _):
        leaving(i).wait()
        return 0

    lax.fori_loop(0, count, done, 0)


def sea_outer_kernel(
    before, after, nbr, coef, vertical, mix, flux, ocean, laid_in, out, ends, x2, wa, wb, ma, mb, laid, staged, sems, osems
):
    fields = flux.shape[0]
    rows, columns = ocean.shape
    levels = rows // fields
    blocks = columns // BLK
    around = 1 + 2 * HO // BLK
    first = -(-HO // BLK)
    count = blocks - 2 * first
    width = ends.shape[2]
    arriving = [
        pltpu.make_async_copy(ocean.at[:, :width], ends.at[0], sems.at[0]),
        pltpu.make_async_copy(ocean.at[:, columns - width :], ends.at[1], sems.at[1]),
        pltpu.make_async_copy(laid_in, laid.at[first : first + count], sems.at[2]),
    ]
    for copy in arriving:
        copy.start()
    eye = iota((levels, levels), 0) == iota((levels, levels), 1)
    top = jnp.broadcast_to((mix[...] + jnp.where(eye, 1.0, 0.0))[:, 0:1], (levels, BLK))
    outer = list(range(first)) + list(range(blocks - first, blocks))
    bands, sums = (wa, wb), (ma, mb)
    interleave(sea_build(nbr, coef, outer[0], wa))
    arriving[0].wait()
    arriving[1].wait()
    spans = ((before, -HO, HO), (ends.at[0], 0, width), (ends.at[1], columns - width, width), (after, columns, HO))
    held = list(range(first + around - 1)) + list(range(blocks - first, blocks + around - 1))
    for i, e in enumerate(held):
        start = e * BLK - HO
        pieces = []
        for ref, begin, size in spans:
            lo, hi = max(start, begin), min(start + BLK, begin + size)
            if lo < hi:
                pieces.append(ref[:, lo - begin : hi - begin])
        x2[i] = stacked(pieces[0] if len(pieces) == 1 else jnp.concatenate(pieces, axis=1))

    def move(b, w, moved):
        yield from product_pieces([x2[held.index(b + d)] for d in range(around)], w, moved)

    for k, b in enumerate(outer):
        works = [move(b, bands[k % 2], sums[k % 2])]
        if k + 1 < len(outer):
            works.insert(0, sea_build(nbr, coef, outer[k + 1], bands[(k + 1) % 2]))
        interleave(*works)
        laid[b] = stacked(sums[k % 2][...])
    arriving[2].wait()
    pair = 2 * levels

    def leaving(b):
        at = pl.ds(pl.multiple_of(b * BLK, BLK), BLK)
        return pltpu.make_async_copy(staged.at[b], out.at[:, at], osems.at[b])

    def mixed(b, p):
        at = pl.ds(pl.multiple_of(b * BLK, BLK), BLK)

        def begin():
            high = laid[b, p * pair : (p + 1) * pair]
            low = laid[b, rows + p * pair : rows + (p + 1) * pair]
            return mm(vertical[...], high), mm(vertical[:pair], low)

        def finish(value):
            for k in range(2):
                f = 2 * p + k
                staged[b, f * levels : (f + 1) * levels] = (
                    value[k * levels : (k + 1) * levels] + top * flux[f : f + 1, at]
                )

        return begin, finish

    def four(i, _):
        in_turn([mixed(4 * i + k, p) for k in range(4) for p in range(fields // 2)])
        for k in range(4):
            leaving(4 * i + k).start()
        return 0

    lax.fori_loop(0, blocks // 4, four, 0)

    def done(b, _):
        leaving(b).wait()
        return 0

    lax.fori_loop(0, blocks, done, 0)


def after_all(value, *others):
    return lax.optimization_barrier((value, *others))[0]


def per_device(
    atm_state,
    atm_surface,
    bulk_coef,
    atm_nbr,
    atm_nbr_coef,
    atm_mix,
    ocean_state,
    ocean_nbr,
    ocean_nbr_coef,
    ocean_mix,
    send_cols,
    remap_slot,
    remap_weight,
):
    fields, la, columns = atm_state.shape
    lo, cells = ocean_state.shape[1:]
    blocks = columns // BLK
    rows = fields * la
    states = fields * ASTEPS
    picked = send_cols[0]
    peers, slots = picked.shape
    lanes = min(BLK, slots)
    parts = slots // lanes
    atm = atm_state.reshape(rows, columns)
    ocean = ocean_state.reshape(fields * lo, cells)
    depth = lax.axis_size(AXES)
    up = [(i, (i + 1) % depth) for i in range(depth)]
    down = [(j, i) for i, j in up]
    window = BLK + 2 * HA
    vmem = pl.BlockSpec(memory_space=pltpu.VMEM)
    anywhere = pl.BlockSpec(memory_space=pl.ANY)

    depth_k = rows + states
    half = fields // 2
    p_of = np.arange(half)[:, None, None]
    r_of = np.arange(2 * la)[None, :, None]
    c_of = np.arange(2 * la + states)[None, None, :]
    code = np.where(
        c_of < 2 * la,
        (c_of // la == r_of // la) * 1,
        ((c_of - 2 * la) % fields == 2 * p_of + r_of // la) * (2 + (c_of - 2 * la) // fields),
    )
    code = np.broadcast_to(code, (half, 2 * la, 2 * la + states)).astype(np.int32)
    spread = ((c_of[0] % la == np.arange(la)[:, None]) & (c_of[0] < 2 * la)).astype(np.float32)
    sea_spread = (np.arange(2 * lo)[None, :] % lo == np.arange(lo)[:, None]).astype(np.float32)

    wide_rows = rows + 16
    sea_rows = fields * lo
    halo_shapes = (shape((rows, WIDE)),) * 2 + (shape((sea_rows, HO)),) * 2
    wide_first, wide_last, sea_first, sea_last = call(
        pack_kernel,
        (shape((wide_rows, WIDE)),) * 2 + halo_shapes[2:],
        in_specs=[vmem] * 4 + [anywhere] * 2,
        out_specs=(anywhere,) * 4,
        scratch=[pltpu.VMEM(h.shape, F32) for h in halo_shapes]
        + [pltpu.VMEM((2, 16, WIDE), F32), pltpu.SemaphoreType.DMA((10,))],
    )(atm_nbr, atm_nbr_coef, bulk_coef, atm_surface, atm, ocean)
    wide_before = lax.ppermute(wide_last, AXES, up)
    wide_after = lax.ppermute(wide_first, AXES, down)

    y, yo, gains, lift, vertical, sea_vertical = call(
        prepare_kernel(fields),
        (
            shape((states, columns)),
            shape((1, columns)),
            shape((states, 128)),
            shape((ASTEPS - 1, la, 128)),
            shape((half, 4 * la, 2 * la + states), BF),
            shape((4 * lo, 2 * lo), BF),
        ),
        in_specs=[vmem] * 6 + [anywhere],
        scratch=[pltpu.VMEM((lo, cells), F32), pltpu.SemaphoreType.DMA(())],
    )(
        after_all(atm_mix, wide_first),
        ocean_mix,
        atm,
        jnp.asarray(spread),
        jnp.asarray(code),
        jnp.asarray(sea_spread),
        ocean,
    )

    ends = 2 * ASTEPS
    q_mid, kept, mid, band = call(
        interior_kernel,
        (
            shape((blocks - ends, states, BLK)),
            shape((4 * (ASTEPS - 1), 2 * depth_k, BLK), BF),
            shape((blocks - ends, 2 * rows, BLK), BF),
            shape((ends, 2, window, BLK), BF),
        ),
        in_specs=[vmem] * 7,
        out_specs=(vmem, anywhere, anywhere, anywhere),
        scratch=[
            pltpu.VMEM((blocks, 2, window, BLK), BF),
            pltpu.VMEM((blocks, 2 * depth_k, BLK), BF),
            pltpu.VMEM((blocks, 2 * depth_k, BLK), BF),
            pltpu.VMEM((depth_k, BLK), F32),
            pltpu.VMEM((depth_k, BLK), F32),
            pltpu.VMEM((4 * (ASTEPS - 1), 2 * depth_k, BLK), BF),
            pltpu.VMEM((blocks - ends, 2 * rows, BLK), BF),
            pltpu.SemaphoreType.DMA((ends + ASTEPS,)),
        ],
    )(atm, y, atm_nbr, atm_nbr_coef, bulk_coef, atm_surface, gains)

    sea_blocks = cells // BLK
    outer = -(-HO // BLK)
    around = 1 + 2 * HO // BLK
    sea_window = BLK + 2 * HO
    inner = sea_blocks - 2 * outer
    sea_inner = call(
        sea_inner_kernel,
        shape((inner, 2 * sea_rows, BLK), BF),
        in_specs=[vmem] * 3,
        out_specs=anywhere,
        scratch=[
            pltpu.VMEM((inner + around - 1, 2 * sea_rows, BLK), BF),
            pltpu.VMEM((2, sea_window, BLK), BF),
            pltpu.VMEM((2, sea_window, BLK), BF),
            pltpu.VMEM((sea_rows, BLK), F32),
            pltpu.VMEM((sea_rows, BLK), F32),
            pltpu.VMEM((inner, 2 * sea_rows, BLK), BF),
            pltpu.SemaphoreType.DMA((inner,)),
        ],
    )(ocean, after_all(ocean_nbr, q_mid), ocean_nbr_coef)

    sea_first, sea_last, wide_before, wide_after = lax.optimization_barrier(
        (sea_first, sea_last, wide_before, wide_after, sea_inner)
    )[:4]
    sea_before = lax.ppermute(sea_last, AXES, up)
    sea_after = lax.ppermute(sea_first, AXES, down)

    q_ends, tips, outgoing = call(
        edge_kernel,
        (
            shape((ends, states, BLK)),
            shape((ends, 2 * rows, BLK), BF),
            shape((peers, parts * fields, lanes)),
        ),
        in_specs=[vmem] * 7 + [anywhere] * 5,
        out_specs=(vmem, anywhere, vmem),
        scratch=[
            pltpu.VMEM((2 * (2 * ASTEPS - 1), 2, window, BLK), BF),
            pltpu.VMEM((2, wide_rows, WIDE), F32),
            pltpu.VMEM((2, rows, 2 * BLK), F32),
            pltpu.VMEM((4 * (ASTEPS - 1), 2 * depth_k, BLK), BF),
            pltpu.VMEM((12, 2 * depth_k, BLK), BF),
            pltpu.VMEM((12, 2 * depth_k, BLK), BF),
            pltpu.VMEM((depth_k, BLK), F32),
            pltpu.VMEM((depth_k, BLK), F32),
            pltpu.VMEM((ends, 2 * rows, BLK), BF),
            pltpu.VMEM((blocks * fields, BLK), F32),
            pltpu.SemaphoreType.DMA((6 + 2 * ASTEPS,)),
        ],
    )(after_all(y, sea_inner), bulk_coef, atm_surface, gains, lift, q_mid, picked, wide_before, wide_after, atm, kept, band)

    sea_before, sea_after, outgoing = lax.optimization_barrier((sea_before, sea_after, outgoing))
    received = lax.all_to_all(outgoing, AXES, split_axis=0, concat_axis=0, tiled=True)

    atm_final = call(
        finish_kernel,
        shape((rows, columns)),
        in_specs=[vmem] * 3 + [anywhere] * 2,
        out_specs=anywhere,
        scratch=[
            pltpu.VMEM((ends, 2 * rows, BLK), BF),
            pltpu.VMEM((blocks - ends, 2 * rows, BLK), BF),
            pltpu.VMEM((blocks, rows, BLK), F32),
            pltpu.SemaphoreType.DMA((2,)),
            pltpu.SemaphoreType.DMA((blocks,)),
        ],
    )(after_all(q_ends, outgoing), q_mid, vertical, tips, mid)

    sea_row = call(
        sea_row_kernel,
        shape((1, cells)),
        in_specs=[vmem] * 4 + [anywhere] * 2,
        scratch=[
            pltpu.VMEM((cells // 128 + 2 * HO // 128, 8, 128), F32),
            pltpu.VMEM((2, lo, HO), F32),
            pltpu.SemaphoreType.DMA((2,)),
        ],
    )(after_all(yo, atm_final), ocean_nbr, ocean_nbr_coef, ocean_mix, sea_before, sea_after)

    flux, back = call(
        exchange_kernel,
        (shape((fields, cells)), shape((peers, 2 * parts, lanes))),
        in_specs=[vmem] * 5,
        scratch=[
            pltpu.VMEM((2 * peers * parts * fields, lanes), BF),
            pltpu.VMEM((cells // BLK, lanes, remap_slot.shape[0] * BLK), BF),
            pltpu.VMEM((1, cells), F32),
            pltpu.VMEM((4 * peers * parts, lanes), F32),
        ],
    )(after_all(received, sea_row), remap_slot, remap_weight, sea_row, ocean_mix)
    returned = lax.all_to_all(back, AXES, split_axis=0, concat_axis=0, tiled=True)

    ocean_final = call(
        sea_outer_kernel,
        shape((sea_rows, cells)),
        in_specs=[vmem] * 7 + [anywhere] * 2,
        out_specs=anywhere,
        scratch=[
            pltpu.VMEM((2, sea_rows, (outer + around - 1) * BLK - HO), F32),
            pltpu.VMEM((2 * (outer + around - 1), 2 * sea_rows, BLK), BF),
            pltpu.VMEM((2, sea_window, BLK), BF),
            pltpu.VMEM((2, sea_window, BLK), BF),
            pltpu.VMEM((sea_rows, BLK), F32),
            pltpu.VMEM((sea_rows, BLK), F32),
            pltpu.VMEM((sea_blocks, 2 * sea_rows, BLK), BF),
            pltpu.VMEM((sea_blocks, sea_rows, BLK), F32),
            pltpu.SemaphoreType.DMA((3,)),
            pltpu.SemaphoreType.DMA((sea_blocks,)),
        ],
    )(
        after_all(sea_before, back),
        sea_after,
        ocean_nbr,
        ocean_nbr_coef,
        sea_vertical,
        ocean_mix,
        flux,
        ocean,
        sea_inner,
    )

    surface_temp = call(
        settle_kernel,
        shape((columns // 128, 128)),
        in_specs=[vmem] * 3,
        scratch=[pltpu.VMEM((4 * blocks, BLK), F32)],
    )(after_all(returned, ocean_final), picked, atm_surface)

    return (
        atm_final.reshape(fields, la, columns),
        ocean_final.reshape(fields, lo, cells),
        surface_temp.reshape(columns),
    )


def solution(mesh):
    placed = (
        P(None, None, AXES),
        P(None, AXES),
        P(None, AXES),
        P(None, AXES),
        P(None, AXES),
        P(),
        P(None, None, AXES),
        P(None, AXES),
        P(None, AXES),
        P(),
        P(AXES, None, None),
        P(None, AXES),
        P(None, AXES),
    )
    return jax.shard_map(
        per_device,
        mesh=mesh,
        in_specs=placed,
        out_specs=(P(None, None, AXES), P(None, None, AXES), P(AXES)),
        check_vma=False,
    )
```
